32 devices in a mesh: dp: 2 (over z_hi), head: 8 (over y, x, core), state: 2 (over z_lo).
Axes of the slice: x: 2, y: 2, z: 4 (z_hi: 2, z_lo: 2; z = z_hi * 2 + z_lo), core: 2. Of those that a mesh axis runs over, the one named last changes fastest.
Arguments:
- hidden: bfloat16 [4096, 2048], P(('dp', 'state')), may hold values from -6 to 6
- embedding: bfloat16 [4096, 2048], P(('dp', 'state')), may hold values from -6 to 6
- cotangent: bfloat16 [4096, 2048], P('dp'), may hold values from -6 to 6
- lengths: int32 [2, 4], P('dp'), may hold values from 1 to 1024, as said below
- gain_attn: bfloat16 [4096], P(('dp', 'state')), may hold values from 0.5 to 1.5
- w_query: bfloat16 [4096, 4096], P(('dp', 'state'), 'head'), may hold values from -0.09375 to 0.09375
- w_key: bfloat16 [4096, 4096], P(('dp', 'state'), 'head'), may hold values from -0.09375 to 0.09375
- w_value: bfloat16 [4096, 4096], P(('dp', 'state'), 'head'), may hold values from -0.09375 to 0.09375
- down_query: bfloat16 [4096, 128], P(('dp', 'state')), may hold values from -0.09375 to 0.09375
- down_key: bfloat16 [4096, 128], P(('dp', 'state')), may hold values from -0.09375 to 0.09375
- down_value: bfloat16 [4096, 128], P(('dp', 'state')), may hold values from -0.09375 to 0.09375
- up_query: bfloat16 [128, 4096], P(('dp', 'state'), 'head'), may hold values from -0.5 to 0.5
- up_key: bfloat16 [128, 4096], P(('dp', 'state'), 'head'), may hold values from -0.5 to 0.5
- up_value: bfloat16 [128, 4096], P(('dp', 'state'), 'head'), may hold values from -0.5 to 0.5
- attn_output: bfloat16 [4096, 2048], P('head', ('dp', 'state')), may hold values from -0.25 to 0.25
- gain_mlp: bfloat16 [2048], P(('dp', 'state')), may hold values from 0.5 to 1.5
- mlp_input: bfloat16 [2048, 8192], P(('dp', 'state'), 'head'), may hold values from -0.125 to 0.125
- down_mlp: bfloat16 [2048, 128], P(('dp', 'state')), may hold values from -0.125 to 0.125
- up_mlp: bfloat16 [128, 8192], P(('dp', 'state'), 'head'), may hold values from -0.5 to 0.5
- mlp_output: bfloat16 [8192, 2048], P('head', ('dp', 'state')), may hold values from -0.0625 to 0.0625
- gain_mixer: bfloat16 [2048], P(('dp', 'state')), may hold values from 0.5 to 1.5
- proj_inner: bfloat16 [2048, 4096], P(('dp', 'state'), 'head'), may hold values from -0.125 to 0.125
- proj_gate: bfloat16 [2048, 4096], P(('dp', 'state'), 'head'), may hold values from -0.125 to 0.125
- proj_step: bfloat16 [2048, 64], P(('dp', 'state'), 'head'), may hold values from -0.125 to 0.125
- proj_input: bfloat16 [2048, 64], replicated, may hold values from -0.125 to 0.125
- proj_read: bfloat16 [2048, 64], replicated, may hold values from -0.125 to 0.125
- taps_inner: bfloat16 [4, 4096], P(None, 'head'), may hold values from -3 to 3
- taps_input: bfloat16 [4, 64], replicated, may hold values from -3 to 3
- taps_read: bfloat16 [4, 64], replicated, may hold values from -3 to 3
- step_bias: bfloat16 [64], P('head'), may hold values from -4 to -1
- log_rate: bfloat16 [64], P('head'), may hold values from -2.5 to 1.5
- skip_gain: bfloat16 [64], P('head'), may hold values from 0.5 to 1.5
- gain_gated: bfloat16 [4096], P('head'), may hold values from 0.5 to 1.5
- proj_output: bfloat16 [4096, 2048], P('head', ('dp', 'state')), may hold values from -0.09375 to 0.09375
Outputs:
- layer_out: bfloat16 [4096, 2048], P('dp')
- grad_hidden: bfloat16 [4096, 2048], P(('dp', 'state'))
- grad_embedding: bfloat16 [4096, 2048], P(('dp', 'state'))
- grad_gain_attn: float32 [4096], P(('dp', 'state'))
- grad_w_query: float32 [4096, 4096], P(('dp', 'state'), 'head')
- grad_w_key: float32 [4096, 4096], P(('dp', 'state'), 'head')
- grad_w_value: float32 [4096, 4096], P(('dp', 'state'), 'head')
- grad_down_query: float32 [4096, 128], P(('dp', 'state'))
- grad_down_key: float32 [4096, 128], P(('dp', 'state'))
- grad_down_value: float32 [4096, 128], P(('dp', 'state'))
- grad_up_query: float32 [128, 4096], P(('dp', 'state'), 'head')
- grad_up_key: float32 [128, 4096], P(('dp', 'state'), 'head')
- grad_up_value: float32 [128, 4096], P(('dp', 'state'), 'head')
- grad_attn_output: float32 [4096, 2048], P('head', ('dp', 'state'))
- grad_gain_mlp: float32 [2048], P(('dp', 'state'))
- grad_mlp_input: float32 [2048, 8192], P(('dp', 'state'), 'head')
- grad_down_mlp: float32 [2048, 128], P(('dp', 'state'))
- grad_up_mlp: float32 [128, 8192], P(('dp', 'state'), 'head')
- grad_mlp_output: float32 [8192, 2048], P('head', ('dp', 'state'))
- grad_gain_mixer: float32 [2048], P(('dp', 'state'))
- grad_proj_inner: float32 [2048, 4096], P(('dp', 'state'), 'head')
- grad_proj_gate: float32 [2048, 4096], P(('dp', 'state'), 'head')
- grad_proj_step: float32 [2048, 64], P(('dp', 'state'), 'head')
- grad_proj_input: float32 [2048, 64], replicated
- grad_proj_read: float32 [2048, 64], replicated
- grad_taps_inner: float32 [4, 4096], P(None, 'head')
- grad_taps_input: float32 [4, 64], replicated
- grad_taps_read: float32 [4, 64], replicated
- grad_step_bias: float32 [64], P('head')
- grad_log_rate: float32 [64], P('head')
- grad_skip_gain: float32 [64], P('head')
- grad_gain_gated: float32 [4096], P('head')
- grad_proj_output: float32 [4096, 2048], P('head', ('dp', 'state'))
- grad_norm: float32 [], replicated
The draws below stay inside these ranges and needn't reach their ends.
Inputs may be any that keep to these rules, and one draw needn't show every extreme that they name: `lengths`: each row has 4 documents and a padding tail of 1 to 256 positions; the second document starts before position 768 and ends at or after position 1280.
All inputs are finite; a program needn't handle non-finite values.
Results may differ from the reference program's by a relative error of at most 0.028.
The reference program's roundings to bfloat16 on the way count: a program that leaves them out, or rounds other values in their place, can miss the bound.
Values may be sent and summed in bfloat16 or wider, within the bound.
No kernel may reach another device: no remote copies, remote signals or barrier semaphores. Data moves between devices by JAX's collectives and lax.ppermute only.
A program may use at most 448 MiB of HBM per device.

```python
import jax
import jax.numpy as jnp
from jax import lax

D = 2048
CAT = 4096
HDIM = 128
ATT = 4096
FFN = 8192
RANK = 128
MHEADS = 64
MDIM = 64
DIN = 4096
NSTATE = 64
CONV = 4
GROUP = 256
LENGTH = 2048
TOKENS = 4096
N_DP = 2


def draw_lengths(key, part):
    key = jax.random.fold_in(key, 7)
    keys = jax.random.split(key, 5)
    second = jax.random.randint(keys[0], (N_DP,), 5 * LENGTH // 8, 6 * LENGTH // 8)
    span = jax.random.randint(keys[1], (N_DP,), 3 * LENGTH // 8, LENGTH // 2 + 1)
    chosen = jax.random.randint(keys[4], (), 0, N_DP)
    rows = jnp.arange(N_DP, dtype=jnp.int32)
    span = jnp.where(rows == chosen, LENGTH // 2, span)
    first = second - span
    padding = jax.random.randint(keys[2], (N_DP,), 1, LENGTH // 8 + 1)
    used = LENGTH - padding
    third = jax.random.randint(keys[3], (N_DP,), second + 1, used)
    return jnp.stack([first, second - first, third - second, used - third], 1).astype(jnp.int32)


def shard_levels(stream_key, dims, cuts, least, high):
    def one(dim, parts):
        draws = jax.random.uniform(jax.random.fold_in(jax.random.fold_in(stream_key, 6), dim), (parts,), jnp.float32, least / len(cuts), high / len(cuts))
        return jnp.repeat(jnp.exp(draws), dims[dim] // parts).reshape((-1,) + (1,) * (len(dims) - dim - 1))

    loudness = one(*cuts[0])
    for cut in cuts[1:]:
        loudness = loudness * one(*cut)
    return loudness


def gaussian(own_key, extent, deviation, most, cuts=(), kind=jnp.bfloat16):
    factor_of = shard_levels(own_key, extent, cuts, -0.22, 0.18) if cuts else 1.0
    values = jax.random.normal(own_key, extent, jnp.float32) * deviation * factor_of
    return jnp.minimum(jnp.maximum(values, -most), most).astype(kind)


def setup_inputs(seed: int = 0) -> dict:
    arg_keys = jax.random.split(jax.random.key(seed), 35)
    return {
        "hidden": gaussian(arg_keys[0], (TOKENS, D), 1.0, 6.0, ((0, 4),)),
        "embedding": gaussian(arg_keys[1], (TOKENS, D), 1.0, 6.0, ((0, 4),)),
        "cotangent": gaussian(arg_keys[2], (TOKENS, D), 1.0, 6.0, ((0, 2),)),
        "lengths": draw_lengths(jax.random.fold_in(arg_keys[34], 71), 0),
        "gain_attn": jnp.clip(1.0 + 0.1 * jax.random.normal(arg_keys[4], (CAT,), jnp.float32), 0.5, 1.5).astype(jnp.bfloat16),
        "w_query": gaussian(arg_keys[5], (CAT, ATT), CAT ** -0.5, 0.09375, ((0, 4), (1, 8))),
        "w_key": gaussian(arg_keys[6], (CAT, ATT), CAT ** -0.5, 0.09375, ((0, 4), (1, 8))),
        "w_value": gaussian(arg_keys[7], (CAT, ATT), CAT ** -0.5, 0.09375, ((0, 4), (1, 8))),
        "down_query": gaussian(arg_keys[8], (CAT, RANK), CAT ** -0.5, 0.09375, ((0, 4),)),
        "down_key": gaussian(arg_keys[9], (CAT, RANK), CAT ** -0.5, 0.09375, ((0, 4),)),
        "down_value": gaussian(arg_keys[10], (CAT, RANK), CAT ** -0.5, 0.09375, ((0, 4),)),
        "up_query": gaussian(arg_keys[11], (RANK, ATT), RANK ** -0.5, 0.5, ((0, 4), (1, 8))),
        "up_key": gaussian(arg_keys[12], (RANK, ATT), RANK ** -0.5, 0.5, ((0, 4), (1, 8))),
        "up_value": gaussian(arg_keys[13], (RANK, ATT), RANK ** -0.5, 0.5, ((0, 4), (1, 8))),
        "attn_output": gaussian(arg_keys[14], (ATT, D), (ATT // 8) ** -0.5, 0.25, ((0, 8), (1, 4))),
        "gain_mlp": jnp.clip(1.0 + 0.1 * jax.random.normal(arg_keys[15], (D,), jnp.float32), 0.5, 1.5).astype(jnp.bfloat16),
        "mlp_input": gaussian(arg_keys[16], (D, FFN), D ** -0.5, 0.125, ((0, 4), (1, 8))),
        "down_mlp": gaussian(arg_keys[17], (D, RANK), D ** -0.5, 0.125, ((0, 4),)),
        "up_mlp": gaussian(arg_keys[18], (RANK, FFN), RANK ** -0.5, 0.5, ((0, 4), (1, 8))),
        "mlp_output": gaussian(arg_keys[19], (FFN, D), FFN ** -0.5, 0.0625, ((0, 8), (1, 4))),
        "gain_mixer": jnp.clip(1.0 + 0.1 * jax.random.normal(arg_keys[20], (D,), jnp.float32), 0.5, 1.5).astype(jnp.bfloat16),
        "proj_inner": gaussian(arg_keys[21], (D, DIN), D ** -0.5, 0.125, ((0, 4), (1, 8))),
        "proj_gate": gaussian(arg_keys[22], (D, DIN), D ** -0.5, 0.125, ((0, 4), (1, 8))),
        "proj_step": gaussian(arg_keys[23], (D, MHEADS), D ** -0.5, 0.125, ((0, 4), (1, 8))),
        "proj_input": gaussian(arg_keys[24], (D, NSTATE), D ** -0.5, 0.125),
        "proj_read": gaussian(arg_keys[25], (D, NSTATE), D ** -0.5, 0.125),
        "taps_inner": gaussian(arg_keys[26], (CONV, DIN), CONV ** -0.5, 3.0, ((1, 8),)),
        "taps_input": gaussian(arg_keys[27], (CONV, NSTATE), CONV ** -0.5, 3.0),
        "taps_read": gaussian(arg_keys[28], (CONV, NSTATE), CONV ** -0.5, 3.0),
        "step_bias": jnp.clip(-4.0 + 3.0 * jax.random.uniform(arg_keys[29], (MHEADS,), jnp.float32) ** shard_levels(arg_keys[29], (MHEADS,), ((0, 8),), -0.2, 0.2), -4.0, -1.0).astype(jnp.bfloat16),
        "log_rate": jnp.clip(-2.5 + 4.0 * jax.random.uniform(arg_keys[30], (MHEADS,), jnp.float32) ** shard_levels(arg_keys[30], (MHEADS,), ((0, 8),), -0.2, 0.2), -2.5, 1.5).astype(jnp.bfloat16),
        "skip_gain": jnp.clip(0.5 + 1.0 * jax.random.uniform(arg_keys[31], (MHEADS,), jnp.float32) ** shard_levels(arg_keys[31], (MHEADS,), ((0, 8),), -0.2, 0.2), 0.5, 1.5).astype(jnp.bfloat16),
        "gain_gated": jnp.clip(1.0 + 0.1 * jax.random.normal(arg_keys[32], (DIN,), jnp.float32), 0.5, 1.5).astype(jnp.bfloat16),
        "proj_output": gaussian(arg_keys[33], (DIN, D), DIN ** -0.5, 0.09375, ((0, 8), (1, 4))),
    }


@jax.custom_vjp
def low(v):
    return lax.optimization_barrier(v.astype(jnp.bfloat16)).astype(jnp.float32)

@jax.custom_vjp
def low_back(v):
    return v

def low_keep(v):
    return (low(v), None)

def low_pass(kept, grad):
    return (grad,)

def back_keep(v):
    return (v, None)

def back_low(kept, grad):
    return (low(grad),)
low.defvjp(low_keep, low_pass)
low_back.defvjp(back_keep, back_low)
highest = lax.Precision.HIGHEST
epsilon = 1e-05

def exact_dot(left, right):
    return jnp.dot(left, right, precision=highest)

def rms_norm(values, gain):
    return values * lax.rsqrt(lax.optimization_barrier(jnp.mean(values * values, -1, keepdims=True)) + epsilon) * gain

def row_layout(doc_lengths, length):
    ends = jnp.cumsum(doc_lengths).astype(jnp.int32)
    places = jnp.arange(length, dtype=jnp.int32)
    segment = lax.optimization_barrier(jnp.sum((places[:, None] >= ends[None, :]).astype(jnp.int32), axis=1)).astype(jnp.int32)
    starts = jnp.concatenate([ends - doc_lengths, ends[-1:]]).astype(jnp.int32)
    choose = segment[:, None] == jnp.arange(starts.shape[0], dtype=jnp.int32)[None, :]
    first_place = lax.optimization_barrier(jnp.sum(jnp.where(choose, starts[None, :], 0), axis=1)).astype(jnp.int32)
    position = (places - first_place).astype(jnp.float32)
    valid = (segment < doc_lengths.shape[0]).astype(jnp.float32)
    return (segment, position, valid)

def rotate(values, position):
    half = values.shape[-1] // 2
    freqs = 10000.0 ** (-jnp.arange(half, dtype=jnp.float32) / half)
    angle = position[:, None] * freqs[None, :]
    cosine = jnp.cos(angle)[:, None, :]
    sine = jnp.sin(angle)[:, None, :]
    former = values[..., :half]
    latter = values[..., half:]
    return jnp.concatenate([former * cosine - latter * sine, former * sine + latter * cosine], -1)

def attend_head(queries, keys, values, query_seg, key_seg, query_place, key_place):
    scale = queries.shape[-1] ** (-0.5)
    scores = low_back(jnp.dot(queries, keys.T, precision=highest) * scale)
    allowed = (query_seg[:, None] == key_seg[None, :]) & (key_place[None, :] <= query_place[:, None])
    scores = jnp.where(allowed, scores, -1e+30)
    shifted = scores - lax.optimization_barrier(jnp.max(scores, -1, keepdims=True))
    weights = jnp.exp(shifted)
    probs = low(weights / lax.optimization_barrier(jnp.sum(weights, -1, keepdims=True)))
    return low(low_back(jnp.dot(probs, values, precision=highest)))

def conv_mask(values, taps, segment):
    total = taps[0][None, :] * values
    for offset in range(1, taps.shape[0]):
        moved = jnp.concatenate([jnp.zeros((offset, values.shape[1]), values.dtype), values[:-offset]], 0)
        moved_seg = jnp.concatenate([jnp.full((offset,), -1, jnp.int32), segment[:-offset]], 0)
        same = (moved_seg == segment).astype(values.dtype)[:, None]
        total = total + taps[offset][None, :] * moved * same
    return total

def state_scan(inputs, step_sizes, decay, input_vecs, read_vecs, segment, block):
    length, heads, width = inputs.shape
    count = length // block
    states = input_vecs.shape[1]

    def one_block(carry, pieces):
        state, before = carry
        group_in, group_dt, group_b, group_c, group_seg = pieces
        logs = group_dt * decay[None, :]
        cumul = jnp.cumsum(logs, 0)
        places = jnp.arange(block, dtype=jnp.int32)
        allowed = (group_seg[:, None] == group_seg[None, :]) & (places[None, :] <= places[:, None])
        gaps = cumul[:, None, :] - cumul[None, :, :]
        fading = jnp.where(allowed[:, :, None], jnp.exp(jnp.where(allowed[:, :, None], gaps, 0.0)), 0.0)
        inner = jnp.dot(group_c, group_b.T, precision=highest)
        scaled = group_in * group_dt[:, :, None]
        local_out = jnp.einsum('tsh,shp->thp', inner[:, :, None] * fading, scaled, precision=highest)
        carried = (group_seg == before).astype(inputs.dtype)
        entry = jnp.exp(cumul) * carried[:, None]
        from_state = jnp.einsum('tn,hnp->thp', group_c, state, precision=highest) * entry[:, :, None]
        last_seg = group_seg[-1]
        reach = (group_seg == last_seg).astype(inputs.dtype)
        to_end = jnp.exp(cumul[-1][None, :] - cumul) * reach[:, None]
        retain = jnp.exp(cumul[-1]) * (last_seg == before).astype(inputs.dtype)
        fresh = jnp.einsum('sn,sh,shp->hnp', group_b, to_end, scaled, precision=highest)
        state = state * retain[:, None, None] + fresh
        return ((state, last_seg), local_out + from_state)
    pieces = (inputs.reshape(count, block, heads, width), step_sizes.reshape(count, block, heads), input_vecs.reshape(count, block, states), read_vecs.reshape(count, block, states), segment.reshape(count, block))
    start = (jnp.zeros((heads, states, width), inputs.dtype), jnp.array(-1, jnp.int32))
    unused, outputs = lax.scan(jax.checkpoint(one_block), start, pieces)
    return outputs.reshape(length, heads, width)

def mixer_core(inner_pre, input_pre, read_pre, step_pre, taps_x, taps_b, taps_c, shift_in, rate_in, segment, width, block):
    inner_conv = jax.nn.silu(conv_mask(inner_pre, taps_x, segment))
    input_conv = jax.nn.silu(conv_mask(input_pre, taps_b, segment))
    read_conv = jax.nn.silu(conv_mask(read_pre, taps_c, segment))
    step_sizes = jax.nn.softplus(step_pre + shift_in[None, :])
    heads = step_sizes.shape[1]
    length = inner_conv.shape[0]
    outputs = state_scan(inner_conv.reshape(length, heads, width), step_sizes, -jnp.exp(rate_in), input_conv, read_conv, segment, block)
    return (outputs.reshape(length, heads * width), inner_conv)

def forward_row(weights, hidden, embedding, segment, position, valid):
    gain_attn, w_query, w_key, w_value, down_query, down_key, down_value, up_query, up_key, up_value, attn_output, gain_mlp, mlp_input, down_mlp, up_mlp, mlp_output, gain_mixer, proj_inner, proj_gate, proj_step, proj_input, proj_read, taps_inner, taps_input, taps_read, step_bias, log_rate, skip_gain, gain_gated, proj_output = weights
    length = hidden.shape[0]
    joined = jnp.concatenate([hidden, embedding], -1)
    normed = low(rms_norm(joined, gain_attn))

    def project(main, down, upper):
        reduced = low(low_back(exact_dot(normed, down)))
        return low_back(exact_dot(normed, main) + exact_dot(reduced, upper))
    head_count = w_query.shape[1] // HDIM
    queries = low(rotate(project(w_query, down_query, up_query).reshape(length, head_count, HDIM), position))
    keys = low(rotate(project(w_key, down_key, up_key).reshape(length, head_count, HDIM), position))
    values = low(project(w_value, down_value, up_value).reshape(length, head_count, HDIM))
    places = jnp.arange(length, dtype=jnp.int32)

    def one_head(triple):
        return attend_head(triple[0], triple[1], triple[2], segment, segment, places, places)
    mixed = lax.map(jax.checkpoint(one_head), (jnp.moveaxis(queries, 1, 0), jnp.moveaxis(keys, 1, 0), jnp.moveaxis(values, 1, 0)))
    attended = jnp.moveaxis(mixed, 0, 1).reshape(length, head_count * HDIM)
    first = hidden + valid[:, None] * low_back(exact_dot(attended, attn_output))
    mlp_normed = low(rms_norm(first, gain_mlp))
    reduced_mlp = low(low_back(exact_dot(mlp_normed, down_mlp)))
    hidden_pre = low_back(exact_dot(mlp_normed, mlp_input) + exact_dot(reduced_mlp, up_mlp))
    activated = low(jax.nn.gelu(hidden_pre, approximate=False))
    second = first + valid[:, None] * low_back(exact_dot(activated, mlp_output))
    mixer_normed = low(rms_norm(second, gain_mixer))
    inner_pre = exact_dot(mixer_normed, proj_inner)
    gate_pre = exact_dot(mixer_normed, proj_gate)
    step_pre = exact_dot(mixer_normed, proj_step)
    input_pre = exact_dot(mixer_normed, proj_input)
    read_pre = exact_dot(mixer_normed, proj_read)
    scanned, inner_conv = mixer_core(inner_pre, input_pre, read_pre, step_pre, taps_inner, taps_input, taps_read, step_bias, log_rate, segment, MDIM, GROUP)
    skip_full = jnp.repeat(skip_gain, MDIM)
    united = (scanned + skip_full[None, :] * inner_conv) * jax.nn.silu(gate_pre)
    gated = low(rms_norm(united, gain_gated))
    return second + valid[:, None] * low_back(exact_dot(gated, proj_output))

def reference(hidden, embedding, cotangent, lengths, gain_attn, w_query, w_key, w_value, down_query, down_key, down_value, up_query, up_key, up_value, attn_output, gain_mlp, mlp_input, down_mlp, up_mlp, mlp_output, gain_mixer, proj_inner, proj_gate, proj_step, proj_input, proj_read, taps_inner, taps_input, taps_read, step_bias, log_rate, skip_gain, gain_gated, proj_output):
    weights = tuple((tensor.astype(jnp.float32) for tensor in (gain_attn, w_query, w_key, w_value, down_query, down_key, down_value, up_query, up_key, up_value, attn_output, gain_mlp, mlp_input, down_mlp, up_mlp, mlp_output, gain_mixer, proj_inner, proj_gate, proj_step, proj_input, proj_read, taps_inner, taps_input, taps_read, step_bias, log_rate, skip_gain, gain_gated, proj_output)))
    row_total = lengths.shape[0]
    length = hidden.shape[0] // row_total
    totals = tuple((jnp.zeros_like(tensor) for tensor in weights))
    outputs, hidden_grads, embed_grads = ([], [], [])
    for row_index in range(row_total):
        segment, position, valid = row_layout(lengths[row_index], length)
        lower = row_index * length
        hidden_row = hidden[lower:lower + length].astype(jnp.float32)
        embed_row = embedding[lower:lower + length].astype(jnp.float32)

        def closure(params, hidden_in, embed_in):
            return forward_row(params, hidden_in, embed_in, segment, position, valid)
        result, pullback = jax.vjp(closure, weights, hidden_row, embed_row)
        grad_weights, grad_row, grad_embed = pullback(cotangent[lower:lower + length].astype(jnp.float32))
        totals = tuple((total + grad for total, grad in zip(totals, grad_weights)))
        outputs.append(result)
        hidden_grads.append(grad_row)
        embed_grads.append(grad_embed)
    shared = [1, 2, 3, 4, 5, 6, 7, 8, 9, 10, 12, 13, 14, 15]
    squares = jnp.zeros((), jnp.float32)
    for index in shared:
        squares = squares + jnp.sum(totals[index] * totals[index])
    layer_out = jnp.concatenate(outputs, 0).astype(jnp.bfloat16)
    grad_hidden = jnp.concatenate(hidden_grads, 0).astype(jnp.bfloat16)
    grad_embedding = jnp.concatenate(embed_grads, 0).astype(jnp.bfloat16)
    return (layer_out, grad_hidden, grad_embedding, totals[0], totals[1], totals[2], totals[3], totals[4], totals[5], totals[6], totals[7], totals[8], totals[9], totals[10], totals[11], totals[12], totals[13], totals[14], totals[15], totals[16], totals[17], totals[18], totals[19], totals[20], totals[21], totals[22], totals[23], totals[24], totals[25], totals[26], totals[27], totals[28], totals[29], jnp.sqrt(squares))
```

```python
import jax
import jax.numpy as jnp
from jax import lax
from jax.sharding import PartitionSpec as P

HDIM = 128
MDIM = 64
DIN = 4096
GROUP = 256
DP, HEAD, STATE = "dp", "head", "state"
ZED = (DP, STATE)
EVERY = (DP, HEAD, STATE)


highest = lax.Precision.HIGHEST
epsilon = 1e-05


def plain_dot(left, right):
    return jnp.dot(left, right, preferred_element_type=jnp.float32)


def left_dot(left, right):
    return lax.dot_general(
        left, right, (((0,), (0,)), ((), ())), preferred_element_type=jnp.float32
    )


def right_dot(left, right):
    return lax.dot_general(
        left, right, (((1,), (1,)), ((), ())), preferred_element_type=jnp.float32
    )


def exact_left(left, right):
    return lax.dot_general(
        left.astype(jnp.float32), right, (((0,), (0,)), ((), ())), precision=highest
    )


def exact_right(left, right):
    return lax.dot_general(
        left, right.astype(jnp.float32), (((1,), (1,)), ((), ())), precision=highest
    )


def rms_norm(values, gain):
    return values * lax.rsqrt(jnp.mean(values * values, -1, keepdims=True) + epsilon) * gain


def row_layout(doc_lengths, length):
    ends = jnp.cumsum(doc_lengths)
    places = jnp.arange(length, dtype=jnp.int32)
    segment = jnp.sum((places[:, None] >= ends[None, :]).astype(jnp.int32), axis=1)
    starts = jnp.concatenate([ends - doc_lengths, ends[-1:]])
    choose = segment[:, None] == jnp.arange(starts.shape[0], dtype=jnp.int32)[None, :]
    first_place = jnp.sum(jnp.where(choose, starts[None, :], 0), axis=1)
    position = (places - first_place).astype(jnp.float32)
    valid = (segment < doc_lengths.shape[0]).astype(jnp.float32)
    return (segment, position, valid)


def rotate(values, position):
    half = values.shape[-1] // 2
    freqs = 10000.0 ** (-jnp.arange(half, dtype=jnp.float32) / half)
    angle = position[:, None] * freqs[None, :]
    cosine = jnp.cos(angle)[:, None, :]
    sine = jnp.sin(angle)[:, None, :]
    former = values[..., :half]
    latter = values[..., half:]
    return jnp.concatenate([former * cosine - latter * sine, former * sine + latter * cosine], -1)


def head_probs(query_in, key_in, allowed):
    scale = query_in.shape[-1] ** (-0.5)
    scores = (
        jnp.einsum("thd,shd->hts", query_in, key_in, preferred_element_type=jnp.float32) * scale
    )
    scores = jnp.where(allowed[None, :, :], scores, -1e30)
    shifted = scores - jnp.max(scores, -1, keepdims=True)
    weights = jnp.exp(shifted)
    return weights / jnp.sum(weights, -1, keepdims=True)


def conv_mask(values, taps, segment):
    total = taps[0][None, :] * values
    for offset in range(1, taps.shape[0]):
        moved = jnp.concatenate(
            [jnp.zeros((offset, values.shape[1]), values.dtype), values[:-offset]], 0
        )
        moved_seg = jnp.concatenate([jnp.full((offset,), -1, jnp.int32), segment[:-offset]], 0)
        same = (moved_seg == segment).astype(values.dtype)[:, None]
        total = total + taps[offset][None, :] * moved * same
    return total


def state_scan(inputs, step_sizes, decay, input_vecs, read_vecs, segment, block):
    length, heads, width = inputs.shape
    count = length // block
    states = input_vecs.shape[1]

    def one_block(carry, pieces):
        state, before = carry
        group_in, group_dt, group_b, group_c, group_seg = pieces
        logs = group_dt * decay[None, :]
        cumul = jnp.cumsum(logs, 0)
        places = jnp.arange(block, dtype=jnp.int32)
        allowed = (group_seg[:, None] == group_seg[None, :]) & (places[None, :] <= places[:, None])
        gaps = cumul[:, None, :] - cumul[None, :, :]
        fading = jnp.where(
            allowed[:, :, None], jnp.exp(jnp.where(allowed[:, :, None], gaps, 0.0)), 0.0
        )
        inner = jnp.dot(group_c, group_b.T, precision=highest)
        scaled = group_in * group_dt[:, :, None]
        local_out = jnp.einsum(
            "tsh,shp->thp", inner[:, :, None] * fading, scaled, precision=highest
        )
        carried = (group_seg == before).astype(inputs.dtype)
        entry = jnp.exp(cumul) * carried[:, None]
        from_state = (
            jnp.einsum("tn,hnp->thp", group_c, state, precision=highest) * entry[:, :, None]
        )
        last_seg = group_seg[-1]
        reach = (group_seg == last_seg).astype(inputs.dtype)
        to_end = jnp.exp(cumul[-1][None, :] - cumul) * reach[:, None]
        retain = jnp.exp(cumul[-1]) * (last_seg == before).astype(inputs.dtype)
        fresh = jnp.einsum("sn,sh,shp->hnp", group_b, to_end, scaled, precision=highest)
        state = state * retain[:, None, None] + fresh
        return ((state, last_seg), local_out + from_state)

    pieces = (
        inputs.reshape(count, block, heads, width),
        step_sizes.reshape(count, block, heads),
        input_vecs.reshape(count, block, states),
        read_vecs.reshape(count, block, states),
        segment.reshape(count, block),
    )
    start = (jnp.zeros((heads, states, width), inputs.dtype), jnp.array(-1, jnp.int32))
    unused, outputs = lax.scan(jax.checkpoint(one_block), start, pieces)
    return outputs.reshape(length, heads, width)


def mixer_core(
    inner_pre,
    input_pre,
    read_pre,
    step_pre,
    taps_x,
    taps_b,
    taps_c,
    shift_in,
    rate_in,
    segment,
    width,
    block,
):
    inner_conv = jax.nn.silu(conv_mask(inner_pre, taps_x, segment))
    input_conv = jax.nn.silu(conv_mask(input_pre, taps_b, segment))
    read_conv = jax.nn.silu(conv_mask(read_pre, taps_c, segment))
    step_sizes = jax.nn.softplus(step_pre + shift_in[None, :])
    heads = step_sizes.shape[1]
    length = inner_conv.shape[0]
    outputs = state_scan(
        inner_conv.reshape(length, heads, width),
        step_sizes,
        -jnp.exp(rate_in),
        input_conv,
        read_conv,
        segment,
        block,
    )
    return (outputs.reshape(length, heads * width), inner_conv)


def place_slice(piece, index, parts, axis):
    shape = list(piece.shape)
    shape[axis] = shape[axis] * parts
    holder = jnp.zeros(tuple(shape), jnp.float32)
    return lax.dynamic_update_slice_in_dim(holder, piece, index * piece.shape[axis], axis)


def take_slice(whole, index, width, axis):
    return lax.dynamic_slice_in_dim(whole, index * width, width, axis)


def general_device(
    hidden,
    embedding,
    cotangent,
    lengths,
    gain_attn,
    w_query,
    w_key,
    w_value,
    down_query,
    down_key,
    down_value,
    up_query,
    up_key,
    up_value,
    attn_output,
    gain_mlp,
    mlp_input,
    down_mlp,
    up_mlp,
    mlp_output,
    gain_mixer,
    proj_inner,
    proj_gate,
    proj_step,
    proj_input,
    proj_read,
    taps_inner,
    taps_input,
    taps_read,
    step_bias,
    log_rate,
    skip_gain,
    gain_gated,
    proj_output,
):
    row_count = hidden.shape[0]
    length = cotangent.shape[0]
    model_width = hidden.shape[1]
    head_parts = lax.axis_size(HEAD)
    state_parts = lax.axis_size(STATE)
    state_index = lax.axis_index(STATE)
    head_index = lax.axis_index(HEAD)
    own_start = state_index * row_count
    segment, position, valid = row_layout(lengths[0], length)
    own_segment = lax.dynamic_slice_in_dim(segment, own_start, row_count)
    own_position = lax.dynamic_slice_in_dim(position, own_start, row_count)
    own_valid = lax.dynamic_slice_in_dim(valid, own_start, row_count)[:, None]
    full_valid = valid[:, None]
    places = jnp.arange(length, dtype=jnp.int32)
    own_places = own_start + jnp.arange(row_count, dtype=jnp.int32)
    own_mask = ((places >= own_start) & (places < own_start + row_count)).astype(jnp.float32)[
        :, None
    ]
    allowed = (own_segment[:, None] == segment[None, :]) & (places[None, :] <= own_places[:, None])
    gathered = (
        lax.all_gather(gain_attn, ZED, axis=0, tiled=True),
        lax.all_gather(w_query, ZED, axis=0, tiled=True),
        lax.all_gather(w_key, ZED, axis=0, tiled=True),
        lax.all_gather(w_value, ZED, axis=0, tiled=True),
        lax.all_gather(down_query, ZED, axis=0, tiled=True),
        lax.all_gather(down_key, ZED, axis=0, tiled=True),
        lax.all_gather(down_value, ZED, axis=0, tiled=True),
        lax.all_gather(up_query, ZED, axis=0, tiled=True),
        lax.all_gather(up_key, ZED, axis=0, tiled=True),
        lax.all_gather(up_value, ZED, axis=0, tiled=True),
        lax.all_gather(attn_output, ZED, axis=1, tiled=True),
        lax.all_gather(gain_mlp, ZED, axis=0, tiled=True),
        lax.all_gather(mlp_input, ZED, axis=0, tiled=True),
        lax.all_gather(down_mlp, ZED, axis=0, tiled=True),
        lax.all_gather(up_mlp, ZED, axis=0, tiled=True),
        lax.all_gather(mlp_output, ZED, axis=1, tiled=True),
        lax.all_gather(gain_mixer, ZED, axis=0, tiled=True),
        lax.all_gather(proj_inner, ZED, axis=0, tiled=True),
        lax.all_gather(proj_gate, ZED, axis=0, tiled=True),
        lax.all_gather(proj_step, ZED, axis=0, tiled=True),
        lax.all_gather(proj_output, ZED, axis=1, tiled=True),
    )
    (
        attn_gain,
        query_main,
        key_main,
        value_main,
        query_down,
        key_down,
        value_down,
        query_upper,
        key_upper,
        value_upper,
        attn_proj,
        mlp_gain,
        mlp_main,
        mlp_down,
        mlp_upper,
        mlp_proj,
        mixer_gain,
        inner_main,
        gate_main,
        step_main,
        output_main,
    ) = gathered
    joined = jnp.concatenate([hidden, embedding], 1).astype(jnp.float32)
    attn_gain_f = attn_gain.astype(jnp.float32)
    normed = rms_norm(joined, attn_gain_f).astype(jnp.bfloat16)
    head_count = query_main.shape[1] // HDIM

    def project(main, down, upper):
        reduced = plain_dot(normed, down).astype(jnp.bfloat16)
        return (plain_dot(normed, main) + plain_dot(reduced, upper), reduced)

    query_pre, query_red = project(query_main, query_down, query_upper)
    key_pre, key_red = project(key_main, key_down, key_upper)
    value_pre, value_red = project(value_main, value_down, value_upper)
    queries = rotate(query_pre.reshape(row_count, head_count, HDIM), own_position).astype(
        jnp.bfloat16
    )
    keys_own = rotate(key_pre.reshape(row_count, head_count, HDIM), own_position).astype(
        jnp.bfloat16
    )
    values_own = value_pre.reshape(row_count, head_count, HDIM).astype(jnp.bfloat16)
    keys_all, values_all = (
        lax.all_gather(keys_own, STATE, axis=0, tiled=True),
        lax.all_gather(values_own, STATE, axis=0, tiled=True),
    )
    probs_full = head_probs(queries, keys_all, allowed)
    attended_f = jnp.einsum(
        "hts,shd->thd",
        probs_full.astype(jnp.bfloat16),
        values_all,
        preferred_element_type=jnp.float32,
    )
    attended = attended_f.reshape(row_count, head_count * HDIM).astype(jnp.bfloat16)
    branch = lax.psum(plain_dot(attended, attn_proj), HEAD)
    first = hidden.astype(jnp.float32) + own_valid * branch
    mlp_gain_f = mlp_gain.astype(jnp.float32)
    mlp_normed = rms_norm(first, mlp_gain_f).astype(jnp.bfloat16)
    mlp_red = plain_dot(mlp_normed, mlp_down).astype(jnp.bfloat16)
    hidden_pre = plain_dot(mlp_normed, mlp_main) + plain_dot(mlp_red, mlp_upper)
    activated = jax.nn.gelu(hidden_pre, approximate=False).astype(jnp.bfloat16)
    mlp_branch = lax.psum(plain_dot(activated, mlp_proj), HEAD)
    second = first + own_valid * mlp_branch
    second_all = lax.all_gather(second, STATE, axis=0, tiled=True)
    mixer_gain_f = mixer_gain.astype(jnp.float32)
    mixer_normed = rms_norm(second_all, mixer_gain_f).astype(jnp.bfloat16)
    states_own = proj_input.shape[1] // state_parts
    input_half = take_slice(proj_input, state_index, states_own, 1)
    read_half = take_slice(proj_read, state_index, states_own, 1)
    taps_input_half = take_slice(taps_input, state_index, states_own, 1).astype(jnp.float32)
    taps_read_half = take_slice(taps_read, state_index, states_own, 1).astype(jnp.float32)
    inner_pre = plain_dot(mixer_normed, inner_main)
    gate_pre = plain_dot(mixer_normed, gate_main)
    step_pre = plain_dot(mixer_normed, step_main)
    input_pre = plain_dot(mixer_normed, input_half)
    read_pre = plain_dot(mixer_normed, read_half)

    def mixer_piece(
        inner_in, input_in, read_in, step_in, taps_x, taps_b, taps_c, shift_in, rate_in
    ):
        return mixer_core(
            inner_in,
            input_in,
            read_in,
            step_in,
            taps_x,
            taps_b,
            taps_c,
            shift_in,
            rate_in,
            segment,
            MDIM,
            GROUP,
        )

    (scanned_part, inner_conv), mixer_back = jax.vjp(
        mixer_piece,
        inner_pre,
        input_pre,
        read_pre,
        step_pre,
        taps_inner.astype(jnp.float32),
        taps_input_half,
        taps_read_half,
        step_bias.astype(jnp.float32),
        log_rate.astype(jnp.float32),
    )
    scanned = lax.psum(scanned_part, STATE)
    skip_full = jnp.repeat(skip_gain.astype(jnp.float32), MDIM)[None, :]
    combined = scanned + skip_full * inner_conv
    gate_act = jax.nn.silu(gate_pre)
    united = combined * gate_act
    squares = lax.psum(jnp.sum(united * united, 1), HEAD)
    row_scale = lax.rsqrt(squares / DIN + epsilon)[:, None]
    gated_gain = gain_gated.astype(jnp.float32)[None, :]
    united_own = lax.dynamic_slice_in_dim(united, own_start, row_count, 0)
    scale_own = lax.dynamic_slice_in_dim(row_scale, own_start, row_count, 0)
    gated_own = (united_own * scale_own * gated_gain).astype(jnp.bfloat16)
    mixed_own = lax.psum(plain_dot(gated_own, output_main), HEAD)
    mixed = lax.all_gather(mixed_own, STATE, axis=0, tiled=True)
    layer_out = (second_all + full_valid * mixed).astype(jnp.bfloat16)
    upstream = cotangent.astype(jnp.float32)
    mix_grad = (full_valid * upstream).astype(jnp.bfloat16)
    mix_grad_own = lax.dynamic_slice_in_dim(mix_grad, own_start, row_count, 0)
    grad_output_main = left_dot(gated_own, mix_grad_own)
    gated_grad = right_dot(mix_grad, output_main)
    row_total = jnp.sum(mix_grad.astype(jnp.float32) * mixed, 1)[:, None] / row_scale
    grad_gated_gain = jnp.sum(gated_grad * united * row_scale * own_mask, 0)
    united_grad = (
        row_scale * gated_gain * gated_grad
        - united * row_scale * row_scale * row_scale * row_total / DIN
    )
    combined_grad = united_grad * gate_act
    sigmoid_gate = jax.nn.sigmoid(gate_pre)
    gate_grad = (
        united_grad * combined * sigmoid_gate * (1.0 + gate_pre * (1.0 - sigmoid_gate)) * own_mask
    )
    mixer_heads = step_pre.shape[1]
    grad_skip = jnp.sum(
        (combined_grad * inner_conv * own_mask).reshape(length, mixer_heads, MDIM), (0, 2)
    )
    conv_extra = skip_full * combined_grad * own_mask
    (
        inner_grad,
        input_grad,
        read_grad,
        step_grad,
        grad_taps_x,
        grad_taps_b,
        grad_taps_c,
        grad_shift,
        grad_rate,
    ) = mixer_back((combined_grad, conv_extra))
    mixer_part = (
        exact_right(inner_grad, inner_main)
        + exact_right(gate_grad, gate_main)
        + exact_right(step_grad, step_main)
        + exact_right(input_grad, input_half)
        + exact_right(read_grad, read_half)
    )
    grad_inner_main = exact_left(mixer_normed, inner_grad)
    grad_gate_main = exact_left(mixer_normed, gate_grad)
    grad_step_main = exact_left(mixer_normed, step_grad)
    grad_input_half = exact_left(mixer_normed, input_grad)
    grad_read_half = exact_left(mixer_normed, read_grad)
    mixer_rows_own = lax.psum_scatter(mixer_part, STATE, scatter_dimension=0, tiled=True)
    mixer_own = lax.psum(mixer_rows_own, HEAD)
    unused_norm, second_back = jax.vjp(rms_norm, second, mixer_gain_f)
    second_norm_grad, grad_mixer_gain = second_back(mixer_own)
    upstream_own = lax.dynamic_slice_in_dim(upstream, own_start, row_count, 0)
    second_grad = upstream_own + second_norm_grad
    mlp_grad = (own_valid * second_grad).astype(jnp.bfloat16)
    grad_mlp_proj = left_dot(activated, mlp_grad)
    activated_grad = right_dot(mlp_grad, mlp_proj)
    unused_gelu, gelu_back = jax.vjp(
        lambda preact: jax.nn.gelu(preact, approximate=False), hidden_pre
    )
    hidden_grad = gelu_back(activated_grad)[0].astype(jnp.bfloat16)
    grad_mlp_main = left_dot(mlp_normed, hidden_grad)
    grad_mlp_upper = left_dot(mlp_red, hidden_grad)
    mlp_middle = right_dot(hidden_grad, mlp_upper)
    mlp_part = right_dot(hidden_grad, mlp_main)
    mlp_sum, middle_sum = lax.psum((mlp_part, mlp_middle), HEAD)
    middle_low = middle_sum.astype(jnp.bfloat16)
    mlp_normed_grad = mlp_sum + right_dot(middle_low, mlp_down)
    grad_mlp_down = left_dot(mlp_normed, middle_low)
    unused_first, first_back = jax.vjp(rms_norm, first, mlp_gain_f)
    first_norm_grad, grad_mlp_gain = first_back(mlp_normed_grad)
    first_grad = second_grad + first_norm_grad
    branch_grad = (own_valid * first_grad).astype(jnp.bfloat16)
    grad_attn_proj = left_dot(attended, branch_grad)
    attended_grad = right_dot(branch_grad, attn_proj).reshape(row_count, head_count, HDIM)
    probs_back = head_probs(queries, keys_all, allowed)
    score_scale = HDIM ** (-0.5)
    out_low = attended_grad.astype(jnp.bfloat16)
    prob_grad = jnp.einsum("thd,shd->hts", out_low, values_all, preferred_element_type=jnp.float32)
    score_grad = probs_back * (prob_grad - jnp.sum(probs_back * prob_grad, -1, keepdims=True))
    score_low = score_grad.astype(jnp.bfloat16)
    query_back = (
        jnp.einsum("hts,shd->thd", score_low, keys_all, preferred_element_type=jnp.float32)
        * score_scale
    )
    keys_back = (
        jnp.einsum("hts,thd->shd", score_low, queries, preferred_element_type=jnp.float32)
        * score_scale
    )
    values_back = jnp.einsum(
        "hts,thd->shd", probs_back.astype(jnp.bfloat16), out_low, preferred_element_type=jnp.float32
    )
    keys_grad_own, values_grad_own = (
        lax.psum_scatter(keys_back, STATE, scatter_dimension=0, tiled=True),
        lax.psum_scatter(values_back, STATE, scatter_dimension=0, tiled=True),
    )
    query_grad = (
        rotate(query_back, -own_position).reshape(row_count, head_count * HDIM).astype(jnp.bfloat16)
    )
    key_grad = (
        rotate(keys_grad_own, -own_position)
        .reshape(row_count, head_count * HDIM)
        .astype(jnp.bfloat16)
    )
    value_grad = values_grad_own.reshape(row_count, head_count * HDIM).astype(jnp.bfloat16)
    grad_query_main = left_dot(normed, query_grad)
    grad_key_main = left_dot(normed, key_grad)
    grad_value_main = left_dot(normed, value_grad)
    grad_query_upper = left_dot(query_red, query_grad)
    grad_key_upper = left_dot(key_red, key_grad)
    grad_value_upper = left_dot(value_red, value_grad)
    query_middle = right_dot(query_grad, query_upper)
    key_middle = right_dot(key_grad, key_upper)
    value_middle = right_dot(value_grad, value_upper)
    normed_part = (
        right_dot(query_grad, query_main)
        + right_dot(key_grad, key_main)
        + right_dot(value_grad, value_main)
    )
    normed_sum, query_msum, key_msum, value_msum = lax.psum(
        (normed_part, query_middle, key_middle, value_middle), HEAD
    )
    query_low = query_msum.astype(jnp.bfloat16)
    key_low = key_msum.astype(jnp.bfloat16)
    value_low = value_msum.astype(jnp.bfloat16)
    normed_grad = (
        normed_sum
        + right_dot(query_low, query_down)
        + right_dot(key_low, key_down)
        + right_dot(value_low, value_down)
    )
    grad_query_down = left_dot(normed, query_low)
    grad_key_down = left_dot(normed, key_low)
    grad_value_down = left_dot(normed, value_low)
    unused_joined, joined_back = jax.vjp(rms_norm, joined, attn_gain_f)
    joined_grad, grad_attn_gain = joined_back(normed_grad)
    grad_hidden = (first_grad + joined_grad[:, :model_width]).astype(jnp.bfloat16)
    grad_embedding = joined_grad[:, model_width:].astype(jnp.bfloat16)
    scattered = (
        lax.psum_scatter(grad_attn_gain, ZED, scatter_dimension=0, tiled=True),
        lax.psum_scatter(grad_query_main, ZED, scatter_dimension=0, tiled=True),
        lax.psum_scatter(grad_key_main, ZED, scatter_dimension=0, tiled=True),
        lax.psum_scatter(grad_value_main, ZED, scatter_dimension=0, tiled=True),
        lax.psum_scatter(grad_query_down, ZED, scatter_dimension=0, tiled=True),
        lax.psum_scatter(grad_key_down, ZED, scatter_dimension=0, tiled=True),
        lax.psum_scatter(grad_value_down, ZED, scatter_dimension=0, tiled=True),
        lax.psum_scatter(grad_query_upper, ZED, scatter_dimension=0, tiled=True),
        lax.psum_scatter(grad_key_upper, ZED, scatter_dimension=0, tiled=True),
        lax.psum_scatter(grad_value_upper, ZED, scatter_dimension=0, tiled=True),
        lax.psum_scatter(grad_attn_proj, ZED, scatter_dimension=1, tiled=True),
        lax.psum_scatter(grad_mlp_gain, ZED, scatter_dimension=0, tiled=True),
        lax.psum_scatter(grad_mlp_main, ZED, scatter_dimension=0, tiled=True),
        lax.psum_scatter(grad_mlp_down, ZED, scatter_dimension=0, tiled=True),
        lax.psum_scatter(grad_mlp_upper, ZED, scatter_dimension=0, tiled=True),
        lax.psum_scatter(grad_mlp_proj, ZED, scatter_dimension=1, tiled=True),
        lax.psum_scatter(grad_mixer_gain, ZED, scatter_dimension=0, tiled=True),
        lax.psum_scatter(grad_inner_main, ZED, scatter_dimension=0, tiled=True),
        lax.psum_scatter(grad_gate_main, ZED, scatter_dimension=0, tiled=True),
        lax.psum_scatter(grad_step_main, ZED, scatter_dimension=0, tiled=True),
        lax.psum_scatter(grad_output_main, ZED, scatter_dimension=1, tiled=True),
    )
    first_head = (head_index == 0).astype(jnp.float32)
    square_sum = jnp.zeros((), jnp.float32)
    for index in [1, 2, 3, 7, 8, 9, 10, 12, 14, 15]:
        square_sum = square_sum + jnp.sum(scattered[index] * scattered[index])
    for index in [4, 5, 6, 13]:
        square_sum = square_sum + first_head * jnp.sum(scattered[index] * scattered[index])
    head_params = jnp.stack([grad_shift, grad_rate, grad_skip], 0)
    totals = lax.psum(
        (
            square_sum,
            place_slice(grad_gated_gain, head_index, head_parts, 0),
            place_slice(grad_taps_x, head_index, head_parts, 1),
            place_slice(head_params, head_index, head_parts, 1),
            place_slice(grad_input_half, state_index, state_parts, 1),
            place_slice(grad_read_half, state_index, state_parts, 1),
            place_slice(grad_taps_b, state_index, state_parts, 1),
            place_slice(grad_taps_c, state_index, state_parts, 1),
        ),
        EVERY,
    )
    (
        square_total,
        gated_full,
        taps_full,
        heads_full,
        input_full,
        read_full,
        taps_input_full,
        taps_read_full,
    ) = totals
    head_width = gain_gated.shape[0]
    tap_width = taps_inner.shape[1]
    param_width = step_bias.shape[0]
    heads_own = take_slice(heads_full, head_index, param_width, 1)
    return (
        layer_out,
        grad_hidden,
        grad_embedding,
        scattered[0],
        scattered[1],
        scattered[2],
        scattered[3],
        scattered[4],
        scattered[5],
        scattered[6],
        scattered[7],
        scattered[8],
        scattered[9],
        scattered[10],
        scattered[11],
        scattered[12],
        scattered[13],
        scattered[14],
        scattered[15],
        scattered[16],
        scattered[17],
        scattered[18],
        scattered[19],
        input_full,
        read_full,
        take_slice(taps_full, head_index, tap_width, 1),
        taps_input_full,
        taps_read_full,
        heads_own[0],
        heads_own[1],
        heads_own[2],
        take_slice(gated_full, head_index, head_width, 0),
        scattered[20],
        jnp.sqrt(square_total),
    )


low = jnp.bfloat16
full = jnp.float32


def head_masks():
    count = lax.axis_size(HEAD)
    masks = [1 << bit for bit in range(count.bit_length() - 1)]
    return masks[:1] + masks[1:], masks[:1] + masks[1:][::-1]


def head_swap(value, mask):
    count = lax.axis_size(HEAD)
    return lax.ppermute(value, HEAD, [(i, i ^ mask) for i in range(count)])


def state_swap(value):
    return lax.ppermute(value, STATE, [(0, 1), (1, 0)])


def dp_swap(value):
    return lax.ppermute(value, DP, [(0, 1), (1, 0)])


def state_forward(value):
    return lax.ppermute(value, STATE, [(0, 1)])


def state_backward(value):
    return lax.ppermute(value, STATE, [(1, 0)])


def bit_of(mask):
    return (lax.axis_index(HEAD) // mask) % 2


def chunk_of(masks):
    chunk = 0
    for mask in masks:
        chunk = chunk * 2 + bit_of(mask)
    return chunk


def sum_rows(value, masks, axis):
    for mask in masks:
        bit = bit_of(mask)
        half = value.shape[axis] // 2
        away = lax.dynamic_slice_in_dim(value, (1 - bit) * half, half, axis).astype(low)
        kept = lax.dynamic_slice_in_dim(value, bit * half, half, axis)
        value = kept.astype(full) + head_swap(away, mask).astype(full)
    return value


def gather_rows(value, masks, axis):
    for mask in masks[::-1]:
        bit = bit_of(mask)
        got = head_swap(value, mask)
        value = jnp.concatenate(
            [jnp.where(bit == 1, got, value), jnp.where(bit == 1, value, got)], axis
        )
    return value


def sum_row16(value, masks):
    state = lax.axis_index(STATE)
    value = sum_rows(value, masks, 1)
    away = lax.dynamic_index_in_dim(value, 1 - state, 0, False).astype(low)
    kept = lax.dynamic_index_in_dim(value, state, 0, False)
    return kept + state_swap(away).astype(full)


def gather_row16(value, masks):
    state = lax.axis_index(STATE)
    got = state_swap(value)
    both = jnp.stack([jnp.where(state == 0, value, got), jnp.where(state == 0, got, value)], 0)
    return gather_rows(both, masks, 1)


def pick_state(pair, index):
    return jnp.where(index == 0, pair[0], pair[1])


def weight_pieces(shard, axis):
    state = lax.axis_index(STATE)
    dp = lax.axis_index(DP)
    half = shard.shape[axis] // 2
    mine = lax.dynamic_slice_in_dim(shard, state * half, half, axis)
    got = state_swap(lax.dynamic_slice_in_dim(shard, (1 - state) * half, half, axis))
    far_mine = dp_swap(mine)
    far_got = dp_swap(got)
    near = [jnp.where(state == 0, mine, got), jnp.where(state == 0, got, mine)]
    far = [jnp.where(state == 0, far_mine, far_got), jnp.where(state == 0, far_got, far_mine)]
    lower = [jnp.where(dp == 0, a, b) for a, b in zip(near, far)]
    upper = [jnp.where(dp == 0, b, a) for a, b in zip(near, far)]
    return jnp.concatenate(lower + upper, 1 - axis)


def grad_pieces(grad, axis):
    state = lax.axis_index(STATE)
    dp = lax.axis_index(DP)
    half = grad.shape[1 - axis] // 2
    away = lax.dynamic_slice_in_dim(grad, (1 - dp) * half, half, 1 - axis).astype(low)
    kept = lax.dynamic_slice_in_dim(grad, dp * half, half, 1 - axis)
    total = kept + dp_swap(away).astype(full)
    quarter = half // 2
    away = lax.dynamic_slice_in_dim(total, (1 - state) * quarter, quarter, 1 - axis).astype(low)
    kept = lax.dynamic_slice_in_dim(total, state * quarter, quarter, 1 - axis)
    got = state_swap(away).astype(full)
    return jnp.concatenate(
        [jnp.where(state == 0, kept, got), jnp.where(state == 0, got, kept)], axis
    )


def norm_scale(values):
    return lax.rsqrt(jnp.mean(values * values, -1, keepdims=True) + epsilon)


def norm_back(values, gain, grad):
    scale = norm_scale(values)
    scaled = grad * gain
    inner = jnp.mean(scaled * values, -1, keepdims=True)
    return (
        scale * scaled - values * (scale * scale * scale * inner),
        jnp.sum(grad * values * scale, 0),
    )


def conv_edge(values, edge, taps, segment, edge_segment):
    reach = taps.shape[0] - 1
    rows = values.shape[0]
    joined = jnp.concatenate([edge, values], 0)
    segs = jnp.concatenate([edge_segment, segment], 0)
    total = taps[0][None, :] * values
    for offset in range(1, taps.shape[0]):
        lower = reach - offset
        same = (segs[lower : lower + rows] == segment).astype(values.dtype)[:, None]
        total = total + taps[offset][None, :] * joined[lower : lower + rows] * same
    return total


def scan_blocks(inputs, step_sizes, decay, input_vecs, read_vecs, segment, before, block):
    length, heads = step_sizes.shape
    width = inputs.shape[1] // heads
    count = length // block
    states = input_vecs.shape[1]
    state = jnp.zeros((heads, states, width), full)
    last = before
    outputs, entries = [], []
    since = jnp.zeros((heads,), full)
    for index in range(count):
        part = slice(index * block, (index + 1) * block)
        group_in = inputs[part].reshape(block, heads, width).transpose(1, 0, 2)
        group_dt = step_sizes[part].T
        group_b, group_c, group_seg = input_vecs[part], read_vecs[part], segment[part]
        cumul = jnp.cumsum(group_dt * decay[:, None], 1)
        places = jnp.arange(block, dtype=jnp.int32)
        allowed = (group_seg[:, None] == group_seg[None, :]) & (places[None, :] <= places[:, None])
        gaps = cumul[:, :, None] - cumul[:, None, :]
        fading = jnp.where(allowed, jnp.exp(jnp.where(allowed, gaps, 0.0)), 0.0)
        inner = right_dot(group_c, group_b)
        scaled = group_in * group_dt[:, :, None]
        local_out = jnp.einsum(
            "hts,hsp->htp", inner[None] * fading, scaled, preferred_element_type=full
        )
        carried = (group_seg == last).astype(full)
        entry = jnp.exp(cumul) * carried[None, :]
        from_state = jnp.einsum("tn,hnp->htp", group_c, state) * entry[:, :, None]
        first_seg = (group_seg == before).astype(full)
        entries.append((jnp.exp(cumul + since[:, None]) * first_seg[None, :]).T)
        since = since + cumul[:, -1]
        last_seg = group_seg[-1]
        reach = (group_seg == last_seg).astype(full)
        to_end = jnp.exp(cumul[:, -1:] - cumul) * reach[None, :]
        retain = jnp.exp(cumul[:, -1]) * (last_seg == last).astype(full)
        fresh = jnp.einsum("sn,hsp->hnp", group_b, to_end[:, :, None] * scaled)
        state = state * retain[:, None, None] + fresh
        last = last_seg
        outputs.append(
            (local_out + from_state).transpose(1, 0, 2).reshape(block, heads * width)
        )
    carry = jnp.exp(since) * (last == before).astype(full)
    return jnp.concatenate(outputs, 0), state, jnp.concatenate(entries, 0), carry


def fast_device(
    hidden,
    embedding,
    cotangent,
    lengths,
    gain_attn,
    w_query,
    w_key,
    w_value,
    down_query,
    down_key,
    down_value,
    up_query,
    up_key,
    up_value,
    attn_output,
    gain_mlp,
    mlp_input,
    down_mlp,
    up_mlp,
    mlp_output,
    gain_mixer,
    proj_inner,
    proj_gate,
    proj_step,
    proj_input,
    proj_read,
    taps_inner,
    taps_input,
    taps_read,
    step_bias,
    log_rate,
    skip_gain,
    gain_gated,
    proj_output,
):
    zed = ZED
    everywhere = EVERY
    rows = hidden.shape[0]
    length = cotangent.shape[0]
    width = hidden.shape[1]
    middle = rows // 2
    head_parts = lax.axis_size(HEAD)
    piece = middle // head_parts
    state = lax.axis_index(STATE)
    dp = lax.axis_index(DP)
    head = lax.axis_index(HEAD)
    own_start = state * rows
    orders = head_masks()
    offsets = [chunk_of(orders[0]) * piece, middle + chunk_of(orders[1]) * piece]
    halves = [(offset, order) for offset, order in zip(offsets, orders)]
    segment, position, valid = row_layout(lengths[0], length)
    own_segment = lax.dynamic_slice_in_dim(segment, own_start, rows)
    own_valid = lax.dynamic_slice_in_dim(valid, own_start, rows)[:, None]

    def cut(value):
        return [lax.dynamic_slice_in_dim(value, offset, piece, 0) for offset in offsets]

    valid_cut = cut(own_valid)

    gains = lax.all_gather(
        jnp.concatenate([gain_attn, gain_mlp, gain_mixer]), zed, axis=0, tiled=False
    ).astype(full)
    split_a, split_m = gain_attn.shape[0], gain_mlp.shape[0]
    attn_gain = gains[:, :split_a].reshape(-1)
    mlp_gain = gains[:, split_a : split_a + split_m].reshape(-1)
    mixer_gain = gains[:, split_a + split_m :].reshape(-1)

    query_main = weight_pieces(w_query, 1)
    key_main = weight_pieces(w_key, 1)
    value_main = weight_pieces(w_value, 1)
    ups = jnp.stack([up_query, up_key, up_value], 0)
    half_cols = up_query.shape[1] // 2
    ups_mine = lax.dynamic_slice_in_dim(ups, state * half_cols, half_cols, 2)
    ups_got = state_swap(lax.dynamic_slice_in_dim(ups, (1 - state) * half_cols, half_cols, 2))
    ups_near = jnp.concatenate(
        [jnp.where(state == 0, ups_mine, ups_got), jnp.where(state == 0, ups_got, ups_mine)], 1
    )
    ups_far = dp_swap(ups_near)
    ups_all = jnp.concatenate(
        [jnp.where(dp == 0, ups_near, ups_far), jnp.where(dp == 0, ups_far, ups_near)], 1
    )
    query_upper, key_upper, value_upper = ups_all[0], ups_all[1], ups_all[2]

    rank = down_query.shape[1]
    part_a = down_query.shape[0] // head_parts
    part_m = down_mlp.shape[0] // head_parts
    downs = jnp.concatenate(
        [
            lax.dynamic_slice_in_dim(down_query, head * part_a, part_a, 0),
            lax.dynamic_slice_in_dim(down_key, head * part_a, part_a, 0),
            lax.dynamic_slice_in_dim(down_value, head * part_a, part_a, 0),
            lax.dynamic_slice_in_dim(down_mlp, head * part_m, part_m, 0),
        ],
        0,
    )
    downs_got = state_swap(downs)
    downs_near = jnp.stack(
        [jnp.where(state == 0, downs, downs_got), jnp.where(state == 0, downs_got, downs)], 0
    )
    downs_far = dp_swap(downs_near)
    downs_all = jnp.concatenate(
        [jnp.where(dp == 0, downs_near, downs_far), jnp.where(dp == 0, downs_far, downs_near)], 0
    )
    masks = orders[0][::-1]
    downs_all = gather_rows(downs_all[None], masks, 0)

    def down_of(lower, part):
        return downs_all[:, :, lower : lower + part].transpose(1, 0, 2, 3).reshape(-1, rank)

    query_down = down_of(0, part_a)
    key_down = down_of(part_a, part_a)
    value_down = down_of(2 * part_a, part_a)
    mlp_down = down_of(3 * part_a, part_m)

    joined = jnp.concatenate([hidden, embedding], 1).astype(full)
    normed_own = rms_norm(joined, attn_gain).astype(low)
    joined_cut = [
        jnp.concatenate([a, b], 1).astype(full) for a, b in zip(cut(hidden), cut(embedding))
    ]
    normed_far = jnp.concatenate(
        [
            gather_rows(state_swap(rms_norm(value, attn_gain).astype(low)), order, 0)
            for value, (offset, order) in zip(joined_cut, halves)
        ],
        0,
    )
    normed = jnp.concatenate(
        [
            jnp.where(state == 0, normed_own, normed_far),
            jnp.where(state == 0, normed_far, normed_own),
        ],
        0,
    )
    head_count = query_main.shape[1] // HDIM

    def project(main, down, upper):
        reduced = plain_dot(normed, down).astype(low)
        return (plain_dot(normed, main) + plain_dot(reduced, upper), reduced)

    def as_heads(value):
        return value.reshape(length, head_count, HDIM)

    query_pre, query_red = project(query_main, query_down, query_upper)
    key_pre, key_red = project(key_main, key_down, key_upper)
    value_pre, value_red = project(value_main, value_down, value_upper)
    queries = rotate(as_heads(query_pre), position).astype(low)
    keys = rotate(as_heads(key_pre), position).astype(low)
    values = as_heads(value_pre).astype(low)

    (
        mlp_input,
        up_mlp,
        mlp_output,
        proj_inner,
        proj_gate,
        proj_step,
        proj_output,
        value_main,
    ) = lax.optimization_barrier(
        (
            mlp_input,
            up_mlp,
            mlp_output,
            proj_inner,
            proj_gate,
            proj_step,
            proj_output,
            value_main,
        )
    )
    attn_proj = weight_pieces(attn_output, 0)
    mlp_main = lax.all_gather(mlp_input, zed, axis=0, tiled=True)
    mlp_upper = lax.all_gather(up_mlp, zed, axis=0, tiled=True)
    mlp_proj = lax.all_gather(mlp_output, zed, axis=1, tiled=True)
    inner_main = lax.all_gather(proj_inner, zed, axis=0, tiled=True)
    gate_main = lax.all_gather(proj_gate, zed, axis=0, tiled=True)
    step_main = lax.all_gather(proj_step, zed, axis=0, tiled=True)
    output_main = lax.all_gather(proj_output, zed, axis=1, tiled=True)

    places = jnp.arange(length, dtype=jnp.int32)
    allowed = (segment[:, None] == segment[None, :]) & (places[None, :] <= places[:, None])
    probs = head_probs(queries, keys, allowed)
    attended = (
        jnp.einsum("hts,shd->thd", probs.astype(low), values, preferred_element_type=full)
        .reshape(length, head_count * HDIM)
        .astype(low)
    )

    def state_halves(value):
        cubes = value.reshape(2, 2, middle, value.shape[1])
        return [cubes[:, 0], cubes[:, 1]]

    def from_halves(pair):
        return jnp.stack(pair, 1).reshape(length, pair[0].shape[-1])

    branch_cut = [
        sum_row16(plain_dot(part.reshape(rows, -1), attn_proj).reshape(2, middle, width), order)
        for part, (offset, order) in zip(state_halves(attended), halves)
    ]
    first_cut = [
        value.astype(full) + good * branch
        for value, good, branch in zip(cut(hidden), valid_cut, branch_cut)
    ]
    mlp_normed = [
        gather_rows(rms_norm(value, mlp_gain).astype(low), order, 0)
        for value, (offset, order) in zip(first_cut, halves)
    ]
    mlp_red = [plain_dot(value, mlp_down).astype(low) for value in mlp_normed]
    hidden_pre = [
        plain_dot(value, mlp_main) + plain_dot(red, mlp_upper)
        for value, red in zip(mlp_normed, mlp_red)
    ]
    activated = [jax.nn.gelu(value, approximate=False).astype(low) for value in hidden_pre]
    second_cut = [
        value + good * sum_rows(plain_dot(part, mlp_proj), order, 0)
        for value, good, part, (offset, order) in zip(first_cut, valid_cut, activated, halves)
    ]
    mixer_halves = [
        gather_rows(rms_norm(value, mixer_gain).astype(low), order, 0)
        for value, (offset, order) in zip(second_cut, halves)
    ]
    mixer_normed = jnp.concatenate(mixer_halves, 0)

    inner_pre = plain_dot(mixer_normed, inner_main)
    gate_pre = plain_dot(mixer_normed, gate_main)
    small_main = jnp.concatenate([step_main, proj_input, proj_read], 1)
    small_pre = plain_dot(mixer_normed, small_main)
    mixer_heads = step_main.shape[1]
    states = proj_input.shape[1]
    reach = taps_inner.shape[0] - 1
    edge = state_forward(
        jnp.concatenate([inner_pre[rows - reach :], small_pre[rows - reach :, mixer_heads:]], 1)
    )
    inner_width = inner_pre.shape[1]
    edge_start = jnp.maximum(own_start - reach, 0)
    edge_segment = jnp.where(
        state == 0, -1, lax.dynamic_slice_in_dim(segment, edge_start, reach)
    )
    before = edge_segment[-1]

    def mixer_piece(inner_in, small_in, edge_in, taps_x, taps_b, taps_c, shift_in, rate_in):
        step_in = small_in[:, :mixer_heads]
        input_in = small_in[:, mixer_heads : mixer_heads + states]
        read_in = small_in[:, mixer_heads + states :]
        edge_b = edge_in[:, inner_width : inner_width + states]
        edge_c = edge_in[:, inner_width + states :]
        inner_conv = jax.nn.silu(
            conv_edge(inner_in, edge_in[:, :inner_width], taps_x, own_segment, edge_segment)
        )
        input_conv = jax.nn.silu(conv_edge(input_in, edge_b, taps_b, own_segment, edge_segment))
        read_conv = jax.nn.silu(conv_edge(read_in, edge_c, taps_c, own_segment, edge_segment))
        step_sizes = jax.nn.softplus(step_in + shift_in[None, :])
        outputs, last_state, entry, carry = scan_blocks(
            inner_conv,
            step_sizes,
            -jnp.exp(rate_in),
            input_conv,
            read_conv,
            own_segment,
            before,
            GROUP,
        )
        return outputs, inner_conv, last_state, read_conv, entry

    (scanned_own, inner_conv, last_state, read_conv, entry), mixer_back = jax.vjp(
        mixer_piece,
        inner_pre,
        small_pre,
        edge,
        taps_inner.astype(full),
        taps_input.astype(full),
        taps_read.astype(full),
        step_bias.astype(full),
        log_rate.astype(full),
    )
    first_state = state_forward(last_state)

    def by_head(value):
        return value.reshape(rows, mixer_heads, MDIM)

    def flat(value):
        return value.reshape(rows, mixer_heads * MDIM)

    from_first = jnp.einsum("tn,hnp->thp", read_conv, first_state)
    scanned = scanned_own + flat(from_first * entry[:, :, None])
    skip_full = jnp.repeat(skip_gain.astype(full), MDIM)[None, :]
    combined = scanned + skip_full * inner_conv
    gate_act = jax.nn.silu(gate_pre)
    united = combined * gate_act
    gated_gain = gain_gated.astype(full)[None, :]
    cot_own = lax.dynamic_slice_in_dim(cotangent, own_start, rows, 0)
    mix_grad = cot_own * own_valid.astype(low)
    gated_grad = right_dot(mix_grad, output_main)
    pair = jnp.stack(
        [jnp.sum(united * united, 1), jnp.sum(united * gated_gain * gated_grad, 1)], 0
    )
    for mask in orders[0]:
        pair = pair + head_swap(pair, mask)
    channels = inner_width * head_parts
    row_scale = lax.rsqrt(pair[0] / channels + epsilon)[:, None]
    row_total = pair[1][:, None]
    gated = (united * row_scale * gated_gain).astype(low)
    out_cut = [
        (
            value
            + good
            * sum_rows(
                plain_dot(gated[index * middle : (index + 1) * middle], output_main), order, 0
            )
        ).astype(low)
        for index, (value, good, (offset, order)) in enumerate(
            zip(second_cut, valid_cut, halves)
        )
    ]
    layer_out = from_halves(
        [gather_row16(value, order) for value, (offset, order) in zip(out_cut, halves)]
    )

    grad_output_main = left_dot(gated, mix_grad).astype(low)
    grad_gated_gain = jnp.sum(gated_grad * united * row_scale, 0)
    united_grad = (
        row_scale * gated_gain * gated_grad
        - united * row_scale * row_scale * row_scale * row_total / channels
    )
    combined_grad = united_grad * gate_act
    sigmoid_gate = jax.nn.sigmoid(gate_pre)
    gate_grad = united_grad * combined * sigmoid_gate * (1.0 + gate_pre * (1.0 - sigmoid_gate))
    grad_skip = jnp.sum(by_head(combined_grad * inner_conv), (0, 2))
    conv_extra = skip_full * combined_grad
    entry_grad = by_head(combined_grad) * entry[:, :, None]
    first_state_grad = jnp.einsum("tn,thp->hnp", read_conv, entry_grad)
    last_state_grad = state_backward(first_state_grad)
    read_extra = jnp.einsum("thp,hnp->tn", entry_grad, first_state)
    entry_extra = jnp.sum(by_head(combined_grad) * from_first, 2)
    (
        inner_grad,
        small_grad,
        edge_grad,
        grad_taps_x,
        grad_taps_b,
        grad_taps_c,
        grad_shift,
        grad_rate,
    ) = mixer_back((combined_grad, conv_extra, last_state_grad, read_extra, entry_extra))
    edge_back = state_backward(edge_grad)
    inner_grad = inner_grad.at[rows - reach :].add(edge_back[:, :inner_width])
    small_grad = small_grad.at[rows - reach :, mixer_heads:].add(edge_back[:, inner_width:])
    inner_low = inner_grad.astype(low)
    gate_low = gate_grad.astype(low)
    small_low = small_grad.astype(low)
    mixer_sum = [
        sum_rows(
            right_dot(inner_low[part], inner_main)
            + right_dot(gate_low[part], gate_main)
            + right_dot(small_low[part], small_main),
            order,
            0,
        )
        for part, (offset, order) in zip((slice(0, middle), slice(middle, rows)), halves)
    ]
    grad_inner_main = left_dot(mixer_normed, inner_low).astype(low)
    grad_gate_main = left_dot(mixer_normed, gate_low).astype(low)
    grad_small_main = left_dot(mixer_normed, small_low)
    upstream_cut = [value.astype(full) for value in cut(cot_own)]
    mixer_backs = [
        norm_back(value, mixer_gain, grad) for value, grad in zip(second_cut, mixer_sum)
    ]
    second_grad = [up + back[0] for up, back in zip(upstream_cut, mixer_backs)]
    grad_mixer_gain = mixer_backs[0][1] + mixer_backs[1][1]
    mlp_grad = [
        gather_rows((good * grad).astype(low), order, 0)
        for good, grad, (offset, order) in zip(valid_cut, second_grad, halves)
    ]

    def gelu_part(value):
        return jax.nn.gelu(value, approximate=False)

    hidden_grad = [
        jax.vjp(gelu_part, pre)[1](right_dot(grad, mlp_proj))[0].astype(low)
        for pre, grad in zip(hidden_pre, mlp_grad)
    ]
    mlp_sums = [
        sum_rows(
            jnp.concatenate([right_dot(grad, mlp_main), right_dot(grad, mlp_upper)], 1), order, 0
        )
        for grad, (offset, order) in zip(hidden_grad, halves)
    ]
    middle_low = [value[:, width:].astype(low) for value in mlp_sums]
    mlp_backs = [
        norm_back(value, mlp_gain, total[:, :width] + right_dot(mid, mlp_down))
        for value, total, mid in zip(first_cut, mlp_sums, middle_low)
    ]
    first_grad = [grad + back[0] for grad, back in zip(second_grad, mlp_backs)]
    grad_mlp_gain = mlp_backs[0][1] + mlp_backs[1][1]
    branch_wide = [
        gather_row16(jnp.concatenate([(good * grad).astype(low), mid], 1), order)
        for good, grad, mid, (offset, order) in zip(valid_cut, first_grad, middle_low, halves)
    ]
    branch_all = from_halves(branch_wide)
    branch_grad = branch_all[:, :width]
    middle_own = lax.dynamic_slice(branch_all, (own_start, width), (rows, rank))
    activated_own = jnp.concatenate(activated, 0)
    mlp_normed_own = jnp.concatenate(mlp_normed, 0)
    hidden_grad_own = jnp.concatenate(hidden_grad, 0)
    grad_mlp_proj = left_dot(activated_own, jnp.concatenate(mlp_grad, 0)).astype(low)
    grad_mlp_main = left_dot(mlp_normed_own, hidden_grad_own).astype(low)
    grad_mlp_upper = left_dot(jnp.concatenate(mlp_red, 0), hidden_grad_own).astype(low)
    grad_mlp_down = left_dot(mlp_normed_own, middle_own).astype(low)

    def scatter(value, axis):
        return lax.psum_scatter(value, zed, scatter_dimension=axis, tiled=True).astype(full)

    out_output = scatter(grad_output_main, 1)
    out_inner = scatter(grad_inner_main, 0)
    out_gate = scatter(grad_gate_main, 0)
    out_mlp_output = scatter(grad_mlp_proj, 1)
    out_mlp_input = scatter(grad_mlp_main, 0)
    out_up_mlp = scatter(grad_mlp_upper, 0)
    out_down_mlp = scatter(grad_mlp_down, 0)

    out_attn = grad_pieces(left_dot(attended, branch_grad), 0)
    attended_grad = as_heads(right_dot(branch_grad, attn_proj))
    probs_back = head_probs(queries, keys, allowed)
    score_scale = HDIM ** (-0.5)
    out_low = attended_grad.astype(low)
    prob_grad = jnp.einsum("thd,shd->hts", out_low, values, preferred_element_type=full)
    score_grad = probs_back * (prob_grad - jnp.sum(probs_back * prob_grad, -1, keepdims=True))
    score_low = score_grad.astype(low)
    query_back = (
        jnp.einsum("hts,shd->thd", score_low, keys, preferred_element_type=full) * score_scale
    )
    keys_back = (
        jnp.einsum("hts,thd->shd", score_low, queries, preferred_element_type=full) * score_scale
    )
    values_back = jnp.einsum(
        "hts,thd->shd", probs_back.astype(low), out_low, preferred_element_type=full
    )

    def as_flat(value):
        return value.reshape(length, head_count * HDIM).astype(low)

    query_grad = as_flat(rotate(query_back, -position))
    key_grad = as_flat(rotate(keys_back, -position))
    value_grad = as_flat(values_back)
    out_query = grad_pieces(left_dot(normed, query_grad), 1)
    out_key = grad_pieces(left_dot(normed, key_grad), 1)
    out_value = grad_pieces(left_dot(normed, value_grad), 1)
    out_ups = jnp.concatenate(
        [
            left_dot(query_red, query_grad),
            left_dot(key_red, key_grad),
            left_dot(value_red, value_grad),
        ],
        1,
    )
    rank_half = rank // 2
    ups_away = lax.dynamic_slice_in_dim(out_ups, (1 - dp) * rank_half, rank_half, 0)
    ups_sum = lax.dynamic_slice_in_dim(out_ups, dp * rank_half, rank_half, 0) + dp_swap(ups_away)
    rank_quarter = rank_half // 2
    ups_kept = lax.dynamic_slice_in_dim(ups_sum, state * rank_quarter, rank_quarter, 0)
    ups_back = state_swap(
        lax.dynamic_slice_in_dim(ups_sum, (1 - state) * rank_quarter, rank_quarter, 0)
    )

    def up_of(index):
        part = slice(index * half_cols, (index + 1) * half_cols)
        return jnp.concatenate(
            [
                jnp.where(state == 0, ups_kept[:, part], ups_back[:, part]),
                jnp.where(state == 0, ups_back[:, part], ups_kept[:, part]),
            ],
            1,
        )

    normed_parts = state_halves(
        jnp.concatenate(
            [
                right_dot(query_grad, query_main)
                + right_dot(key_grad, key_main)
                + right_dot(value_grad, value_main),
                right_dot(query_grad, query_upper),
                right_dot(key_grad, key_upper),
                right_dot(value_grad, value_upper),
            ],
            1,
        )
    )
    normed_sums = [sum_row16(part, order) for part, (offset, order) in zip(normed_parts, halves)]
    joint = 2 * width
    lows = [value[:, joint:].astype(low) for value in normed_sums]
    joined_backs = [
        norm_back(
            value,
            attn_gain,
            total[:, :joint]
            + right_dot(mid[:, :rank], query_down)
            + right_dot(mid[:, rank : 2 * rank], key_down)
            + right_dot(mid[:, 2 * rank :], value_down),
        )
        for value, total, mid in zip(joined_cut, normed_sums, lows)
    ]
    grad_attn_gain = joined_backs[0][1] + joined_backs[1][1]
    input_grads = jnp.concatenate(
        [
            gather_rows(
                jnp.concatenate(
                    [(grad + back[0][:, :width]).astype(low), back[0][:, width:].astype(low)], 1
                ),
                order,
                0,
            )
            for grad, back, (offset, order) in zip(first_grad, joined_backs, halves)
        ],
        0,
    )
    grad_hidden = input_grads[:, :width]
    grad_embedding = input_grads[:, width:]

    lows_all = from_halves(
        [gather_row16(value, order) for value, (offset, order) in zip(lows, halves)]
    )
    quarter = gain_attn.shape[0]

    def down_rows(index):
        start = (index * 2 + state) * quarter + head * part_a
        columns = lax.dynamic_slice_in_dim(normed, start, part_a, 1)
        return left_dot(columns, lows_all)

    down_sum = down_rows(dp) + dp_swap(down_rows(1 - dp).astype(low)).astype(full)
    down_all = gather_rows(down_sum.astype(low)[None], masks, 0)
    down_all = down_all.reshape(quarter, 3 * rank).astype(full)
    out_downs = [down_all[:, index * rank : (index + 1) * rank] for index in range(3)]

    small_total, taps_b_total, taps_c_total = lax.psum(
        (grad_small_main[:, mixer_heads:], grad_taps_b, grad_taps_c), everywhere
    )
    out_step = lax.psum_scatter(
        grad_small_main[:, :mixer_heads], zed, scatter_dimension=0, tiled=True
    )
    gated_total, taps_x_total, head_total = lax.psum(
        (grad_gated_gain, grad_taps_x, jnp.stack([grad_shift, grad_rate, grad_skip], 0)), zed
    )
    once = (head == 0).astype(full)
    square_sum = jnp.zeros((), full)
    out_up = [up_of(index) for index in range(3)]
    for value in [out_query, out_key, out_value, out_attn, out_mlp_input, out_up_mlp]:
        square_sum = square_sum + jnp.sum(value * value)
    for value in [out_mlp_output] + out_up:
        square_sum = square_sum + jnp.sum(value * value)
    for value in out_downs + [out_down_mlp]:
        square_sum = square_sum + once * jnp.sum(value * value)
    square_total, gain_total = lax.psum(
        (square_sum, jnp.concatenate([grad_attn_gain, grad_mlp_gain, grad_mixer_gain])),
        everywhere,
    )
    place = dp * 2 + state
    wide = 2 * width

    def gain_of(start, size, total):
        return lax.dynamic_slice_in_dim(gain_total[start : start + total], place * size, size)

    return (
        layer_out,
        grad_hidden,
        grad_embedding,
        gain_of(0, split_a, wide),
        out_query,
        out_key,
        out_value,
        out_downs[0],
        out_downs[1],
        out_downs[2],
        out_up[0],
        out_up[1],
        out_up[2],
        out_attn,
        gain_of(wide, split_m, width),
        out_mlp_input,
        out_down_mlp,
        out_up_mlp,
        out_mlp_output,
        gain_of(wide + width, split_m, width),
        out_inner,
        out_gate,
        out_step,
        small_total[:, :states],
        small_total[:, states:],
        taps_x_total,
        taps_b_total,
        taps_c_total,
        head_total[0],
        head_total[1],
        head_total[2],
        gated_total,
        out_output,
        jnp.sqrt(square_total),
    )


def pick_device(mesh):
    heads = mesh.shape[HEAD]
    per_head = DIN // HDIM // heads
    halves = mesh.shape[DP] == 2 and mesh.shape[STATE] == 2
    return fast_device if halves and heads & (heads - 1) == 0 and per_head % 2 == 0 else general_device


def solution(mesh):
    in_specs = (
        P(ZED, None),
        P(ZED, None),
        P(DP, None),
        P(DP, None),
        P(ZED),
        P(ZED, HEAD),
        P(ZED, HEAD),
        P(ZED, HEAD),
        P(ZED, None),
        P(ZED, None),
        P(ZED, None),
        P(ZED, HEAD),
        P(ZED, HEAD),
        P(ZED, HEAD),
        P(HEAD, ZED),
        P(ZED),
        P(ZED, HEAD),
        P(ZED, None),
        P(ZED, HEAD),
        P(HEAD, ZED),
        P(ZED),
        P(ZED, HEAD),
        P(ZED, HEAD),
        P(ZED, HEAD),
        P(),
        P(),
        P(None, HEAD),
        P(),
        P(),
        P(HEAD),
        P(HEAD),
        P(HEAD),
        P(HEAD),
        P(HEAD, ZED),
    )
    out_specs = (
        P(DP, None),
        P(ZED, None),
        P(ZED, None),
        P(ZED),
        P(ZED, HEAD),
        P(ZED, HEAD),
        P(ZED, HEAD),
        P(ZED, None),
        P(ZED, None),
        P(ZED, None),
        P(ZED, HEAD),
        P(ZED, HEAD),
        P(ZED, HEAD),
        P(HEAD, ZED),
        P(ZED),
        P(ZED, HEAD),
        P(ZED, None),
        P(ZED, HEAD),
        P(HEAD, ZED),
        P(ZED),
        P(ZED, HEAD),
        P(ZED, HEAD),
        P(ZED, HEAD),
        P(),
        P(),
        P(None, HEAD),
        P(),
        P(),
        P(HEAD),
        P(HEAD),
        P(HEAD),
        P(HEAD),
        P(HEAD, ZED),
        P(),
    )
    return jax.shard_map(
        pick_device(mesh), mesh=mesh, in_specs=in_specs, out_specs=out_specs, check_vma=False
    )
```

```python
import jax
import jax.numpy as jnp
from jax import lax
from jax.experimental import pallas as pl
from jax.experimental.pallas import tpu as pltpu
from jax.sharding import PartitionSpec as P

HDIM = 128
MDIM = 64
DIN = 4096
GROUP = 256
DP, HEAD, STATE = "dp", "head", "state"
ZED = (DP, STATE)
EVERY = (DP, HEAD, STATE)


highest = lax.Precision.HIGHEST
epsilon = 1e-05


def plain_dot(left, right):
    return jnp.dot(left, right, preferred_element_type=jnp.float32)


def left_dot(left, right):
    return lax.dot_general(
        left, right, (((0,), (0,)), ((), ())), preferred_element_type=jnp.float32
    )


def right_dot(left, right):
    return lax.dot_general(
        left, right, (((1,), (1,)), ((), ())), preferred_element_type=jnp.float32
    )


def exact_left(left, right):
    return lax.dot_general(
        left.astype(jnp.float32), right, (((0,), (0,)), ((), ())), precision=highest
    )


def exact_right(left, right):
    return lax.dot_general(
        left, right.astype(jnp.float32), (((1,), (1,)), ((), ())), precision=highest
    )


def rms_norm(values, gain):
    return values * lax.rsqrt(jnp.mean(values * values, -1, keepdims=True) + epsilon) * gain


def row_layout(doc_lengths, length):
    ends = jnp.cumsum(doc_lengths)
    places = jnp.arange(length, dtype=jnp.int32)
    segment = jnp.sum((places[:, None] >= ends[None, :]).astype(jnp.int32), axis=1)
    starts = jnp.concatenate([ends - doc_lengths, ends[-1:]])
    choose = segment[:, None] == jnp.arange(starts.shape[0], dtype=jnp.int32)[None, :]
    first_place = jnp.sum(jnp.where(choose, starts[None, :], 0), axis=1)
    position = (places - first_place).astype(jnp.float32)
    valid = (segment < doc_lengths.shape[0]).astype(jnp.float32)
    return (segment, position, valid)


def rotate(values, position):
    half = values.shape[-1] // 2
    freqs = 10000.0 ** (-jnp.arange(half, dtype=jnp.float32) / half)
    angle = position[:, None] * freqs[None, :]
    cosine = jnp.cos(angle)[:, None, :]
    sine = jnp.sin(angle)[:, None, :]
    former = values[..., :half]
    latter = values[..., half:]
    return jnp.concatenate([former * cosine - latter * sine, former * sine + latter * cosine], -1)


def head_probs(query_in, key_in, allowed):
    scale = query_in.shape[-1] ** (-0.5)
    scores = (
        jnp.einsum("thd,shd->hts", query_in, key_in, preferred_element_type=jnp.float32) * scale
    )
    scores = jnp.where(allowed[None, :, :], scores, -1e30)
    shifted = scores - jnp.max(scores, -1, keepdims=True)
    weights = jnp.exp(shifted)
    return weights / jnp.sum(weights, -1, keepdims=True)


def conv_mask(values, taps, segment):
    total = taps[0][None, :] * values
    for offset in range(1, taps.shape[0]):
        moved = jnp.concatenate(
            [jnp.zeros((offset, values.shape[1]), values.dtype), values[:-offset]], 0
        )
        moved_seg = jnp.concatenate([jnp.full((offset,), -1, jnp.int32), segment[:-offset]], 0)
        same = (moved_seg == segment).astype(values.dtype)[:, None]
        total = total + taps[offset][None, :] * moved * same
    return total


def state_scan(inputs, step_sizes, decay, input_vecs, read_vecs, segment, block):
    length, heads, width = inputs.shape
    count = length // block
    states = input_vecs.shape[1]

    def one_block(carry, pieces):
        state, before = carry
        group_in, group_dt, group_b, group_c, group_seg = pieces
        logs = group_dt * decay[None, :]
        cumul = jnp.cumsum(logs, 0)
        places = jnp.arange(block, dtype=jnp.int32)
        allowed = (group_seg[:, None] == group_seg[None, :]) & (places[None, :] <= places[:, None])
        gaps = cumul[:, None, :] - cumul[None, :, :]
        fading = jnp.where(
            allowed[:, :, None], jnp.exp(jnp.where(allowed[:, :, None], gaps, 0.0)), 0.0
        )
        inner = jnp.dot(group_c, group_b.T, precision=highest)
        scaled = group_in * group_dt[:, :, None]
        local_out = jnp.einsum(
            "tsh,shp->thp", inner[:, :, None] * fading, scaled, precision=highest
        )
        carried = (group_seg == before).astype(inputs.dtype)
        entry = jnp.exp(cumul) * carried[:, None]
        from_state = (
            jnp.einsum("tn,hnp->thp", group_c, state, precision=highest) * entry[:, :, None]
        )
        last_seg = group_seg[-1]
        reach = (group_seg == last_seg).astype(inputs.dtype)
        to_end = jnp.exp(cumul[-1][None, :] - cumul) * reach[:, None]
        retain = jnp.exp(cumul[-1]) * (last_seg == before).astype(inputs.dtype)
        fresh = jnp.einsum("sn,sh,shp->hnp", group_b, to_end, scaled, precision=highest)
        state = state * retain[:, None, None] + fresh
        return ((state, last_seg), local_out + from_state)

    pieces = (
        inputs.reshape(count, block, heads, width),
        step_sizes.reshape(count, block, heads),
        input_vecs.reshape(count, block, states),
        read_vecs.reshape(count, block, states),
        segment.reshape(count, block),
    )
    start = (jnp.zeros((heads, states, width), inputs.dtype), jnp.array(-1, jnp.int32))
    unused, outputs = lax.scan(jax.checkpoint(one_block), start, pieces)
    return outputs.reshape(length, heads, width)


def mixer_core(
    inner_pre,
    input_pre,
    read_pre,
    step_pre,
    taps_x,
    taps_b,
    taps_c,
    shift_in,
    rate_in,
    segment,
    width,
    block,
):
    inner_conv = jax.nn.silu(conv_mask(inner_pre, taps_x, segment))
    input_conv = jax.nn.silu(conv_mask(input_pre, taps_b, segment))
    read_conv = jax.nn.silu(conv_mask(read_pre, taps_c, segment))
    step_sizes = jax.nn.softplus(step_pre + shift_in[None, :])
    heads = step_sizes.shape[1]
    length = inner_conv.shape[0]
    outputs = state_scan(
        inner_conv.reshape(length, heads, width),
        step_sizes,
        -jnp.exp(rate_in),
        input_conv,
        read_conv,
        segment,
        block,
    )
    return (outputs.reshape(length, heads * width), inner_conv)


def place_slice(piece, index, parts, axis):
    shape = list(piece.shape)
    shape[axis] = shape[axis] * parts
    holder = jnp.zeros(tuple(shape), jnp.float32)
    return lax.dynamic_update_slice_in_dim(holder, piece, index * piece.shape[axis], axis)


def take_slice(whole, index, width, axis):
    return lax.dynamic_slice_in_dim(whole, index * width, width, axis)


def general_device(
    hidden,
    embedding,
    cotangent,
    lengths,
    gain_attn,
    w_query,
    w_key,
    w_value,
    down_query,
    down_key,
    down_value,
    up_query,
    up_key,
    up_value,
    attn_output,
    gain_mlp,
    mlp_input,
    down_mlp,
    up_mlp,
    mlp_output,
    gain_mixer,
    proj_inner,
    proj_gate,
    proj_step,
    proj_input,
    proj_read,
    taps_inner,
    taps_input,
    taps_read,
    step_bias,
    log_rate,
    skip_gain,
    gain_gated,
    proj_output,
):
    row_count = hidden.shape[0]
    length = cotangent.shape[0]
    model_width = hidden.shape[1]
    head_parts = lax.axis_size(HEAD)
    state_parts = lax.axis_size(STATE)
    state_index = lax.axis_index(STATE)
    head_index = lax.axis_index(HEAD)
    own_start = state_index * row_count
    segment, position, valid = row_layout(lengths[0], length)
    own_segment = lax.dynamic_slice_in_dim(segment, own_start, row_count)
    own_position = lax.dynamic_slice_in_dim(position, own_start, row_count)
    own_valid = lax.dynamic_slice_in_dim(valid, own_start, row_count)[:, None]
    full_valid = valid[:, None]
    places = jnp.arange(length, dtype=jnp.int32)
    own_places = own_start + jnp.arange(row_count, dtype=jnp.int32)
    own_mask = ((places >= own_start) & (places < own_start + row_count)).astype(jnp.float32)[
        :, None
    ]
    allowed = (own_segment[:, None] == segment[None, :]) & (places[None, :] <= own_places[:, None])
    gathered = (
        lax.all_gather(gain_attn, ZED, axis=0, tiled=True),
        lax.all_gather(w_query, ZED, axis=0, tiled=True),
        lax.all_gather(w_key, ZED, axis=0, tiled=True),
        lax.all_gather(w_value, ZED, axis=0, tiled=True),
        lax.all_gather(down_query, ZED, axis=0, tiled=True),
        lax.all_gather(down_key, ZED, axis=0, tiled=True),
        lax.all_gather(down_value, ZED, axis=0, tiled=True),
        lax.all_gather(up_query, ZED, axis=0, tiled=True),
        lax.all_gather(up_key, ZED, axis=0, tiled=True),
        lax.all_gather(up_value, ZED, axis=0, tiled=True),
        lax.all_gather(attn_output, ZED, axis=1, tiled=True),
        lax.all_gather(gain_mlp, ZED, axis=0, tiled=True),
        lax.all_gather(mlp_input, ZED, axis=0, tiled=True),
        lax.all_gather(down_mlp, ZED, axis=0, tiled=True),
        lax.all_gather(up_mlp, ZED, axis=0, tiled=True),
        lax.all_gather(mlp_output, ZED, axis=1, tiled=True),
        lax.all_gather(gain_mixer, ZED, axis=0, tiled=True),
        lax.all_gather(proj_inner, ZED, axis=0, tiled=True),
        lax.all_gather(proj_gate, ZED, axis=0, tiled=True),
        lax.all_gather(proj_step, ZED, axis=0, tiled=True),
        lax.all_gather(proj_output, ZED, axis=1, tiled=True),
    )
    (
        attn_gain,
        query_main,
        key_main,
        value_main,
        query_down,
        key_down,
        value_down,
        query_upper,
        key_upper,
        value_upper,
        attn_proj,
        mlp_gain,
        mlp_main,
        mlp_down,
        mlp_upper,
        mlp_proj,
        mixer_gain,
        inner_main,
        gate_main,
        step_main,
        output_main,
    ) = gathered
    joined = jnp.concatenate([hidden, embedding], 1).astype(jnp.float32)
    attn_gain_f = attn_gain.astype(jnp.float32)
    normed = rms_norm(joined, attn_gain_f).astype(jnp.bfloat16)
    head_count = query_main.shape[1] // HDIM

    def project(main, down, upper):
        reduced = plain_dot(normed, down).astype(jnp.bfloat16)
        return (plain_dot(normed, main) + plain_dot(reduced, upper), reduced)

    query_pre, query_red = project(query_main, query_down, query_upper)
    key_pre, key_red = project(key_main, key_down, key_upper)
    value_pre, value_red = project(value_main, value_down, value_upper)
    queries = rotate(query_pre.reshape(row_count, head_count, HDIM), own_position).astype(
        jnp.bfloat16
    )
    keys_own = rotate(key_pre.reshape(row_count, head_count, HDIM), own_position).astype(
        jnp.bfloat16
    )
    values_own = value_pre.reshape(row_count, head_count, HDIM).astype(jnp.bfloat16)
    keys_all, values_all = (
        lax.all_gather(keys_own, STATE, axis=0, tiled=True),
        lax.all_gather(values_own, STATE, axis=0, tiled=True),
    )
    probs_full = head_probs(queries, keys_all, allowed)
    attended_f = jnp.einsum(
        "hts,shd->thd",
        probs_full.astype(jnp.bfloat16),
        values_all,
        preferred_element_type=jnp.float32,
    )
    attended = attended_f.reshape(row_count, head_count * HDIM).astype(jnp.bfloat16)
    branch = lax.psum(plain_dot(attended, attn_proj), HEAD)
    first = hidden.astype(jnp.float32) + own_valid * branch
    mlp_gain_f = mlp_gain.astype(jnp.float32)
    mlp_normed = rms_norm(first, mlp_gain_f).astype(jnp.bfloat16)
    mlp_red = plain_dot(mlp_normed, mlp_down).astype(jnp.bfloat16)
    hidden_pre = plain_dot(mlp_normed, mlp_main) + plain_dot(mlp_red, mlp_upper)
    activated = jax.nn.gelu(hidden_pre, approximate=False).astype(jnp.bfloat16)
    mlp_branch = lax.psum(plain_dot(activated, mlp_proj), HEAD)
    second = first + own_valid * mlp_branch
    second_all = lax.all_gather(second, STATE, axis=0, tiled=True)
    mixer_gain_f = mixer_gain.astype(jnp.float32)
    mixer_normed = rms_norm(second_all, mixer_gain_f).astype(jnp.bfloat16)
    states_own = proj_input.shape[1] // state_parts
    input_half = take_slice(proj_input, state_index, states_own, 1)
    read_half = take_slice(proj_read, state_index, states_own, 1)
    taps_input_half = take_slice(taps_input, state_index, states_own, 1).astype(jnp.float32)
    taps_read_half = take_slice(taps_read, state_index, states_own, 1).astype(jnp.float32)
    inner_pre = plain_dot(mixer_normed, inner_main)
    gate_pre = plain_dot(mixer_normed, gate_main)
    step_pre = plain_dot(mixer_normed, step_main)
    input_pre = plain_dot(mixer_normed, input_half)
    read_pre = plain_dot(mixer_normed, read_half)

    def mixer_piece(
        inner_in, input_in, read_in, step_in, taps_x, taps_b, taps_c, shift_in, rate_in
    ):
        return mixer_core(
            inner_in,
            input_in,
            read_in,
            step_in,
            taps_x,
            taps_b,
            taps_c,
            shift_in,
            rate_in,
            segment,
            MDIM,
            GROUP,
        )

    (scanned_part, inner_conv), mixer_back = jax.vjp(
        mixer_piece,
        inner_pre,
        input_pre,
        read_pre,
        step_pre,
        taps_inner.astype(jnp.float32),
        taps_input_half,
        taps_read_half,
        step_bias.astype(jnp.float32),
        log_rate.astype(jnp.float32),
    )
    scanned = lax.psum(scanned_part, STATE)
    skip_full = jnp.repeat(skip_gain.astype(jnp.float32), MDIM)[None, :]
    combined = scanned + skip_full * inner_conv
    gate_act = jax.nn.silu(gate_pre)
    united = combined * gate_act
    squares = lax.psum(jnp.sum(united * united, 1), HEAD)
    row_scale = lax.rsqrt(squares / DIN + epsilon)[:, None]
    gated_gain = gain_gated.astype(jnp.float32)[None, :]
    united_own = lax.dynamic_slice_in_dim(united, own_start, row_count, 0)
    scale_own = lax.dynamic_slice_in_dim(row_scale, own_start, row_count, 0)
    gated_own = (united_own * scale_own * gated_gain).astype(jnp.bfloat16)
    mixed_own = lax.psum(plain_dot(gated_own, output_main), HEAD)
    mixed = lax.all_gather(mixed_own, STATE, axis=0, tiled=True)
    layer_out = (second_all + full_valid * mixed).astype(jnp.bfloat16)
    upstream = cotangent.astype(jnp.float32)
    mix_grad = (full_valid * upstream).astype(jnp.bfloat16)
    mix_grad_own = lax.dynamic_slice_in_dim(mix_grad, own_start, row_count, 0)
    grad_output_main = left_dot(gated_own, mix_grad_own)
    gated_grad = right_dot(mix_grad, output_main)
    row_total = jnp.sum(mix_grad.astype(jnp.float32) * mixed, 1)[:, None] / row_scale
    grad_gated_gain = jnp.sum(gated_grad * united * row_scale * own_mask, 0)
    united_grad = (
        row_scale * gated_gain * gated_grad
        - united * row_scale * row_scale * row_scale * row_total / DIN
    )
    combined_grad = united_grad * gate_act
    sigmoid_gate = jax.nn.sigmoid(gate_pre)
    gate_grad = (
        united_grad * combined * sigmoid_gate * (1.0 + gate_pre * (1.0 - sigmoid_gate)) * own_mask
    )
    mixer_heads = step_pre.shape[1]
    grad_skip = jnp.sum(
        (combined_grad * inner_conv * own_mask).reshape(length, mixer_heads, MDIM), (0, 2)
    )
    conv_extra = skip_full * combined_grad * own_mask
    (
        inner_grad,
        input_grad,
        read_grad,
        step_grad,
        grad_taps_x,
        grad_taps_b,
        grad_taps_c,
        grad_shift,
        grad_rate,
    ) = mixer_back((combined_grad, conv_extra))
    mixer_part = (
        exact_right(inner_grad, inner_main)
        + exact_right(gate_grad, gate_main)
        + exact_right(step_grad, step_main)
        + exact_right(input_grad, input_half)
        + exact_right(read_grad, read_half)
    )
    grad_inner_main = exact_left(mixer_normed, inner_grad)
    grad_gate_main = exact_left(mixer_normed, gate_grad)
    grad_step_main = exact_left(mixer_normed, step_grad)
    grad_input_half = exact_left(mixer_normed, input_grad)
    grad_read_half = exact_left(mixer_normed, read_grad)
    mixer_rows_own = lax.psum_scatter(mixer_part, STATE, scatter_dimension=0, tiled=True)
    mixer_own = lax.psum(mixer_rows_own, HEAD)
    unused_norm, second_back = jax.vjp(rms_norm, second, mixer_gain_f)
    second_norm_grad, grad_mixer_gain = second_back(mixer_own)
    upstream_own = lax.dynamic_slice_in_dim(upstream, own_start, row_count, 0)
    second_grad = upstream_own + second_norm_grad
    mlp_grad = (own_valid * second_grad).astype(jnp.bfloat16)
    grad_mlp_proj = left_dot(activated, mlp_grad)
    activated_grad = right_dot(mlp_grad, mlp_proj)
    unused_gelu, gelu_back = jax.vjp(
        lambda preact: jax.nn.gelu(preact, approximate=False), hidden_pre
    )
    hidden_grad = gelu_back(activated_grad)[0].astype(jnp.bfloat16)
    grad_mlp_main = left_dot(mlp_normed, hidden_grad)
    grad_mlp_upper = left_dot(mlp_red, hidden_grad)
    mlp_middle = right_dot(hidden_grad, mlp_upper)
    mlp_part = right_dot(hidden_grad, mlp_main)
    mlp_sum, middle_sum = lax.psum((mlp_part, mlp_middle), HEAD)
    middle_low = middle_sum.astype(jnp.bfloat16)
    mlp_normed_grad = mlp_sum + right_dot(middle_low, mlp_down)
    grad_mlp_down = left_dot(mlp_normed, middle_low)
    unused_first, first_back = jax.vjp(rms_norm, first, mlp_gain_f)
    first_norm_grad, grad_mlp_gain = first_back(mlp_normed_grad)
    first_grad = second_grad + first_norm_grad
    branch_grad = (own_valid * first_grad).astype(jnp.bfloat16)
    grad_attn_proj = left_dot(attended, branch_grad)
    attended_grad = right_dot(branch_grad, attn_proj).reshape(row_count, head_count, HDIM)
    probs_back = head_probs(queries, keys_all, allowed)
    score_scale = HDIM ** (-0.5)
    out_low = attended_grad.astype(jnp.bfloat16)
    prob_grad = jnp.einsum("thd,shd->hts", out_low, values_all, preferred_element_type=jnp.float32)
    score_grad = probs_back * (prob_grad - jnp.sum(probs_back * prob_grad, -1, keepdims=True))
    score_low = score_grad.astype(jnp.bfloat16)
    query_back = (
        jnp.einsum("hts,shd->thd", score_low, keys_all, preferred_element_type=jnp.float32)
        * score_scale
    )
    keys_back = (
        jnp.einsum("hts,thd->shd", score_low, queries, preferred_element_type=jnp.float32)
        * score_scale
    )
    values_back = jnp.einsum(
        "hts,thd->shd", probs_back.astype(jnp.bfloat16), out_low, preferred_element_type=jnp.float32
    )
    keys_grad_own, values_grad_own = (
        lax.psum_scatter(keys_back, STATE, scatter_dimension=0, tiled=True),
        lax.psum_scatter(values_back, STATE, scatter_dimension=0, tiled=True),
    )
    query_grad = (
        rotate(query_back, -own_position).reshape(row_count, head_count * HDIM).astype(jnp.bfloat16)
    )
    key_grad = (
        rotate(keys_grad_own, -own_position)
        .reshape(row_count, head_count * HDIM)
        .astype(jnp.bfloat16)
    )
    value_grad = values_grad_own.reshape(row_count, head_count * HDIM).astype(jnp.bfloat16)
    grad_query_main = left_dot(normed, query_grad)
    grad_key_main = left_dot(normed, key_grad)
    grad_value_main = left_dot(normed, value_grad)
    grad_query_upper = left_dot(query_red, query_grad)
    grad_key_upper = left_dot(key_red, key_grad)
    grad_value_upper = left_dot(value_red, value_grad)
    query_middle = right_dot(query_grad, query_upper)
    key_middle = right_dot(key_grad, key_upper)
    value_middle = right_dot(value_grad, value_upper)
    normed_part = (
        right_dot(query_grad, query_main)
        + right_dot(key_grad, key_main)
        + right_dot(value_grad, value_main)
    )
    normed_sum, query_msum, key_msum, value_msum = lax.psum(
        (normed_part, query_middle, key_middle, value_middle), HEAD
    )
    query_low = query_msum.astype(jnp.bfloat16)
    key_low = key_msum.astype(jnp.bfloat16)
    value_low = value_msum.astype(jnp.bfloat16)
    normed_grad = (
        normed_sum
        + right_dot(query_low, query_down)
        + right_dot(key_low, key_down)
        + right_dot(value_low, value_down)
    )
    grad_query_down = left_dot(normed, query_low)
    grad_key_down = left_dot(normed, key_low)
    grad_value_down = left_dot(normed, value_low)
    unused_joined, joined_back = jax.vjp(rms_norm, joined, attn_gain_f)
    joined_grad, grad_attn_gain = joined_back(normed_grad)
    grad_hidden = (first_grad + joined_grad[:, :model_width]).astype(jnp.bfloat16)
    grad_embedding = joined_grad[:, model_width:].astype(jnp.bfloat16)
    scattered = (
        lax.psum_scatter(grad_attn_gain, ZED, scatter_dimension=0, tiled=True),
        lax.psum_scatter(grad_query_main, ZED, scatter_dimension=0, tiled=True),
        lax.psum_scatter(grad_key_main, ZED, scatter_dimension=0, tiled=True),
        lax.psum_scatter(grad_value_main, ZED, scatter_dimension=0, tiled=True),
        lax.psum_scatter(grad_query_down, ZED, scatter_dimension=0, tiled=True),
        lax.psum_scatter(grad_key_down, ZED, scatter_dimension=0, tiled=True),
        lax.psum_scatter(grad_value_down, ZED, scatter_dimension=0, tiled=True),
        lax.psum_scatter(grad_query_upper, ZED, scatter_dimension=0, tiled=True),
        lax.psum_scatter(grad_key_upper, ZED, scatter_dimension=0, tiled=True),
        lax.psum_scatter(grad_value_upper, ZED, scatter_dimension=0, tiled=True),
        lax.psum_scatter(grad_attn_proj, ZED, scatter_dimension=1, tiled=True),
        lax.psum_scatter(grad_mlp_gain, ZED, scatter_dimension=0, tiled=True),
        lax.psum_scatter(grad_mlp_main, ZED, scatter_dimension=0, tiled=True),
        lax.psum_scatter(grad_mlp_down, ZED, scatter_dimension=0, tiled=True),
        lax.psum_scatter(grad_mlp_upper, ZED, scatter_dimension=0, tiled=True),
        lax.psum_scatter(grad_mlp_proj, ZED, scatter_dimension=1, tiled=True),
        lax.psum_scatter(grad_mixer_gain, ZED, scatter_dimension=0, tiled=True),
        lax.psum_scatter(grad_inner_main, ZED, scatter_dimension=0, tiled=True),
        lax.psum_scatter(grad_gate_main, ZED, scatter_dimension=0, tiled=True),
        lax.psum_scatter(grad_step_main, ZED, scatter_dimension=0, tiled=True),
        lax.psum_scatter(grad_output_main, ZED, scatter_dimension=1, tiled=True),
    )
    first_head = (head_index == 0).astype(jnp.float32)
    square_sum = jnp.zeros((), jnp.float32)
    for index in [1, 2, 3, 7, 8, 9, 10, 12, 14, 15]:
        square_sum = square_sum + jnp.sum(scattered[index] * scattered[index])
    for index in [4, 5, 6, 13]:
        square_sum = square_sum + first_head * jnp.sum(scattered[index] * scattered[index])
    head_params = jnp.stack([grad_shift, grad_rate, grad_skip], 0)
    totals = lax.psum(
        (
            square_sum,
            place_slice(grad_gated_gain, head_index, head_parts, 0),
            place_slice(grad_taps_x, head_index, head_parts, 1),
            place_slice(head_params, head_index, head_parts, 1),
            place_slice(grad_input_half, state_index, state_parts, 1),
            place_slice(grad_read_half, state_index, state_parts, 1),
            place_slice(grad_taps_b, state_index, state_parts, 1),
            place_slice(grad_taps_c, state_index, state_parts, 1),
        ),
        EVERY,
    )
    (
        square_total,
        gated_full,
        taps_full,
        heads_full,
        input_full,
        read_full,
        taps_input_full,
        taps_read_full,
    ) = totals
    head_width = gain_gated.shape[0]
    tap_width = taps_inner.shape[1]
    param_width = step_bias.shape[0]
    heads_own = take_slice(heads_full, head_index, param_width, 1)
    return (
        layer_out,
        grad_hidden,
        grad_embedding,
        scattered[0],
        scattered[1],
        scattered[2],
        scattered[3],
        scattered[4],
        scattered[5],
        scattered[6],
        scattered[7],
        scattered[8],
        scattered[9],
        scattered[10],
        scattered[11],
        scattered[12],
        scattered[13],
        scattered[14],
        scattered[15],
        scattered[16],
        scattered[17],
        scattered[18],
        scattered[19],
        input_full,
        read_full,
        take_slice(taps_full, head_index, tap_width, 1),
        taps_input_full,
        taps_read_full,
        heads_own[0],
        heads_own[1],
        heads_own[2],
        take_slice(gated_full, head_index, head_width, 0),
        scattered[20],
        jnp.sqrt(square_total),
    )


low = jnp.bfloat16
full = jnp.float32


def head_masks():
    count = lax.axis_size(HEAD)
    masks = [1 << bit for bit in range(count.bit_length() - 1)]
    return masks[:1] + masks[1:], masks[:1] + masks[1:][::-1]


def head_swap(value, mask):
    count = lax.axis_size(HEAD)
    return lax.ppermute(value, HEAD, [(i, i ^ mask) for i in range(count)])


def state_swap(value):
    return lax.ppermute(value, STATE, [(0, 1), (1, 0)])


def dp_swap(value):
    return lax.ppermute(value, DP, [(0, 1), (1, 0)])


def state_forward(value):
    return lax.ppermute(value, STATE, [(0, 1)])


def state_backward(value):
    return lax.ppermute(value, STATE, [(1, 0)])


def bit_of(mask):
    return (lax.axis_index(HEAD) // mask) % 2


def chunk_of(masks):
    chunk = 0
    for mask in masks:
        chunk = chunk * 2 + bit_of(mask)
    return chunk


def sum_rows(value, masks, axis):
    for mask in masks:
        bit = bit_of(mask)
        half = value.shape[axis] // 2
        away = lax.dynamic_slice_in_dim(value, (1 - bit) * half, half, axis).astype(low)
        kept = lax.dynamic_slice_in_dim(value, bit * half, half, axis)
        value = kept.astype(full) + head_swap(away, mask).astype(full)
    return value


def gather_rows(value, masks, axis):
    for mask in masks[::-1]:
        bit = bit_of(mask)
        got = head_swap(value, mask)
        value = jnp.concatenate(
            [jnp.where(bit == 1, got, value), jnp.where(bit == 1, value, got)], axis
        )
    return value


def sum_row16(value, masks):
    state = lax.axis_index(STATE)
    value = sum_rows(value, masks, 1)
    away = lax.dynamic_index_in_dim(value, 1 - state, 0, False).astype(low)
    kept = lax.dynamic_index_in_dim(value, state, 0, False)
    return kept + state_swap(away).astype(full)


def gather_row16(value, masks):
    state = lax.axis_index(STATE)
    got = state_swap(value)
    both = jnp.stack([jnp.where(state == 0, value, got), jnp.where(state == 0, got, value)], 0)
    return gather_rows(both, masks, 1)


def pick_state(pair, index):
    return jnp.where(index == 0, pair[0], pair[1])


def weight_pieces(shard, axis):
    state = lax.axis_index(STATE)
    dp = lax.axis_index(DP)
    half = shard.shape[axis] // 2
    mine = lax.dynamic_slice_in_dim(shard, state * half, half, axis)
    got = state_swap(lax.dynamic_slice_in_dim(shard, (1 - state) * half, half, axis))
    far_mine = dp_swap(mine)
    far_got = dp_swap(got)
    near = [jnp.where(state == 0, mine, got), jnp.where(state == 0, got, mine)]
    far = [jnp.where(state == 0, far_mine, far_got), jnp.where(state == 0, far_got, far_mine)]
    lower = [jnp.where(dp == 0, a, b) for a, b in zip(near, far)]
    upper = [jnp.where(dp == 0, b, a) for a, b in zip(near, far)]
    return jnp.concatenate(lower + upper, 1 - axis)


def grad_pieces(grad, axis):
    state = lax.axis_index(STATE)
    dp = lax.axis_index(DP)
    half = grad.shape[1 - axis] // 2
    away = lax.dynamic_slice_in_dim(grad, (1 - dp) * half, half, 1 - axis).astype(low)
    kept = lax.dynamic_slice_in_dim(grad, dp * half, half, 1 - axis)
    total = kept + dp_swap(away).astype(full)
    quarter = half // 2
    away = lax.dynamic_slice_in_dim(total, (1 - state) * quarter, quarter, 1 - axis).astype(low)
    kept = lax.dynamic_slice_in_dim(total, state * quarter, quarter, 1 - axis)
    got = state_swap(away).astype(full)
    return jnp.concatenate(
        [jnp.where(state == 0, kept, got), jnp.where(state == 0, got, kept)], axis
    )


def norm_scale(values):
    return lax.rsqrt(jnp.mean(values * values, -1, keepdims=True) + epsilon)


def norm_back(values, gain, grad):
    scale = norm_scale(values)
    scaled = grad * gain
    inner = jnp.mean(scaled * values, -1, keepdims=True)
    return (
        scale * scaled - values * (scale * scale * scale * inner),
        jnp.sum(grad * values * scale, 0),
    )


def conv_edge(values, edge, taps, segment, edge_segment):
    reach = taps.shape[0] - 1
    rows = values.shape[0]
    joined = jnp.concatenate([edge, values], 0)
    segs = jnp.concatenate([edge_segment, segment], 0)
    total = taps[0][None, :] * values
    for offset in range(1, taps.shape[0]):
        lower = reach - offset
        same = (segs[lower : lower + rows] == segment).astype(values.dtype)[:, None]
        total = total + taps[offset][None, :] * joined[lower : lower + rows] * same
    return total


def vmem_limit(mebibytes):
    return pltpu.CompilerParams(vmem_limit_bytes=mebibytes * 1024 * 1024)


def dot_nt(left, right):
    return lax.dot_general(left, right, (((1,), (1,)), ((), ())), preferred_element_type=full)


def dot_tn(left, right):
    return lax.dot_general(left, right, (((0,), (0,)), ((), ())), preferred_element_type=full)


def dot_nn(left, right):
    return lax.dot_general(left, right, (((1,), (0,)), ((), ())), preferred_element_type=full)


def dot_exact(left, right):
    return jnp.dot(left, right, preferred_element_type=full, precision=highest)


ROWS_Q = 256
ROWS_K = 512


def attend_kernel(low_ref, q_ref, k_ref, v_ref, seg_col, seg_row, out_ref, lse_ref):
    index = pl.program_id(1)
    scale = q_ref.shape[1] ** (-0.5)
    query = q_ref[...]
    own = seg_col[...]
    place = index * ROWS_Q + lax.broadcasted_iota(jnp.int32, (ROWS_Q, ROWS_K), 0)

    def step(block, carry):
        top, total, acc = carry
        span = pl.ds(pl.multiple_of(block * ROWS_K, ROWS_K), ROWS_K)
        scores = dot_nt(query, k_ref[span, :]) * scale
        other = block * ROWS_K + lax.broadcasted_iota(jnp.int32, (ROWS_Q, ROWS_K), 1)
        scores = jnp.where((own == seg_row[:, span]) & (other <= place), scores, -1e30)
        higher = jnp.maximum(top, jnp.max(scores, -1, keepdims=True))
        weights = jnp.exp(scores - higher)
        fade = jnp.exp(top - higher)
        total = total * fade + jnp.sum(weights, -1, keepdims=True)
        acc = acc * fade + dot_nn(weights.astype(low), v_ref[span, :])
        return higher, total, acc

    start = (
        jnp.full((ROWS_Q, 1), -1e30, full),
        jnp.zeros((ROWS_Q, 1), full),
        jnp.zeros((ROWS_Q, v_ref.shape[1]), full),
    )
    stop = (index * ROWS_Q + ROWS_Q + ROWS_K - 1) // ROWS_K
    top, total, acc = lax.fori_loop(low_ref[index], stop, step, start)
    out_ref[...] = (acc / total).astype(low)
    lse = jnp.broadcast_to(top + jnp.log(total), (ROWS_Q, 128))
    lse_ref[...] = lse.T[0:1, :][None]


def attend(queries, keys, values, segment, lows):
    length, columns = queries.shape
    heads = columns // HDIM
    whole = pl.BlockSpec((length, HDIM), lambda h, i, *_: (0, h))
    block = pl.BlockSpec((ROWS_Q, HDIM), lambda h, i, *_: (i, h))
    return pl.pallas_call(
        attend_kernel,
        grid_spec=pltpu.PrefetchScalarGridSpec(
            num_scalar_prefetch=1,
            grid=(heads, length // ROWS_Q),
            in_specs=[
                block,
                whole,
                whole,
                pl.BlockSpec((ROWS_Q, 1), lambda h, i, *_: (i, 0)),
                pl.BlockSpec((1, length), lambda h, i, *_: (0, 0)),
            ],
            out_specs=[block, pl.BlockSpec((1, 1, ROWS_Q), lambda h, i, *_: (h, 0, i))],
        ),
        out_shape=[
            jax.ShapeDtypeStruct((length, columns), low),
            jax.ShapeDtypeStruct((heads, 1, length), full),
        ],
        compiler_params=vmem_limit(40),
        cost_estimate=pl.CostEstimate(
            flops=2 * length * length * columns, bytes_accessed=8 * length * columns,
            transcendentals=length * length * heads // 2,
        ),
    )(lows, queries, keys, values, segment[:, None], segment[None, :])


def attend_back_kernel(
    low_ref, q_ref, k_ref, v_ref, do_ref, lse_ref, delta_ref, seg_col, seg_row, dq_ref, dk_ref, dv_ref
):
    index = pl.program_id(1)
    scale = q_ref.shape[1] ** (-0.5)
    query = q_ref[...]
    grad = do_ref[...]
    own = seg_row[...]
    lse = lse_ref[0]
    delta = delta_ref[0]
    place = index * ROWS_Q + lax.broadcasted_iota(jnp.int32, (ROWS_K, ROWS_Q), 1)

    @pl.when(index == 0)
    def clear():
        dk_ref[...] = jnp.zeros_like(dk_ref)
        dv_ref[...] = jnp.zeros_like(dv_ref)

    def step(block, total):
        span = pl.ds(pl.multiple_of(block * ROWS_K, ROWS_K), ROWS_K)
        key = k_ref[span, :]
        scores = dot_nt(key, query) * scale
        other = block * ROWS_K + lax.broadcasted_iota(jnp.int32, (ROWS_K, ROWS_Q), 0)
        counted = (seg_col[span, :] == own) & (other <= place)
        probs = jnp.exp(jnp.where(counted, scores - lse, -1e30))
        dv_ref[span, :] += dot_nn(probs.astype(low), grad)
        slope = probs * (dot_nt(v_ref[span, :], grad) - delta)
        slope = slope.astype(low)
        dk_ref[span, :] += dot_nn(slope, query) * scale
        return total + dot_tn(slope, key)

    stop = (index * ROWS_Q + ROWS_Q + ROWS_K - 1) // ROWS_K
    total = lax.fori_loop(low_ref[index], stop, step, jnp.zeros((ROWS_Q, HDIM), full))
    dq_ref[...] = total * scale


def attend_back(queries, keys, values, grads, lse, delta, segment, lows):
    length, columns = queries.shape
    heads = columns // HDIM
    whole = pl.BlockSpec((length, HDIM), lambda h, i, *_: (0, h))
    block = pl.BlockSpec((ROWS_Q, HDIM), lambda h, i, *_: (i, h))
    line = pl.BlockSpec((1, 1, ROWS_Q), lambda h, i, *_: (h, 0, i))
    shape = jax.ShapeDtypeStruct((length, columns), full)
    return pl.pallas_call(
        attend_back_kernel,
        grid_spec=pltpu.PrefetchScalarGridSpec(
            num_scalar_prefetch=1,
            grid=(heads, length // ROWS_Q),
            in_specs=[
                block,
                whole,
                whole,
                block,
                line,
                line,
                pl.BlockSpec((length, 1), lambda h, i, *_: (0, 0)),
                pl.BlockSpec((1, ROWS_Q), lambda h, i, *_: (0, i)),
            ],
            out_specs=[block, whole, whole],
        ),
        out_shape=[shape, shape, shape],
        compiler_params=vmem_limit(40),
        cost_estimate=pl.CostEstimate(
            flops=5 * length * length * columns, bytes_accessed=20 * length * columns,
            transcendentals=length * length * heads // 2,
        ),
    )(lows, queries, keys, values, grads, lse, delta, segment[:, None], segment[None, :])


def first_blocks(segment):
    length = segment.shape[0]
    heads = segment[::ROWS_Q]
    starts = jnp.sum((segment[None, :] < heads[:, None]).astype(jnp.int32), 1)
    return starts // ROWS_K


def pair_lanes(left, right):
    lane = lax.broadcasted_iota(jnp.int32, (1, 2 * MDIM), 1)
    return jnp.where(lane < MDIM, left, right)


def block_decay(dt_ref, dt_row_ref, rate_ref, rate_col_ref):
    rows = lax.broadcasted_iota(jnp.int32, (GROUP, GROUP), 0)
    cols = lax.broadcasted_iota(jnp.int32, (GROUP, GROUP), 1)
    cumul = dot_exact((cols <= rows).astype(full), dt_ref[...] * rate_ref[...])
    cumul_row = dot_exact(dt_row_ref[...] * rate_col_ref[...], (rows <= cols).astype(full))
    return cumul, cumul_row, rows, cols


def edge_flags(ends_ref, index, seg_col):
    before = ends_ref[index]
    last = ends_ref[index + 1]
    carried = (seg_col[...] == before).astype(full)
    reach = (seg_col[...] == last).astype(full)
    keep = (before == last).astype(full)
    return carried, reach, keep


def pair_columns(values, pair):
    return pair_lanes(values[:, 2 * pair : 2 * pair + 1], values[:, 2 * pair + 1 : 2 * pair + 2])


def step_state(state, pair, scaled, cumul, reach, keep, vec_low):
    column = pair_columns(cumul, pair)
    end = column[GROUP - 1 : GROUP, :]
    weight = jnp.exp(end - column) * reach
    return state * (jnp.exp(end) * keep) + dot_tn(vec_low, (scaled * weight).astype(low)), weight


def scan_end_kernel(
    ends_ref, x_ref, dt_ref, dt_row_ref, rate_ref, rate_col_ref, b_ref, seg_col, out_ref
):
    index = pl.program_id(0)
    cumul, unused_row, unused_a, unused_b = block_decay(dt_ref, dt_row_ref, rate_ref, rate_col_ref)
    unused_c, reach, keep = edge_flags(ends_ref, index, seg_col)
    vec_low = b_ref[...].astype(low)

    @pl.when(index == 0)
    def clear():
        out_ref[...] = jnp.zeros_like(out_ref)

    for pair in range(dt_ref.shape[1] // 2):
        lanes = slice(pair * 2 * MDIM, (pair + 1) * 2 * MDIM)
        scaled = x_ref[:, lanes] * pair_columns(dt_ref[...], pair)
        out_ref[:, lanes], unused_d = step_state(
            out_ref[:, lanes], pair, scaled, cumul, reach, keep, vec_low
        )


def scan_kernel(
    ends_ref,
    x_ref,
    dt_ref,
    dt_row_ref,
    rate_ref,
    rate_col_ref,
    b_ref,
    c_ref,
    seg_col,
    seg_row,
    first_ref,
    out_ref,
    states_ref,
    state,
):
    index = pl.program_id(0)
    cumul, cumul_row, rows, cols = block_decay(dt_ref, dt_row_ref, rate_ref, rate_col_ref)
    carried, reach, keep = edge_flags(ends_ref, index, seg_col)
    vec_low = b_ref[...].astype(low)
    read_low = c_ref[...].astype(low)
    allowed = (seg_col[...] == seg_row[...]) & (cols <= rows)
    inner = jnp.where(allowed, dot_nt(read_low, vec_low), 0.0)

    @pl.when(index == 0)
    def begin():
        state[...] = first_ref[...]

    states_ref[0] = state[...]
    for pair in range(dt_ref.shape[1] // 2):
        lanes = slice(pair * 2 * MDIM, (pair + 1) * 2 * MDIM)
        scaled = x_ref[:, lanes] * pair_columns(dt_ref[...], pair)
        scaled_low = scaled.astype(low)
        parts = []
        for head in (2 * pair, 2 * pair + 1):
            gaps = cumul[:, head : head + 1] - cumul_row[head : head + 1, :]
            mixed = inner * jnp.exp(jnp.minimum(gaps, 0.0))
            parts.append(dot_nn(mixed.astype(low), scaled_low))
        entry = jnp.exp(pair_columns(cumul, pair)) * carried
        held = state[:, lanes]
        out_ref[:, lanes] = pair_lanes(*parts) + dot_nn(read_low, held.astype(low)) * entry
        state[:, lanes], unused = step_state(
            held, pair, scaled, cumul, reach, keep, vec_low
        )


def scan_start_grad_kernel(
    ends_ref, dt_ref, dt_row_ref, rate_ref, rate_col_ref, c_ref, seg_col, dy_ref, out_ref
):
    index = pl.num_programs(0) - 1 - pl.program_id(0)
    cumul, unused_row, unused_a, unused_b = block_decay(dt_ref, dt_row_ref, rate_ref, rate_col_ref)
    carried, unused_c, keep = edge_flags(ends_ref, index, seg_col)
    read_low = c_ref[...].astype(low)

    @pl.when(pl.program_id(0) == 0)
    def clear():
        out_ref[...] = jnp.zeros_like(out_ref)

    for pair in range(dt_ref.shape[1] // 2):
        lanes = slice(pair * 2 * MDIM, (pair + 1) * 2 * MDIM)
        column = pair_columns(cumul, pair)
        retain = jnp.exp(column[GROUP - 1 : GROUP, :]) * keep
        entry = jnp.exp(column) * carried
        out_ref[:, lanes] = out_ref[:, lanes] * retain + dot_tn(
            read_low, (dy_ref[:, lanes] * entry).astype(low)
        )


def scan_back_kernel(
    ends_ref,
    x_ref,
    dt_ref,
    dt_row_ref,
    rate_ref,
    rate_col_ref,
    b_ref,
    c_ref,
    seg_col,
    seg_row,
    dy_ref,
    states_ref,
    last_ref,
    dx_ref,
    ddt_ref,
    dlog_ref,
    dlog_row_ref,
    db_ref,
    dc_ref,
    state_grad,
    inner_grad,
):
    index = pl.num_programs(0) - 1 - pl.program_id(0)
    heads = dt_ref.shape[1]
    cumul, cumul_row, rows, cols = block_decay(dt_ref, dt_row_ref, rate_ref, rate_col_ref)
    carried, reach, keep = edge_flags(ends_ref, index, seg_col)
    vec_low = b_ref[...].astype(low)
    read_low = c_ref[...].astype(low)
    allowed = (seg_col[...] == seg_row[...]) & (cols <= rows)
    inner = jnp.where(allowed, dot_nt(read_low, vec_low), 0.0)
    head_lane = lax.broadcasted_iota(jnp.int32, (GROUP, heads), 1)
    head_row = lax.broadcasted_iota(jnp.int32, (heads, GROUP), 0)
    last_row = lax.broadcasted_iota(jnp.int32, (GROUP, 1), 0) == GROUP - 1
    lane = lax.broadcasted_iota(jnp.int32, (1, 2 * MDIM), 1)

    @pl.when(pl.program_id(0) == 0)
    def begin():
        state_grad[...] = last_ref[...]

    inner_grad[...] = jnp.zeros_like(inner_grad)
    decay_grad = jnp.zeros((GROUP, heads), full)
    decay_row = jnp.zeros((heads, GROUP), full)
    step_grad = jnp.zeros((GROUP, heads), full)
    vec_grad = jnp.zeros(b_ref.shape, full)
    read_grad = jnp.zeros(c_ref.shape, full)
    for pair in range(heads // 2):
        lanes = slice(pair * 2 * MDIM, (pair + 1) * 2 * MDIM)
        values = x_ref[:, lanes]
        steps = pair_columns(dt_ref[...], pair)
        scaled = values * steps
        scaled_low = scaled.astype(low)
        grad = dy_ref[:, lanes]
        grad_low = grad.astype(low)
        held = states_ref[0, :, lanes]
        held_low = held.astype(low)
        later = state_grad[:, lanes]
        later_low = later.astype(low)
        column = pair_columns(cumul, pair)
        end = column[GROUP - 1 : GROUP, :]
        weight = jnp.exp(end - column) * reach
        retain = jnp.exp(end) * keep
        entry = jnp.exp(column) * carried
        parts = []
        for side in range(2):
            head = 2 * pair + side
            gaps = cumul[:, head : head + 1] - cumul_row[head : head + 1, :]
            fading = jnp.where(allowed, jnp.exp(jnp.minimum(gaps, 0.0)), 0.0)
            mixed = inner * fading
            own_lanes = (lane < MDIM) == (side == 0)
            outer = dot_nt(jnp.where(own_lanes, grad, 0.0).astype(low), scaled_low)
            inner_grad[...] += outer * fading
            slope = outer * mixed
            decay_grad = jnp.where(
                head_lane == head, decay_grad + jnp.sum(slope, 1, keepdims=True), decay_grad
            )
            decay_row = jnp.where(
                head_row == head, jnp.sum(slope, 0, keepdims=True), decay_row
            )
            parts.append(dot_tn(mixed.astype(low), grad_low))
        weighted = scaled * weight
        entered = grad * entry
        entered_low = entered.astype(low)
        from_later = dot_nn(vec_low, later_low)
        scaled_grad = pair_lanes(*parts) + weight * from_later
        dx_ref[:, lanes] = scaled_grad * steps
        read_grad += dot_nt(entered_low, held_low)
        vec_grad += dot_nt(weighted.astype(low), later_low)
        fresh = weighted * from_later
        flow = entered * dot_nn(read_low, held_low) - fresh
        finish = jnp.sum(fresh, 0, keepdims=True) + retain * jnp.sum(later * held, 0, keepdims=True)
        steps_part = scaled_grad * values
        for side in range(2):
            head = 2 * pair + side
            own_lanes = (lane < MDIM) == (side == 0)
            total = jnp.sum(jnp.where(own_lanes, flow, 0.0), 1, keepdims=True)
            ending = jnp.sum(jnp.where(own_lanes, finish, 0.0), 1, keepdims=True)
            total = total + jnp.where(last_row, ending, 0.0)
            decay_grad = jnp.where(head_lane == head, decay_grad + total, decay_grad)
            step_grad = jnp.where(
                head_lane == head,
                jnp.sum(jnp.where(own_lanes, steps_part, 0.0), 1, keepdims=True),
                step_grad,
            )
        state_grad[:, lanes] = later * retain + dot_tn(read_low, entered_low)
    inner_low = inner_grad[...].astype(low)
    ddt_ref[...] = step_grad
    dlog_ref[...] = dot_exact((cols >= rows).astype(full), decay_grad)
    dlog_row_ref[...] = dot_exact(decay_row, (rows >= cols).astype(full))
    dc_ref[...] = read_grad + dot_nn(inner_low, vec_low)
    db_ref[...] = vec_grad + dot_tn(inner_low, read_low)


def scan_specs(heads, channels, states, reverse, count):
    def at(i):
        return count - 1 - i if reverse else i

    tall = lambda columns: pl.BlockSpec((GROUP, columns), lambda i, *_: (at(i), 0))
    flat = lambda rows: pl.BlockSpec((rows, GROUP), lambda i, *_: (0, at(i)))
    same = lambda rows, columns: pl.BlockSpec((rows, columns), lambda i, *_: (0, 0))
    return tall, flat, same, pl.BlockSpec((1, states, channels), lambda i, *_: (at(i), 0, 0))


def scan_call(kernel, reverse, ends, inputs, kinds, outs, out_kinds, scratch, dims, flops):
    heads, channels, states, count = dims
    tall, flat, same, cube = scan_specs(heads, channels, states, reverse, count)

    def spec(kind, shape):
        if kind == 0:
            return tall(shape[1])
        if kind == 1:
            return flat(shape[0])
        return same(*shape) if kind == 2 else cube

    return pl.pallas_call(
        kernel,
        grid_spec=pltpu.PrefetchScalarGridSpec(
            num_scalar_prefetch=1,
            grid=(count,),
            in_specs=[spec(kind, value.shape) for kind, value in zip(kinds, inputs)],
            out_specs=[spec(kind, shape) for kind, shape in zip(out_kinds, outs)],
            scratch_shapes=scratch,
        ),
        out_shape=[jax.ShapeDtypeStruct(shape, full) for shape in outs],
        compiler_params=vmem_limit(40),
        cost_estimate=pl.CostEstimate(
            flops=flops, bytes_accessed=8 * count * GROUP * channels, transcendentals=flops // 256
        ),
    )(ends, *inputs)


class Scan:
    def __init__(self, x, dt, rate, b, c, segment, before):
        self.rows, self.heads = dt.shape
        self.channels, self.states = x.shape[1], b.shape[1]
        self.count = self.rows // GROUP
        self.dims = (self.heads, self.channels, self.states, self.count)
        self.ends = jnp.concatenate([before[None], segment[GROUP - 1 :: GROUP]])
        self.x, self.b, self.c = x, b, c
        self.decay = [dt, dt.T, rate[None, :], rate[:, None]]
        self.seg_col, self.seg_row = segment[:, None], segment[None, :]
        self.state_shape = (self.states, self.channels)

    def end(self):
        return scan_call(
            scan_end_kernel,
            False,
            self.ends,
            [self.x, *self.decay, self.b, self.seg_col],
            [0, 0, 1, 2, 2, 0, 0],
            [self.state_shape],
            [2],
            [],
            self.dims,
            2 * self.rows * self.channels * self.states,
        )[0]

    def forward(self, first):
        return scan_call(
            scan_kernel,
            False,
            self.ends,
            [self.x, *self.decay, self.b, self.c, self.seg_col, self.seg_row, first],
            [0, 0, 1, 2, 2, 0, 0, 0, 1, 2],
            [self.x.shape, (self.count,) + self.state_shape],
            [0, 3],
            [pltpu.VMEM(self.state_shape, full)],
            self.dims,
            8 * self.rows * self.channels * GROUP,
        )

    def start_grad(self, grad):
        return scan_call(
            scan_start_grad_kernel,
            True,
            self.ends,
            [*self.decay, self.c, self.seg_col, grad],
            [0, 1, 2, 2, 0, 0, 0],
            [self.state_shape],
            [2],
            [],
            self.dims,
            2 * self.rows * self.channels * self.states,
        )[0]

    def backward(self, grad, states, last):
        wide = (self.rows, self.heads)
        return scan_call(
            scan_back_kernel,
            True,
            self.ends,
            [
                self.x,
                *self.decay,
                self.b,
                self.c,
                self.seg_col,
                self.seg_row,
                grad,
                states,
                last,
            ],
            [0, 0, 1, 2, 2, 0, 0, 0, 1, 0, 3, 2],
            [self.x.shape, wide, wide, wide[::-1], self.b.shape, self.c.shape],
            [0, 0, 0, 1, 0, 0],
            [pltpu.VMEM(self.state_shape, full), pltpu.VMEM((GROUP, GROUP), full)],
            self.dims,
            24 * self.rows * self.channels * GROUP,
        )


def natural_quarters(relative):
    state = lax.axis_index(STATE)
    dp = lax.axis_index(DP)
    near = [jnp.where(state == 0, *relative[:2]), jnp.where(state == 0, *relative[1::-1])]
    far = [jnp.where(state == 0, *relative[2:]), jnp.where(state == 0, *relative[:1:-1])]
    return [jnp.where(dp == 0, a, b) for a, b in zip(near, far)] + [
        jnp.where(dp == 0, b, a) for a, b in zip(near, far)
    ]


def z_pieces(value):
    beside = state_swap(value)
    return [value, beside, dp_swap(value), dp_swap(beside)]


def swap_quarters(value):
    quarter = value.shape[-1] // 4
    part = [value[..., i * quarter : (i + 1) * quarter] for i in range(4)]
    return jnp.concatenate([part[1], part[0], part[3], part[2]], -1)


def add_everywhere(value):
    for mask in head_masks()[0]:
        value = value + head_swap(value, mask)
    return add_zed(value)


def add_zed(value):
    value = value + state_swap(value)
    return value + dp_swap(value)


def by_state(own, other):
    state = lax.axis_index(STATE)
    return jnp.concatenate([jnp.where(state == 0, own, other), jnp.where(state == 0, other, own)], 0)


def turn(value, cosine, sine):
    rows = value.shape[0]
    cubes = value.reshape(rows, -1, HDIM)
    half = HDIM // 2
    swapped = jnp.concatenate([cubes[..., half:], cubes[..., :half]], -1)
    return (cubes * cosine[:, None, :] + swapped * sine[:, None, :]).reshape(value.shape)


def fast_device(
    hidden,
    embedding,
    cotangent,
    lengths,
    gain_attn,
    w_query,
    w_key,
    w_value,
    down_query,
    down_key,
    down_value,
    up_query,
    up_key,
    up_value,
    attn_output,
    gain_mlp,
    mlp_input,
    down_mlp,
    up_mlp,
    mlp_output,
    gain_mixer,
    proj_inner,
    proj_gate,
    proj_step,
    proj_input,
    proj_read,
    taps_inner,
    taps_input,
    taps_read,
    step_bias,
    log_rate,
    skip_gain,
    gain_gated,
    proj_output,
):
    rows = hidden.shape[0]
    length = cotangent.shape[0]
    width = hidden.shape[1]
    middle = rows // 2
    head_parts = lax.axis_size(HEAD)
    piece = middle // head_parts
    state = lax.axis_index(STATE)
    dp = lax.axis_index(DP)
    head = lax.axis_index(HEAD)
    place = dp * 2 + state
    own_start = state * rows
    orders = head_masks()
    offsets = [chunk_of(orders[0]) * piece, middle + chunk_of(orders[1]) * piece]

    heads_wide = w_query.shape[1]
    half_cols = heads_wide // 2

    def state_columns(values, index):
        return jnp.concatenate(
            [lax.dynamic_slice_in_dim(v, index * half_cols, half_cols, 1) for v in values], 1
        )

    main_pieces = z_pieces_columns(
        state_columns((w_query, w_key, w_value), state),
        state_columns((w_query, w_key, w_value), 1 - state),
    )
    main_near = jnp.concatenate(main_pieces[:2], 0)
    main_far = jnp.concatenate(main_pieces[2:], 0)
    up_pieces = z_pieces_columns(
        state_columns((up_query, up_key, up_value), state),
        state_columns((up_query, up_key, up_value), 1 - state),
    )
    ups = jnp.concatenate(natural_quarters(up_pieces), 0)
    rank = down_query.shape[1]
    column = lax.broadcasted_iota(jnp.int32, (1, 3 * half_cols), 1) // half_cols
    up_wide = jnp.concatenate(
        [jnp.where(column == index, ups, jnp.zeros_like(ups)) for index in range(3)], 0
    )

    split_a, split_m = gain_attn.shape[0], gain_mlp.shape[0]
    gains = z_pieces(jnp.concatenate([gain_attn, gain_mlp, gain_mixer]).reshape(-1, 128))
    gains = [value.reshape(-1).astype(full) for value in gains]
    attn_gain = jnp.concatenate([value[:split_a] for value in gains])
    gains = natural_quarters(gains)
    mlp_gain = jnp.concatenate([value[split_a : split_a + split_m] for value in gains])
    mixer_gain = jnp.concatenate([value[split_a + split_m :] for value in gains])
    up_rows = up_mlp.shape[0]
    step_width = proj_step.shape[1]
    small = jnp.concatenate([up_mlp, proj_step.reshape(-1, up_mlp.shape[1])], 0)
    small = natural_quarters(z_pieces(small))
    mlp_upper = jnp.concatenate([value[:up_rows] for value in small], 0)
    step_main = jnp.concatenate([value[up_rows:].reshape(-1, step_width) for value in small], 0)

    part_a = down_query.shape[0] // head_parts
    part_m = down_mlp.shape[0] // head_parts
    downs = jnp.concatenate(
        [
            lax.dynamic_slice_in_dim(down_query, head * part_a, part_a, 0),
            lax.dynamic_slice_in_dim(down_key, head * part_a, part_a, 0),
            lax.dynamic_slice_in_dim(down_value, head * part_a, part_a, 0),
            lax.dynamic_slice_in_dim(down_mlp, head * part_m, part_m, 0),
        ],
        0,
    )
    masks = orders[0][::-1]
    downs_all = gather_rows(jnp.stack(z_pieces(downs), 0)[None], masks, 0)

    def down_of(lower, part):
        return downs_all[:, :, lower : lower + part].transpose(1, 0, 2, 3)

    down_wide = jnp.concatenate(
        [down_of(index * part_a, part_a).reshape(-1, rank) for index in range(3)], 1
    )
    down_m = down_of(3 * part_a, part_m)
    mlp_down = jnp.concatenate(natural_quarters([down_m[i] for i in range(4)]), 0)
    mlp_down = mlp_down.reshape(-1, rank)

    segment, position, valid = row_layout(lengths[0], length)
    own_segment = lax.dynamic_slice_in_dim(segment, own_start, rows)
    own_valid = lax.dynamic_slice_in_dim(valid, own_start, rows)[:, None]
    lows = first_blocks(segment)
    half = HDIM // 2
    angle = position[:, None] * 10000.0 ** (-jnp.arange(half, dtype=full) / half)[None, :]
    cosine = jnp.concatenate([jnp.cos(angle), jnp.cos(angle)], 1)
    sine = jnp.concatenate([-jnp.sin(angle), jnp.sin(angle)], 1)

    def cut(value):
        return [lax.dynamic_slice_in_dim(value, offset, piece, 0) for offset in offsets]

    valid_cut = cut(own_valid)

    quarter = gain_attn.shape[0]

    def quarters(first, second):
        both = jnp.concatenate([first, second], 1)
        return jnp.concatenate(
            [
                lax.dynamic_slice_in_dim(both, (place ^ index) * quarter, quarter, 1)
                for index in range(4)
            ],
            1,
        ).astype(full)

    normed_own = rms_norm(quarters(hidden, embedding), attn_gain).astype(low)
    near_own, far_own = normed_own[:, :width], normed_own[:, width:]
    joined_cut = [quarters(a, b) for a, b in zip(cut(hidden), cut(embedding))]

    def other_rows(value, order):
        share = rows // head_parts
        sent = lax.dynamic_slice_in_dim(value, chunk_of(order) * share, share, 0)
        sent = jnp.concatenate([sent[:, quarter:], sent[:, :quarter]], 1)
        return gather_rows(state_swap(sent), order, 0)

    near_other = other_rows(near_own, orders[0])
    far_other = other_rows(far_own, orders[1])

    def project(near, far):
        reduced = (plain_dot(near, down_wide[:width]) + plain_dot(far, down_wide[width:])).astype(low)
        total = plain_dot(near, main_near) + plain_dot(reduced, up_wide)
        return total + plain_dot(far, main_far), reduced

    pre_own, red_own = project(near_own, far_own)
    pre_other, red_other = project(near_other, far_other)
    pre = by_state(pre_own, pre_other)
    queries = turn(pre[:, :half_cols], cosine, sine).astype(low)
    keys = turn(pre[:, half_cols : 2 * half_cols], cosine, sine).astype(low)
    values = pre[:, 2 * half_cols :].astype(low)

    (
        mlp_input,
        mlp_output,
        proj_inner,
        proj_gate,
        proj_output,
        main_far,
    ) = lax.optimization_barrier(
        (mlp_input, mlp_output, proj_inner, proj_gate, proj_output, main_far)
    )
    attn_pieces = z_pieces_columns(
        lax.dynamic_slice_in_dim(attn_output, state * half_cols, half_cols, 0),
        lax.dynamic_slice_in_dim(attn_output, (1 - state) * half_cols, half_cols, 0),
    )
    attn_proj = jnp.concatenate(natural_quarters(attn_pieces), 1)
    mlp_main = lax.all_gather(mlp_input, ZED, axis=0, tiled=True)
    mlp_proj = lax.all_gather(mlp_output, ZED, axis=1, tiled=True)
    mixer_main = lax.all_gather(
        jnp.concatenate([proj_inner, proj_gate], 1), ZED, axis=0, tiled=True
    )
    output_main = lax.all_gather(proj_output, ZED, axis=1, tiled=True)

    attended, lse = attend(queries, keys, values, segment, lows)

    def state_halves(value):
        cubes = value.reshape(2, 2, middle, value.shape[1])
        return [cubes[:, 0].reshape(rows, -1), cubes[:, 1].reshape(rows, -1)]

    def from_halves(pair):
        return jnp.stack([p.reshape(2, middle, -1) for p in pair], 1).reshape(length, -1)

    attended_halves = state_halves(attended)
    branch_cut = [
        sum_row16(plain_dot(part, attn_proj).astype(low).reshape(2, middle, width), order)
        for part, order in zip(attended_halves, orders)
    ]
    first_cut = [
        value.astype(full) + good * branch
        for value, good, branch in zip(cut(hidden), valid_cut, branch_cut)
    ]
    mlp_normed = [
        gather_rows(rms_norm(value, mlp_gain).astype(low), order, 0)
        for value, order in zip(first_cut, orders)
    ]
    mlp_red = [plain_dot(value, mlp_down).astype(low) for value in mlp_normed]
    hidden_pre = [
        plain_dot(value, mlp_main) + plain_dot(red, mlp_upper)
        for value, red in zip(mlp_normed, mlp_red)
    ]
    activated = [jax.nn.gelu(value, approximate=False).astype(low) for value in hidden_pre]
    second_cut = [
        value + good * sum_rows(plain_dot(part, mlp_proj).astype(low), order, 0)
        for value, good, part, order in zip(first_cut, valid_cut, activated, orders)
    ]
    mixer_normed = jnp.concatenate(
        [
            gather_rows(rms_norm(value, mixer_gain).astype(low), order, 0)
            for value, order in zip(second_cut, orders)
        ],
        0,
    )

    inner_width = proj_inner.shape[1]
    mixer_heads = step_width
    states = proj_input.shape[1]
    small_main = jnp.concatenate([step_main, proj_input, proj_read], 1)
    small_pre = plain_dot(mixer_normed, small_main)
    mixer_pre = plain_dot(mixer_normed, mixer_main)
    inner_pre, gate_pre = mixer_pre[:, :inner_width], mixer_pre[:, inner_width:]
    reach = taps_inner.shape[0] - 1
    edge = state_forward(
        jnp.concatenate([inner_pre[rows - reach :], small_pre[rows - reach :, mixer_heads:]], 1)
    )
    edge_start = jnp.maximum(own_start - reach, 0)
    edge_segment = jnp.where(state == 0, -1, lax.dynamic_slice_in_dim(segment, edge_start, reach))

    def conv_piece(inner_in, small_in, edge_in, taps_x, taps_b, taps_c, shift_in):
        input_in = small_in[:, mixer_heads : mixer_heads + states]
        read_in = small_in[:, mixer_heads + states :]
        edge_b = edge_in[:, inner_width : inner_width + states]
        edge_c = edge_in[:, inner_width + states :]
        return (
            jax.nn.silu(
                conv_edge(inner_in, edge_in[:, :inner_width], taps_x, own_segment, edge_segment)
            ),
            jax.nn.silu(conv_edge(input_in, edge_b, taps_b, own_segment, edge_segment)),
            jax.nn.silu(conv_edge(read_in, edge_c, taps_c, own_segment, edge_segment)),
            jax.nn.softplus(small_in[:, :mixer_heads] + shift_in[None, :]),
        )

    (inner_conv, input_conv, read_conv, steps), conv_back = jax.vjp(
        conv_piece,
        inner_pre,
        small_pre,
        edge,
        taps_inner.astype(full),
        taps_input.astype(full),
        taps_read.astype(full),
        step_bias.astype(full),
    )
    rate = -jnp.exp(log_rate.astype(full))
    scan = Scan(inner_conv, steps, rate, input_conv, read_conv, own_segment, edge_segment[-1])
    first_state = state_forward(scan.end())
    scanned, block_states = scan.forward(first_state)

    def by_head(value):
        return value.reshape(rows, mixer_heads, MDIM)

    skip_full = jnp.repeat(skip_gain.astype(full), MDIM)[None, :]
    combined = scanned + skip_full * inner_conv
    gate_act = jax.nn.silu(gate_pre)
    united = combined * gate_act
    gated_gain = gain_gated.astype(full)[None, :]
    cot_own = lax.dynamic_slice_in_dim(cotangent, own_start, rows, 0)
    mix_grad = cot_own * own_valid.astype(low)
    gated_grad = right_dot(mix_grad, output_main)
    pair = jnp.stack(
        [jnp.sum(united * united, 1), jnp.sum(united * gated_gain * gated_grad, 1)], 0
    )
    for mask in orders[0]:
        pair = pair + head_swap(pair, mask)
    channels = inner_width * head_parts
    row_scale = lax.rsqrt(pair[0] / channels + epsilon)[:, None]
    row_total = pair[1][:, None]
    gated = (united * row_scale * gated_gain).astype(low)
    united_grad = (
        row_scale * gated_gain * gated_grad
        - united * row_scale * row_scale * row_scale * row_total / channels
    )
    combined_grad = united_grad * gate_act
    last_state_grad = state_backward(scan.start_grad(combined_grad))

    sigmoid_gate = jax.nn.sigmoid(gate_pre)
    gate_grad = united_grad * combined * sigmoid_gate * (1.0 + gate_pre * (1.0 - sigmoid_gate))
    grad_gated_gain = jnp.sum(gated_grad * united * row_scale, 0)
    grad_skip = jnp.sum(by_head(combined_grad * inner_conv), (0, 2))
    scan_grad, step_grad, log_grad, log_rows, input_grad, read_grad = scan.backward(
        combined_grad, block_states, last_state_grad
    )
    log_grad = log_grad - log_rows.T
    grad_rate = jnp.sum(log_grad * steps, 0) * rate
    (
        inner_grad,
        small_grad,
        edge_grad,
        grad_taps_x,
        grad_taps_b,
        grad_taps_c,
        grad_shift,
    ) = conv_back(
        (
            scan_grad + skip_full * combined_grad,
            input_grad,
            read_grad,
            step_grad + log_grad * rate[None, :],
        )
    )
    edge_back = state_backward(edge_grad)
    inner_grad = inner_grad.at[rows - reach :].add(edge_back[:, :inner_width])
    small_grad = small_grad.at[rows - reach :, mixer_heads:].add(edge_back[:, inner_width:])
    inner_low = jnp.concatenate([inner_grad, gate_grad], 1).astype(low)
    small_low = small_grad.astype(low)
    mixer_sum = [
        sum_rows(
            (right_dot(inner_low[part], mixer_main) + right_dot(small_low[part], small_main)).astype(
                low
            ),
            order,
            0,
        )
        for part, order in zip((slice(0, middle), slice(middle, rows)), orders)
    ]
    upstream_cut = [value.astype(full) for value in cut(cot_own)]
    mixer_backs = [
        norm_back(value, mixer_gain, grad) for value, grad in zip(second_cut, mixer_sum)
    ]
    second_grad = [up + back[0] for up, back in zip(upstream_cut, mixer_backs)]
    grad_mixer_gain = mixer_backs[0][1] + mixer_backs[1][1]
    mlp_grad = [
        gather_rows((good * grad).astype(low), order, 0)
        for good, grad, order in zip(valid_cut, second_grad, orders)
    ]

    def gelu_part(value):
        return jax.nn.gelu(value, approximate=False)

    hidden_grad = [
        jax.vjp(gelu_part, pre)[1](right_dot(grad, mlp_proj))[0].astype(low)
        for pre, grad in zip(hidden_pre, mlp_grad)
    ]
    mlp_wide = jnp.concatenate([mlp_main, mlp_upper], 0)
    mlp_sums = [
        sum_rows(right_dot(grad, mlp_wide).astype(low), order, 0)
        for grad, order in zip(hidden_grad, orders)
    ]
    middle_low = [value[:, width:].astype(low) for value in mlp_sums]
    mlp_backs = [
        norm_back(value, mlp_gain, total[:, :width] + right_dot(mid, mlp_down))
        for value, total, mid in zip(first_cut, mlp_sums, middle_low)
    ]
    first_grad = [grad + back[0] for grad, back in zip(second_grad, mlp_backs)]
    grad_mlp_gain = mlp_backs[0][1] + mlp_backs[1][1]
    branch_halves = [
        gather_row16((good * grad).astype(low), order).reshape(rows, width)
        for good, grad, order in zip(valid_cut, first_grad, orders)
    ]

    attended_grad = from_halves([right_dot(value, attn_proj).astype(low) for value in branch_halves])
    delta = jnp.sum(
        (attended_grad.astype(full) * attended.astype(full)).reshape(length, -1, HDIM), -1
    ).T[:, None, :]
    query_back, key_back, value_back = attend_back(
        queries, keys, values, attended_grad, lse, delta, segment, lows
    )
    pre_grad = jnp.concatenate(
        [
            turn(query_back, cosine, -sine).astype(low),
            turn(key_back, cosine, -sine).astype(low),
            value_back.astype(low),
        ],
        1,
    )
    main_wide = jnp.concatenate([main_near, main_far, up_wide], 0)
    joint = 2 * width
    normed_sums = []
    for part, order in zip(state_halves(pre_grad), orders):
        total = right_dot(part, main_wide).astype(low).reshape(2, middle, -1)
        total = sum_rows(total, order, 1)
        away = lax.dynamic_index_in_dim(total, 1 - state, 0, False).astype(low)
        away = jnp.concatenate([swap_quarters(away[:, :joint]), away[:, joint:]], 1)
        kept = lax.dynamic_index_in_dim(total, state, 0, False)
        normed_sums.append(kept + state_swap(away).astype(full))
    grad_own = lax.dynamic_slice_in_dim(pre_grad, own_start, rows, 0)
    grad_other = lax.dynamic_slice_in_dim(pre_grad, rows - own_start, rows, 0)

    def main_grad(own, other, lower):
        part = slice(lower * quarter, (lower + 1) * quarter)
        return left_dot(own[:, part], grad_own) + left_dot(other[:, part], grad_other)

    beside = main_grad(near_own, near_other, 1) + dp_swap(
        main_grad(far_own, far_other, 1).astype(low)
    ).astype(full)
    beside = state_swap(beside.astype(low)).astype(full)
    main_total = main_grad(near_own, near_other, 0) + dp_swap(
        main_grad(far_own, far_other, 0).astype(low)
    ).astype(full)

    def spread(own, got, index):
        part = slice(index * half_cols, (index + 1) * half_cols)
        own, got = own[:, part], got[:, part]
        return jnp.concatenate(
            [jnp.where(state == 0, own, got), jnp.where(state == 0, got, own)], 1
        )

    out_main = [spread(main_total, beside, index) for index in range(3)]
    red_all = by_state(red_own, red_other)
    up_grad = jnp.concatenate(
        [
            left_dot(
                red_all[:, index * rank : (index + 1) * rank],
                pre_grad[:, index * half_cols : (index + 1) * half_cols],
            )
            for index in range(3)
        ],
        1,
    )
    rank_half = rank // 2
    up_sum = lax.dynamic_slice_in_dim(up_grad, dp * rank_half, rank_half, 0) + dp_swap(
        lax.dynamic_slice_in_dim(up_grad, (1 - dp) * rank_half, rank_half, 0)
    )
    rank_quarter = rank_half // 2
    up_kept = lax.dynamic_slice_in_dim(up_sum, state * rank_quarter, rank_quarter, 0)
    up_got = state_swap(
        lax.dynamic_slice_in_dim(up_sum, (1 - state) * rank_quarter, rank_quarter, 0)
    )
    out_up = [spread(up_kept, up_got, index) for index in range(3)]
    attn_grad = left_dot(attended_halves[0], branch_halves[0]) + left_dot(
        attended_halves[1], branch_halves[1]
    )
    out_attn = grad_pieces(attn_grad.astype(low), 0)

    lows_cut = [value[:, joint:].astype(low) for value in normed_sums]
    joined_backs = [
        norm_back(value, attn_gain, total[:, :joint] + right_dot(mid, down_wide))
        for value, total, mid in zip(joined_cut, normed_sums, lows_cut)
    ]
    grad_attn_gain = joined_backs[0][1] + joined_backs[1][1]

    def natural_columns(value):
        return jnp.concatenate(
            [
                lax.dynamic_slice_in_dim(value, (place ^ index) * quarter, quarter, -1)
                for index in range(4)
            ],
            -1,
        )

    input_cut = []
    for grad, back in zip(first_grad, joined_backs):
        joined_grad = natural_columns(back[0])
        input_cut.append(
            (
                (grad + joined_grad[:, :width]).astype(low),
                joined_grad[:, width:].astype(low),
            )
        )
    grad_hidden, grad_embedding = (
        jnp.concatenate(
            [gather_rows(pieces[index], order, 0) for pieces, order in zip(input_cut, orders)], 0
        )
        for index in range(2)
    )

    out_cut = [
        (
            value
            + good
            * sum_rows(
                plain_dot(gated[index * middle : (index + 1) * middle], output_main).astype(low),
                order,
                0,
            )
        ).astype(low)
        for index, (value, good, order) in enumerate(zip(second_cut, valid_cut, orders))
    ]
    layer_out = from_halves([gather_row16(value, order) for value, order in zip(out_cut, orders)])

    def scatter(value, axis):
        return lax.psum_scatter(
            value.astype(low), ZED, scatter_dimension=axis, tiled=True
        ).astype(full)

    out_output = scatter(left_dot(gated, mix_grad), 1)
    out_mixer = scatter(left_dot(mixer_normed, inner_low), 0)
    mlp_normed_own = jnp.concatenate(mlp_normed, 0)
    hidden_grad_own = jnp.concatenate(hidden_grad, 0)
    out_mlp_output = scatter(
        left_dot(jnp.concatenate(activated, 0), jnp.concatenate(mlp_grad, 0)), 1
    )
    out_mlp_input = scatter(left_dot(mlp_normed_own, hidden_grad_own), 0)
    out_up_mlp = scatter(left_dot(jnp.concatenate(mlp_red, 0), hidden_grad_own), 0)

    middle_own = jnp.concatenate(
        [gather_rows(value, order, 0) for value, order in zip(middle_low, orders)], 0
    )
    lows_halves = [gather_row16(value, order) for value, order in zip(lows_cut, orders)]
    lows_own, lows_other = (
        jnp.concatenate(
            [lax.dynamic_index_in_dim(value, index, 0, False) for value in lows_halves], 0
        )
        for index in (state, 1 - state)
    )

    def down_rows(own, other):
        start = head * part_a
        own = lax.dynamic_slice_in_dim(own, start, part_a, 1)
        other = lax.dynamic_slice_in_dim(other, start, part_a, 1)
        return left_dot(own, lows_own) + left_dot(other, lows_other)

    down_sum = down_rows(near_own, near_other) + dp_swap(
        down_rows(far_own, far_other).astype(low)
    ).astype(full)
    columns = mlp_normed_own.reshape(rows, 4, head_parts, part_m)
    columns = lax.dynamic_index_in_dim(columns, head, 2, False).reshape(rows, 4 * part_m)
    mlp_down_grad = left_dot(columns, middle_own).reshape(4, part_m, rank)
    kept = lax.dynamic_slice_in_dim(mlp_down_grad, 2 * dp, 2, 0) + dp_swap(
        lax.dynamic_slice_in_dim(mlp_down_grad, 2 * (1 - dp), 2, 0)
    )
    kept = lax.dynamic_index_in_dim(kept, state, 0, False) + state_swap(
        lax.dynamic_index_in_dim(kept, 1 - state, 0, False)
    )
    down_all = gather_rows(down_sum.astype(low)[None], masks, 0).reshape(quarter, 3 * rank)
    down_all = down_all.astype(full)
    out_downs = [down_all[:, index * rank : (index + 1) * rank] for index in range(3)]
    out_down_mlp = gather_rows(kept.astype(low)[None], masks, 0).reshape(-1, rank).astype(full)

    small_main_grad = left_dot(mixer_normed, small_low)
    vector_grad = sum_rows(small_main_grad[:, mixer_heads:], masks, 0)
    vector_grad = gather_rows(add_zed(vector_grad), masks, 0)
    step_rows = small_main_grad[:, :mixer_heads].reshape(4, -1, mixer_heads)
    kept = lax.dynamic_slice_in_dim(step_rows, 2 * dp, 2, 0) + dp_swap(
        lax.dynamic_slice_in_dim(step_rows, 2 * (1 - dp), 2, 0)
    )
    out_step = lax.dynamic_index_in_dim(kept, state, 0, False) + state_swap(
        lax.dynamic_index_in_dim(kept, 1 - state, 0, False)
    )
    taps_total = add_everywhere(jnp.concatenate([grad_taps_b, grad_taps_c], 1))
    own_total = add_zed(
        jnp.concatenate(
            [grad_gated_gain, grad_taps_x.reshape(-1), grad_shift, grad_rate, grad_skip]
        )
    )
    gated_total = own_total[:inner_width]
    taps_end = inner_width * (reach + 2)
    taps_x_total = own_total[inner_width:taps_end].reshape(reach + 1, inner_width)
    head_total = own_total[taps_end:].reshape(3, mixer_heads)
    attn_gain_grad = natural_columns(grad_attn_gain)
    gain_total = add_everywhere(
        jnp.concatenate([attn_gain_grad, grad_mlp_gain, grad_mixer_gain]).reshape(-1, 128)
    ).reshape(-1)

    def gain_of(start, size):
        return lax.dynamic_slice_in_dim(gain_total, start + place * size, size)

    once = (head == 0).astype(full)
    square_sum = jnp.zeros((), full)
    for value in out_main + out_up + [out_attn, out_mlp_input, out_up_mlp, out_mlp_output]:
        square_sum = square_sum + jnp.sum(value * value)
    for value in out_downs + [out_down_mlp]:
        square_sum = square_sum + once * jnp.sum(value * value)
    square_total = lax.psum(square_sum, EVERY)
    return (
        layer_out,
        grad_hidden,
        grad_embedding,
        gain_of(0, split_a),
        out_main[0],
        out_main[1],
        out_main[2],
        out_downs[0],
        out_downs[1],
        out_downs[2],
        out_up[0],
        out_up[1],
        out_up[2],
        out_attn,
        gain_of(joint, split_m),
        out_mlp_input,
        out_down_mlp,
        out_up_mlp,
        out_mlp_output,
        gain_of(joint + width, split_m),
        out_mixer[:, :inner_width],
        out_mixer[:, inner_width:],
        out_step,
        vector_grad[:, :states],
        vector_grad[:, states:],
        taps_x_total,
        taps_total[:, :states],
        taps_total[:, states:],
        head_total[0],
        head_total[1],
        head_total[2],
        gated_total,
        out_output,
        jnp.sqrt(square_total),
    )


def z_pieces_columns(mine, theirs):
    got = state_swap(theirs)
    return [mine, got, dp_swap(mine), dp_swap(got)]


def pick_device(mesh):
    heads = mesh.shape[HEAD]
    per_head = DIN // HDIM // heads
    halves = mesh.shape[DP] == 2 and mesh.shape[STATE] == 2
    return fast_device if halves and heads & (heads - 1) == 0 and per_head % 2 == 0 else general_device


def solution(mesh):
    in_specs = (
        P(ZED, None),
        P(ZED, None),
        P(DP, None),
        P(DP, None),
        P(ZED),
        P(ZED, HEAD),
        P(ZED, HEAD),
        P(ZED, HEAD),
        P(ZED, None),
        P(ZED, None),
        P(ZED, None),
        P(ZED, HEAD),
        P(ZED, HEAD),
        P(ZED, HEAD),
        P(HEAD, ZED),
        P(ZED),
        P(ZED, HEAD),
        P(ZED, None),
        P(ZED, HEAD),
        P(HEAD, ZED),
        P(ZED),
        P(ZED, HEAD),
        P(ZED, HEAD),
        P(ZED, HEAD),
        P(),
        P(),
        P(None, HEAD),
        P(),
        P(),
        P(HEAD),
        P(HEAD),
        P(HEAD),
        P(HEAD),
        P(HEAD, ZED),
    )
    out_specs = (
        P(DP, None),
        P(ZED, None),
        P(ZED, None),
        P(ZED),
        P(ZED, HEAD),
        P(ZED, HEAD),
        P(ZED, HEAD),
        P(ZED, None),
        P(ZED, None),
        P(ZED, None),
        P(ZED, HEAD),
        P(ZED, HEAD),
        P(ZED, HEAD),
        P(HEAD, ZED),
        P(ZED),
        P(ZED, HEAD),
        P(ZED, None),
        P(ZED, HEAD),
        P(HEAD, ZED),
        P(ZED),
        P(ZED, HEAD),
        P(ZED, HEAD),
        P(ZED, HEAD),
        P(),
        P(),
        P(None, HEAD),
        P(),
        P(),
        P(HEAD),
        P(HEAD),
        P(HEAD),
        P(HEAD),
        P(HEAD, ZED),
        P(),
    )
    return jax.shard_map(
        pick_device(mesh), mesh=mesh, in_specs=in_specs, out_specs=out_specs, check_vma=False
    )
```

```python
import jax
import jax.numpy as jnp
from jax import lax
from jax.experimental import pallas as pl
from jax.experimental.pallas import tpu as pltpu
from jax.sharding import PartitionSpec as P

HDIM = 128
MDIM = 64
DIN = 4096
GROUP = 256
DP, HEAD, STATE = "dp", "head", "state"
ZED = (DP, STATE)
EVERY = (DP, HEAD, STATE)


highest = lax.Precision.HIGHEST
epsilon = 1e-05


def plain_dot(left, right):
    return jnp.dot(left, right, preferred_element_type=jnp.float32)


def left_dot(left, right):
    return lax.dot_general(
        left, right, (((0,), (0,)), ((), ())), preferred_element_type=jnp.float32
    )


def right_dot(left, right):
    return lax.dot_general(
        left, right, (((1,), (1,)), ((), ())), preferred_element_type=jnp.float32
    )


def exact_left(left, right):
    return lax.dot_general(
        left.astype(jnp.float32), right, (((0,), (0,)), ((), ())), precision=highest
    )


def exact_right(left, right):
    return lax.dot_general(
        left, right.astype(jnp.float32), (((1,), (1,)), ((), ())), precision=highest
    )


def rms_norm(values, gain):
    return values * lax.rsqrt(jnp.mean(values * values, -1, keepdims=True) + epsilon) * gain


def row_layout(doc_lengths, length):
    ends = jnp.cumsum(doc_lengths)
    places = jnp.arange(length, dtype=jnp.int32)
    segment = jnp.sum((places[:, None] >= ends[None, :]).astype(jnp.int32), axis=1)
    starts = jnp.concatenate([ends - doc_lengths, ends[-1:]])
    choose = segment[:, None] == jnp.arange(starts.shape[0], dtype=jnp.int32)[None, :]
    first_place = jnp.sum(jnp.where(choose, starts[None, :], 0), axis=1)
    position = (places - first_place).astype(jnp.float32)
    valid = (segment < doc_lengths.shape[0]).astype(jnp.float32)
    return (segment, position, valid)


def rotate(values, position):
    half = values.shape[-1] // 2
    freqs = 10000.0 ** (-jnp.arange(half, dtype=jnp.float32) / half)
    angle = position[:, None] * freqs[None, :]
    cosine = jnp.cos(angle)[:, None, :]
    sine = jnp.sin(angle)[:, None, :]
    former = values[..., :half]
    latter = values[..., half:]
    return jnp.concatenate([former * cosine - latter * sine, former * sine + latter * cosine], -1)


def head_probs(query_in, key_in, allowed):
    scale = query_in.shape[-1] ** (-0.5)
    scores = (
        jnp.einsum("thd,shd->hts", query_in, key_in, preferred_element_type=jnp.float32) * scale
    )
    scores = jnp.where(allowed[None, :, :], scores, -1e30)
    shifted = scores - jnp.max(scores, -1, keepdims=True)
    weights = jnp.exp(shifted)
    return weights / jnp.sum(weights, -1, keepdims=True)


def conv_mask(values, taps, segment):
    total = taps[0][None, :] * values
    for offset in range(1, taps.shape[0]):
        moved = jnp.concatenate(
            [jnp.zeros((offset, values.shape[1]), values.dtype), values[:-offset]], 0
        )
        moved_seg = jnp.concatenate([jnp.full((offset,), -1, jnp.int32), segment[:-offset]], 0)
        same = (moved_seg == segment).astype(values.dtype)[:, None]
        total = total + taps[offset][None, :] * moved * same
    return total


def state_scan(inputs, step_sizes, decay, input_vecs, read_vecs, segment, block):
    length, heads, width = inputs.shape
    count = length // block
    states = input_vecs.shape[1]

    def one_block(carry, pieces):
        state, before = carry
        group_in, group_dt, group_b, group_c, group_seg = pieces
        logs = group_dt * decay[None, :]
        cumul = jnp.cumsum(logs, 0)
        places = jnp.arange(block, dtype=jnp.int32)
        allowed = (group_seg[:, None] == group_seg[None, :]) & (places[None, :] <= places[:, None])
        gaps = cumul[:, None, :] - cumul[None, :, :]
        fading = jnp.where(
            allowed[:, :, None], jnp.exp(jnp.where(allowed[:, :, None], gaps, 0.0)), 0.0
        )
        inner = jnp.dot(group_c, group_b.T, precision=highest)
        scaled = group_in * group_dt[:, :, None]
        local_out = jnp.einsum(
            "tsh,shp->thp", inner[:, :, None] * fading, scaled, precision=highest
        )
        carried = (group_seg == before).astype(inputs.dtype)
        entry = jnp.exp(cumul) * carried[:, None]
        from_state = (
            jnp.einsum("tn,hnp->thp", group_c, state, precision=highest) * entry[:, :, None]
        )
        last_seg = group_seg[-1]
        reach = (group_seg == last_seg).astype(inputs.dtype)
        to_end = jnp.exp(cumul[-1][None, :] - cumul) * reach[:, None]
        retain = jnp.exp(cumul[-1]) * (last_seg == before).astype(inputs.dtype)
        fresh = jnp.einsum("sn,sh,shp->hnp", group_b, to_end, scaled, precision=highest)
        state = state * retain[:, None, None] + fresh
        return ((state, last_seg), local_out + from_state)

    pieces = (
        inputs.reshape(count, block, heads, width),
        step_sizes.reshape(count, block, heads),
        input_vecs.reshape(count, block, states),
        read_vecs.reshape(count, block, states),
        segment.reshape(count, block),
    )
    start = (jnp.zeros((heads, states, width), inputs.dtype), jnp.array(-1, jnp.int32))
    unused, outputs = lax.scan(jax.checkpoint(one_block), start, pieces)
    return outputs.reshape(length, heads, width)


def mixer_core(
    inner_pre,
    input_pre,
    read_pre,
    step_pre,
    taps_x,
    taps_b,
    taps_c,
    shift_in,
    rate_in,
    segment,
    width,
    block,
):
    inner_conv = jax.nn.silu(conv_mask(inner_pre, taps_x, segment))
    input_conv = jax.nn.silu(conv_mask(input_pre, taps_b, segment))
    read_conv = jax.nn.silu(conv_mask(read_pre, taps_c, segment))
    step_sizes = jax.nn.softplus(step_pre + shift_in[None, :])
    heads = step_sizes.shape[1]
    length = inner_conv.shape[0]
    outputs = state_scan(
        inner_conv.reshape(length, heads, width),
        step_sizes,
        -jnp.exp(rate_in),
        input_conv,
        read_conv,
        segment,
        block,
    )
    return (outputs.reshape(length, heads * width), inner_conv)


def place_slice(piece, index, parts, axis):
    shape = list(piece.shape)
    shape[axis] = shape[axis] * parts
    holder = jnp.zeros(tuple(shape), jnp.float32)
    return lax.dynamic_update_slice_in_dim(holder, piece, index * piece.shape[axis], axis)


def take_slice(whole, index, width, axis):
    return lax.dynamic_slice_in_dim(whole, index * width, width, axis)


def general_device(
    hidden,
    embedding,
    cotangent,
    lengths,
    gain_attn,
    w_query,
    w_key,
    w_value,
    down_query,
    down_key,
    down_value,
    up_query,
    up_key,
    up_value,
    attn_output,
    gain_mlp,
    mlp_input,
    down_mlp,
    up_mlp,
    mlp_output,
    gain_mixer,
    proj_inner,
    proj_gate,
    proj_step,
    proj_input,
    proj_read,
    taps_inner,
    taps_input,
    taps_read,
    step_bias,
    log_rate,
    skip_gain,
    gain_gated,
    proj_output,
):
    row_count = hidden.shape[0]
    length = cotangent.shape[0]
    model_width = hidden.shape[1]
    head_parts = lax.axis_size(HEAD)
    state_parts = lax.axis_size(STATE)
    state_index = lax.axis_index(STATE)
    head_index = lax.axis_index(HEAD)
    own_start = state_index * row_count
    segment, position, valid = row_layout(lengths[0], length)
    own_segment = lax.dynamic_slice_in_dim(segment, own_start, row_count)
    own_position = lax.dynamic_slice_in_dim(position, own_start, row_count)
    own_valid = lax.dynamic_slice_in_dim(valid, own_start, row_count)[:, None]
    full_valid = valid[:, None]
    places = jnp.arange(length, dtype=jnp.int32)
    own_places = own_start + jnp.arange(row_count, dtype=jnp.int32)
    own_mask = ((places >= own_start) & (places < own_start + row_count)).astype(jnp.float32)[
        :, None
    ]
    allowed = (own_segment[:, None] == segment[None, :]) & (places[None, :] <= own_places[:, None])
    gathered = (
        lax.all_gather(gain_attn, ZED, axis=0, tiled=True),
        lax.all_gather(w_query, ZED, axis=0, tiled=True),
        lax.all_gather(w_key, ZED, axis=0, tiled=True),
        lax.all_gather(w_value, ZED, axis=0, tiled=True),
        lax.all_gather(down_query, ZED, axis=0, tiled=True),
        lax.all_gather(down_key, ZED, axis=0, tiled=True),
        lax.all_gather(down_value, ZED, axis=0, tiled=True),
        lax.all_gather(up_query, ZED, axis=0, tiled=True),
        lax.all_gather(up_key, ZED, axis=0, tiled=True),
        lax.all_gather(up_value, ZED, axis=0, tiled=True),
        lax.all_gather(attn_output, ZED, axis=1, tiled=True),
        lax.all_gather(gain_mlp, ZED, axis=0, tiled=True),
        lax.all_gather(mlp_input, ZED, axis=0, tiled=True),
        lax.all_gather(down_mlp, ZED, axis=0, tiled=True),
        lax.all_gather(up_mlp, ZED, axis=0, tiled=True),
        lax.all_gather(mlp_output, ZED, axis=1, tiled=True),
        lax.all_gather(gain_mixer, ZED, axis=0, tiled=True),
        lax.all_gather(proj_inner, ZED, axis=0, tiled=True),
        lax.all_gather(proj_gate, ZED, axis=0, tiled=True),
        lax.all_gather(proj_step, ZED, axis=0, tiled=True),
        lax.all_gather(proj_output, ZED, axis=1, tiled=True),
    )
    (
        attn_gain,
        query_main,
        key_main,
        value_main,
        query_down,
        key_down,
        value_down,
        query_upper,
        key_upper,
        value_upper,
        attn_proj,
        mlp_gain,
        mlp_main,
        mlp_down,
        mlp_upper,
        mlp_proj,
        mixer_gain,
        inner_main,
        gate_main,
        step_main,
        output_main,
    ) = gathered
    joined = jnp.concatenate([hidden, embedding], 1).astype(jnp.float32)
    attn_gain_f = attn_gain.astype(jnp.float32)
    normed = rms_norm(joined, attn_gain_f).astype(jnp.bfloat16)
    head_count = query_main.shape[1] // HDIM

    def project(main, down, upper):
        reduced = plain_dot(normed, down).astype(jnp.bfloat16)
        return (plain_dot(normed, main) + plain_dot(reduced, upper), reduced)

    query_pre, query_red = project(query_main, query_down, query_upper)
    key_pre, key_red = project(key_main, key_down, key_upper)
    value_pre, value_red = project(value_main, value_down, value_upper)
    queries = rotate(query_pre.reshape(row_count, head_count, HDIM), own_position).astype(
        jnp.bfloat16
    )
    keys_own = rotate(key_pre.reshape(row_count, head_count, HDIM), own_position).astype(
        jnp.bfloat16
    )
    values_own = value_pre.reshape(row_count, head_count, HDIM).astype(jnp.bfloat16)
    keys_all, values_all = (
        lax.all_gather(keys_own, STATE, axis=0, tiled=True),
        lax.all_gather(values_own, STATE, axis=0, tiled=True),
    )
    probs_full = head_probs(queries, keys_all, allowed)
    attended_f = jnp.einsum(
        "hts,shd->thd",
        probs_full.astype(jnp.bfloat16),
        values_all,
        preferred_element_type=jnp.float32,
    )
    attended = attended_f.reshape(row_count, head_count * HDIM).astype(jnp.bfloat16)
    branch = lax.psum(plain_dot(attended, attn_proj), HEAD)
    first = hidden.astype(jnp.float32) + own_valid * branch
    mlp_gain_f = mlp_gain.astype(jnp.float32)
    mlp_normed = rms_norm(first, mlp_gain_f).astype(jnp.bfloat16)
    mlp_red = plain_dot(mlp_normed, mlp_down).astype(jnp.bfloat16)
    hidden_pre = plain_dot(mlp_normed, mlp_main) + plain_dot(mlp_red, mlp_upper)
    activated = jax.nn.gelu(hidden_pre, approximate=False).astype(jnp.bfloat16)
    mlp_branch = lax.psum(plain_dot(activated, mlp_proj), HEAD)
    second = first + own_valid * mlp_branch
    second_all = lax.all_gather(second, STATE, axis=0, tiled=True)
    mixer_gain_f = mixer_gain.astype(jnp.float32)
    mixer_normed = rms_norm(second_all, mixer_gain_f).astype(jnp.bfloat16)
    states_own = proj_input.shape[1] // state_parts
    input_half = take_slice(proj_input, state_index, states_own, 1)
    read_half = take_slice(proj_read, state_index, states_own, 1)
    taps_input_half = take_slice(taps_input, state_index, states_own, 1).astype(jnp.float32)
    taps_read_half = take_slice(taps_read, state_index, states_own, 1).astype(jnp.float32)
    inner_pre = plain_dot(mixer_normed, inner_main)
    gate_pre = plain_dot(mixer_normed, gate_main)
    step_pre = plain_dot(mixer_normed, step_main)
    input_pre = plain_dot(mixer_normed, input_half)
    read_pre = plain_dot(mixer_normed, read_half)

    def mixer_piece(
        inner_in, input_in, read_in, step_in, taps_x, taps_b, taps_c, shift_in, rate_in
    ):
        return mixer_core(
            inner_in,
            input_in,
            read_in,
            step_in,
            taps_x,
            taps_b,
            taps_c,
            shift_in,
            rate_in,
            segment,
            MDIM,
            GROUP,
        )

    (scanned_part, inner_conv), mixer_back = jax.vjp(
        mixer_piece,
        inner_pre,
        input_pre,
        read_pre,
        step_pre,
        taps_inner.astype(jnp.float32),
        taps_input_half,
        taps_read_half,
        step_bias.astype(jnp.float32),
        log_rate.astype(jnp.float32),
    )
    scanned = lax.psum(scanned_part, STATE)
    skip_full = jnp.repeat(skip_gain.astype(jnp.float32), MDIM)[None, :]
    combined = scanned + skip_full * inner_conv
    gate_act = jax.nn.silu(gate_pre)
    united = combined * gate_act
    squares = lax.psum(jnp.sum(united * united, 1), HEAD)
    row_scale = lax.rsqrt(squares / DIN + epsilon)[:, None]
    gated_gain = gain_gated.astype(jnp.float32)[None, :]
    united_own = lax.dynamic_slice_in_dim(united, own_start, row_count, 0)
    scale_own = lax.dynamic_slice_in_dim(row_scale, own_start, row_count, 0)
    gated_own = (united_own * scale_own * gated_gain).astype(jnp.bfloat16)
    mixed_own = lax.psum(plain_dot(gated_own, output_main), HEAD)
    mixed = lax.all_gather(mixed_own, STATE, axis=0, tiled=True)
    layer_out = (second_all + full_valid * mixed).astype(jnp.bfloat16)
    upstream = cotangent.astype(jnp.float32)
    mix_grad = (full_valid * upstream).astype(jnp.bfloat16)
    mix_grad_own = lax.dynamic_slice_in_dim(mix_grad, own_start, row_count, 0)
    grad_output_main = left_dot(gated_own, mix_grad_own)
    gated_grad = right_dot(mix_grad, output_main)
    row_total = jnp.sum(mix_grad.astype(jnp.float32) * mixed, 1)[:, None] / row_scale
    grad_gated_gain = jnp.sum(gated_grad * united * row_scale * own_mask, 0)
    united_grad = (
        row_scale * gated_gain * gated_grad
        - united * row_scale * row_scale * row_scale * row_total / DIN
    )
    combined_grad = united_grad * gate_act
    sigmoid_gate = jax.nn.sigmoid(gate_pre)
    gate_grad = (
        united_grad * combined * sigmoid_gate * (1.0 + gate_pre * (1.0 - sigmoid_gate)) * own_mask
    )
    mixer_heads = step_pre.shape[1]
    grad_skip = jnp.sum(
        (combined_grad * inner_conv * own_mask).reshape(length, mixer_heads, MDIM), (0, 2)
    )
    conv_extra = skip_full * combined_grad * own_mask
    (
        inner_grad,
        input_grad,
        read_grad,
        step_grad,
        grad_taps_x,
        grad_taps_b,
        grad_taps_c,
        grad_shift,
        grad_rate,
    ) = mixer_back((combined_grad, conv_extra))
    mixer_part = (
        exact_right(inner_grad, inner_main)
        + exact_right(gate_grad, gate_main)
        + exact_right(step_grad, step_main)
        + exact_right(input_grad, input_half)
        + exact_right(read_grad, read_half)
    )
    grad_inner_main = exact_left(mixer_normed, inner_grad)
    grad_gate_main = exact_left(mixer_normed, gate_grad)
    grad_step_main = exact_left(mixer_normed, step_grad)
    grad_input_half = exact_left(mixer_normed, input_grad)
    grad_read_half = exact_left(mixer_normed, read_grad)
    mixer_rows_own = lax.psum_scatter(mixer_part, STATE, scatter_dimension=0, tiled=True)
    mixer_own = lax.psum(mixer_rows_own, HEAD)
    unused_norm, second_back = jax.vjp(rms_norm, second, mixer_gain_f)
    second_norm_grad, grad_mixer_gain = second_back(mixer_own)
    upstream_own = lax.dynamic_slice_in_dim(upstream, own_start, row_count, 0)
    second_grad = upstream_own + second_norm_grad
    mlp_grad = (own_valid * second_grad).astype(jnp.bfloat16)
    grad_mlp_proj = left_dot(activated, mlp_grad)
    activated_grad = right_dot(mlp_grad, mlp_proj)
    unused_gelu, gelu_back = jax.vjp(
        lambda preact: jax.nn.gelu(preact, approximate=False), hidden_pre
    )
    hidden_grad = gelu_back(activated_grad)[0].astype(jnp.bfloat16)
    grad_mlp_main = left_dot(mlp_normed, hidden_grad)
    grad_mlp_upper = left_dot(mlp_red, hidden_grad)
    mlp_middle = right_dot(hidden_grad, mlp_upper)
    mlp_part = right_dot(hidden_grad, mlp_main)
    mlp_sum, middle_sum = lax.psum((mlp_part, mlp_middle), HEAD)
    middle_low = middle_sum.astype(jnp.bfloat16)
    mlp_normed_grad = mlp_sum + right_dot(middle_low, mlp_down)
    grad_mlp_down = left_dot(mlp_normed, middle_low)
    unused_first, first_back = jax.vjp(rms_norm, first, mlp_gain_f)
    first_norm_grad, grad_mlp_gain = first_back(mlp_normed_grad)
    first_grad = second_grad + first_norm_grad
    branch_grad = (own_valid * first_grad).astype(jnp.bfloat16)
    grad_attn_proj = left_dot(attended, branch_grad)
    attended_grad = right_dot(branch_grad, attn_proj).reshape(row_count, head_count, HDIM)
    probs_back = head_probs(queries, keys_all, allowed)
    score_scale = HDIM ** (-0.5)
    out_low = attended_grad.astype(jnp.bfloat16)
    prob_grad = jnp.einsum("thd,shd->hts", out_low, values_all, preferred_element_type=jnp.float32)
    score_grad = probs_back * (prob_grad - jnp.sum(probs_back * prob_grad, -1, keepdims=True))
    score_low = score_grad.astype(jnp.bfloat16)
    query_back = (
        jnp.einsum("hts,shd->thd", score_low, keys_all, preferred_element_type=jnp.float32)
        * score_scale
    )
    keys_back = (
        jnp.einsum("hts,thd->shd", score_low, queries, preferred_element_type=jnp.float32)
        * score_scale
    )
    values_back = jnp.einsum(
        "hts,thd->shd", probs_back.astype(jnp.bfloat16), out_low, preferred_element_type=jnp.float32
    )
    keys_grad_own, values_grad_own = (
        lax.psum_scatter(keys_back, STATE, scatter_dimension=0, tiled=True),
        lax.psum_scatter(values_back, STATE, scatter_dimension=0, tiled=True),
    )
    query_grad = (
        rotate(query_back, -own_position).reshape(row_count, head_count * HDIM).astype(jnp.bfloat16)
    )
    key_grad = (
        rotate(keys_grad_own, -own_position)
        .reshape(row_count, head_count * HDIM)
        .astype(jnp.bfloat16)
    )
    value_grad = values_grad_own.reshape(row_count, head_count * HDIM).astype(jnp.bfloat16)
    grad_query_main = left_dot(normed, query_grad)
    grad_key_main = left_dot(normed, key_grad)
    grad_value_main = left_dot(normed, value_grad)
    grad_query_upper = left_dot(query_red, query_grad)
    grad_key_upper = left_dot(key_red, key_grad)
    grad_value_upper = left_dot(value_red, value_grad)
    query_middle = right_dot(query_grad, query_upper)
    key_middle = right_dot(key_grad, key_upper)
    value_middle = right_dot(value_grad, value_upper)
    normed_part = (
        right_dot(query_grad, query_main)
        + right_dot(key_grad, key_main)
        + right_dot(value_grad, value_main)
    )
    normed_sum, query_msum, key_msum, value_msum = lax.psum(
        (normed_part, query_middle, key_middle, value_middle), HEAD
    )
    query_low = query_msum.astype(jnp.bfloat16)
    key_low = key_msum.astype(jnp.bfloat16)
    value_low = value_msum.astype(jnp.bfloat16)
    normed_grad = (
        normed_sum
        + right_dot(query_low, query_down)
        + right_dot(key_low, key_down)
        + right_dot(value_low, value_down)
    )
    grad_query_down = left_dot(normed, query_low)
    grad_key_down = left_dot(normed, key_low)
    grad_value_down = left_dot(normed, value_low)
    unused_joined, joined_back = jax.vjp(rms_norm, joined, attn_gain_f)
    joined_grad, grad_attn_gain = joined_back(normed_grad)
    grad_hidden = (first_grad + joined_grad[:, :model_width]).astype(jnp.bfloat16)
    grad_embedding = joined_grad[:, model_width:].astype(jnp.bfloat16)
    scattered = (
        lax.psum_scatter(grad_attn_gain, ZED, scatter_dimension=0, tiled=True),
        lax.psum_scatter(grad_query_main, ZED, scatter_dimension=0, tiled=True),
        lax.psum_scatter(grad_key_main, ZED, scatter_dimension=0, tiled=True),
        lax.psum_scatter(grad_value_main, ZED, scatter_dimension=0, tiled=True),
        lax.psum_scatter(grad_query_down, ZED, scatter_dimension=0, tiled=True),
        lax.psum_scatter(grad_key_down, ZED, scatter_dimension=0, tiled=True),
        lax.psum_scatter(grad_value_down, ZED, scatter_dimension=0, tiled=True),
        lax.psum_scatter(grad_query_upper, ZED, scatter_dimension=0, tiled=True),
        lax.psum_scatter(grad_key_upper, ZED, scatter_dimension=0, tiled=True),
        lax.psum_scatter(grad_value_upper, ZED, scatter_dimension=0, tiled=True),
        lax.psum_scatter(grad_attn_proj, ZED, scatter_dimension=1, tiled=True),
        lax.psum_scatter(grad_mlp_gain, ZED, scatter_dimension=0, tiled=True),
        lax.psum_scatter(grad_mlp_main, ZED, scatter_dimension=0, tiled=True),
        lax.psum_scatter(grad_mlp_down, ZED, scatter_dimension=0, tiled=True),
        lax.psum_scatter(grad_mlp_upper, ZED, scatter_dimension=0, tiled=True),
        lax.psum_scatter(grad_mlp_proj, ZED, scatter_dimension=1, tiled=True),
        lax.psum_scatter(grad_mixer_gain, ZED, scatter_dimension=0, tiled=True),
        lax.psum_scatter(grad_inner_main, ZED, scatter_dimension=0, tiled=True),
        lax.psum_scatter(grad_gate_main, ZED, scatter_dimension=0, tiled=True),
        lax.psum_scatter(grad_step_main, ZED, scatter_dimension=0, tiled=True),
        lax.psum_scatter(grad_output_main, ZED, scatter_dimension=1, tiled=True),
    )
    first_head = (head_index == 0).astype(jnp.float32)
    square_sum = jnp.zeros((), jnp.float32)
    for index in [1, 2, 3, 7, 8, 9, 10, 12, 14, 15]:
        square_sum = square_sum + jnp.sum(scattered[index] * scattered[index])
    for index in [4, 5, 6, 13]:
        square_sum = square_sum + first_head * jnp.sum(scattered[index] * scattered[index])
    head_params = jnp.stack([grad_shift, grad_rate, grad_skip], 0)
    totals = lax.psum(
        (
            square_sum,
            place_slice(grad_gated_gain, head_index, head_parts, 0),
            place_slice(grad_taps_x, head_index, head_parts, 1),
            place_slice(head_params, head_index, head_parts, 1),
            place_slice(grad_input_half, state_index, state_parts, 1),
            place_slice(grad_read_half, state_index, state_parts, 1),
            place_slice(grad_taps_b, state_index, state_parts, 1),
            place_slice(grad_taps_c, state_index, state_parts, 1),
        ),
        EVERY,
    )
    (
        square_total,
        gated_full,
        taps_full,
        heads_full,
        input_full,
        read_full,
        taps_input_full,
        taps_read_full,
    ) = totals
    head_width = gain_gated.shape[0]
    tap_width = taps_inner.shape[1]
    param_width = step_bias.shape[0]
    heads_own = take_slice(heads_full, head_index, param_width, 1)
    return (
        layer_out,
        grad_hidden,
        grad_embedding,
        scattered[0],
        scattered[1],
        scattered[2],
        scattered[3],
        scattered[4],
        scattered[5],
        scattered[6],
        scattered[7],
        scattered[8],
        scattered[9],
        scattered[10],
        scattered[11],
        scattered[12],
        scattered[13],
        scattered[14],
        scattered[15],
        scattered[16],
        scattered[17],
        scattered[18],
        scattered[19],
        input_full,
        read_full,
        take_slice(taps_full, head_index, tap_width, 1),
        taps_input_full,
        taps_read_full,
        heads_own[0],
        heads_own[1],
        heads_own[2],
        take_slice(gated_full, head_index, head_width, 0),
        scattered[20],
        jnp.sqrt(square_total),
    )


low = jnp.bfloat16
full = jnp.float32


def head_masks():
    count = lax.axis_size(HEAD)
    masks = [1 << bit for bit in range(count.bit_length() - 1)]
    return masks[:1] + masks[1:], masks[:1] + masks[1:][::-1]


def head_swap(value, mask):
    count = lax.axis_size(HEAD)
    return lax.ppermute(value, HEAD, [(i, i ^ mask) for i in range(count)])


def state_swap(value):
    return lax.ppermute(value, STATE, [(0, 1), (1, 0)])


def dp_swap(value):
    return lax.ppermute(value, DP, [(0, 1), (1, 0)])


def state_forward(value):
    return lax.ppermute(value, STATE, [(0, 1)])


def state_backward(value):
    return lax.ppermute(value, STATE, [(1, 0)])


def bit_of(mask):
    return (lax.axis_index(HEAD) // mask) % 2


def chunk_of(masks):
    chunk = 0
    for mask in masks:
        chunk = chunk * 2 + bit_of(mask)
    return chunk


def sum_rows(value, masks, axis):
    for mask in masks:
        bit = bit_of(mask)
        half = value.shape[axis] // 2
        away = lax.dynamic_slice_in_dim(value, (1 - bit) * half, half, axis).astype(low)
        kept = lax.dynamic_slice_in_dim(value, bit * half, half, axis)
        value = kept.astype(full) + head_swap(away, mask).astype(full)
    return value


def gather_rows(value, masks, axis):
    for mask in masks[::-1]:
        bit = bit_of(mask)
        got = head_swap(value, mask)
        value = jnp.concatenate(
            [jnp.where(bit == 1, got, value), jnp.where(bit == 1, value, got)], axis
        )
    return value


def sum_row16(value, masks):
    state = lax.axis_index(STATE)
    value = sum_rows(value, masks, 1)
    away = lax.dynamic_index_in_dim(value, 1 - state, 0, False).astype(low)
    kept = lax.dynamic_index_in_dim(value, state, 0, False)
    return kept + state_swap(away).astype(full)


def gather_row16(value, masks):
    state = lax.axis_index(STATE)
    got = state_swap(value)
    both = jnp.stack([jnp.where(state == 0, value, got), jnp.where(state == 0, got, value)], 0)
    return gather_rows(both, masks, 1)


def pick_state(pair, index):
    return jnp.where(index == 0, pair[0], pair[1])


def weight_pieces(shard, axis):
    state = lax.axis_index(STATE)
    dp = lax.axis_index(DP)
    half = shard.shape[axis] // 2
    mine = lax.dynamic_slice_in_dim(shard, state * half, half, axis)
    got = state_swap(lax.dynamic_slice_in_dim(shard, (1 - state) * half, half, axis))
    far_mine = dp_swap(mine)
    far_got = dp_swap(got)
    near = [jnp.where(state == 0, mine, got), jnp.where(state == 0, got, mine)]
    far = [jnp.where(state == 0, far_mine, far_got), jnp.where(state == 0, far_got, far_mine)]
    lower = [jnp.where(dp == 0, a, b) for a, b in zip(near, far)]
    upper = [jnp.where(dp == 0, b, a) for a, b in zip(near, far)]
    return jnp.concatenate(lower + upper, 1 - axis)


def grad_pieces(grad, axis):
    state = lax.axis_index(STATE)
    dp = lax.axis_index(DP)
    half = grad.shape[1 - axis] // 2
    away = lax.dynamic_slice_in_dim(grad, (1 - dp) * half, half, 1 - axis).astype(low)
    kept = lax.dynamic_slice_in_dim(grad, dp * half, half, 1 - axis)
    total = kept + dp_swap(away).astype(full)
    quarter = half // 2
    away = lax.dynamic_slice_in_dim(total, (1 - state) * quarter, quarter, 1 - axis).astype(low)
    kept = lax.dynamic_slice_in_dim(total, state * quarter, quarter, 1 - axis)
    got = state_swap(away).astype(full)
    return jnp.concatenate(
        [jnp.where(state == 0, kept, got), jnp.where(state == 0, got, kept)], axis
    )


def norm_scale(values):
    return lax.rsqrt(jnp.mean(values * values, -1, keepdims=True) + epsilon)


def norm_back(values, gain, grad):
    scale = norm_scale(values)
    scaled = grad * gain
    inner = jnp.mean(scaled * values, -1, keepdims=True)
    return (
        scale * scaled - values * (scale * scale * scale * inner),
        jnp.sum(grad * values * scale, 0),
    )


def conv_edge(values, edge, taps, segment, edge_segment):
    reach = taps.shape[0] - 1
    rows = values.shape[0]
    joined = jnp.concatenate([edge, values], 0)
    segs = jnp.concatenate([edge_segment, segment], 0)
    total = taps[0][None, :] * values
    for offset in range(1, taps.shape[0]):
        lower = reach - offset
        same = (segs[lower : lower + rows] == segment).astype(values.dtype)[:, None]
        total = total + taps[offset][None, :] * joined[lower : lower + rows] * same
    return total


def vmem_limit(mebibytes):
    return pltpu.CompilerParams(vmem_limit_bytes=mebibytes * 1024 * 1024)


def dot_nt(left, right):
    return lax.dot_general(left, right, (((1,), (1,)), ((), ())), preferred_element_type=full)


def dot_tn(left, right):
    return lax.dot_general(left, right, (((0,), (0,)), ((), ())), preferred_element_type=full)


def dot_nn(left, right):
    return lax.dot_general(left, right, (((1,), (0,)), ((), ())), preferred_element_type=full)


def dot_exact(left, right):
    return jnp.dot(left, right, preferred_element_type=full, precision=highest)


ROWS_Q = 256
ROWS_K = 512


def attend_kernel(low_ref, q_ref, k_ref, v_ref, seg_col, seg_row, out_ref, lse_ref):
    index = pl.program_id(1)
    scale = q_ref.shape[1] ** (-0.5)
    query = q_ref[...]
    own = seg_col[...]
    place = index * ROWS_Q + lax.broadcasted_iota(jnp.int32, (ROWS_Q, ROWS_K), 0)

    def step(block, carry):
        top, total, acc = carry
        span = pl.ds(pl.multiple_of(block * ROWS_K, ROWS_K), ROWS_K)
        scores = dot_nt(query, k_ref[span, :]) * scale
        other = block * ROWS_K + lax.broadcasted_iota(jnp.int32, (ROWS_Q, ROWS_K), 1)
        scores = jnp.where((own == seg_row[:, span]) & (other <= place), scores, -1e30)
        higher = jnp.maximum(top, jnp.max(scores, -1, keepdims=True))
        weights = jnp.exp(scores - higher)
        fade = jnp.exp(top - higher)
        total = total * fade + jnp.sum(weights, -1, keepdims=True)
        acc = acc * fade + dot_nn(weights.astype(low), v_ref[span, :])
        return higher, total, acc

    start = (
        jnp.full((ROWS_Q, 1), -1e30, full),
        jnp.zeros((ROWS_Q, 1), full),
        jnp.zeros((ROWS_Q, v_ref.shape[1]), full),
    )
    stop = (index * ROWS_Q + ROWS_Q + ROWS_K - 1) // ROWS_K
    top, total, acc = lax.fori_loop(low_ref[index], stop, step, start)
    out_ref[...] = (acc / total).astype(low)
    lse = jnp.broadcast_to(top + jnp.log(total), (ROWS_Q, 128))
    lse_ref[...] = lse.T[0:1, :][None]


def half_block(index, blocks):
    per_state = blocks // 2
    per_half = per_state // 2
    inside = index % per_state
    return inside // per_half * per_state + index // per_state * per_half + inside % per_half


def attend(queries, keys, values, segment, lows):
    length, columns = queries.shape
    heads = columns // HDIM
    blocks = length // ROWS_Q
    whole = pl.BlockSpec((length, HDIM), lambda h, i, *_: (0, h))
    block = pl.BlockSpec((ROWS_Q, HDIM), lambda h, i, *_: (i, h))
    placed = pl.BlockSpec((ROWS_Q, HDIM), lambda h, i, *_: (half_block(i, blocks), h))
    return pl.pallas_call(
        attend_kernel,
        grid_spec=pltpu.PrefetchScalarGridSpec(
            num_scalar_prefetch=1,
            grid=(heads, length // ROWS_Q),
            in_specs=[
                block,
                whole,
                whole,
                pl.BlockSpec((ROWS_Q, 1), lambda h, i, *_: (i, 0)),
                pl.BlockSpec((1, length), lambda h, i, *_: (0, 0)),
            ],
            out_specs=[placed, pl.BlockSpec((1, 1, ROWS_Q), lambda h, i, *_: (h, 0, i))],
        ),
        out_shape=[
            jax.ShapeDtypeStruct((length, columns), low),
            jax.ShapeDtypeStruct((heads, 1, length), full),
        ],
        compiler_params=vmem_limit(40),
        cost_estimate=pl.CostEstimate(
            flops=2 * length * length * columns, bytes_accessed=8 * length * columns,
            transcendentals=length * length * heads // 2,
        ),
    )(lows, queries, keys, values, segment[:, None], segment[None, :])


def attend_back_kernel(
    low_ref, q_ref, k_ref, v_ref, do_ref, o_ref, lse_ref, seg_col, seg_row, dq_ref, dk_ref, dv_ref
):
    index = pl.program_id(1)
    scale = q_ref.shape[1] ** (-0.5)
    query = q_ref[...]
    grad = do_ref[...]
    own = seg_row[...]
    lse = lse_ref[0]
    ones = jnp.ones((8, HDIM), full)
    delta = lax.dot_general(
        ones,
        grad.astype(full) * o_ref[...].astype(full),
        (((1,), (1,)), ((), ())),
        precision=highest,
        preferred_element_type=full,
    )[0:1, :]
    place = index * ROWS_Q + lax.broadcasted_iota(jnp.int32, (ROWS_K, ROWS_Q), 1)

    @pl.when(index == 0)
    def clear():
        dk_ref[...] = jnp.zeros_like(dk_ref)
        dv_ref[...] = jnp.zeros_like(dv_ref)

    def step(block, total):
        span = pl.ds(pl.multiple_of(block * ROWS_K, ROWS_K), ROWS_K)
        key = k_ref[span, :]
        scores = dot_nt(key, query) * scale
        other = block * ROWS_K + lax.broadcasted_iota(jnp.int32, (ROWS_K, ROWS_Q), 0)
        counted = (seg_col[span, :] == own) & (other <= place)
        probs = jnp.exp(jnp.where(counted, scores - lse, -1e30))
        dv_ref[span, :] += dot_nn(probs.astype(low), grad)
        slope = probs * (dot_nt(v_ref[span, :], grad) - delta)
        slope = slope.astype(low)
        dk_ref[span, :] += dot_nn(slope, query) * scale
        return total + dot_tn(slope, key)

    stop = (index * ROWS_Q + ROWS_Q + ROWS_K - 1) // ROWS_K
    total = lax.fori_loop(low_ref[index], stop, step, jnp.zeros((ROWS_Q, HDIM), full))
    dq_ref[...] = total * scale


def attend_back(queries, keys, values, grads, outs, lse, segment, lows):
    length, columns = queries.shape
    heads = columns // HDIM
    blocks = length // ROWS_Q
    whole = pl.BlockSpec((length, HDIM), lambda h, i, *_: (0, h))
    block = pl.BlockSpec((ROWS_Q, HDIM), lambda h, i, *_: (i, h))
    placed = pl.BlockSpec((ROWS_Q, HDIM), lambda h, i, *_: (half_block(i, blocks), h))
    line = pl.BlockSpec((1, 1, ROWS_Q), lambda h, i, *_: (h, 0, i))
    shape = jax.ShapeDtypeStruct((length, columns), full)
    return pl.pallas_call(
        attend_back_kernel,
        grid_spec=pltpu.PrefetchScalarGridSpec(
            num_scalar_prefetch=1,
            grid=(heads, length // ROWS_Q),
            in_specs=[
                block,
                whole,
                whole,
                placed,
                placed,
                line,
                pl.BlockSpec((length, 1), lambda h, i, *_: (0, 0)),
                pl.BlockSpec((1, ROWS_Q), lambda h, i, *_: (0, i)),
            ],
            out_specs=[block, whole, whole],
        ),
        out_shape=[shape, shape, shape],
        compiler_params=vmem_limit(40),
        cost_estimate=pl.CostEstimate(
            flops=5 * length * length * columns, bytes_accessed=20 * length * columns,
            transcendentals=length * length * heads // 2,
        ),
    )(lows, queries, keys, values, grads, outs, lse, segment[:, None], segment[None, :])


def rope_kernel(state_ref, own_ref, other_ref, cos_ref, sin_ref, q_ref, k_ref, v_ref):
    per_state = pl.num_programs(0) // 2
    own = pl.program_id(0) // per_state == state_ref[0]
    columns = q_ref.shape[1]
    for index, out in enumerate((q_ref, k_ref, v_ref)):
        for start in range(0, columns, HDIM):
            lanes = slice(index * columns + start, index * columns + start + HDIM)
            value = jnp.where(own, own_ref[:, lanes], other_ref[:, lanes])
            if index < 2:
                value = value * cos_ref[...] + pltpu.roll(value, HDIM // 2, 1) * sin_ref[...]
            out[:, start : start + HDIM] = value.astype(low)


def rope(state, own, other, cosine, sine):
    length = cosine.shape[0]
    columns = own.shape[1] // 3
    per_state = length // ROWS_Q // 2
    part = pl.BlockSpec((ROWS_Q, own.shape[1]), lambda i, *_: (i % per_state, 0))
    angle = pl.BlockSpec((ROWS_Q, HDIM), lambda i, *_: (i, 0))
    out = pl.BlockSpec((ROWS_Q, columns), lambda i, *_: (i, 0))
    return pl.pallas_call(
        rope_kernel,
        grid_spec=pltpu.PrefetchScalarGridSpec(
            num_scalar_prefetch=1,
            grid=(length // ROWS_Q,),
            in_specs=[part, part, angle, angle],
            out_specs=[out] * 3,
        ),
        out_shape=[jax.ShapeDtypeStruct((length, columns), low)] * 3,
        compiler_params=vmem_limit(32),
        cost_estimate=pl.CostEstimate(
            flops=12 * length * columns, bytes_accessed=36 * length * columns, transcendentals=0
        ),
    )(state[None], own, other, cosine, sine)


def rope_back_kernel(q_ref, k_ref, v_ref, cos_ref, sin_ref, out_ref):
    columns = q_ref.shape[1]
    for index, part in enumerate((q_ref, k_ref, v_ref)):
        for start in range(0, columns, HDIM):
            value = part[:, start : start + HDIM]
            if index < 2:
                value = value * cos_ref[...] - pltpu.roll(value, HDIM // 2, 1) * sin_ref[...]
            lanes = slice(index * columns + start, index * columns + start + HDIM)
            out_ref[:, lanes] = value.astype(low)


def rope_back(query, key, value, cosine, sine):
    length, columns = query.shape
    blocks = length // ROWS_Q
    part = pl.BlockSpec((ROWS_Q, columns), lambda i: (i, 0))
    angle = pl.BlockSpec((ROWS_Q, HDIM), lambda i: (i, 0))
    return pl.pallas_call(
        rope_back_kernel,
        grid=(blocks,),
        in_specs=[part, part, part, angle, angle],
        out_specs=pl.BlockSpec((ROWS_Q, 3 * columns), lambda i: (half_block(i, blocks), 0)),
        out_shape=jax.ShapeDtypeStruct((length, 3 * columns), low),
        compiler_params=vmem_limit(32),
        cost_estimate=pl.CostEstimate(
            flops=12 * length * columns, bytes_accessed=24 * length * columns, transcendentals=0
        ),
    )(query, key, value, cosine, sine)


def hold_kernel(*refs):
    pass


def hold(value, *after):
    anywhere = pl.BlockSpec(memory_space=pl.ANY)
    return pl.pallas_call(
        hold_kernel,
        in_specs=[anywhere] * (1 + len(after)),
        out_specs=anywhere,
        out_shape=jax.ShapeDtypeStruct(value.shape, value.dtype),
        input_output_aliases={0: 0},
        cost_estimate=pl.CostEstimate(flops=0, bytes_accessed=0, transcendentals=0),
    )(value, *after)


def first_blocks(segment):
    length = segment.shape[0]
    heads = segment[::ROWS_Q]
    starts = jnp.sum((segment[None, :] < heads[:, None]).astype(jnp.int32), 1)
    return starts // ROWS_K


def pair_lanes(left, right):
    lane = lax.broadcasted_iota(jnp.int32, (1, 2 * MDIM), 1)
    return jnp.where(lane < MDIM, left, right)


def block_decay(dt_ref, dt_row_ref, rate_ref, rate_col_ref):
    rows = lax.broadcasted_iota(jnp.int32, (GROUP, GROUP), 0)
    cols = lax.broadcasted_iota(jnp.int32, (GROUP, GROUP), 1)
    cumul = dot_exact((cols <= rows).astype(full), dt_ref[...] * rate_ref[...])
    cumul_row = dot_exact(dt_row_ref[...] * rate_col_ref[...], (rows <= cols).astype(full))
    return cumul, cumul_row, rows, cols


def edge_flags(ends_ref, index, seg_col):
    before = ends_ref[index]
    last = ends_ref[index + 1]
    carried = (seg_col[...] == before).astype(full)
    reach = (seg_col[...] == last).astype(full)
    keep = (before == last).astype(full)
    return carried, reach, keep


def pair_columns(values, pair):
    return pair_lanes(values[:, 2 * pair : 2 * pair + 1], values[:, 2 * pair + 1 : 2 * pair + 2])


def step_state(state, pair, scaled, cumul, reach, keep, vec_low):
    column = pair_columns(cumul, pair)
    end = column[GROUP - 1 : GROUP, :]
    weight = jnp.exp(end - column) * reach
    return state * (jnp.exp(end) * keep) + dot_tn(vec_low, (scaled * weight).astype(low)), weight


def scan_end_kernel(
    ends_ref, x_ref, dt_ref, dt_row_ref, rate_ref, rate_col_ref, b_ref, seg_col, out_ref
):
    index = pl.program_id(0)
    cumul, unused_row, unused_a, unused_b = block_decay(dt_ref, dt_row_ref, rate_ref, rate_col_ref)
    unused_c, reach, keep = edge_flags(ends_ref, index, seg_col)
    vec_low = b_ref[...].astype(low)

    @pl.when(index == 0)
    def clear():
        out_ref[...] = jnp.zeros_like(out_ref)

    for pair in range(dt_ref.shape[1] // 2):
        lanes = slice(pair * 2 * MDIM, (pair + 1) * 2 * MDIM)
        scaled = x_ref[:, lanes] * pair_columns(dt_ref[...], pair)
        out_ref[:, lanes], unused_d = step_state(
            out_ref[:, lanes], pair, scaled, cumul, reach, keep, vec_low
        )


def scan_kernel(
    ends_ref,
    x_ref,
    dt_ref,
    dt_row_ref,
    rate_ref,
    rate_col_ref,
    b_ref,
    c_ref,
    seg_col,
    seg_row,
    first_ref,
    out_ref,
    states_ref,
    state,
):
    index = pl.program_id(0)
    cumul, cumul_row, rows, cols = block_decay(dt_ref, dt_row_ref, rate_ref, rate_col_ref)
    carried, reach, keep = edge_flags(ends_ref, index, seg_col)
    vec_low = b_ref[...].astype(low)
    read_low = c_ref[...].astype(low)
    allowed = (seg_col[...] == seg_row[...]) & (cols <= rows)
    inner = jnp.where(allowed, dot_nt(read_low, vec_low), 0.0)

    @pl.when(index == 0)
    def begin():
        state[...] = first_ref[...]

    states_ref[0] = state[...]
    for pair in range(dt_ref.shape[1] // 2):
        lanes = slice(pair * 2 * MDIM, (pair + 1) * 2 * MDIM)
        scaled = x_ref[:, lanes] * pair_columns(dt_ref[...], pair)
        scaled_low = scaled.astype(low)
        parts = []
        for head in (2 * pair, 2 * pair + 1):
            gaps = cumul[:, head : head + 1] - cumul_row[head : head + 1, :]
            mixed = inner * jnp.exp(jnp.minimum(gaps, 0.0))
            parts.append(dot_nn(mixed.astype(low), scaled_low))
        entry = jnp.exp(pair_columns(cumul, pair)) * carried
        held = state[:, lanes]
        out_ref[:, lanes] = pair_lanes(*parts) + dot_nn(read_low, held.astype(low)) * entry
        state[:, lanes], unused = step_state(
            held, pair, scaled, cumul, reach, keep, vec_low
        )


def scan_start_grad_kernel(
    ends_ref, dt_ref, dt_row_ref, rate_ref, rate_col_ref, c_ref, seg_col, dy_ref, out_ref
):
    index = pl.num_programs(0) - 1 - pl.program_id(0)
    cumul, unused_row, unused_a, unused_b = block_decay(dt_ref, dt_row_ref, rate_ref, rate_col_ref)
    carried, unused_c, keep = edge_flags(ends_ref, index, seg_col)
    read_low = c_ref[...].astype(low)

    @pl.when(pl.program_id(0) == 0)
    def clear():
        out_ref[...] = jnp.zeros_like(out_ref)

    for pair in range(dt_ref.shape[1] // 2):
        lanes = slice(pair * 2 * MDIM, (pair + 1) * 2 * MDIM)
        column = pair_columns(cumul, pair)
        retain = jnp.exp(column[GROUP - 1 : GROUP, :]) * keep
        entry = jnp.exp(column) * carried
        out_ref[:, lanes] = out_ref[:, lanes] * retain + dot_tn(
            read_low, (dy_ref[:, lanes] * entry).astype(low)
        )


def scan_back_kernel(
    ends_ref,
    x_ref,
    dt_ref,
    dt_row_ref,
    rate_ref,
    rate_col_ref,
    b_ref,
    c_ref,
    seg_col,
    seg_row,
    dy_ref,
    states_ref,
    last_ref,
    dx_ref,
    ddt_ref,
    dlog_ref,
    dlog_row_ref,
    db_ref,
    dc_ref,
    state_grad,
    inner_grad,
):
    index = pl.num_programs(0) - 1 - pl.program_id(0)
    heads = dt_ref.shape[1]
    cumul, cumul_row, rows, cols = block_decay(dt_ref, dt_row_ref, rate_ref, rate_col_ref)
    carried, reach, keep = edge_flags(ends_ref, index, seg_col)
    vec_low = b_ref[...].astype(low)
    read_low = c_ref[...].astype(low)
    allowed = (seg_col[...] == seg_row[...]) & (cols <= rows)
    inner = jnp.where(allowed, dot_nt(read_low, vec_low), 0.0)
    head_lane = lax.broadcasted_iota(jnp.int32, (GROUP, heads), 1)
    head_row = lax.broadcasted_iota(jnp.int32, (heads, GROUP), 0)
    last_row = lax.broadcasted_iota(jnp.int32, (GROUP, 1), 0) == GROUP - 1
    lane = lax.broadcasted_iota(jnp.int32, (1, 2 * MDIM), 1)

    @pl.when(pl.program_id(0) == 0)
    def begin():
        state_grad[...] = last_ref[...]

    inner_grad[...] = jnp.zeros_like(inner_grad)
    decay_grad = jnp.zeros((GROUP, heads), full)
    decay_row = jnp.zeros((heads, GROUP), full)
    step_grad = jnp.zeros((GROUP, heads), full)
    vec_grad = jnp.zeros(b_ref.shape, full)
    read_grad = jnp.zeros(c_ref.shape, full)
    for pair in range(heads // 2):
        lanes = slice(pair * 2 * MDIM, (pair + 1) * 2 * MDIM)
        values = x_ref[:, lanes]
        steps = pair_columns(dt_ref[...], pair)
        scaled = values * steps
        scaled_low = scaled.astype(low)
        grad = dy_ref[:, lanes]
        grad_low = grad.astype(low)
        held = states_ref[0, :, lanes]
        held_low = held.astype(low)
        later = state_grad[:, lanes]
        later_low = later.astype(low)
        column = pair_columns(cumul, pair)
        end = column[GROUP - 1 : GROUP, :]
        weight = jnp.exp(end - column) * reach
        retain = jnp.exp(end) * keep
        entry = jnp.exp(column) * carried
        parts = []
        for side in range(2):
            head = 2 * pair + side
            gaps = cumul[:, head : head + 1] - cumul_row[head : head + 1, :]
            fading = jnp.where(allowed, jnp.exp(jnp.minimum(gaps, 0.0)), 0.0)
            mixed = inner * fading
            own_lanes = (lane < MDIM) == (side == 0)
            outer = dot_nt(jnp.where(own_lanes, grad, 0.0).astype(low), scaled_low)
            inner_grad[...] += outer * fading
            slope = outer * mixed
            decay_grad = jnp.where(
                head_lane == head, decay_grad + jnp.sum(slope, 1, keepdims=True), decay_grad
            )
            decay_row = jnp.where(
                head_row == head, jnp.sum(slope, 0, keepdims=True), decay_row
            )
            parts.append(dot_tn(mixed.astype(low), grad_low))
        weighted = scaled * weight
        entered = grad * entry
        entered_low = entered.astype(low)
        from_later = dot_nn(vec_low, later_low)
        scaled_grad = pair_lanes(*parts) + weight * from_later
        dx_ref[:, lanes] = scaled_grad * steps
        read_grad += dot_nt(entered_low, held_low)
        vec_grad += dot_nt(weighted.astype(low), later_low)
        fresh = weighted * from_later
        flow = entered * dot_nn(read_low, held_low) - fresh
        finish = jnp.sum(fresh, 0, keepdims=True) + retain * jnp.sum(later * held, 0, keepdims=True)
        steps_part = scaled_grad * values
        for side in range(2):
            head = 2 * pair + side
            own_lanes = (lane < MDIM) == (side == 0)
            total = jnp.sum(jnp.where(own_lanes, flow, 0.0), 1, keepdims=True)
            ending = jnp.sum(jnp.where(own_lanes, finish, 0.0), 1, keepdims=True)
            total = total + jnp.where(last_row, ending, 0.0)
            decay_grad = jnp.where(head_lane == head, decay_grad + total, decay_grad)
            step_grad = jnp.where(
                head_lane == head,
                jnp.sum(jnp.where(own_lanes, steps_part, 0.0), 1, keepdims=True),
                step_grad,
            )
        state_grad[:, lanes] = later * retain + dot_tn(read_low, entered_low)
    inner_low = inner_grad[...].astype(low)
    ddt_ref[...] = step_grad
    dlog_ref[...] = dot_exact((cols >= rows).astype(full), decay_grad)
    dlog_row_ref[...] = dot_exact(decay_row, (rows >= cols).astype(full))
    dc_ref[...] = read_grad + dot_nn(inner_low, vec_low)
    db_ref[...] = vec_grad + dot_tn(inner_low, read_low)


def scan_specs(heads, channels, states, reverse, count):
    def at(i):
        return count - 1 - i if reverse else i

    tall = lambda columns: pl.BlockSpec((GROUP, columns), lambda i, *_: (at(i), 0))
    flat = lambda rows: pl.BlockSpec((rows, GROUP), lambda i, *_: (0, at(i)))
    same = lambda rows, columns: pl.BlockSpec((rows, columns), lambda i, *_: (0, 0))
    return tall, flat, same, pl.BlockSpec((1, states, channels), lambda i, *_: (at(i), 0, 0))


def scan_call(kernel, reverse, ends, inputs, kinds, outs, out_kinds, scratch, dims, flops):
    heads, channels, states, count = dims
    tall, flat, same, cube = scan_specs(heads, channels, states, reverse, count)

    def spec(kind, shape):
        if kind == 0:
            return tall(shape[1])
        if kind == 1:
            return flat(shape[0])
        return same(*shape) if kind == 2 else cube

    return pl.pallas_call(
        kernel,
        grid_spec=pltpu.PrefetchScalarGridSpec(
            num_scalar_prefetch=1,
            grid=(count,),
            in_specs=[spec(kind, value.shape) for kind, value in zip(kinds, inputs)],
            out_specs=[spec(kind, shape) for kind, shape in zip(out_kinds, outs)],
            scratch_shapes=scratch,
        ),
        out_shape=[jax.ShapeDtypeStruct(shape, full) for shape in outs],
        compiler_params=vmem_limit(40),
        cost_estimate=pl.CostEstimate(
            flops=flops, bytes_accessed=8 * count * GROUP * channels, transcendentals=flops // 256
        ),
    )(ends, *inputs)


class Scan:
    def __init__(self, x, dt, rate, b, c, segment, before):
        self.rows, self.heads = dt.shape
        self.channels, self.states = x.shape[1], b.shape[1]
        self.count = self.rows // GROUP
        self.dims = (self.heads, self.channels, self.states, self.count)
        self.ends = jnp.concatenate([before[None], segment[GROUP - 1 :: GROUP]])
        self.x, self.b, self.c = x, b, c
        self.decay = [dt, dt.T, rate[None, :], rate[:, None]]
        self.seg_col, self.seg_row = segment[:, None], segment[None, :]
        self.state_shape = (self.states, self.channels)

    def end(self):
        return scan_call(
            scan_end_kernel,
            False,
            self.ends,
            [self.x, *self.decay, self.b, self.seg_col],
            [0, 0, 1, 2, 2, 0, 0],
            [self.state_shape],
            [2],
            [],
            self.dims,
            2 * self.rows * self.channels * self.states,
        )[0]

    def forward(self, first):
        return scan_call(
            scan_kernel,
            False,
            self.ends,
            [self.x, *self.decay, self.b, self.c, self.seg_col, self.seg_row, first],
            [0, 0, 1, 2, 2, 0, 0, 0, 1, 2],
            [self.x.shape, (self.count,) + self.state_shape],
            [0, 3],
            [pltpu.VMEM(self.state_shape, full)],
            self.dims,
            8 * self.rows * self.channels * GROUP,
        )

    def start_grad(self, grad):
        return scan_call(
            scan_start_grad_kernel,
            True,
            self.ends,
            [*self.decay, self.c, self.seg_col, grad],
            [0, 1, 2, 2, 0, 0, 0],
            [self.state_shape],
            [2],
            [],
            self.dims,
            2 * self.rows * self.channels * self.states,
        )[0]

    def backward(self, grad, states, last):
        wide = (self.rows, self.heads)
        return scan_call(
            scan_back_kernel,
            True,
            self.ends,
            [
                self.x,
                *self.decay,
                self.b,
                self.c,
                self.seg_col,
                self.seg_row,
                grad,
                states,
                last,
            ],
            [0, 0, 1, 2, 2, 0, 0, 0, 1, 0, 3, 2],
            [self.x.shape, wide, wide, wide[::-1], self.b.shape, self.c.shape],
            [0, 0, 0, 1, 0, 0],
            [pltpu.VMEM(self.state_shape, full), pltpu.VMEM((GROUP, GROUP), full)],
            self.dims,
            24 * self.rows * self.channels * GROUP,
        )


def natural_quarters(relative):
    state = lax.axis_index(STATE)
    dp = lax.axis_index(DP)
    near = [jnp.where(state == 0, *relative[:2]), jnp.where(state == 0, *relative[1::-1])]
    far = [jnp.where(state == 0, *relative[2:]), jnp.where(state == 0, *relative[:1:-1])]
    return [jnp.where(dp == 0, a, b) for a, b in zip(near, far)] + [
        jnp.where(dp == 0, b, a) for a, b in zip(near, far)
    ]


def swap_quarters(value):
    quarter = value.shape[-1] // 4
    part = [value[..., i * quarter : (i + 1) * quarter] for i in range(4)]
    return jnp.concatenate([part[1], part[0], part[3], part[2]], -1)


def fast_device(
    hidden,
    embedding,
    cotangent,
    lengths,
    gain_attn,
    w_query,
    w_key,
    w_value,
    down_query,
    down_key,
    down_value,
    up_query,
    up_key,
    up_value,
    attn_output,
    gain_mlp,
    mlp_input,
    down_mlp,
    up_mlp,
    mlp_output,
    gain_mixer,
    proj_inner,
    proj_gate,
    proj_step,
    proj_input,
    proj_read,
    taps_inner,
    taps_input,
    taps_read,
    step_bias,
    log_rate,
    skip_gain,
    gain_gated,
    proj_output,
):
    rows = hidden.shape[0]
    length = cotangent.shape[0]
    width = hidden.shape[1]
    middle = rows // 2
    head_parts = lax.axis_size(HEAD)
    piece = middle // head_parts
    state = lax.axis_index(STATE)
    dp = lax.axis_index(DP)
    head = lax.axis_index(HEAD)
    place = dp * 2 + state
    own_start = state * rows
    orders = head_masks()
    offsets = [chunk_of(orders[0]) * piece, middle + chunk_of(orders[1]) * piece]

    heads_wide = w_query.shape[1]
    half_cols = heads_wide // 2

    def state_columns(values, index):
        return jnp.concatenate(
            [lax.dynamic_slice_in_dim(v, index * half_cols, half_cols, 1) for v in values], 1
        )

    mine = state_columns((w_query, w_key, w_value), state)
    got = state_swap(state_columns((w_query, w_key, w_value), 1 - state))
    cutting = mine.shape[0] // 2
    far_mine = [dp_swap(mine[:cutting]), dp_swap(mine[cutting:])]
    far_got = [dp_swap(got[:cutting]), dp_swap(got[cutting:])]

    rank = down_query.shape[1]
    part_a = down_query.shape[0] // head_parts
    part_m = down_mlp.shape[0] // head_parts
    split_a, split_m = gain_attn.shape[0], gain_mlp.shape[0]
    up_rows = up_query.shape[0]

    def small_pack(index):
        return jnp.concatenate(
            [
                jnp.concatenate([gain_attn, gain_mlp, gain_mixer]).reshape(-1, rank),
                lax.dynamic_slice_in_dim(down_query, head * part_a, part_a, 0),
                lax.dynamic_slice_in_dim(down_key, head * part_a, part_a, 0),
                lax.dynamic_slice_in_dim(down_value, head * part_a, part_a, 0),
                lax.dynamic_slice_in_dim(down_mlp, head * part_m, part_m, 0),
                state_columns((up_query, up_key, up_value), index).reshape(-1, rank),
            ],
            0,
        )

    pack = jnp.stack([small_pack(state), state_swap(small_pack(1 - state))], 0)
    pack = jnp.concatenate([pack, dp_swap(pack)], 0)
    gain_rows = (split_a + 2 * split_m) // rank
    gains = pack[:, :gain_rows].reshape(4, -1).astype(full)
    attn_gain = gains[:, :split_a].reshape(-1)
    gains = natural_quarters([gains[index] for index in range(4)])
    mlp_gain = jnp.concatenate([value[split_a : split_a + split_m] for value in gains])
    mixer_gain = jnp.concatenate([value[split_a + split_m :] for value in gains])
    down_end = gain_rows + 3 * part_a + part_m
    ups = natural_quarters(
        [pack[index, down_end:].reshape(up_rows, 3 * half_cols) for index in range(4)]
    )
    ups = jnp.concatenate(ups, 0)
    column = lax.broadcasted_iota(jnp.int32, (1, 3 * half_cols), 1) // half_cols
    up_wide = jnp.concatenate(
        [jnp.where(column == index, ups, jnp.zeros_like(ups)) for index in range(3)], 0
    )
    masks = orders[0][::-1]
    downs_all = gather_rows(pack[None, :, gain_rows:down_end], masks, 0)

    def down_of(lower, part):
        return downs_all[:, :, lower : lower + part].transpose(1, 0, 2, 3)

    down_wide = jnp.concatenate(
        [down_of(index * part_a, part_a).reshape(-1, rank) for index in range(3)], 1
    )
    down_m = down_of(3 * part_a, part_m)
    mlp_down = jnp.concatenate(natural_quarters([down_m[i] for i in range(4)]), 0)
    mlp_down = mlp_down.reshape(-1, rank)

    segment, position, valid = row_layout(lengths[0], length)
    own_segment = lax.dynamic_slice_in_dim(segment, own_start, rows)
    own_valid = lax.dynamic_slice_in_dim(valid, own_start, rows)[:, None]
    lows = first_blocks(segment)
    half = HDIM // 2
    angle = position[:, None] * 10000.0 ** (-jnp.arange(half, dtype=full) / half)[None, :]
    cosine = jnp.concatenate([jnp.cos(angle), jnp.cos(angle)], 1)
    sine = jnp.concatenate([-jnp.sin(angle), jnp.sin(angle)], 1)

    def cut(value):
        return [lax.dynamic_slice_in_dim(value, offset, piece, 0) for offset in offsets]

    valid_cut = cut(own_valid)

    quarter = gain_attn.shape[0]

    def quarters(first, second):
        both = jnp.concatenate([first, second], 1)
        return jnp.concatenate(
            [
                lax.dynamic_slice_in_dim(both, (place ^ index) * quarter, quarter, 1)
                for index in range(4)
            ],
            1,
        ).astype(full)

    normed_own = rms_norm(quarters(hidden, embedding), attn_gain).astype(low)
    near_own, far_own = normed_own[:, :width], normed_own[:, width:]
    joined_cut = [quarters(a, b) for a, b in zip(cut(hidden), cut(embedding))]

    share = rows // head_parts

    def sent_rows(value, order):
        sent = lax.dynamic_slice_in_dim(value, chunk_of(order) * share, share, 0)
        return jnp.concatenate([sent[:, quarter:], sent[:, :quarter]], 1)

    sent = jnp.stack([sent_rows(near_own, orders[0]), sent_rows(far_own, orders[1])], 0)
    sent = state_swap(hold(sent, far_mine[0]))
    sent = hold(sent, far_mine[1])
    near_other = gather_rows(sent[0], orders[0][1:], 0)
    far_other = gather_rows(sent[1], orders[1][1:], 0)
    near_other = hold(near_other, far_got[0])
    near_other = gather_rows(near_other, orders[0][:1], 0)
    far_other = gather_rows(far_other, orders[1][:1], 0)
    main_near = jnp.concatenate([mine, got], 0)
    main_far = jnp.concatenate(far_mine + far_got, 0)

    def project(near, far):
        reduced = (plain_dot(near, down_wide[:width]) + plain_dot(far, down_wide[width:])).astype(low)
        total = plain_dot(near, main_near) + plain_dot(reduced, up_wide)
        return total + plain_dot(far, main_far), reduced

    pre_own, red_own = project(near_own, far_own)
    pre_other, red_other = project(near_other, far_other)
    queries, keys, values = rope(state, pre_own, pre_other, cosine, sine)

    attn_mine = lax.dynamic_slice_in_dim(attn_output, state * half_cols, half_cols, 0)
    attn_got = state_swap(
        lax.dynamic_slice_in_dim(attn_output, (1 - state) * half_cols, half_cols, 0)
    )
    attn_pair = jnp.stack([attn_mine, attn_got], 0)
    attn_far = dp_swap(attn_pair)
    attn_proj = jnp.concatenate(
        natural_quarters([attn_pair[0], attn_pair[1], attn_far[0], attn_far[1]]), 1
    )
    mlp_cut = mlp_input.shape[1] // 2
    mlp_input = hold(mlp_input, far_got[1])
    mlp_first = lax.all_gather(mlp_input[:, :mlp_cut], ZED, axis=0, tiled=True)
    mlp_second = lax.all_gather(mlp_input[:, mlp_cut:], ZED, axis=0, tiled=True)
    mlp_main = jnp.concatenate([mlp_first, mlp_second], 1)
    mlp_proj = lax.all_gather(mlp_output, ZED, axis=1, tiled=True)
    mixer_main = lax.all_gather(
        jnp.concatenate([proj_inner, proj_gate], 1), ZED, axis=0, tiled=True
    )
    output_main = lax.all_gather(proj_output, ZED, axis=1, tiled=True)
    step_width = proj_step.shape[1]
    small = jnp.concatenate([up_mlp, proj_step.reshape(-1, up_mlp.shape[1])], 0)
    small = hold(small, far_got[1])
    small = jnp.stack([small, state_swap(small)], 0)
    small_far = dp_swap(small)
    small = natural_quarters([small[0], small[1], small_far[0], small_far[1]])
    mlp_upper = jnp.concatenate([value[: up_mlp.shape[0]] for value in small], 0)
    step_main = jnp.concatenate(
        [value[up_mlp.shape[0] :].reshape(-1, step_width) for value in small], 0
    )

    attended, lse = attend(queries, keys, values, segment, lows)

    attended = hold(attended, mlp_first)
    attended_halves = [attended[:rows], attended[rows:]]
    branch_cut = [
        sum_row16(plain_dot(part, attn_proj).astype(low).reshape(2, middle, width), order)
        for part, order in zip(attended_halves, orders)
    ]
    first_cut = [
        value.astype(full) + good * branch
        for value, good, branch in zip(cut(hidden), valid_cut, branch_cut)
    ]
    mlp_normed = [
        gather_rows(rms_norm(value, mlp_gain).astype(low), order, 0)
        for value, order in zip(first_cut, orders)
    ]
    mlp_red = [plain_dot(value, mlp_down).astype(low) for value in mlp_normed]
    hidden_pre = [
        plain_dot(value, mlp_main) + plain_dot(red, mlp_upper)
        for value, red in zip(mlp_normed, mlp_red)
    ]
    activated = [jax.nn.gelu(value, approximate=False).astype(low) for value in hidden_pre]
    second_cut = [
        value + good * sum_rows(plain_dot(part, mlp_proj).astype(low), order, 0)
        for value, good, part, order in zip(first_cut, valid_cut, activated, orders)
    ]
    mixer_normed = jnp.concatenate(
        [
            gather_rows(rms_norm(value, mixer_gain).astype(low), order, 0)
            for value, order in zip(second_cut, orders)
        ],
        0,
    )

    inner_width = proj_inner.shape[1]
    mixer_heads = step_width
    states = proj_input.shape[1]
    small_main = jnp.concatenate([step_main, proj_input, proj_read], 1)
    small_pre = plain_dot(mixer_normed, small_main)
    mixer_pre = plain_dot(mixer_normed, mixer_main)
    inner_pre, gate_pre = mixer_pre[:, :inner_width], mixer_pre[:, inner_width:]
    reach = taps_inner.shape[0] - 1
    edge = state_forward(
        jnp.concatenate([inner_pre[rows - reach :], small_pre[rows - reach :, mixer_heads:]], 1)
    )
    edge_start = jnp.maximum(own_start - reach, 0)
    edge_segment = jnp.where(state == 0, -1, lax.dynamic_slice_in_dim(segment, edge_start, reach))

    def conv_piece(inner_in, small_in, edge_in, taps_x, taps_b, taps_c, shift_in):
        input_in = small_in[:, mixer_heads : mixer_heads + states]
        read_in = small_in[:, mixer_heads + states :]
        edge_b = edge_in[:, inner_width : inner_width + states]
        edge_c = edge_in[:, inner_width + states :]
        return (
            jax.nn.silu(
                conv_edge(inner_in, edge_in[:, :inner_width], taps_x, own_segment, edge_segment)
            ),
            jax.nn.silu(conv_edge(input_in, edge_b, taps_b, own_segment, edge_segment)),
            jax.nn.silu(conv_edge(read_in, edge_c, taps_c, own_segment, edge_segment)),
            jax.nn.softplus(small_in[:, :mixer_heads] + shift_in[None, :]),
        )

    (inner_conv, input_conv, read_conv, steps), conv_back = jax.vjp(
        conv_piece,
        inner_pre,
        small_pre,
        edge,
        taps_inner.astype(full),
        taps_input.astype(full),
        taps_read.astype(full),
        step_bias.astype(full),
    )
    rate = -jnp.exp(log_rate.astype(full))
    scan = Scan(inner_conv, steps, rate, input_conv, read_conv, own_segment, edge_segment[-1])
    first_state = state_forward(scan.end())
    scanned, block_states = scan.forward(first_state)

    def by_head(value):
        return value.reshape(rows, mixer_heads, MDIM)

    skip_full = jnp.repeat(skip_gain.astype(full), MDIM)[None, :]
    combined = scanned + skip_full * inner_conv
    gate_act = jax.nn.silu(gate_pre)
    united = combined * gate_act
    gated_gain = gain_gated.astype(full)[None, :]
    cot_own = lax.dynamic_slice_in_dim(cotangent, own_start, rows, 0)
    mix_grad = cot_own * own_valid.astype(low)
    gated_grad = right_dot(mix_grad, output_main)
    pair = jnp.stack(
        [jnp.sum(united * united, 1), jnp.sum(united * gated_gain * gated_grad, 1)], 0
    )
    for mask in orders[0]:
        pair = pair + head_swap(pair, mask)
    channels = inner_width * head_parts
    row_scale = lax.rsqrt(pair[0] / channels + epsilon)[:, None]
    row_total = pair[1][:, None]
    gated = (united * row_scale * gated_gain).astype(low)
    united_grad = (
        row_scale * gated_gain * gated_grad
        - united * row_scale * row_scale * row_scale * row_total / channels
    )
    combined_grad = united_grad * gate_act
    last_state_grad = state_backward(scan.start_grad(combined_grad))

    sigmoid_gate = jax.nn.sigmoid(gate_pre)
    gate_grad = united_grad * combined * sigmoid_gate * (1.0 + gate_pre * (1.0 - sigmoid_gate))
    grad_gated_gain = jnp.sum(gated_grad * united * row_scale, 0)
    grad_skip = jnp.sum(by_head(combined_grad * inner_conv), (0, 2))
    scan_grad, step_grad, log_grad, log_rows, input_grad, read_grad = scan.backward(
        combined_grad, block_states, last_state_grad
    )
    log_grad = log_grad - log_rows.T
    grad_rate = jnp.sum(log_grad * steps, 0) * rate
    (
        inner_grad,
        small_grad,
        edge_grad,
        grad_taps_x,
        grad_taps_b,
        grad_taps_c,
        grad_shift,
    ) = conv_back(
        (
            scan_grad + skip_full * combined_grad,
            input_grad,
            read_grad,
            step_grad + log_grad * rate[None, :],
        )
    )
    edge_back = state_backward(edge_grad)
    inner_grad = inner_grad.at[rows - reach :].add(edge_back[:, :inner_width])
    small_grad = small_grad.at[rows - reach :, mixer_heads:].add(edge_back[:, inner_width:])
    out_cut = [
        (
            value
            + good
            * sum_rows(
                plain_dot(gated[index * middle : (index + 1) * middle], output_main).astype(low),
                order,
                0,
            )
        ).astype(low)
        for index, (value, good, order) in enumerate(zip(second_cut, valid_cut, orders))
    ]
    inner_low = jnp.concatenate([inner_grad, gate_grad], 1).astype(low)
    inner_low = hold(inner_low, *out_cut)
    small_low = small_grad.astype(low)
    mixer_sum = [
        sum_rows(
            (right_dot(inner_low[part], mixer_main) + right_dot(small_low[part], small_main)).astype(
                low
            ),
            order,
            0,
        )
        for part, order in zip((slice(0, middle), slice(middle, rows)), orders)
    ]
    upstream_cut = [value.astype(full) for value in cut(cot_own)]
    mixer_backs = [
        norm_back(value, mixer_gain, grad) for value, grad in zip(second_cut, mixer_sum)
    ]
    second_grad = [up + back[0] for up, back in zip(upstream_cut, mixer_backs)]
    grad_mixer_gain = mixer_backs[0][1] + mixer_backs[1][1]
    mlp_grad = [
        gather_rows((good * grad).astype(low), order, 0)
        for good, grad, order in zip(valid_cut, second_grad, orders)
    ]

    def gelu_part(value):
        return jax.nn.gelu(value, approximate=False)

    hidden_grad = [
        jax.vjp(gelu_part, pre)[1](right_dot(grad, mlp_proj))[0].astype(low)
        for pre, grad in zip(hidden_pre, mlp_grad)
    ]
    mlp_wide = jnp.concatenate([mlp_main, mlp_upper], 0)
    mlp_sums = [
        sum_rows(right_dot(grad, mlp_wide).astype(low), order, 0)
        for grad, order in zip(hidden_grad, orders)
    ]
    middle_low = [value[:, width:].astype(low) for value in mlp_sums]
    mlp_backs = [
        norm_back(value, mlp_gain, total[:, :width] + right_dot(mid, mlp_down))
        for value, total, mid in zip(first_cut, mlp_sums, middle_low)
    ]
    first_grad = [grad + back[0] for grad, back in zip(second_grad, mlp_backs)]
    grad_mlp_gain = mlp_backs[0][1] + mlp_backs[1][1]
    branch_halves = [
        gather_row16((good * grad).astype(low), order).reshape(rows, width)
        for good, grad, order in zip(valid_cut, first_grad, orders)
    ]

    layer_halves = [gather_row16(value, order) for value, order in zip(out_cut, orders)]
    layer_out = jnp.stack(layer_halves, 1).reshape(length, width)
    attended_grad = jnp.concatenate(
        [right_dot(value, attn_proj).astype(low) for value in branch_halves], 0
    )
    query_back, key_back, value_back = attend_back(
        queries, keys, values, attended_grad, attended, lse, segment, lows
    )
    attn_grad = left_dot(attended_halves[0], branch_halves[0]) + left_dot(
        attended_halves[1], branch_halves[1]
    )
    out_attn = grad_pieces(attn_grad.astype(low), 0)
    pre_grad = rope_back(query_back, key_back, value_back, cosine, sine)
    pre_grad = hold(pre_grad, *layer_halves, out_attn)
    main_wide = jnp.concatenate([main_near, main_far, up_wide], 0)
    joint = 2 * width
    normed_sums = []
    for part, order in zip((pre_grad[:rows], pre_grad[rows:]), orders):
        total = right_dot(part, main_wide).astype(low).reshape(2, middle, -1)
        total = sum_rows(total, order, 1)
        away = lax.dynamic_index_in_dim(total, 1 - state, 0, False).astype(low)
        away = jnp.concatenate([swap_quarters(away[:, :joint]), away[:, joint:]], 1)
        kept = lax.dynamic_index_in_dim(total, state, 0, False)
        normed_sums.append(kept + state_swap(away).astype(full))
    cubes = pre_grad.reshape(2, 2, middle, -1)
    grad_own, grad_other = (
        lax.dynamic_index_in_dim(cubes, index, 1, False).reshape(rows, -1)
        for index in (state, 1 - state)
    )
    wide_grad = left_dot(red_own, grad_own) + left_dot(red_other, grad_other)
    up_grad = jnp.concatenate(
        [
            wide_grad[index * rank : (index + 1) * rank, index * half_cols : (index + 1) * half_cols]
            for index in range(3)
        ],
        1,
    )

    def main_grad(own, other, lower, index):
        part = slice(lower * quarter, (lower + 1) * quarter)
        main = left_dot(own[:, part], grad_own) + left_dot(other[:, part], grad_other)
        ups = lax.dynamic_slice_in_dim(up_grad, (place ^ index) * up_rows, up_rows, 0)
        return jnp.concatenate([main, ups], 0).astype(low)

    def by_dp(near, far):
        both = jnp.concatenate([jnp.where(dp == 0, near, far), jnp.where(dp == 0, far, near)], 0)
        return lax.psum_scatter(both, DP, scatter_dimension=0, tiled=True)

    beside = by_dp(main_grad(near_own, near_other, 1, 1), main_grad(far_own, far_other, 1, 3))
    main_total = by_dp(main_grad(near_own, near_other, 0, 0), main_grad(far_own, far_other, 0, 2))
    beside_got = state_swap(beside)

    def spread(own, got, index):
        part = slice(index * half_cols, (index + 1) * half_cols)
        own, got = own[:, part].astype(full), got[:, part].astype(full)
        return jnp.concatenate(
            [jnp.where(state == 0, own, got), jnp.where(state == 0, got, own)], 1
        )

    lows_cut = [value[:, joint:].astype(low) for value in normed_sums]
    joined_backs = [
        norm_back(value, attn_gain, total[:, :joint] + right_dot(mid, down_wide))
        for value, total, mid in zip(joined_cut, normed_sums, lows_cut)
    ]
    grad_attn_gain = joined_backs[0][1] + joined_backs[1][1]

    def natural_columns(value):
        return jnp.concatenate(
            [
                lax.dynamic_slice_in_dim(value, (place ^ index) * quarter, quarter, -1)
                for index in range(4)
            ],
            -1,
        )

    input_cut = []
    for grad, back in zip(first_grad, joined_backs):
        joined_grad = natural_columns(back[0])
        input_cut.append(
            (
                (grad + joined_grad[:, :width]).astype(low),
                joined_grad[:, width:].astype(low),
            )
        )
    grad_hidden, grad_embedding = (
        jnp.concatenate(
            [gather_rows(pieces[index], order, 0) for pieces, order in zip(input_cut, orders)], 0
        )
        for index in range(2)
    )

    def scatter(value, axis):
        return lax.psum_scatter(
            value.astype(low), ZED, scatter_dimension=axis, tiled=True
        ).astype(full)

    out_output = scatter(left_dot(gated, mix_grad), 1)
    out_mixer = scatter(left_dot(mixer_normed, inner_low), 0)
    mlp_normed_own = jnp.concatenate(mlp_normed, 0)
    hidden_grad_own = jnp.concatenate(hidden_grad, 0)
    out_mlp_output = scatter(
        left_dot(jnp.concatenate(activated, 0), jnp.concatenate(mlp_grad, 0)), 1
    )
    out_mlp_input = scatter(left_dot(mlp_normed_own, hidden_grad_own), 0)
    out_up_mlp = scatter(left_dot(jnp.concatenate(mlp_red, 0), hidden_grad_own), 0)

    lows_halves = [gather_row16(value, order) for value, order in zip(lows_cut, orders)]
    lows_own, lows_other = (
        jnp.concatenate(
            [lax.dynamic_index_in_dim(value, index, 0, False) for value in lows_halves], 0
        )
        for index in (state, 1 - state)
    )

    def down_rows(own, other):
        start = head * part_a
        own = lax.dynamic_slice_in_dim(own, start, part_a, 1)
        other = lax.dynamic_slice_in_dim(other, start, part_a, 1)
        return left_dot(own, lows_own) + left_dot(other, lows_other)

    down_sum = down_rows(near_own, near_other) + dp_swap(
        down_rows(far_own, far_other).astype(low)
    ).astype(full)
    down_all = gather_rows(down_sum.astype(low)[None], masks, 0).reshape(quarter, 3 * rank)
    down_all = down_all.astype(full)
    out_downs = [down_all[:, index * rank : (index + 1) * rank] for index in range(3)]

    def placed(value, axis):
        shape = list(value.shape)
        shape[axis] *= head_parts
        return lax.dynamic_update_slice_in_dim(
            jnp.zeros(shape, full), value, head * value.shape[axis], axis
        )

    small_main_grad = left_dot(mixer_normed, small_low)
    small_sum = jnp.concatenate(
        [small_main_grad[:, mixer_heads:], placed(small_main_grad[:, :mixer_heads], 1)], 1
    )
    small_sum = lax.psum(small_sum, EVERY)
    vector_grad = small_sum[:, : 2 * states]
    out_step = lax.dynamic_slice(
        small_sum,
        (place * split_m, 2 * states + head * mixer_heads),
        (split_m, mixer_heads),
    )
    normed_cut = [
        lax.dynamic_slice_in_dim(value, chunk_of(order) * piece, piece, 0)
        for value, order in zip(mlp_normed, orders)
    ]
    mlp_down_grad = left_dot(jnp.concatenate(normed_cut, 0), jnp.concatenate(middle_low, 0))
    mlp_down_grad = lax.psum(hold(mlp_down_grad, main_total), EVERY)
    out_down_mlp = lax.dynamic_slice_in_dim(mlp_down_grad, place * split_m, split_m, 0)

    beside_got = hold(beside_got, grad_hidden)
    out_all = [spread(main_total, beside_got, index) for index in range(3)]
    out_main = [value[:quarter] for value in out_all]
    out_up = [value[quarter:] for value in out_all]
    flat_sums = [
        placed(grad_taps_x, 1),
        placed(jnp.stack([grad_shift, grad_rate, grad_skip]), 1),
        placed(grad_gated_gain, 0),
        jnp.concatenate([grad_taps_b, grad_taps_c], 1),
        natural_columns(grad_attn_gain),
        grad_mlp_gain,
        grad_mixer_gain,
    ]

    once = (head == 0).astype(full)
    square_sum = jnp.zeros((), full)
    for value in out_main + out_up + [out_attn, out_mlp_input, out_up_mlp, out_mlp_output]:
        square_sum = square_sum + jnp.sum(value * value)
    for value in out_downs + [out_down_mlp]:
        square_sum = square_sum + once * jnp.sum(value * value)
    totals = lax.psum(
        jnp.concatenate([value.reshape(-1) for value in flat_sums] + [square_sum[None]]), EVERY
    )
    pieces = []
    for value in flat_sums:
        pieces.append(totals[: value.size].reshape(value.shape))
        totals = totals[value.size :]
    taps_x_total, head_total, gated_total, taps_total, attn_total, mlp_total, mixer_total = pieces

    def of_head(value, size):
        return lax.dynamic_slice_in_dim(value, head * size, size, value.ndim - 1)

    def of_place(value, size):
        return lax.dynamic_slice_in_dim(value, place * size, size)

    head_total = of_head(head_total, mixer_heads)
    return (
        layer_out,
        grad_hidden,
        grad_embedding,
        of_place(attn_total, split_a),
        out_main[0],
        out_main[1],
        out_main[2],
        out_downs[0],
        out_downs[1],
        out_downs[2],
        out_up[0],
        out_up[1],
        out_up[2],
        out_attn,
        of_place(mlp_total, split_m),
        out_mlp_input,
        out_down_mlp,
        out_up_mlp,
        out_mlp_output,
        of_place(mixer_total, split_m),
        out_mixer[:, :inner_width],
        out_mixer[:, inner_width:],
        out_step,
        vector_grad[:, :states],
        vector_grad[:, states:],
        of_head(taps_x_total, inner_width),
        taps_total[:, :states],
        taps_total[:, states:],
        head_total[0],
        head_total[1],
        head_total[2],
        of_head(gated_total, inner_width),
        out_output,
        jnp.sqrt(totals[0]),
    )


def pick_device(mesh):
    heads = mesh.shape[HEAD]
    per_head = DIN // HDIM // heads
    halves = mesh.shape[DP] == 2 and mesh.shape[STATE] == 2
    return fast_device if halves and heads & (heads - 1) == 0 and per_head % 2 == 0 else general_device


def solution(mesh):
    in_specs = (
        P(ZED, None),
        P(ZED, None),
        P(DP, None),
        P(DP, None),
        P(ZED),
        P(ZED, HEAD),
        P(ZED, HEAD),
        P(ZED, HEAD),
        P(ZED, None),
        P(ZED, None),
        P(ZED, None),
        P(ZED, HEAD),
        P(ZED, HEAD),
        P(ZED, HEAD),
        P(HEAD, ZED),
        P(ZED),
        P(ZED, HEAD),
        P(ZED, None),
        P(ZED, HEAD),
        P(HEAD, ZED),
        P(ZED),
        P(ZED, HEAD),
        P(ZED, HEAD),
        P(ZED, HEAD),
        P(),
        P(),
        P(None, HEAD),
        P(),
        P(),
        P(HEAD),
        P(HEAD),
        P(HEAD),
        P(HEAD),
        P(HEAD, ZED),
    )
    out_specs = (
        P(DP, None),
        P(ZED, None),
        P(ZED, None),
        P(ZED),
        P(ZED, HEAD),
        P(ZED, HEAD),
        P(ZED, HEAD),
        P(ZED, None),
        P(ZED, None),
        P(ZED, None),
        P(ZED, HEAD),
        P(ZED, HEAD),
        P(ZED, HEAD),
        P(HEAD, ZED),
        P(ZED),
        P(ZED, HEAD),
        P(ZED, None),
        P(ZED, HEAD),
        P(HEAD, ZED),
        P(ZED),
        P(ZED, HEAD),
        P(ZED, HEAD),
        P(ZED, HEAD),
        P(),
        P(),
        P(None, HEAD),
        P(),
        P(),
        P(HEAD),
        P(HEAD),
        P(HEAD),
        P(HEAD),
        P(HEAD, ZED),
        P(),
    )
    return jax.shard_map(
        pick_device(mesh), mesh=mesh, in_specs=in_specs, out_specs=out_specs, check_vma=False
    )
```

```python
import jax
import jax.numpy as jnp
from jax import lax
from jax.experimental import pallas as pl
from jax.experimental.pallas import tpu as pltpu
from jax.sharding import PartitionSpec as P

HDIM = 128
MDIM = 64
DIN = 4096
GROUP = 256
DP, HEAD, STATE = "dp", "head", "state"
ZED = (DP, STATE)
EVERY = (DP, HEAD, STATE)


highest = lax.Precision.HIGHEST
epsilon = 1e-05


def plain_dot(left, right):
    return jnp.dot(left, right, preferred_element_type=jnp.float32)


def left_dot(left, right):
    return lax.dot_general(
        left, right, (((0,), (0,)), ((), ())), preferred_element_type=jnp.float32
    )


def right_dot(left, right):
    return lax.dot_general(
        left, right, (((1,), (1,)), ((), ())), preferred_element_type=jnp.float32
    )


def exact_left(left, right):
    return lax.dot_general(
        left.astype(jnp.float32), right, (((0,), (0,)), ((), ())), precision=highest
    )


def exact_right(left, right):
    return lax.dot_general(
        left, right.astype(jnp.float32), (((1,), (1,)), ((), ())), precision=highest
    )


def rms_norm(values, gain):
    return values * lax.rsqrt(jnp.mean(values * values, -1, keepdims=True) + epsilon) * gain


def row_layout(doc_lengths, length):
    ends = jnp.cumsum(doc_lengths)
    places = jnp.arange(length, dtype=jnp.int32)
    segment = jnp.sum((places[:, None] >= ends[None, :]).astype(jnp.int32), axis=1)
    starts = jnp.concatenate([ends - doc_lengths, ends[-1:]])
    choose = segment[:, None] == jnp.arange(starts.shape[0], dtype=jnp.int32)[None, :]
    first_place = jnp.sum(jnp.where(choose, starts[None, :], 0), axis=1)
    position = (places - first_place).astype(jnp.float32)
    valid = (segment < doc_lengths.shape[0]).astype(jnp.float32)
    return (segment, position, valid)


def rotate(values, position):
    half = values.shape[-1] // 2
    freqs = 10000.0 ** (-jnp.arange(half, dtype=jnp.float32) / half)
    angle = position[:, None] * freqs[None, :]
    cosine = jnp.cos(angle)[:, None, :]
    sine = jnp.sin(angle)[:, None, :]
    former = values[..., :half]
    latter = values[..., half:]
    return jnp.concatenate([former * cosine - latter * sine, former * sine + latter * cosine], -1)


def head_probs(query_in, key_in, allowed):
    scale = query_in.shape[-1] ** (-0.5)
    scores = (
        jnp.einsum("thd,shd->hts", query_in, key_in, preferred_element_type=jnp.float32) * scale
    )
    scores = jnp.where(allowed[None, :, :], scores, -1e30)
    shifted = scores - jnp.max(scores, -1, keepdims=True)
    weights = jnp.exp(shifted)
    return weights / jnp.sum(weights, -1, keepdims=True)


def conv_mask(values, taps, segment):
    total = taps[0][None, :] * values
    for offset in range(1, taps.shape[0]):
        moved = jnp.concatenate(
            [jnp.zeros((offset, values.shape[1]), values.dtype), values[:-offset]], 0
        )
        moved_seg = jnp.concatenate([jnp.full((offset,), -1, jnp.int32), segment[:-offset]], 0)
        same = (moved_seg == segment).astype(values.dtype)[:, None]
        total = total + taps[offset][None, :] * moved * same
    return total


def state_scan(inputs, step_sizes, decay, input_vecs, read_vecs, segment, block):
    length, heads, width = inputs.shape
    count = length // block
    states = input_vecs.shape[1]

    def one_block(carry, pieces):
        state, before = carry
        group_in, group_dt, group_b, group_c, group_seg = pieces
        logs = group_dt * decay[None, :]
        cumul = jnp.cumsum(logs, 0)
        places = jnp.arange(block, dtype=jnp.int32)
        allowed = (group_seg[:, None] == group_seg[None, :]) & (places[None, :] <= places[:, None])
        gaps = cumul[:, None, :] - cumul[None, :, :]
        fading = jnp.where(
            allowed[:, :, None], jnp.exp(jnp.where(allowed[:, :, None], gaps, 0.0)), 0.0
        )
        inner = jnp.dot(group_c, group_b.T, precision=highest)
        scaled = group_in * group_dt[:, :, None]
        local_out = jnp.einsum(
            "tsh,shp->thp", inner[:, :, None] * fading, scaled, precision=highest
        )
        carried = (group_seg == before).astype(inputs.dtype)
        entry = jnp.exp(cumul) * carried[:, None]
        from_state = (
            jnp.einsum("tn,hnp->thp", group_c, state, precision=highest) * entry[:, :, None]
        )
        last_seg = group_seg[-1]
        reach = (group_seg == last_seg).astype(inputs.dtype)
        to_end = jnp.exp(cumul[-1][None, :] - cumul) * reach[:, None]
        retain = jnp.exp(cumul[-1]) * (last_seg == before).astype(inputs.dtype)
        fresh = jnp.einsum("sn,sh,shp->hnp", group_b, to_end, scaled, precision=highest)
        state = state * retain[:, None, None] + fresh
        return ((state, last_seg), local_out + from_state)

    pieces = (
        inputs.reshape(count, block, heads, width),
        step_sizes.reshape(count, block, heads),
        input_vecs.reshape(count, block, states),
        read_vecs.reshape(count, block, states),
        segment.reshape(count, block),
    )
    start = (jnp.zeros((heads, states, width), inputs.dtype), jnp.array(-1, jnp.int32))
    unused, outputs = lax.scan(jax.checkpoint(one_block), start, pieces)
    return outputs.reshape(length, heads, width)


def mixer_core(
    inner_pre,
    input_pre,
    read_pre,
    step_pre,
    taps_x,
    taps_b,
    taps_c,
    shift_in,
    rate_in,
    segment,
    width,
    block,
):
    inner_conv = jax.nn.silu(conv_mask(inner_pre, taps_x, segment))
    input_conv = jax.nn.silu(conv_mask(input_pre, taps_b, segment))
    read_conv = jax.nn.silu(conv_mask(read_pre, taps_c, segment))
    step_sizes = jax.nn.softplus(step_pre + shift_in[None, :])
    heads = step_sizes.shape[1]
    length = inner_conv.shape[0]
    outputs = state_scan(
        inner_conv.reshape(length, heads, width),
        step_sizes,
        -jnp.exp(rate_in),
        input_conv,
        read_conv,
        segment,
        block,
    )
    return (outputs.reshape(length, heads * width), inner_conv)


def place_slice(piece, index, parts, axis):
    shape = list(piece.shape)
    shape[axis] = shape[axis] * parts
    holder = jnp.zeros(tuple(shape), jnp.float32)
    return lax.dynamic_update_slice_in_dim(holder, piece, index * piece.shape[axis], axis)


def take_slice(whole, index, width, axis):
    return lax.dynamic_slice_in_dim(whole, index * width, width, axis)


def general_device(
    hidden,
    embedding,
    cotangent,
    lengths,
    gain_attn,
    w_query,
    w_key,
    w_value,
    down_query,
    down_key,
    down_value,
    up_query,
    up_key,
    up_value,
    attn_output,
    gain_mlp,
    mlp_input,
    down_mlp,
    up_mlp,
    mlp_output,
    gain_mixer,
    proj_inner,
    proj_gate,
    proj_step,
    proj_input,
    proj_read,
    taps_inner,
    taps_input,
    taps_read,
    step_bias,
    log_rate,
    skip_gain,
    gain_gated,
    proj_output,
):
    row_count = hidden.shape[0]
    length = cotangent.shape[0]
    model_width = hidden.shape[1]
    head_parts = lax.axis_size(HEAD)
    state_parts = lax.axis_size(STATE)
    state_index = lax.axis_index(STATE)
    head_index = lax.axis_index(HEAD)
    own_start = state_index * row_count
    segment, position, valid = row_layout(lengths[0], length)
    own_segment = lax.dynamic_slice_in_dim(segment, own_start, row_count)
    own_position = lax.dynamic_slice_in_dim(position, own_start, row_count)
    own_valid = lax.dynamic_slice_in_dim(valid, own_start, row_count)[:, None]
    full_valid = valid[:, None]
    places = jnp.arange(length, dtype=jnp.int32)
    own_places = own_start + jnp.arange(row_count, dtype=jnp.int32)
    own_mask = ((places >= own_start) & (places < own_start + row_count)).astype(jnp.float32)[
        :, None
    ]
    allowed = (own_segment[:, None] == segment[None, :]) & (places[None, :] <= own_places[:, None])
    gathered = (
        lax.all_gather(gain_attn, ZED, axis=0, tiled=True),
        lax.all_gather(w_query, ZED, axis=0, tiled=True),
        lax.all_gather(w_key, ZED, axis=0, tiled=True),
        lax.all_gather(w_value, ZED, axis=0, tiled=True),
        lax.all_gather(down_query, ZED, axis=0, tiled=True),
        lax.all_gather(down_key, ZED, axis=0, tiled=True),
        lax.all_gather(down_value, ZED, axis=0, tiled=True),
        lax.all_gather(up_query, ZED, axis=0, tiled=True),
        lax.all_gather(up_key, ZED, axis=0, tiled=True),
        lax.all_gather(up_value, ZED, axis=0, tiled=True),
        lax.all_gather(attn_output, ZED, axis=1, tiled=True),
        lax.all_gather(gain_mlp, ZED, axis=0, tiled=True),
        lax.all_gather(mlp_input, ZED, axis=0, tiled=True),
        lax.all_gather(down_mlp, ZED, axis=0, tiled=True),
        lax.all_gather(up_mlp, ZED, axis=0, tiled=True),
        lax.all_gather(mlp_output, ZED, axis=1, tiled=True),
        lax.all_gather(gain_mixer, ZED, axis=0, tiled=True),
        lax.all_gather(proj_inner, ZED, axis=0, tiled=True),
        lax.all_gather(proj_gate, ZED, axis=0, tiled=True),
        lax.all_gather(proj_step, ZED, axis=0, tiled=True),
        lax.all_gather(proj_output, ZED, axis=1, tiled=True),
    )
    (
        attn_gain,
        query_main,
        key_main,
        value_main,
        query_down,
        key_down,
        value_down,
        query_upper,
        key_upper,
        value_upper,
        attn_proj,
        mlp_gain,
        mlp_main,
        mlp_down,
        mlp_upper,
        mlp_proj,
        mixer_gain,
        inner_main,
        gate_main,
        step_main,
        output_main,
    ) = gathered
    joined = jnp.concatenate([hidden, embedding], 1).astype(jnp.float32)
    attn_gain_f = attn_gain.astype(jnp.float32)
    normed = rms_norm(joined, attn_gain_f).astype(jnp.bfloat16)
    head_count = query_main.shape[1] // HDIM

    def project(main, down, upper):
        reduced = plain_dot(normed, down).astype(jnp.bfloat16)
        return (plain_dot(normed, main) + plain_dot(reduced, upper), reduced)

    query_pre, query_red = project(query_main, query_down, query_upper)
    key_pre, key_red = project(key_main, key_down, key_upper)
    value_pre, value_red = project(value_main, value_down, value_upper)
    queries = rotate(query_pre.reshape(row_count, head_count, HDIM), own_position).astype(
        jnp.bfloat16
    )
    keys_own = rotate(key_pre.reshape(row_count, head_count, HDIM), own_position).astype(
        jnp.bfloat16
    )
    values_own = value_pre.reshape(row_count, head_count, HDIM).astype(jnp.bfloat16)
    keys_all, values_all = (
        lax.all_gather(keys_own, STATE, axis=0, tiled=True),
        lax.all_gather(values_own, STATE, axis=0, tiled=True),
    )
    probs_full = head_probs(queries, keys_all, allowed)
    attended_f = jnp.einsum(
        "hts,shd->thd",
        probs_full.astype(jnp.bfloat16),
        values_all,
        preferred_element_type=jnp.float32,
    )
    attended = attended_f.reshape(row_count, head_count * HDIM).astype(jnp.bfloat16)
    branch = lax.psum(plain_dot(attended, attn_proj), HEAD)
    first = hidden.astype(jnp.float32) + own_valid * branch
    mlp_gain_f = mlp_gain.astype(jnp.float32)
    mlp_normed = rms_norm(first, mlp_gain_f).astype(jnp.bfloat16)
    mlp_red = plain_dot(mlp_normed, mlp_down).astype(jnp.bfloat16)
    hidden_pre = plain_dot(mlp_normed, mlp_main) + plain_dot(mlp_red, mlp_upper)
    activated = jax.nn.gelu(hidden_pre, approximate=False).astype(jnp.bfloat16)
    mlp_branch = lax.psum(plain_dot(activated, mlp_proj), HEAD)
    second = first + own_valid * mlp_branch
    second_all = lax.all_gather(second, STATE, axis=0, tiled=True)
    mixer_gain_f = mixer_gain.astype(jnp.float32)
    mixer_normed = rms_norm(second_all, mixer_gain_f).astype(jnp.bfloat16)
    states_own = proj_input.shape[1] // state_parts
    input_half = take_slice(proj_input, state_index, states_own, 1)
    read_half = take_slice(proj_read, state_index, states_own, 1)
    taps_input_half = take_slice(taps_input, state_index, states_own, 1).astype(jnp.float32)
    taps_read_half = take_slice(taps_read, state_index, states_own, 1).astype(jnp.float32)
    inner_pre = plain_dot(mixer_normed, inner_main)
    gate_pre = plain_dot(mixer_normed, gate_main)
    step_pre = plain_dot(mixer_normed, step_main)
    input_pre = plain_dot(mixer_normed, input_half)
    read_pre = plain_dot(mixer_normed, read_half)

    def mixer_piece(
        inner_in, input_in, read_in, step_in, taps_x, taps_b, taps_c, shift_in, rate_in
    ):
        return mixer_core(
            inner_in,
            input_in,
            read_in,
            step_in,
            taps_x,
            taps_b,
            taps_c,
            shift_in,
            rate_in,
            segment,
            MDIM,
            GROUP,
        )

    (scanned_part, inner_conv), mixer_back = jax.vjp(
        mixer_piece,
        inner_pre,
        input_pre,
        read_pre,
        step_pre,
        taps_inner.astype(jnp.float32),
        taps_input_half,
        taps_read_half,
        step_bias.astype(jnp.float32),
        log_rate.astype(jnp.float32),
    )
    scanned = lax.psum(scanned_part, STATE)
    skip_full = jnp.repeat(skip_gain.astype(jnp.float32), MDIM)[None, :]
    combined = scanned + skip_full * inner_conv
    gate_act = jax.nn.silu(gate_pre)
    united = combined * gate_act
    squares = lax.psum(jnp.sum(united * united, 1), HEAD)
    row_scale = lax.rsqrt(squares / DIN + epsilon)[:, None]
    gated_gain = gain_gated.astype(jnp.float32)[None, :]
    united_own = lax.dynamic_slice_in_dim(united, own_start, row_count, 0)
    scale_own = lax.dynamic_slice_in_dim(row_scale, own_start, row_count, 0)
    gated_own = (united_own * scale_own * gated_gain).astype(jnp.bfloat16)
    mixed_own = lax.psum(plain_dot(gated_own, output_main), HEAD)
    mixed = lax.all_gather(mixed_own, STATE, axis=0, tiled=True)
    layer_out = (second_all + full_valid * mixed).astype(jnp.bfloat16)
    upstream = cotangent.astype(jnp.float32)
    mix_grad = (full_valid * upstream).astype(jnp.bfloat16)
    mix_grad_own = lax.dynamic_slice_in_dim(mix_grad, own_start, row_count, 0)
    grad_output_main = left_dot(gated_own, mix_grad_own)
    gated_grad = right_dot(mix_grad, output_main)
    row_total = jnp.sum(mix_grad.astype(jnp.float32) * mixed, 1)[:, None] / row_scale
    grad_gated_gain = jnp.sum(gated_grad * united * row_scale * own_mask, 0)
    united_grad = (
        row_scale * gated_gain * gated_grad
        - united * row_scale * row_scale * row_scale * row_total / DIN
    )
    combined_grad = united_grad * gate_act
    sigmoid_gate = jax.nn.sigmoid(gate_pre)
    gate_grad = (
        united_grad * combined * sigmoid_gate * (1.0 + gate_pre * (1.0 - sigmoid_gate)) * own_mask
    )
    mixer_heads = step_pre.shape[1]
    grad_skip = jnp.sum(
        (combined_grad * inner_conv * own_mask).reshape(length, mixer_heads, MDIM), (0, 2)
    )
    conv_extra = skip_full * combined_grad * own_mask
    (
        inner_grad,
        input_grad,
        read_grad,
        step_grad,
        grad_taps_x,
        grad_taps_b,
        grad_taps_c,
        grad_shift,
        grad_rate,
    ) = mixer_back((combined_grad, conv_extra))
    mixer_part = (
        exact_right(inner_grad, inner_main)
        + exact_right(gate_grad, gate_main)
        + exact_right(step_grad, step_main)
        + exact_right(input_grad, input_half)
        + exact_right(read_grad, read_half)
    )
    grad_inner_main = exact_left(mixer_normed, inner_grad)
    grad_gate_main = exact_left(mixer_normed, gate_grad)
    grad_step_main = exact_left(mixer_normed, step_grad)
    grad_input_half = exact_left(mixer_normed, input_grad)
    grad_read_half = exact_left(mixer_normed, read_grad)
    mixer_rows_own = lax.psum_scatter(mixer_part, STATE, scatter_dimension=0, tiled=True)
    mixer_own = lax.psum(mixer_rows_own, HEAD)
    unused_norm, second_back = jax.vjp(rms_norm, second, mixer_gain_f)
    second_norm_grad, grad_mixer_gain = second_back(mixer_own)
    upstream_own = lax.dynamic_slice_in_dim(upstream, own_start, row_count, 0)
    second_grad = upstream_own + second_norm_grad
    mlp_grad = (own_valid * second_grad).astype(jnp.bfloat16)
    grad_mlp_proj = left_dot(activated, mlp_grad)
    activated_grad = right_dot(mlp_grad, mlp_proj)
    unused_gelu, gelu_back = jax.vjp(
        lambda preact: jax.nn.gelu(preact, approximate=False), hidden_pre
    )
    hidden_grad = gelu_back(activated_grad)[0].astype(jnp.bfloat16)
    grad_mlp_main = left_dot(mlp_normed, hidden_grad)
    grad_mlp_upper = left_dot(mlp_red, hidden_grad)
    mlp_middle = right_dot(hidden_grad, mlp_upper)
    mlp_part = right_dot(hidden_grad, mlp_main)
    mlp_sum, middle_sum = lax.psum((mlp_part, mlp_middle), HEAD)
    middle_low = middle_sum.astype(jnp.bfloat16)
    mlp_normed_grad = mlp_sum + right_dot(middle_low, mlp_down)
    grad_mlp_down = left_dot(mlp_normed, middle_low)
    unused_first, first_back = jax.vjp(rms_norm, first, mlp_gain_f)
    first_norm_grad, grad_mlp_gain = first_back(mlp_normed_grad)
    first_grad = second_grad + first_norm_grad
    branch_grad = (own_valid * first_grad).astype(jnp.bfloat16)
    grad_attn_proj = left_dot(attended, branch_grad)
    attended_grad = right_dot(branch_grad, attn_proj).reshape(row_count, head_count, HDIM)
    probs_back = head_probs(queries, keys_all, allowed)
    score_scale = HDIM ** (-0.5)
    out_low = attended_grad.astype(jnp.bfloat16)
    prob_grad = jnp.einsum("thd,shd->hts", out_low, values_all, preferred_element_type=jnp.float32)
    score_grad = probs_back * (prob_grad - jnp.sum(probs_back * prob_grad, -1, keepdims=True))
    score_low = score_grad.astype(jnp.bfloat16)
    query_back = (
        jnp.einsum("hts,shd->thd", score_low, keys_all, preferred_element_type=jnp.float32)
        * score_scale
    )
    keys_back = (
        jnp.einsum("hts,thd->shd", score_low, queries, preferred_element_type=jnp.float32)
        * score_scale
    )
    values_back = jnp.einsum(
        "hts,thd->shd", probs_back.astype(jnp.bfloat16), out_low, preferred_element_type=jnp.float32
    )
    keys_grad_own, values_grad_own = (
        lax.psum_scatter(keys_back, STATE, scatter_dimension=0, tiled=True),
        lax.psum_scatter(values_back, STATE, scatter_dimension=0, tiled=True),
    )
    query_grad = (
        rotate(query_back, -own_position).reshape(row_count, head_count * HDIM).astype(jnp.bfloat16)
    )
    key_grad = (
        rotate(keys_grad_own, -own_position)
        .reshape(row_count, head_count * HDIM)
        .astype(jnp.bfloat16)
    )
    value_grad = values_grad_own.reshape(row_count, head_count * HDIM).astype(jnp.bfloat16)
    grad_query_main = left_dot(normed, query_grad)
    grad_key_main = left_dot(normed, key_grad)
    grad_value_main = left_dot(normed, value_grad)
    grad_query_upper = left_dot(query_red, query_grad)
    grad_key_upper = left_dot(key_red, key_grad)
    grad_value_upper = left_dot(value_red, value_grad)
    query_middle = right_dot(query_grad, query_upper)
    key_middle = right_dot(key_grad, key_upper)
    value_middle = right_dot(value_grad, value_upper)
    normed_part = (
        right_dot(query_grad, query_main)
        + right_dot(key_grad, key_main)
        + right_dot(value_grad, value_main)
    )
    normed_sum, query_msum, key_msum, value_msum = lax.psum(
        (normed_part, query_middle, key_middle, value_middle), HEAD
    )
    query_low = query_msum.astype(jnp.bfloat16)
    key_low = key_msum.astype(jnp.bfloat16)
    value_low = value_msum.astype(jnp.bfloat16)
    normed_grad = (
        normed_sum
        + right_dot(query_low, query_down)
        + right_dot(key_low, key_down)
        + right_dot(value_low, value_down)
    )
    grad_query_down = left_dot(normed, query_low)
    grad_key_down = left_dot(normed, key_low)
    grad_value_down = left_dot(normed, value_low)
    unused_joined, joined_back = jax.vjp(rms_norm, joined, attn_gain_f)
    joined_grad, grad_attn_gain = joined_back(normed_grad)
    grad_hidden = (first_grad + joined_grad[:, :model_width]).astype(jnp.bfloat16)
    grad_embedding = joined_grad[:, model_width:].astype(jnp.bfloat16)
    scattered = (
        lax.psum_scatter(grad_attn_gain, ZED, scatter_dimension=0, tiled=True),
        lax.psum_scatter(grad_query_main, ZED, scatter_dimension=0, tiled=True),
        lax.psum_scatter(grad_key_main, ZED, scatter_dimension=0, tiled=True),
        lax.psum_scatter(grad_value_main, ZED, scatter_dimension=0, tiled=True),
        lax.psum_scatter(grad_query_down, ZED, scatter_dimension=0, tiled=True),
        lax.psum_scatter(grad_key_down, ZED, scatter_dimension=0, tiled=True),
        lax.psum_scatter(grad_value_down, ZED, scatter_dimension=0, tiled=True),
        lax.psum_scatter(grad_query_upper, ZED, scatter_dimension=0, tiled=True),
        lax.psum_scatter(grad_key_upper, ZED, scatter_dimension=0, tiled=True),
        lax.psum_scatter(grad_value_upper, ZED, scatter_dimension=0, tiled=True),
        lax.psum_scatter(grad_attn_proj, ZED, scatter_dimension=1, tiled=True),
        lax.psum_scatter(grad_mlp_gain, ZED, scatter_dimension=0, tiled=True),
        lax.psum_scatter(grad_mlp_main, ZED, scatter_dimension=0, tiled=True),
        lax.psum_scatter(grad_mlp_down, ZED, scatter_dimension=0, tiled=True),
        lax.psum_scatter(grad_mlp_upper, ZED, scatter_dimension=0, tiled=True),
        lax.psum_scatter(grad_mlp_proj, ZED, scatter_dimension=1, tiled=True),
        lax.psum_scatter(grad_mixer_gain, ZED, scatter_dimension=0, tiled=True),
        lax.psum_scatter(grad_inner_main, ZED, scatter_dimension=0, tiled=True),
        lax.psum_scatter(grad_gate_main, ZED, scatter_dimension=0, tiled=True),
        lax.psum_scatter(grad_step_main, ZED, scatter_dimension=0, tiled=True),
        lax.psum_scatter(grad_output_main, ZED, scatter_dimension=1, tiled=True),
    )
    first_head = (head_index == 0).astype(jnp.float32)
    square_sum = jnp.zeros((), jnp.float32)
    for index in [1, 2, 3, 7, 8, 9, 10, 12, 14, 15]:
        square_sum = square_sum + jnp.sum(scattered[index] * scattered[index])
    for index in [4, 5, 6, 13]:
        square_sum = square_sum + first_head * jnp.sum(scattered[index] * scattered[index])
    head_params = jnp.stack([grad_shift, grad_rate, grad_skip], 0)
    totals = lax.psum(
        (
            square_sum,
            place_slice(grad_gated_gain, head_index, head_parts, 0),
            place_slice(grad_taps_x, head_index, head_parts, 1),
            place_slice(head_params, head_index, head_parts, 1),
            place_slice(grad_input_half, state_index, state_parts, 1),
            place_slice(grad_read_half, state_index, state_parts, 1),
            place_slice(grad_taps_b, state_index, state_parts, 1),
            place_slice(grad_taps_c, state_index, state_parts, 1),
        ),
        EVERY,
    )
    (
        square_total,
        gated_full,
        taps_full,
        heads_full,
        input_full,
        read_full,
        taps_input_full,
        taps_read_full,
    ) = totals
    head_width = gain_gated.shape[0]
    tap_width = taps_inner.shape[1]
    param_width = step_bias.shape[0]
    heads_own = take_slice(heads_full, head_index, param_width, 1)
    return (
        layer_out,
        grad_hidden,
        grad_embedding,
        scattered[0],
        scattered[1],
        scattered[2],
        scattered[3],
        scattered[4],
        scattered[5],
        scattered[6],
        scattered[7],
        scattered[8],
        scattered[9],
        scattered[10],
        scattered[11],
        scattered[12],
        scattered[13],
        scattered[14],
        scattered[15],
        scattered[16],
        scattered[17],
        scattered[18],
        scattered[19],
        input_full,
        read_full,
        take_slice(taps_full, head_index, tap_width, 1),
        taps_input_full,
        taps_read_full,
        heads_own[0],
        heads_own[1],
        heads_own[2],
        take_slice(gated_full, head_index, head_width, 0),
        scattered[20],
        jnp.sqrt(square_total),
    )


low = jnp.bfloat16
full = jnp.float32


def head_masks():
    count = lax.axis_size(HEAD)
    masks = [1 << bit for bit in range(count.bit_length() - 1)]
    return masks[:1] + masks[1:], masks[:1] + masks[1:][::-1]


def head_swap(value, mask):
    count = lax.axis_size(HEAD)
    return lax.ppermute(value, HEAD, [(i, i ^ mask) for i in range(count)])


def state_swap(value):
    return lax.ppermute(value, STATE, [(0, 1), (1, 0)])


def dp_swap(value):
    return lax.ppermute(value, DP, [(0, 1), (1, 0)])


def state_forward(value):
    return lax.ppermute(value, STATE, [(0, 1)])


def state_backward(value):
    return lax.ppermute(value, STATE, [(1, 0)])


def bit_of(mask):
    return (lax.axis_index(HEAD) // mask) % 2


def chunk_of(masks):
    chunk = 0
    for mask in masks:
        chunk = chunk * 2 + bit_of(mask)
    return chunk


def sum_rows(value, masks, axis):
    for mask in masks:
        bit = bit_of(mask)
        half = value.shape[axis] // 2
        away = lax.dynamic_slice_in_dim(value, (1 - bit) * half, half, axis).astype(low)
        kept = lax.dynamic_slice_in_dim(value, bit * half, half, axis)
        value = kept.astype(full) + head_swap(away, mask).astype(full)
    return value


def gather_rows(value, masks, axis):
    for mask in masks[::-1]:
        bit = bit_of(mask)
        got = head_swap(value, mask)
        value = jnp.concatenate(
            [jnp.where(bit == 1, got, value), jnp.where(bit == 1, value, got)], axis
        )
    return value


def sum_row16(value, masks):
    state = lax.axis_index(STATE)
    value = sum_rows(value, masks, 1)
    away = lax.dynamic_index_in_dim(value, 1 - state, 0, False).astype(low)
    kept = lax.dynamic_index_in_dim(value, state, 0, False)
    return kept + state_swap(away).astype(full)


def gather_row16(value, masks):
    state = lax.axis_index(STATE)
    got = state_swap(value)
    both = jnp.stack([jnp.where(state == 0, value, got), jnp.where(state == 0, got, value)], 0)
    return gather_rows(both, masks, 1)


def pick_state(pair, index):
    return jnp.where(index == 0, pair[0], pair[1])


def weight_pieces(shard, axis):
    state = lax.axis_index(STATE)
    dp = lax.axis_index(DP)
    half = shard.shape[axis] // 2
    mine = lax.dynamic_slice_in_dim(shard, state * half, half, axis)
    got = state_swap(lax.dynamic_slice_in_dim(shard, (1 - state) * half, half, axis))
    far_mine = dp_swap(mine)
    far_got = dp_swap(got)
    near = [jnp.where(state == 0, mine, got), jnp.where(state == 0, got, mine)]
    far = [jnp.where(state == 0, far_mine, far_got), jnp.where(state == 0, far_got, far_mine)]
    lower = [jnp.where(dp == 0, a, b) for a, b in zip(near, far)]
    upper = [jnp.where(dp == 0, b, a) for a, b in zip(near, far)]
    return jnp.concatenate(lower + upper, 1 - axis)


def grad_pieces(grad, axis):
    state = lax.axis_index(STATE)
    dp = lax.axis_index(DP)
    half = grad.shape[1 - axis] // 2
    away = lax.dynamic_slice_in_dim(grad, (1 - dp) * half, half, 1 - axis).astype(low)
    kept = lax.dynamic_slice_in_dim(grad, dp * half, half, 1 - axis)
    total = kept + dp_swap(away).astype(full)
    quarter = half // 2
    away = lax.dynamic_slice_in_dim(total, (1 - state) * quarter, quarter, 1 - axis).astype(low)
    kept = lax.dynamic_slice_in_dim(total, state * quarter, quarter, 1 - axis)
    got = state_swap(away).astype(full)
    return jnp.concatenate(
        [jnp.where(state == 0, kept, got), jnp.where(state == 0, got, kept)], axis
    )


def norm_scale(values):
    return lax.rsqrt(jnp.mean(values * values, -1, keepdims=True) + epsilon)


def norm_back(values, gain, grad):
    scale = norm_scale(values)
    scaled = grad * gain
    inner = jnp.mean(scaled * values, -1, keepdims=True)
    return (
        scale * scaled - values * (scale * scale * scale * inner),
        jnp.sum(grad * values * scale, 0),
    )


def conv_edge(values, edge, taps, segment, edge_segment):
    reach = taps.shape[0] - 1
    rows = values.shape[0]
    joined = jnp.concatenate([edge, values], 0)
    segs = jnp.concatenate([edge_segment, segment], 0)
    total = taps[0][None, :] * values
    for offset in range(1, taps.shape[0]):
        lower = reach - offset
        same = (segs[lower : lower + rows] == segment).astype(values.dtype)[:, None]
        total = total + taps[offset][None, :] * joined[lower : lower + rows] * same
    return total


def vmem_limit(mebibytes):
    return pltpu.CompilerParams(vmem_limit_bytes=mebibytes * 1024 * 1024)


def dot_nt(left, right):
    return lax.dot_general(left, right, (((1,), (1,)), ((), ())), preferred_element_type=full)


def dot_tn(left, right):
    return lax.dot_general(left, right, (((0,), (0,)), ((), ())), preferred_element_type=full)


def dot_nn(left, right):
    return lax.dot_general(left, right, (((1,), (0,)), ((), ())), preferred_element_type=full)


def dot_exact(left, right):
    return jnp.dot(left, right, preferred_element_type=full, precision=highest)


ROWS_Q = 256
ROWS_K = 512


def attend_kernel(low_ref, q_ref, k_ref, v_ref, seg_col, seg_row, out_ref, lse_ref):
    index = pl.program_id(1)
    scale = q_ref.shape[1] ** (-0.5)
    query = q_ref[...]
    own = seg_col[...]
    place = index * ROWS_Q + lax.broadcasted_iota(jnp.int32, (ROWS_Q, ROWS_K), 0)

    def step(block, carry):
        top, total, acc = carry
        span = pl.ds(pl.multiple_of(block * ROWS_K, ROWS_K), ROWS_K)
        scores = dot_nt(query, k_ref[span, :]) * scale
        other = block * ROWS_K + lax.broadcasted_iota(jnp.int32, (ROWS_Q, ROWS_K), 1)
        scores = jnp.where((own == seg_row[:, span]) & (other <= place), scores, -1e30)
        higher = jnp.maximum(top, jnp.max(scores, -1, keepdims=True))
        weights = jnp.exp(scores - higher)
        fade = jnp.exp(top - higher)
        total = total * fade + jnp.sum(weights, -1, keepdims=True)
        acc = acc * fade + dot_nn(weights.astype(low), v_ref[span, :])
        return higher, total, acc

    start = (
        jnp.full((ROWS_Q, 1), -1e30, full),
        jnp.zeros((ROWS_Q, 1), full),
        jnp.zeros((ROWS_Q, v_ref.shape[1]), full),
    )
    stop = (index * ROWS_Q + ROWS_Q + ROWS_K - 1) // ROWS_K
    top, total, acc = lax.fori_loop(low_ref[index], stop, step, start)
    out_ref[...] = (acc / total).astype(low)
    lse = jnp.broadcast_to(top + jnp.log(total), (ROWS_Q, 128))
    lse_ref[...] = lse.T[0:1, :][None]


def half_block(index, blocks):
    per_state = blocks // 2
    per_half = per_state // 2
    inside = index % per_state
    return inside // per_half * per_state + index // per_state * per_half + inside % per_half


def attend(queries, keys, values, segment, lows):
    length, columns = queries.shape
    heads = columns // HDIM
    blocks = length // ROWS_Q
    whole = pl.BlockSpec((length, HDIM), lambda h, i, *_: (0, h))
    block = pl.BlockSpec((ROWS_Q, HDIM), lambda h, i, *_: (i, h))
    placed = pl.BlockSpec((ROWS_Q, HDIM), lambda h, i, *_: (half_block(i, blocks), h))
    return pl.pallas_call(
        attend_kernel,
        grid_spec=pltpu.PrefetchScalarGridSpec(
            num_scalar_prefetch=1,
            grid=(heads, length // ROWS_Q),
            in_specs=[
                block,
                whole,
                whole,
                pl.BlockSpec((ROWS_Q, 1), lambda h, i, *_: (i, 0)),
                pl.BlockSpec((1, length), lambda h, i, *_: (0, 0)),
            ],
            out_specs=[placed, pl.BlockSpec((1, 1, ROWS_Q), lambda h, i, *_: (h, 0, i))],
        ),
        out_shape=[
            jax.ShapeDtypeStruct((length, columns), low),
            jax.ShapeDtypeStruct((heads, 1, length), full),
        ],
        compiler_params=vmem_limit(40),
        cost_estimate=pl.CostEstimate(
            flops=22 * length * length * columns, bytes_accessed=8 * length * columns,
            transcendentals=0,
        ),
    )(lows, queries, keys, values, segment[:, None], segment[None, :])


def attend_back_kernel(
    low_ref, q_ref, k_ref, v_ref, do_ref, o_ref, lse_ref, seg_col, seg_row, dq_ref, dk_ref, dv_ref
):
    index = pl.program_id(1)
    scale = q_ref.shape[1] ** (-0.5)
    query = q_ref[...]
    grad = do_ref[...]
    own = seg_row[...]
    lse = lse_ref[0]
    ones = jnp.ones((8, HDIM), full)
    delta = lax.dot_general(
        ones,
        grad.astype(full) * o_ref[...].astype(full),
        (((1,), (1,)), ((), ())),
        precision=highest,
        preferred_element_type=full,
    )[0:1, :]
    place = index * ROWS_Q + lax.broadcasted_iota(jnp.int32, (ROWS_K, ROWS_Q), 1)

    @pl.when(index == 0)
    def clear():
        dk_ref[...] = jnp.zeros_like(dk_ref)
        dv_ref[...] = jnp.zeros_like(dv_ref)

    def step(block, total):
        span = pl.ds(pl.multiple_of(block * ROWS_K, ROWS_K), ROWS_K)
        key = k_ref[span, :]
        scores = dot_nt(key, query) * scale
        other = block * ROWS_K + lax.broadcasted_iota(jnp.int32, (ROWS_K, ROWS_Q), 0)
        counted = (seg_col[span, :] == own) & (other <= place)
        probs = jnp.exp(jnp.where(counted, scores - lse, -1e30))
        dv_ref[span, :] += dot_nn(probs.astype(low), grad)
        slope = probs * (dot_nt(v_ref[span, :], grad) - delta)
        slope = slope.astype(low)
        dk_ref[span, :] += dot_nn(slope, query) * scale
        return total + dot_tn(slope, key)

    stop = (index * ROWS_Q + ROWS_Q + ROWS_K - 1) // ROWS_K
    total = lax.fori_loop(low_ref[index], stop, step, jnp.zeros((ROWS_Q, HDIM), full))
    dq_ref[...] = total * scale


def attend_back(queries, keys, values, grads, outs, lse, segment, lows):
    length, columns = queries.shape
    heads = columns // HDIM
    blocks = length // ROWS_Q
    whole = pl.BlockSpec((length, HDIM), lambda h, i, *_: (0, h))
    block = pl.BlockSpec((ROWS_Q, HDIM), lambda h, i, *_: (i, h))
    placed = pl.BlockSpec((ROWS_Q, HDIM), lambda h, i, *_: (half_block(i, blocks), h))
    line = pl.BlockSpec((1, 1, ROWS_Q), lambda h, i, *_: (h, 0, i))
    shape = jax.ShapeDtypeStruct((length, columns), full)
    return pl.pallas_call(
        attend_back_kernel,
        grid_spec=pltpu.PrefetchScalarGridSpec(
            num_scalar_prefetch=1,
            grid=(heads, length // ROWS_Q),
            in_specs=[
                block,
                whole,
                whole,
                placed,
                placed,
                line,
                pl.BlockSpec((length, 1), lambda h, i, *_: (0, 0)),
                pl.BlockSpec((1, ROWS_Q), lambda h, i, *_: (0, i)),
            ],
            out_specs=[block, whole, whole],
        ),
        out_shape=[shape, shape, shape],
        compiler_params=vmem_limit(40),
        cost_estimate=pl.CostEstimate(
            flops=30 * length * length * columns, bytes_accessed=20 * length * columns,
            transcendentals=0,
        ),
    )(lows, queries, keys, values, grads, outs, lse, segment[:, None], segment[None, :])


def rope_kernel(state_ref, own_ref, other_ref, cos_ref, sin_ref, q_ref, k_ref, v_ref):
    per_state = pl.num_programs(0) // 2
    own = pl.program_id(0) // per_state == state_ref[0]
    columns = q_ref.shape[1]
    for index, out in enumerate((q_ref, k_ref, v_ref)):
        for start in range(0, columns, HDIM):
            lanes = slice(index * columns + start, index * columns + start + HDIM)
            value = jnp.where(own, own_ref[:, lanes], other_ref[:, lanes])
            if index < 2:
                value = value * cos_ref[...] + pltpu.roll(value, HDIM // 2, 1) * sin_ref[...]
            out[:, start : start + HDIM] = value.astype(low)


def rope(state, own, other, cosine, sine):
    length = cosine.shape[0]
    columns = own.shape[1] // 3
    per_state = length // ROWS_Q // 2
    part = pl.BlockSpec((ROWS_Q, own.shape[1]), lambda i, *_: (i % per_state, 0))
    angle = pl.BlockSpec((ROWS_Q, HDIM), lambda i, *_: (i, 0))
    out = pl.BlockSpec((ROWS_Q, columns), lambda i, *_: (i, 0))
    return pl.pallas_call(
        rope_kernel,
        grid_spec=pltpu.PrefetchScalarGridSpec(
            num_scalar_prefetch=1,
            grid=(length // ROWS_Q,),
            in_specs=[part, part, angle, angle],
            out_specs=[out] * 3,
        ),
        out_shape=[jax.ShapeDtypeStruct((length, columns), low)] * 3,
        compiler_params=vmem_limit(32),
        cost_estimate=pl.CostEstimate(
            flops=12 * length * columns, bytes_accessed=36 * length * columns, transcendentals=0
        ),
    )(state[None], own, other, cosine, sine)


def rope_back_kernel(q_ref, k_ref, v_ref, cos_ref, sin_ref, out_ref):
    columns = q_ref.shape[1]
    for index, part in enumerate((q_ref, k_ref, v_ref)):
        for start in range(0, columns, HDIM):
            value = part[:, start : start + HDIM]
            if index < 2:
                value = value * cos_ref[...] - pltpu.roll(value, HDIM // 2, 1) * sin_ref[...]
            lanes = slice(index * columns + start, index * columns + start + HDIM)
            out_ref[:, lanes] = value.astype(low)


def rope_back(query, key, value, cosine, sine):
    length, columns = query.shape
    blocks = length // ROWS_Q
    part = pl.BlockSpec((ROWS_Q, columns), lambda i: (i, 0))
    angle = pl.BlockSpec((ROWS_Q, HDIM), lambda i: (i, 0))
    return pl.pallas_call(
        rope_back_kernel,
        grid=(blocks,),
        in_specs=[part, part, part, angle, angle],
        out_specs=pl.BlockSpec((ROWS_Q, 3 * columns), lambda i: (half_block(i, blocks), 0)),
        out_shape=jax.ShapeDtypeStruct((length, 3 * columns), low),
        compiler_params=vmem_limit(32),
        cost_estimate=pl.CostEstimate(
            flops=12 * length * columns, bytes_accessed=24 * length * columns, transcendentals=0
        ),
    )(query, key, value, cosine, sine)


def hold_kernel(*refs):
    pass


def hold(value, *after):
    anywhere = pl.BlockSpec(memory_space=pl.ANY)
    return pl.pallas_call(
        hold_kernel,
        in_specs=[anywhere] * (1 + len(after)),
        out_specs=anywhere,
        out_shape=jax.ShapeDtypeStruct(value.shape, value.dtype),
        input_output_aliases={0: 0},
        cost_estimate=pl.CostEstimate(flops=0, bytes_accessed=0, transcendentals=0),
    )(value, *after)


def first_blocks(segment):
    length = segment.shape[0]
    heads = segment[::ROWS_Q]
    starts = jnp.sum((segment[None, :] < heads[:, None]).astype(jnp.int32), 1)
    return starts // ROWS_K


def pair_lanes(left, right):
    lane = lax.broadcasted_iota(jnp.int32, (1, 2 * MDIM), 1)
    return jnp.where(lane < MDIM, left, right)


def block_decay(dt_ref, dt_row_ref, rate_ref, rate_col_ref):
    rows = lax.broadcasted_iota(jnp.int32, (GROUP, GROUP), 0)
    cols = lax.broadcasted_iota(jnp.int32, (GROUP, GROUP), 1)
    cumul = dot_exact((cols <= rows).astype(full), dt_ref[...] * rate_ref[...])
    cumul_row = dot_exact(dt_row_ref[...] * rate_col_ref[...], (rows <= cols).astype(full))
    return cumul, cumul_row, rows, cols


def edge_flags(ends_ref, index, seg_col):
    before = ends_ref[index]
    last = ends_ref[index + 1]
    carried = (seg_col[...] == before).astype(full)
    reach = (seg_col[...] == last).astype(full)
    keep = (before == last).astype(full)
    return carried, reach, keep


def pair_columns(values, pair):
    return pair_lanes(values[:, 2 * pair : 2 * pair + 1], values[:, 2 * pair + 1 : 2 * pair + 2])


def step_state(state, pair, scaled, cumul, reach, keep, vec_low):
    column = pair_columns(cumul, pair)
    end = column[GROUP - 1 : GROUP, :]
    weight = jnp.exp(end - column) * reach
    return state * (jnp.exp(end) * keep) + dot_tn(vec_low, (scaled * weight).astype(low)), weight


def scan_end_kernel(
    ends_ref, x_ref, dt_ref, dt_row_ref, rate_ref, rate_col_ref, b_ref, seg_col, out_ref
):
    index = pl.program_id(0)
    cumul, unused_row, unused_a, unused_b = block_decay(dt_ref, dt_row_ref, rate_ref, rate_col_ref)
    unused_c, reach, keep = edge_flags(ends_ref, index, seg_col)
    vec_low = b_ref[...].astype(low)

    @pl.when(index == 0)
    def clear():
        out_ref[...] = jnp.zeros_like(out_ref)

    for pair in range(dt_ref.shape[1] // 2):
        lanes = slice(pair * 2 * MDIM, (pair + 1) * 2 * MDIM)
        scaled = x_ref[:, lanes] * pair_columns(dt_ref[...], pair)
        out_ref[:, lanes], unused_d = step_state(
            out_ref[:, lanes], pair, scaled, cumul, reach, keep, vec_low
        )


def scan_kernel(
    ends_ref,
    x_ref,
    dt_ref,
    dt_row_ref,
    rate_ref,
    rate_col_ref,
    b_ref,
    c_ref,
    seg_col,
    seg_row,
    first_ref,
    out_ref,
    states_ref,
    state,
):
    index = pl.program_id(0)
    cumul, cumul_row, rows, cols = block_decay(dt_ref, dt_row_ref, rate_ref, rate_col_ref)
    carried, reach, keep = edge_flags(ends_ref, index, seg_col)
    vec_low = b_ref[...].astype(low)
    read_low = c_ref[...].astype(low)
    allowed = (seg_col[...] == seg_row[...]) & (cols <= rows)
    inner = jnp.where(allowed, dot_nt(read_low, vec_low), 0.0)

    @pl.when(index == 0)
    def begin():
        state[...] = first_ref[...]

    states_ref[0] = state[...]
    for pair in range(dt_ref.shape[1] // 2):
        lanes = slice(pair * 2 * MDIM, (pair + 1) * 2 * MDIM)
        scaled = x_ref[:, lanes] * pair_columns(dt_ref[...], pair)
        scaled_low = scaled.astype(low)
        parts = []
        for head in (2 * pair, 2 * pair + 1):
            gaps = cumul[:, head : head + 1] - cumul_row[head : head + 1, :]
            mixed = inner * jnp.exp(jnp.minimum(gaps, 0.0))
            parts.append(dot_nn(mixed.astype(low), scaled_low))
        entry = jnp.exp(pair_columns(cumul, pair)) * carried
        held = state[:, lanes]
        out_ref[:, lanes] = pair_lanes(*parts) + dot_nn(read_low, held.astype(low)) * entry
        state[:, lanes], unused = step_state(
            held, pair, scaled, cumul, reach, keep, vec_low
        )


def scan_start_grad_kernel(
    ends_ref, dt_ref, dt_row_ref, rate_ref, rate_col_ref, c_ref, seg_col, dy_ref, out_ref
):
    index = pl.num_programs(0) - 1 - pl.program_id(0)
    cumul, unused_row, unused_a, unused_b = block_decay(dt_ref, dt_row_ref, rate_ref, rate_col_ref)
    carried, unused_c, keep = edge_flags(ends_ref, index, seg_col)
    read_low = c_ref[...].astype(low)

    @pl.when(pl.program_id(0) == 0)
    def clear():
        out_ref[...] = jnp.zeros_like(out_ref)

    for pair in range(dt_ref.shape[1] // 2):
        lanes = slice(pair * 2 * MDIM, (pair + 1) * 2 * MDIM)
        column = pair_columns(cumul, pair)
        retain = jnp.exp(column[GROUP - 1 : GROUP, :]) * keep
        entry = jnp.exp(column) * carried
        out_ref[:, lanes] = out_ref[:, lanes] * retain + dot_tn(
            read_low, (dy_ref[:, lanes] * entry).astype(low)
        )


def scan_back_kernel(
    ends_ref,
    x_ref,
    dt_ref,
    dt_row_ref,
    rate_ref,
    rate_col_ref,
    b_ref,
    c_ref,
    seg_col,
    seg_row,
    dy_ref,
    states_ref,
    last_ref,
    dx_ref,
    ddt_ref,
    dlog_ref,
    dlog_row_ref,
    db_ref,
    dc_ref,
    state_grad,
    inner_grad,
):
    index = pl.num_programs(0) - 1 - pl.program_id(0)
    heads = dt_ref.shape[1]
    cumul, cumul_row, rows, cols = block_decay(dt_ref, dt_row_ref, rate_ref, rate_col_ref)
    carried, reach, keep = edge_flags(ends_ref, index, seg_col)
    vec_low = b_ref[...].astype(low)
    read_low = c_ref[...].astype(low)
    allowed = (seg_col[...] == seg_row[...]) & (cols <= rows)
    inner = jnp.where(allowed, dot_nt(read_low, vec_low), 0.0)
    head_lane = lax.broadcasted_iota(jnp.int32, (GROUP, heads), 1)
    head_row = lax.broadcasted_iota(jnp.int32, (heads, GROUP), 0)
    last_row = lax.broadcasted_iota(jnp.int32, (GROUP, 1), 0) == GROUP - 1
    lane = lax.broadcasted_iota(jnp.int32, (1, 2 * MDIM), 1)

    @pl.when(pl.program_id(0) == 0)
    def begin():
        state_grad[...] = last_ref[...]

    inner_grad[...] = jnp.zeros_like(inner_grad)
    decay_grad = jnp.zeros((GROUP, heads), full)
    decay_row = jnp.zeros((heads, GROUP), full)
    step_grad = jnp.zeros((GROUP, heads), full)
    vec_grad = jnp.zeros(b_ref.shape, full)
    read_grad = jnp.zeros(c_ref.shape, full)
    for pair in range(heads // 2):
        lanes = slice(pair * 2 * MDIM, (pair + 1) * 2 * MDIM)
        values = x_ref[:, lanes]
        steps = pair_columns(dt_ref[...], pair)
        scaled = values * steps
        scaled_low = scaled.astype(low)
        grad = dy_ref[:, lanes]
        grad_low = grad.astype(low)
        held = states_ref[0, :, lanes]
        held_low = held.astype(low)
        later = state_grad[:, lanes]
        later_low = later.astype(low)
        column = pair_columns(cumul, pair)
        end = column[GROUP - 1 : GROUP, :]
        weight = jnp.exp(end - column) * reach
        retain = jnp.exp(end) * keep
        entry = jnp.exp(column) * carried
        parts = []
        for side in range(2):
            head = 2 * pair + side
            gaps = cumul[:, head : head + 1] - cumul_row[head : head + 1, :]
            fading = jnp.where(allowed, jnp.exp(jnp.minimum(gaps, 0.0)), 0.0)
            mixed = inner * fading
            own_lanes = (lane < MDIM) == (side == 0)
            outer = dot_nt(jnp.where(own_lanes, grad, 0.0).astype(low), scaled_low)
            inner_grad[...] += outer * fading
            slope = outer * mixed
            decay_grad = jnp.where(
                head_lane == head, decay_grad + jnp.sum(slope, 1, keepdims=True), decay_grad
            )
            decay_row = jnp.where(
                head_row == head, jnp.sum(slope, 0, keepdims=True), decay_row
            )
            parts.append(dot_tn(mixed.astype(low), grad_low))
        weighted = scaled * weight
        entered = grad * entry
        entered_low = entered.astype(low)
        from_later = dot_nn(vec_low, later_low)
        scaled_grad = pair_lanes(*parts) + weight * from_later
        dx_ref[:, lanes] = scaled_grad * steps
        read_grad += dot_nt(entered_low, held_low)
        vec_grad += dot_nt(weighted.astype(low), later_low)
        fresh = weighted * from_later
        flow = entered * dot_nn(read_low, held_low) - fresh
        finish = jnp.sum(fresh, 0, keepdims=True) + retain * jnp.sum(later * held, 0, keepdims=True)
        steps_part = scaled_grad * values
        for side in range(2):
            head = 2 * pair + side
            own_lanes = (lane < MDIM) == (side == 0)
            total = jnp.sum(jnp.where(own_lanes, flow, 0.0), 1, keepdims=True)
            ending = jnp.sum(jnp.where(own_lanes, finish, 0.0), 1, keepdims=True)
            total = total + jnp.where(last_row, ending, 0.0)
            decay_grad = jnp.where(head_lane == head, decay_grad + total, decay_grad)
            step_grad = jnp.where(
                head_lane == head,
                jnp.sum(jnp.where(own_lanes, steps_part, 0.0), 1, keepdims=True),
                step_grad,
            )
        state_grad[:, lanes] = later * retain + dot_tn(read_low, entered_low)
    inner_low = inner_grad[...].astype(low)
    ddt_ref[...] = step_grad
    dlog_ref[...] = dot_exact((cols >= rows).astype(full), decay_grad)
    dlog_row_ref[...] = dot_exact(decay_row, (rows >= cols).astype(full))
    dc_ref[...] = read_grad + dot_nn(inner_low, vec_low)
    db_ref[...] = vec_grad + dot_tn(inner_low, read_low)


def scan_specs(heads, channels, states, reverse, count):
    def at(i):
        return count - 1 - i if reverse else i

    tall = lambda columns: pl.BlockSpec((GROUP, columns), lambda i, *_: (at(i), 0))
    flat = lambda rows: pl.BlockSpec((rows, GROUP), lambda i, *_: (0, at(i)))
    same = lambda rows, columns: pl.BlockSpec((rows, columns), lambda i, *_: (0, 0))
    return tall, flat, same, pl.BlockSpec((1, states, channels), lambda i, *_: (at(i), 0, 0))


def scan_call(kernel, reverse, ends, inputs, kinds, outs, out_kinds, scratch, dims, flops):
    heads, channels, states, count = dims
    tall, flat, same, cube = scan_specs(heads, channels, states, reverse, count)

    def spec(kind, shape):
        if kind == 0:
            return tall(shape[1])
        if kind == 1:
            return flat(shape[0])
        return same(*shape) if kind == 2 else cube

    return pl.pallas_call(
        kernel,
        grid_spec=pltpu.PrefetchScalarGridSpec(
            num_scalar_prefetch=1,
            grid=(count,),
            in_specs=[spec(kind, value.shape) for kind, value in zip(kinds, inputs)],
            out_specs=[spec(kind, shape) for kind, shape in zip(out_kinds, outs)],
            scratch_shapes=scratch,
        ),
        out_shape=[jax.ShapeDtypeStruct(shape, full) for shape in outs],
        compiler_params=vmem_limit(40),
        cost_estimate=pl.CostEstimate(
            flops=flops, bytes_accessed=8 * count * GROUP * channels, transcendentals=0
        ),
    )(ends, *inputs)


class Scan:
    def __init__(self, x, dt, rate, b, c, segment, before):
        self.rows, self.heads = dt.shape
        self.channels, self.states = x.shape[1], b.shape[1]
        self.count = self.rows // GROUP
        self.dims = (self.heads, self.channels, self.states, self.count)
        self.ends = jnp.concatenate([before[None], segment[GROUP - 1 :: GROUP]])
        self.x, self.b, self.c = x, b, c
        self.decay = [dt, dt.T, rate[None, :], rate[:, None]]
        self.seg_col, self.seg_row = segment[:, None], segment[None, :]
        self.state_shape = (self.states, self.channels)

    def end(self):
        return scan_call(
            scan_end_kernel,
            False,
            self.ends,
            [self.x, *self.decay, self.b, self.seg_col],
            [0, 0, 1, 2, 2, 0, 0],
            [self.state_shape],
            [2],
            [],
            self.dims,
            160 * self.rows * self.channels * self.states,
        )[0]

    def forward(self, first):
        return scan_call(
            scan_kernel,
            False,
            self.ends,
            [self.x, *self.decay, self.b, self.c, self.seg_col, self.seg_row, first],
            [0, 0, 1, 2, 2, 0, 0, 0, 1, 2],
            [self.x.shape, (self.count,) + self.state_shape],
            [0, 3],
            [pltpu.VMEM(self.state_shape, full)],
            self.dims,
            56 * self.rows * self.channels * GROUP,
        )

    def start_grad(self, grad):
        return scan_call(
            scan_start_grad_kernel,
            True,
            self.ends,
            [*self.decay, self.c, self.seg_col, grad],
            [0, 1, 2, 2, 0, 0, 0],
            [self.state_shape],
            [2],
            [],
            self.dims,
            160 * self.rows * self.channels * self.states,
        )[0]

    def backward(self, grad, states, last):
        wide = (self.rows, self.heads)
        return scan_call(
            scan_back_kernel,
            True,
            self.ends,
            [
                self.x,
                *self.decay,
                self.b,
                self.c,
                self.seg_col,
                self.seg_row,
                grad,
                states,
                last,
            ],
            [0, 0, 1, 2, 2, 0, 0, 0, 1, 0, 3, 2],
            [self.x.shape, wide, wide, wide[::-1], self.b.shape, self.c.shape],
            [0, 0, 0, 1, 0, 0],
            [pltpu.VMEM(self.state_shape, full), pltpu.VMEM((GROUP, GROUP), full)],
            self.dims,
            144 * self.rows * self.channels * GROUP,
        )


def natural_quarters(relative):
    state = lax.axis_index(STATE)
    dp = lax.axis_index(DP)
    near = [jnp.where(state == 0, *relative[:2]), jnp.where(state == 0, *relative[1::-1])]
    far = [jnp.where(state == 0, *relative[2:]), jnp.where(state == 0, *relative[:1:-1])]
    return [jnp.where(dp == 0, a, b) for a, b in zip(near, far)] + [
        jnp.where(dp == 0, b, a) for a, b in zip(near, far)
    ]


def swap_quarters(value):
    quarter = value.shape[-1] // 4
    part = [value[..., i * quarter : (i + 1) * quarter] for i in range(4)]
    return jnp.concatenate([part[1], part[0], part[3], part[2]], -1)


def fast_device(
    hidden,
    embedding,
    cotangent,
    lengths,
    gain_attn,
    w_query,
    w_key,
    w_value,
    down_query,
    down_key,
    down_value,
    up_query,
    up_key,
    up_value,
    attn_output,
    gain_mlp,
    mlp_input,
    down_mlp,
    up_mlp,
    mlp_output,
    gain_mixer,
    proj_inner,
    proj_gate,
    proj_step,
    proj_input,
    proj_read,
    taps_inner,
    taps_input,
    taps_read,
    step_bias,
    log_rate,
    skip_gain,
    gain_gated,
    proj_output,
):
    rows = hidden.shape[0]
    length = cotangent.shape[0]
    width = hidden.shape[1]
    middle = rows // 2
    head_parts = lax.axis_size(HEAD)
    piece = middle // head_parts
    state = lax.axis_index(STATE)
    dp = lax.axis_index(DP)
    head = lax.axis_index(HEAD)
    place = dp * 2 + state
    own_start = state * rows
    orders = head_masks()
    offsets = [chunk_of(orders[0]) * piece, middle + chunk_of(orders[1]) * piece]

    heads_wide = w_query.shape[1]
    half_cols = heads_wide // 2

    def state_columns(values, index):
        return jnp.concatenate(
            [lax.dynamic_slice_in_dim(v, index * half_cols, half_cols, 1) for v in values], 1
        )

    rank = down_query.shape[1]
    part_a = down_query.shape[0] // head_parts
    part_m = down_mlp.shape[0] // head_parts
    split_a, split_m = gain_attn.shape[0], gain_mlp.shape[0]
    up_rows = up_query.shape[0]

    def small_pack(index):
        return jnp.concatenate(
            [
                jnp.concatenate([gain_attn, gain_mlp, gain_mixer]).reshape(-1, rank),
                lax.dynamic_slice_in_dim(down_query, head * part_a, part_a, 0),
                lax.dynamic_slice_in_dim(down_key, head * part_a, part_a, 0),
                lax.dynamic_slice_in_dim(down_value, head * part_a, part_a, 0),
                lax.dynamic_slice_in_dim(down_mlp, head * part_m, part_m, 0),
                up_mlp.reshape(-1, rank),
                proj_step.reshape(-1, rank),
                state_columns((up_query, up_key, up_value), index).reshape(-1, rank),
            ],
            0,
        )

    pack = jnp.stack([small_pack(state), state_swap(small_pack(1 - state))], 0)
    pack_far = dp_swap(pack)
    mine = hold(state_columns((w_query, w_key, w_value), state), pack_far)
    got = state_swap(hold(state_columns((w_query, w_key, w_value), 1 - state), pack))
    cutting = mine.shape[0] // 2
    far_mine = [dp_swap(mine[:cutting]), dp_swap(mine[cutting:])]
    far_got = [dp_swap(got[:cutting]), dp_swap(got[cutting:])]

    share = rows // head_parts
    sent = jnp.stack(
        [
            lax.dynamic_slice_in_dim(value, chunk_of(order) * share, share, 0)
            for value, order in zip((hidden, embedding), orders)
        ],
        0,
    )
    sent = state_swap(sent)

    pack = jnp.concatenate([pack, pack_far], 0)
    gain_rows = (split_a + 2 * split_m) // rank
    gains = pack[:, :gain_rows].reshape(4, -1).astype(full)
    attn_gain = gains[:, :split_a].reshape(-1)
    gains = natural_quarters([gains[index] for index in range(4)])
    mlp_gain = jnp.concatenate([value[split_a : split_a + split_m] for value in gains])
    mixer_gain = jnp.concatenate([value[split_a + split_m :] for value in gains])
    down_end = gain_rows + 3 * part_a + part_m
    step_width = proj_step.shape[1]
    step_start = down_end + up_mlp.size // rank
    step_end = step_start + proj_step.size // rank
    mlp_upper = jnp.concatenate(
        natural_quarters(
            [pack[index, down_end:step_start].reshape(up_mlp.shape) for index in range(4)]
        ),
        0,
    )
    step_main = jnp.concatenate(
        natural_quarters(
            [pack[index, step_start:step_end].reshape(proj_step.shape) for index in range(4)]
        ),
        0,
    )
    ups = natural_quarters(
        [pack[index, step_end:].reshape(up_rows, 3 * half_cols) for index in range(4)]
    )
    ups = jnp.concatenate(ups, 0)
    column = lax.broadcasted_iota(jnp.int32, (1, 3 * half_cols), 1) // half_cols
    up_wide = jnp.concatenate(
        [jnp.where(column == index, ups, jnp.zeros_like(ups)) for index in range(3)], 0
    )
    masks = orders[0][::-1]
    downs_all = gather_rows(pack[None, :, gain_rows:down_end], masks, 0)

    def down_of(lower, part):
        return downs_all[:, :, lower : lower + part].transpose(1, 0, 2, 3)

    down_wide = jnp.concatenate(
        [down_of(index * part_a, part_a).reshape(-1, rank) for index in range(3)], 1
    )
    down_m = down_of(3 * part_a, part_m)
    mlp_down = jnp.concatenate(natural_quarters([down_m[i] for i in range(4)]), 0)
    mlp_down = mlp_down.reshape(-1, rank)

    segment, position, valid = row_layout(lengths[0], length)
    own_segment = lax.dynamic_slice_in_dim(segment, own_start, rows)
    own_valid = lax.dynamic_slice_in_dim(valid, own_start, rows)[:, None]
    lows = first_blocks(segment)
    half = HDIM // 2
    angle = position[:, None] * 10000.0 ** (-jnp.arange(half, dtype=full) / half)[None, :]
    cosine = jnp.concatenate([jnp.cos(angle), jnp.cos(angle)], 1)
    sine = jnp.concatenate([-jnp.sin(angle), jnp.sin(angle)], 1)

    def cut(value):
        return [lax.dynamic_slice_in_dim(value, offset, piece, 0) for offset in offsets]

    valid_cut = cut(own_valid)

    quarter = gain_attn.shape[0]

    def quarters(first, second):
        parts = []
        for index in range(4):
            start = (state ^ (index % 2)) * quarter
            part = [lax.dynamic_slice_in_dim(v, start, quarter, 1) for v in (first, second)]
            parts.append(jnp.where(dp == index // 2, *part).astype(full))
        return parts

    def joint_scale(first, second):
        squares = [jnp.sum(jnp.square(v.astype(full)), 1, keepdims=True) for v in (first, second)]
        return lax.rsqrt((squares[0] + squares[1]) / (2 * width) + epsilon)

    def normed_rows(first, second):
        scale = joint_scale(first, second)
        parts = [
            (part * scale * attn_gain[index * quarter : (index + 1) * quarter]).astype(low)
            for index, part in enumerate(quarters(first, second))
        ]
        return jnp.concatenate(parts[:2], 1), jnp.concatenate(parts[2:], 1)

    near_own, far_own = normed_rows(hidden, embedding)
    joined_cut = [
        jnp.concatenate(quarters(a, b), 1) for a, b in zip(cut(hidden), cut(embedding))
    ]

    others = [gather_rows(sent[i], orders[i], 0) for i in range(2)]
    others[0] = hold(others[0], others[1], cosine, sine, down_wide)
    near_other, far_other = normed_rows(*others)
    main_near = jnp.concatenate([mine, got], 0)

    def project_near(near, far):
        reduced = (plain_dot(near, down_wide[:width]) + plain_dot(far, down_wide[width:])).astype(low)
        return plain_dot(near, main_near) + plain_dot(reduced, up_wide), reduced

    pre_own, red_own = project_near(near_own, far_own)
    pre_other, red_other = project_near(near_other, far_other)
    far_got[0] = hold(far_got[0], pre_own, pre_other)
    main_far = jnp.concatenate(far_mine + far_got, 0)
    pre_own = pre_own + plain_dot(far_own, main_far)
    pre_other = pre_other + plain_dot(far_other, main_far)
    queries, keys, values = rope(state, pre_own, pre_other, cosine, sine)

    attn_output = hold(attn_output, *far_mine)
    attn_mine = lax.dynamic_slice_in_dim(attn_output, state * half_cols, half_cols, 0)
    attn_got = state_swap(
        lax.dynamic_slice_in_dim(attn_output, (1 - state) * half_cols, half_cols, 0)
    )
    attn_pair = jnp.stack([attn_mine, attn_got], 0)
    attn_far = dp_swap(attn_pair)
    attn_proj = jnp.concatenate(
        natural_quarters([attn_pair[0], attn_pair[1], attn_far[0], attn_far[1]]), 1
    )
    mlp_cut = mlp_input.shape[1] // 2
    mlp_input = hold(mlp_input, far_got[0], far_got[1], *far_mine, attn_far)
    mlp_first = lax.all_gather(mlp_input[:, :mlp_cut], ZED, axis=0, tiled=True)
    mlp_second = lax.all_gather(mlp_input[:, mlp_cut:], ZED, axis=0, tiled=True)
    mlp_main = jnp.concatenate([mlp_first, mlp_second], 1)
    attended, lse = attend(queries, keys, values, segment, lows)

    attended = hold(attended, mlp_first)
    attended_halves = [attended[:rows], attended[rows:]]
    branch_cut = [
        sum_row16(plain_dot(part, attn_proj).astype(low).reshape(2, middle, width), order)
        for part, order in zip(attended_halves, orders)
    ]
    mlp_proj = lax.all_gather(mlp_output, ZED, axis=1, tiled=True)
    mixer_main = lax.all_gather(
        jnp.concatenate([proj_inner, proj_gate], 1), ZED, axis=0, tiled=True
    )
    output_main = lax.all_gather(proj_output, ZED, axis=1, tiled=True)
    first_cut = [
        value.astype(full) + good * branch
        for value, good, branch in zip(cut(hidden), valid_cut, branch_cut)
    ]
    mlp_normed = [
        gather_rows(rms_norm(value, mlp_gain).astype(low), order, 0)
        for value, order in zip(first_cut, orders)
    ]
    mlp_red = [plain_dot(value, mlp_down).astype(low) for value in mlp_normed]
    hidden_pre = [
        plain_dot(value, mlp_main) + plain_dot(red, mlp_upper)
        for value, red in zip(mlp_normed, mlp_red)
    ]
    activated = [jax.nn.gelu(value, approximate=False).astype(low) for value in hidden_pre]
    second_cut = [
        value + good * sum_rows(plain_dot(part, mlp_proj).astype(low), order, 0)
        for value, good, part, order in zip(first_cut, valid_cut, activated, orders)
    ]
    mixer_normed = jnp.concatenate(
        [
            gather_rows(rms_norm(value, mixer_gain).astype(low), order, 0)
            for value, order in zip(second_cut, orders)
        ],
        0,
    )

    inner_width = proj_inner.shape[1]
    mixer_heads = step_width
    states = proj_input.shape[1]
    small_main = jnp.concatenate([step_main, proj_input, proj_read], 1)
    small_pre = plain_dot(mixer_normed, small_main)
    mixer_pre = plain_dot(mixer_normed, mixer_main)
    inner_pre, gate_pre = mixer_pre[:, :inner_width], mixer_pre[:, inner_width:]
    reach = taps_inner.shape[0] - 1
    edge = state_forward(
        jnp.concatenate([inner_pre[rows - reach :], small_pre[rows - reach :, mixer_heads:]], 1)
    )
    edge_start = jnp.maximum(own_start - reach, 0)
    edge_segment = jnp.where(state == 0, -1, lax.dynamic_slice_in_dim(segment, edge_start, reach))

    def conv_piece(inner_in, small_in, edge_in, taps_x, taps_b, taps_c, shift_in):
        input_in = small_in[:, mixer_heads : mixer_heads + states]
        read_in = small_in[:, mixer_heads + states :]
        edge_b = edge_in[:, inner_width : inner_width + states]
        edge_c = edge_in[:, inner_width + states :]
        return (
            jax.nn.silu(
                conv_edge(inner_in, edge_in[:, :inner_width], taps_x, own_segment, edge_segment)
            ),
            jax.nn.silu(conv_edge(input_in, edge_b, taps_b, own_segment, edge_segment)),
            jax.nn.silu(conv_edge(read_in, edge_c, taps_c, own_segment, edge_segment)),
            jax.nn.softplus(small_in[:, :mixer_heads] + shift_in[None, :]),
        )

    (inner_conv, input_conv, read_conv, steps), conv_back = jax.vjp(
        conv_piece,
        inner_pre,
        small_pre,
        edge,
        taps_inner.astype(full),
        taps_input.astype(full),
        taps_read.astype(full),
        step_bias.astype(full),
    )
    rate = -jnp.exp(log_rate.astype(full))
    scan = Scan(inner_conv, steps, rate, input_conv, read_conv, own_segment, edge_segment[-1])
    first_state = state_forward(scan.end())
    scanned, block_states = scan.forward(first_state)

    def by_head(value):
        return value.reshape(rows, mixer_heads, MDIM)

    skip_full = jnp.repeat(skip_gain.astype(full), MDIM)[None, :]
    combined = scanned + skip_full * inner_conv
    gate_act = jax.nn.silu(gate_pre)
    united = combined * gate_act
    gated_gain = gain_gated.astype(full)[None, :]
    cot_own = lax.dynamic_slice_in_dim(cotangent, own_start, rows, 0)
    mix_grad = cot_own * own_valid.astype(low)
    gated_grad = right_dot(mix_grad, output_main)
    pair = jnp.stack(
        [jnp.sum(united * united, 1), jnp.sum(united * gated_gain * gated_grad, 1)], 0
    )
    for mask in orders[0]:
        pair = pair + head_swap(pair, mask)
    channels = inner_width * head_parts
    row_scale = lax.rsqrt(pair[0] / channels + epsilon)[:, None]
    row_total = pair[1][:, None]
    gated = (united * row_scale * gated_gain).astype(low)
    united_grad = (
        row_scale * gated_gain * gated_grad
        - united * row_scale * row_scale * row_scale * row_total / channels
    )
    combined_grad = united_grad * gate_act
    last_state_grad = state_backward(scan.start_grad(combined_grad))

    sigmoid_gate = jax.nn.sigmoid(gate_pre)
    gate_grad = united_grad * combined * sigmoid_gate * (1.0 + gate_pre * (1.0 - sigmoid_gate))
    grad_gated_gain = jnp.sum(gated_grad * united * row_scale, 0)
    grad_skip = jnp.sum(by_head(combined_grad * inner_conv), (0, 2))
    scan_grad, step_grad, log_grad, log_rows, input_grad, read_grad = scan.backward(
        combined_grad, block_states, last_state_grad
    )
    log_grad = log_grad - log_rows.T
    grad_rate = jnp.sum(log_grad * steps, 0) * rate
    (
        inner_grad,
        small_grad,
        edge_grad,
        grad_taps_x,
        grad_taps_b,
        grad_taps_c,
        grad_shift,
    ) = conv_back(
        (
            scan_grad + skip_full * combined_grad,
            input_grad,
            read_grad,
            step_grad + log_grad * rate[None, :],
        )
    )
    edge_back = state_backward(edge_grad)
    inner_grad = inner_grad.at[rows - reach :].add(edge_back[:, :inner_width])
    small_grad = small_grad.at[rows - reach :, mixer_heads:].add(edge_back[:, inner_width:])
    out_cut = [
        (
            value
            + good
            * sum_rows(
                plain_dot(gated[index * middle : (index + 1) * middle], output_main).astype(low),
                order,
                0,
            )
        ).astype(low)
        for index, (value, good, order) in enumerate(zip(second_cut, valid_cut, orders))
    ]
    inner_low = jnp.concatenate([inner_grad, gate_grad], 1).astype(low)
    inner_low = hold(inner_low, *out_cut)
    small_low = small_grad.astype(low)
    mixer_parts = [
        (right_dot(inner_low[part], mixer_main) + right_dot(small_low[part], small_main)).astype(low)
        for part in (slice(0, middle), slice(middle, rows))
    ]
    mixer_sum = [sum_rows(part, order, 0) for part, order in zip(mixer_parts, orders)]
    inner_later = hold(inner_low, *mixer_parts)
    small_later = hold(small_low, *mixer_parts)
    upstream_cut = [value.astype(full) for value in cut(cot_own)]
    mixer_backs = [
        norm_back(value, mixer_gain, grad) for value, grad in zip(second_cut, mixer_sum)
    ]
    second_grad = [up + back[0] for up, back in zip(upstream_cut, mixer_backs)]
    grad_mixer_gain = mixer_backs[0][1] + mixer_backs[1][1]
    mlp_grad = [
        gather_rows((good * grad).astype(low), order, 0)
        for good, grad, order in zip(valid_cut, second_grad, orders)
    ]

    def gelu_part(value):
        return jax.nn.gelu(value, approximate=False)

    hidden_grad = [
        jax.vjp(gelu_part, pre)[1](right_dot(grad, mlp_proj))[0].astype(low)
        for pre, grad in zip(hidden_pre, mlp_grad)
    ]
    mlp_wide = jnp.concatenate([mlp_main, mlp_upper], 0)
    mlp_parts = [right_dot(grad, mlp_wide).astype(low) for grad in hidden_grad]
    mlp_sums = [sum_rows(part, order, 0) for part, order in zip(mlp_parts, orders)]
    middle_low = [value[:, width:].astype(low) for value in mlp_sums]
    mlp_backs = [
        norm_back(value, mlp_gain, total[:, :width] + right_dot(mid, mlp_down))
        for value, total, mid in zip(first_cut, mlp_sums, middle_low)
    ]
    first_grad = [grad + back[0] for grad, back in zip(second_grad, mlp_backs)]
    grad_mlp_gain = mlp_backs[0][1] + mlp_backs[1][1]
    branch_halves = [
        gather_row16((good * grad).astype(low), order).reshape(rows, width)
        for good, grad, order in zip(valid_cut, first_grad, orders)
    ]

    attended_grad = jnp.concatenate(
        [right_dot(value, attn_proj).astype(low) for value in branch_halves], 0
    )
    query_back, key_back, value_back = attend_back(
        queries, keys, values, attended_grad, attended, lse, segment, lows
    )
    pre_grad = rope_back(query_back, key_back, value_back, cosine, sine)
    main_wide = jnp.concatenate([main_near, main_far, up_wide], 0)
    joint = 2 * width
    normed_parts = [
        right_dot(part, main_wide).astype(low) for part in (pre_grad[:rows], pre_grad[rows:])
    ]
    normed_sums = []
    for part, order in zip(normed_parts, orders):
        total = sum_rows(part.reshape(2, middle, -1), order, 1)
        away = lax.dynamic_index_in_dim(total, 1 - state, 0, False).astype(low)
        away = jnp.concatenate([swap_quarters(away[:, :joint]), away[:, joint:]], 1)
        kept = lax.dynamic_index_in_dim(total, state, 0, False)
        normed_sums.append(kept + state_swap(away).astype(full))
    cubes = pre_grad.reshape(2, 2, middle, -1)
    grad_own, grad_other = (
        lax.dynamic_index_in_dim(cubes, index, 1, False).reshape(rows, -1)
        for index in (state, 1 - state)
    )
    wide_grad = left_dot(red_own, grad_own) + left_dot(red_other, grad_other)
    up_grad = jnp.concatenate(
        [
            wide_grad[index * rank : (index + 1) * rank, index * half_cols : (index + 1) * half_cols]
            for index in range(3)
        ],
        1,
    )

    def main_grad(own, other, lower, index):
        part = slice(lower * quarter, (lower + 1) * quarter)
        main = left_dot(own[:, part], grad_own) + left_dot(other[:, part], grad_other)
        ups = lax.dynamic_slice_in_dim(up_grad, (place ^ index) * up_rows, up_rows, 0)
        return jnp.concatenate([main, ups], 0).astype(low)

    def by_dp(near, far):
        both = jnp.concatenate([jnp.where(dp == 0, near, far), jnp.where(dp == 0, far, near)], 0)
        return lax.psum_scatter(both, DP, scatter_dimension=0, tiled=True)

    beside = by_dp(main_grad(near_own, near_other, 1, 1), main_grad(far_own, far_other, 1, 3))
    main_total = by_dp(
        hold(main_grad(near_own, near_other, 0, 0), *normed_sums),
        main_grad(far_own, far_other, 0, 2),
    )
    beside_got = state_swap(hold(beside, *normed_sums))

    def spread(own, got, index):
        part = slice(index * half_cols, (index + 1) * half_cols)
        own, got = own[:, part].astype(full), got[:, part].astype(full)
        return jnp.concatenate(
            [jnp.where(state == 0, own, got), jnp.where(state == 0, got, own)], 1
        )

    lows_cut = [value[:, joint:].astype(low) for value in normed_sums]
    joined_backs = [
        norm_back(value, attn_gain, total[:, :joint] + right_dot(mid, down_wide))
        for value, total, mid in zip(joined_cut, normed_sums, lows_cut)
    ]
    grad_attn_gain = joined_backs[0][1] + joined_backs[1][1]

    def natural_columns(value):
        return jnp.concatenate(
            [
                lax.dynamic_slice_in_dim(value, (place ^ index) * quarter, quarter, -1)
                for index in range(4)
            ],
            -1,
        )

    input_cut = []
    for grad, back, order in zip(first_grad, joined_backs, orders):
        joined_grad = natural_columns(back[0])
        joined_grad = jnp.concatenate([joined_grad[:, :width] + grad, joined_grad[:, width:]], 1)
        input_cut.append(joined_grad.astype(low))
    input_halves = [gather_rows(value, order, 0) for value, order in zip(input_cut, orders)]
    layer_halves = [
        gather_row16(hold(value, *input_halves), order) for value, order in zip(out_cut, orders)
    ]
    layer_out = jnp.concatenate(
        [layer_halves[0][0], layer_halves[1][0], layer_halves[0][1], layer_halves[1][1]], 0
    )
    grad_hidden = jnp.concatenate([value[:, :width] for value in input_halves], 0)
    grad_embedding = jnp.concatenate([value[:, width:] for value in input_halves], 0)

    def scatter(value, axis):
        value = lax.psum_scatter(value.astype(low), ZED, scatter_dimension=axis, tiled=True)
        return hold(value, *input_cut).astype(full)

    attn_grad = left_dot(attended_halves[0], branch_halves[0]) + left_dot(
        attended_halves[1], branch_halves[1]
    )
    out_attn = grad_pieces(hold(attn_grad.astype(low), *input_halves), 0)
    out_output = scatter(left_dot(gated, mix_grad), 1)
    out_mixer = scatter(left_dot(mixer_normed, inner_later), 0)
    mlp_normed_own = jnp.concatenate(mlp_normed, 0)
    hidden_grad_own = hold(jnp.concatenate(hidden_grad, 0), *mlp_parts)
    mlp_grad_own = hold(jnp.concatenate(mlp_grad, 0), *mlp_parts)
    out_mlp_output = scatter(
        left_dot(jnp.concatenate(activated, 0), mlp_grad_own), 1
    )
    out_mlp_input = scatter(left_dot(mlp_normed_own, hidden_grad_own), 0)
    out_up_mlp = scatter(left_dot(jnp.concatenate(mlp_red, 0), hidden_grad_own), 0)

    def by_order(value):
        bits = value.reshape((2,) * (len(orders[0])) + (piece, value.shape[1]))
        count = len(orders[0])
        turned = [0] + list(range(count - 1, 0, -1)) + [count, count + 1]
        return bits.transpose(turned).reshape(value.shape)

    lows_own = gather_rows(jnp.stack(lows_cut, 0), orders[0], 1)
    lows_own = [lows_own[0], by_order(lows_own[1])]
    lows_own = jnp.concatenate(lows_own, 0)
    down_parts = [
        left_dot(
            lax.dynamic_slice_in_dim(value, index * quarter + head * part_a, part_a, 1), lows_own
        )
        for value in (near_own, far_own)
        for index in range(2)
    ]
    away = hold(jnp.stack([down_parts[1], down_parts[3]], 0).astype(low), *input_halves)
    away = state_swap(away).astype(full)
    down_sum = down_parts[0] + away[0] + dp_swap((down_parts[2] + away[1]).astype(low))
    down_all = gather_rows(down_sum.astype(low)[None], masks, 0).reshape(quarter, 3 * rank)
    down_all = down_all.astype(full)
    out_downs = [down_all[:, index * rank : (index + 1) * rank] for index in range(3)]

    def placed(value, axis):
        shape = list(value.shape)
        shape[axis] *= head_parts
        return lax.dynamic_update_slice_in_dim(
            jnp.zeros(shape, full), value, head * value.shape[axis], axis
        )

    small_main_grad = hold(left_dot(mixer_normed, small_later), *input_halves)
    normed_cut = [
        lax.dynamic_slice_in_dim(value, chunk_of(order) * piece, piece, 0)
        for value, order in zip(mlp_normed, orders)
    ]
    mlp_down_grad = left_dot(jnp.concatenate(normed_cut, 0), jnp.concatenate(middle_low, 0))
    pair_grad = jnp.concatenate([small_main_grad[:, mixer_heads:], mlp_down_grad], 1)
    wide = pair_grad.shape[1]
    heads_grad = placed(jnp.stack([grad_shift, grad_rate, grad_skip]), 1)
    flat_sums = [
        placed(small_main_grad[:, :mixer_heads].T, 0),
        placed(grad_taps_x, 1),
        placed(grad_gated_gain, 0),
        grad_mlp_gain,
        grad_mixer_gain,
        jnp.concatenate([grad_taps_b, grad_taps_c], 1),
        jnp.pad(heads_grad.reshape(-1), (0, -heads_grad.size % wide)),
    ]
    packed = jnp.concatenate([value.reshape(-1, wide) for value in flat_sums], 0)
    lines = pair_grad.shape[0] // 8
    packed = jnp.pad(packed, ((0, -packed.shape[0] % lines), (0, 0)))
    pair_grad = jnp.concatenate([pair_grad, packed], 0)
    pair_grad = sum_rows(pair_grad, masks, 0)
    pair_grad = pair_grad + state_swap(pair_grad)
    pair_grad = pair_grad + dp_swap(pair_grad)
    pair_grad = gather_rows(pair_grad.astype(low), masks, 0).astype(full)
    vector_grad = pair_grad[:width, : 2 * states]
    out_down_mlp = lax.dynamic_slice(pair_grad, (place * split_m, 2 * states), (split_m, rank))
    packed = pair_grad[width:]
    pieces = []
    for value in flat_sums:
        count = value.size // wide
        pieces.append(packed[:count].reshape(value.shape))
        packed = packed[count:]
    step_total, taps_x_total, gated_total, mlp_total, mixer_total, taps_total, head_total = pieces
    head_total = head_total[: heads_grad.size].reshape(heads_grad.shape)

    out_all = [spread(main_total, beside_got, index) for index in range(3)]
    out_main = [value[:quarter] for value in out_all]
    out_up = [value[quarter:] for value in out_all]
    once = (head == 0).astype(full)
    square_sum = jnp.zeros((), full)
    for value in out_main + out_up + [out_attn, out_mlp_input, out_up_mlp, out_mlp_output]:
        square_sum = square_sum + jnp.sum(value * value)
    for value in out_downs + [out_down_mlp]:
        square_sum = square_sum + once * jnp.sum(value * value)
    square_total, attn_total = lax.psum((square_sum, natural_columns(grad_attn_gain)), EVERY)

    def of_head(value, size):
        return lax.dynamic_slice_in_dim(value, head * size, size, value.ndim - 1)

    def of_place(value, size):
        return lax.dynamic_slice_in_dim(value, place * size, size)

    head_total = of_head(head_total, mixer_heads)
    out_step = lax.dynamic_slice(
        step_total, (head * mixer_heads, place * split_m), (mixer_heads, split_m)
    ).T
    return (
        layer_out,
        grad_hidden,
        grad_embedding,
        of_place(attn_total, split_a),
        out_main[0],
        out_main[1],
        out_main[2],
        out_downs[0],
        out_downs[1],
        out_downs[2],
        out_up[0],
        out_up[1],
        out_up[2],
        out_attn,
        of_place(mlp_total, split_m),
        out_mlp_input,
        out_down_mlp,
        out_up_mlp,
        out_mlp_output,
        of_place(mixer_total, split_m),
        out_mixer[:, :inner_width],
        out_mixer[:, inner_width:],
        out_step,
        vector_grad[:, :states],
        vector_grad[:, states:],
        of_head(taps_x_total, inner_width),
        taps_total[:, :states],
        taps_total[:, states:],
        head_total[0],
        head_total[1],
        head_total[2],
        of_head(gated_total, inner_width),
        out_output,
        jnp.sqrt(square_total),
    )


def pick_device(mesh):
    heads = mesh.shape[HEAD]
    per_head = DIN // HDIM // heads
    halves = mesh.shape[DP] == 2 and mesh.shape[STATE] == 2
    return fast_device if halves and heads & (heads - 1) == 0 and per_head % 2 == 0 else general_device


def solution(mesh):
    in_specs = (
        P(ZED, None),
        P(ZED, None),
        P(DP, None),
        P(DP, None),
        P(ZED),
        P(ZED, HEAD),
        P(ZED, HEAD),
        P(ZED, HEAD),
        P(ZED, None),
        P(ZED, None),
        P(ZED, None),
        P(ZED, HEAD),
        P(ZED, HEAD),
        P(ZED, HEAD),
        P(HEAD, ZED),
        P(ZED),
        P(ZED, HEAD),
        P(ZED, None),
        P(ZED, HEAD),
        P(HEAD, ZED),
        P(ZED),
        P(ZED, HEAD),
        P(ZED, HEAD),
        P(ZED, HEAD),
        P(),
        P(),
        P(None, HEAD),
        P(),
        P(),
        P(HEAD),
        P(HEAD),
        P(HEAD),
        P(HEAD),
        P(HEAD, ZED),
    )
    out_specs = (
        P(DP, None),
        P(ZED, None),
        P(ZED, None),
        P(ZED),
        P(ZED, HEAD),
        P(ZED, HEAD),
        P(ZED, HEAD),
        P(ZED, None),
        P(ZED, None),
        P(ZED, None),
        P(ZED, HEAD),
        P(ZED, HEAD),
        P(ZED, HEAD),
        P(HEAD, ZED),
        P(ZED),
        P(ZED, HEAD),
        P(ZED, None),
        P(ZED, HEAD),
        P(HEAD, ZED),
        P(ZED),
        P(ZED, HEAD),
        P(ZED, HEAD),
        P(ZED, HEAD),
        P(),
        P(),
        P(None, HEAD),
        P(),
        P(),
        P(HEAD),
        P(HEAD),
        P(HEAD),
        P(HEAD),
        P(HEAD, ZED),
        P(),
    )
    return jax.shard_map(
        pick_device(mesh), mesh=mesh, in_specs=in_specs, out_specs=out_specs, check_vma=False
    )
```

```python
import jax
import jax.numpy as jnp
from jax import lax
from jax.experimental import pallas as pl
from jax.experimental.pallas import tpu as pltpu
from jax.sharding import PartitionSpec as P

HDIM = 128
MDIM = 64
DIN = 4096
GROUP = 256
DP, HEAD, STATE = "dp", "head", "state"
ZED = (DP, STATE)
EVERY = (DP, HEAD, STATE)


highest = lax.Precision.HIGHEST
epsilon = 1e-05


def plain_dot(left, right):
    return jnp.dot(left, right, preferred_element_type=jnp.float32)


def left_dot(left, right):
    return lax.dot_general(
        left, right, (((0,), (0,)), ((), ())), preferred_element_type=jnp.float32
    )


def right_dot(left, right):
    return lax.dot_general(
        left, right, (((1,), (1,)), ((), ())), preferred_element_type=jnp.float32
    )


def exact_left(left, right):
    return lax.dot_general(
        left.astype(jnp.float32), right, (((0,), (0,)), ((), ())), precision=highest
    )


def exact_right(left, right):
    return lax.dot_general(
        left, right.astype(jnp.float32), (((1,), (1,)), ((), ())), precision=highest
    )


def rms_norm(values, gain):
    return values * lax.rsqrt(jnp.mean(values * values, -1, keepdims=True) + epsilon) * gain


def row_layout(doc_lengths, length):
    ends = jnp.cumsum(doc_lengths)
    places = jnp.arange(length, dtype=jnp.int32)
    segment = jnp.sum((places[:, None] >= ends[None, :]).astype(jnp.int32), axis=1)
    starts = jnp.concatenate([ends - doc_lengths, ends[-1:]])
    choose = segment[:, None] == jnp.arange(starts.shape[0], dtype=jnp.int32)[None, :]
    first_place = jnp.sum(jnp.where(choose, starts[None, :], 0), axis=1)
    position = (places - first_place).astype(jnp.float32)
    valid = (segment < doc_lengths.shape[0]).astype(jnp.float32)
    return (segment, position, valid)


def rotate(values, position):
    half = values.shape[-1] // 2
    freqs = 10000.0 ** (-jnp.arange(half, dtype=jnp.float32) / half)
    angle = position[:, None] * freqs[None, :]
    cosine = jnp.cos(angle)[:, None, :]
    sine = jnp.sin(angle)[:, None, :]
    former = values[..., :half]
    latter = values[..., half:]
    return jnp.concatenate([former * cosine - latter * sine, former * sine + latter * cosine], -1)


def head_probs(query_in, key_in, allowed):
    scale = query_in.shape[-1] ** (-0.5)
    scores = (
        jnp.einsum("thd,shd->hts", query_in, key_in, preferred_element_type=jnp.float32) * scale
    )
    scores = jnp.where(allowed[None, :, :], scores, -1e30)
    shifted = scores - jnp.max(scores, -1, keepdims=True)
    weights = jnp.exp(shifted)
    return weights / jnp.sum(weights, -1, keepdims=True)


def conv_mask(values, taps, segment):
    total = taps[0][None, :] * values
    for offset in range(1, taps.shape[0]):
        moved = jnp.concatenate(
            [jnp.zeros((offset, values.shape[1]), values.dtype), values[:-offset]], 0
        )
        moved_seg = jnp.concatenate([jnp.full((offset,), -1, jnp.int32), segment[:-offset]], 0)
        same = (moved_seg == segment).astype(values.dtype)[:, None]
        total = total + taps[offset][None, :] * moved * same
    return total


def state_scan(inputs, step_sizes, decay, input_vecs, read_vecs, segment, block):
    length, heads, width = inputs.shape
    count = length // block
    states = input_vecs.shape[1]

    def one_block(carry, pieces):
        state, before = carry
        group_in, group_dt, group_b, group_c, group_seg = pieces
        logs = group_dt * decay[None, :]
        cumul = jnp.cumsum(logs, 0)
        places = jnp.arange(block, dtype=jnp.int32)
        allowed = (group_seg[:, None] == group_seg[None, :]) & (places[None, :] <= places[:, None])
        gaps = cumul[:, None, :] - cumul[None, :, :]
        fading = jnp.where(
            allowed[:, :, None], jnp.exp(jnp.where(allowed[:, :, None], gaps, 0.0)), 0.0
        )
        inner = jnp.dot(group_c, group_b.T, precision=highest)
        scaled = group_in * group_dt[:, :, None]
        local_out = jnp.einsum(
            "tsh,shp->thp", inner[:, :, None] * fading, scaled, precision=highest
        )
        carried = (group_seg == before).astype(inputs.dtype)
        entry = jnp.exp(cumul) * carried[:, None]
        from_state = (
            jnp.einsum("tn,hnp->thp", group_c, state, precision=highest) * entry[:, :, None]
        )
        last_seg = group_seg[-1]
        reach = (group_seg == last_seg).astype(inputs.dtype)
        to_end = jnp.exp(cumul[-1][None, :] - cumul) * reach[:, None]
        retain = jnp.exp(cumul[-1]) * (last_seg == before).astype(inputs.dtype)
        fresh = jnp.einsum("sn,sh,shp->hnp", group_b, to_end, scaled, precision=highest)
        state = state * retain[:, None, None] + fresh
        return ((state, last_seg), local_out + from_state)

    pieces = (
        inputs.reshape(count, block, heads, width),
        step_sizes.reshape(count, block, heads),
        input_vecs.reshape(count, block, states),
        read_vecs.reshape(count, block, states),
        segment.reshape(count, block),
    )
    start = (jnp.zeros((heads, states, width), inputs.dtype), jnp.array(-1, jnp.int32))
    unused, outputs = lax.scan(jax.checkpoint(one_block), start, pieces)
    return outputs.reshape(length, heads, width)


def mixer_core(
    inner_pre,
    input_pre,
    read_pre,
    step_pre,
    taps_x,
    taps_b,
    taps_c,
    shift_in,
    rate_in,
    segment,
    width,
    block,
):
    inner_conv = jax.nn.silu(conv_mask(inner_pre, taps_x, segment))
    input_conv = jax.nn.silu(conv_mask(input_pre, taps_b, segment))
    read_conv = jax.nn.silu(conv_mask(read_pre, taps_c, segment))
    step_sizes = jax.nn.softplus(step_pre + shift_in[None, :])
    heads = step_sizes.shape[1]
    length = inner_conv.shape[0]
    outputs = state_scan(
        inner_conv.reshape(length, heads, width),
        step_sizes,
        -jnp.exp(rate_in),
        input_conv,
        read_conv,
        segment,
        block,
    )
    return (outputs.reshape(length, heads * width), inner_conv)


def place_slice(piece, index, parts, axis):
    shape = list(piece.shape)
    shape[axis] = shape[axis] * parts
    holder = jnp.zeros(tuple(shape), jnp.float32)
    return lax.dynamic_update_slice_in_dim(holder, piece, index * piece.shape[axis], axis)


def take_slice(whole, index, width, axis):
    return lax.dynamic_slice_in_dim(whole, index * width, width, axis)


def general_device(
    hidden,
    embedding,
    cotangent,
    lengths,
    gain_attn,
    w_query,
    w_key,
    w_value,
    down_query,
    down_key,
    down_value,
    up_query,
    up_key,
    up_value,
    attn_output,
    gain_mlp,
    mlp_input,
    down_mlp,
    up_mlp,
    mlp_output,
    gain_mixer,
    proj_inner,
    proj_gate,
    proj_step,
    proj_input,
    proj_read,
    taps_inner,
    taps_input,
    taps_read,
    step_bias,
    log_rate,
    skip_gain,
    gain_gated,
    proj_output,
):
    row_count = hidden.shape[0]
    length = cotangent.shape[0]
    model_width = hidden.shape[1]
    head_parts = lax.axis_size(HEAD)
    state_parts = lax.axis_size(STATE)
    state_index = lax.axis_index(STATE)
    head_index = lax.axis_index(HEAD)
    own_start = state_index * row_count
    segment, position, valid = row_layout(lengths[0], length)
    own_segment = lax.dynamic_slice_in_dim(segment, own_start, row_count)
    own_position = lax.dynamic_slice_in_dim(position, own_start, row_count)
    own_valid = lax.dynamic_slice_in_dim(valid, own_start, row_count)[:, None]
    full_valid = valid[:, None]
    places = jnp.arange(length, dtype=jnp.int32)
    own_places = own_start + jnp.arange(row_count, dtype=jnp.int32)
    own_mask = ((places >= own_start) & (places < own_start + row_count)).astype(jnp.float32)[
        :, None
    ]
    allowed = (own_segment[:, None] == segment[None, :]) & (places[None, :] <= own_places[:, None])
    gathered = (
        lax.all_gather(gain_attn, ZED, axis=0, tiled=True),
        lax.all_gather(w_query, ZED, axis=0, tiled=True),
        lax.all_gather(w_key, ZED, axis=0, tiled=True),
        lax.all_gather(w_value, ZED, axis=0, tiled=True),
        lax.all_gather(down_query, ZED, axis=0, tiled=True),
        lax.all_gather(down_key, ZED, axis=0, tiled=True),
        lax.all_gather(down_value, ZED, axis=0, tiled=True),
        lax.all_gather(up_query, ZED, axis=0, tiled=True),
        lax.all_gather(up_key, ZED, axis=0, tiled=True),
        lax.all_gather(up_value, ZED, axis=0, tiled=True),
        lax.all_gather(attn_output, ZED, axis=1, tiled=True),
        lax.all_gather(gain_mlp, ZED, axis=0, tiled=True),
        lax.all_gather(mlp_input, ZED, axis=0, tiled=True),
        lax.all_gather(down_mlp, ZED, axis=0, tiled=True),
        lax.all_gather(up_mlp, ZED, axis=0, tiled=True),
        lax.all_gather(mlp_output, ZED, axis=1, tiled=True),
        lax.all_gather(gain_mixer, ZED, axis=0, tiled=True),
        lax.all_gather(proj_inner, ZED, axis=0, tiled=True),
        lax.all_gather(proj_gate, ZED, axis=0, tiled=True),
        lax.all_gather(proj_step, ZED, axis=0, tiled=True),
        lax.all_gather(proj_output, ZED, axis=1, tiled=True),
    )
    (
        attn_gain,
        query_main,
        key_main,
        value_main,
        query_down,
        key_down,
        value_down,
        query_upper,
        key_upper,
        value_upper,
        attn_proj,
        mlp_gain,
        mlp_main,
        mlp_down,
        mlp_upper,
        mlp_proj,
        mixer_gain,
        inner_main,
        gate_main,
        step_main,
        output_main,
    ) = gathered
    joined = jnp.concatenate([hidden, embedding], 1).astype(jnp.float32)
    attn_gain_f = attn_gain.astype(jnp.float32)
    normed = rms_norm(joined, attn_gain_f).astype(jnp.bfloat16)
    head_count = query_main.shape[1] // HDIM

    def project(main, down, upper):
        reduced = plain_dot(normed, down).astype(jnp.bfloat16)
        return (plain_dot(normed, main) + plain_dot(reduced, upper), reduced)

    query_pre, query_red = project(query_main, query_down, query_upper)
    key_pre, key_red = project(key_main, key_down, key_upper)
    value_pre, value_red = project(value_main, value_down, value_upper)
    queries = rotate(query_pre.reshape(row_count, head_count, HDIM), own_position).astype(
        jnp.bfloat16
    )
    keys_own = rotate(key_pre.reshape(row_count, head_count, HDIM), own_position).astype(
        jnp.bfloat16
    )
    values_own = value_pre.reshape(row_count, head_count, HDIM).astype(jnp.bfloat16)
    keys_all, values_all = (
        lax.all_gather(keys_own, STATE, axis=0, tiled=True),
        lax.all_gather(values_own, STATE, axis=0, tiled=True),
    )
    probs_full = head_probs(queries, keys_all, allowed)
    attended_f = jnp.einsum(
        "hts,shd->thd",
        probs_full.astype(jnp.bfloat16),
        values_all,
        preferred_element_type=jnp.float32,
    )
    attended = attended_f.reshape(row_count, head_count * HDIM).astype(jnp.bfloat16)
    branch = lax.psum(plain_dot(attended, attn_proj), HEAD)
    first = hidden.astype(jnp.float32) + own_valid * branch
    mlp_gain_f = mlp_gain.astype(jnp.float32)
    mlp_normed = rms_norm(first, mlp_gain_f).astype(jnp.bfloat16)
    mlp_red = plain_dot(mlp_normed, mlp_down).astype(jnp.bfloat16)
    hidden_pre = plain_dot(mlp_normed, mlp_main) + plain_dot(mlp_red, mlp_upper)
    activated = jax.nn.gelu(hidden_pre, approximate=False).astype(jnp.bfloat16)
    mlp_branch = lax.psum(plain_dot(activated, mlp_proj), HEAD)
    second = first + own_valid * mlp_branch
    second_all = lax.all_gather(second, STATE, axis=0, tiled=True)
    mixer_gain_f = mixer_gain.astype(jnp.float32)
    mixer_normed = rms_norm(second_all, mixer_gain_f).astype(jnp.bfloat16)
    states_own = proj_input.shape[1] // state_parts
    input_half = take_slice(proj_input, state_index, states_own, 1)
    read_half = take_slice(proj_read, state_index, states_own, 1)
    taps_input_half = take_slice(taps_input, state_index, states_own, 1).astype(jnp.float32)
    taps_read_half = take_slice(taps_read, state_index, states_own, 1).astype(jnp.float32)
    inner_pre = plain_dot(mixer_normed, inner_main)
    gate_pre = plain_dot(mixer_normed, gate_main)
    step_pre = plain_dot(mixer_normed, step_main)
    input_pre = plain_dot(mixer_normed, input_half)
    read_pre = plain_dot(mixer_normed, read_half)

    def mixer_piece(
        inner_in, input_in, read_in, step_in, taps_x, taps_b, taps_c, shift_in, rate_in
    ):
        return mixer_core(
            inner_in,
            input_in,
            read_in,
            step_in,
            taps_x,
            taps_b,
            taps_c,
            shift_in,
            rate_in,
            segment,
            MDIM,
            GROUP,
        )

    (scanned_part, inner_conv), mixer_back = jax.vjp(
        mixer_piece,
        inner_pre,
        input_pre,
        read_pre,
        step_pre,
        taps_inner.astype(jnp.float32),
        taps_input_half,
        taps_read_half,
        step_bias.astype(jnp.float32),
        log_rate.astype(jnp.float32),
    )
    scanned = lax.psum(scanned_part, STATE)
    skip_full = jnp.repeat(skip_gain.astype(jnp.float32), MDIM)[None, :]
    combined = scanned + skip_full * inner_conv
    gate_act = jax.nn.silu(gate_pre)
    united = combined * gate_act
    squares = lax.psum(jnp.sum(united * united, 1), HEAD)
    row_scale = lax.rsqrt(squares / DIN + epsilon)[:, None]
    gated_gain = gain_gated.astype(jnp.float32)[None, :]
    united_own = lax.dynamic_slice_in_dim(united, own_start, row_count, 0)
    scale_own = lax.dynamic_slice_in_dim(row_scale, own_start, row_count, 0)
    gated_own = (united_own * scale_own * gated_gain).astype(jnp.bfloat16)
    mixed_own = lax.psum(plain_dot(gated_own, output_main), HEAD)
    mixed = lax.all_gather(mixed_own, STATE, axis=0, tiled=True)
    layer_out = (second_all + full_valid * mixed).astype(jnp.bfloat16)
    upstream = cotangent.astype(jnp.float32)
    mix_grad = (full_valid * upstream).astype(jnp.bfloat16)
    mix_grad_own = lax.dynamic_slice_in_dim(mix_grad, own_start, row_count, 0)
    grad_output_main = left_dot(gated_own, mix_grad_own)
    gated_grad = right_dot(mix_grad, output_main)
    row_total = jnp.sum(mix_grad.astype(jnp.float32) * mixed, 1)[:, None] / row_scale
    grad_gated_gain = jnp.sum(gated_grad * united * row_scale * own_mask, 0)
    united_grad = (
        row_scale * gated_gain * gated_grad
        - united * row_scale * row_scale * row_scale * row_total / DIN
    )
    combined_grad = united_grad * gate_act
    sigmoid_gate = jax.nn.sigmoid(gate_pre)
    gate_grad = (
        united_grad * combined * sigmoid_gate * (1.0 + gate_pre * (1.0 - sigmoid_gate)) * own_mask
    )
    mixer_heads = step_pre.shape[1]
    grad_skip = jnp.sum(
        (combined_grad * inner_conv * own_mask).reshape(length, mixer_heads, MDIM), (0, 2)
    )
    conv_extra = skip_full * combined_grad * own_mask
    (
        inner_grad,
        input_grad,
        read_grad,
        step_grad,
        grad_taps_x,
        grad_taps_b,
        grad_taps_c,
        grad_shift,
        grad_rate,
    ) = mixer_back((combined_grad, conv_extra))
    mixer_part = (
        exact_right(inner_grad, inner_main)
        + exact_right(gate_grad, gate_main)
        + exact_right(step_grad, step_main)
        + exact_right(input_grad, input_half)
        + exact_right(read_grad, read_half)
    )
    grad_inner_main = exact_left(mixer_normed, inner_grad)
    grad_gate_main = exact_left(mixer_normed, gate_grad)
    grad_step_main = exact_left(mixer_normed, step_grad)
    grad_input_half = exact_left(mixer_normed, input_grad)
    grad_read_half = exact_left(mixer_normed, read_grad)
    mixer_rows_own = lax.psum_scatter(mixer_part, STATE, scatter_dimension=0, tiled=True)
    mixer_own = lax.psum(mixer_rows_own, HEAD)
    unused_norm, second_back = jax.vjp(rms_norm, second, mixer_gain_f)
    second_norm_grad, grad_mixer_gain = second_back(mixer_own)
    upstream_own = lax.dynamic_slice_in_dim(upstream, own_start, row_count, 0)
    second_grad = upstream_own + second_norm_grad
    mlp_grad = (own_valid * second_grad).astype(jnp.bfloat16)
    grad_mlp_proj = left_dot(activated, mlp_grad)
    activated_grad = right_dot(mlp_grad, mlp_proj)
    unused_gelu, gelu_back = jax.vjp(
        lambda preact: jax.nn.gelu(preact, approximate=False), hidden_pre
    )
    hidden_grad = gelu_back(activated_grad)[0].astype(jnp.bfloat16)
    grad_mlp_main = left_dot(mlp_normed, hidden_grad)
    grad_mlp_upper = left_dot(mlp_red, hidden_grad)
    mlp_middle = right_dot(hidden_grad, mlp_upper)
    mlp_part = right_dot(hidden_grad, mlp_main)
    mlp_sum, middle_sum = lax.psum((mlp_part, mlp_middle), HEAD)
    middle_low = middle_sum.astype(jnp.bfloat16)
    mlp_normed_grad = mlp_sum + right_dot(middle_low, mlp_down)
    grad_mlp_down = left_dot(mlp_normed, middle_low)
    unused_first, first_back = jax.vjp(rms_norm, first, mlp_gain_f)
    first_norm_grad, grad_mlp_gain = first_back(mlp_normed_grad)
    first_grad = second_grad + first_norm_grad
    branch_grad = (own_valid * first_grad).astype(jnp.bfloat16)
    grad_attn_proj = left_dot(attended, branch_grad)
    attended_grad = right_dot(branch_grad, attn_proj).reshape(row_count, head_count, HDIM)
    probs_back = head_probs(queries, keys_all, allowed)
    score_scale = HDIM ** (-0.5)
    out_low = attended_grad.astype(jnp.bfloat16)
    prob_grad = jnp.einsum("thd,shd->hts", out_low, values_all, preferred_element_type=jnp.float32)
    score_grad = probs_back * (prob_grad - jnp.sum(probs_back * prob_grad, -1, keepdims=True))
    score_low = score_grad.astype(jnp.bfloat16)
    query_back = (
        jnp.einsum("hts,shd->thd", score_low, keys_all, preferred_element_type=jnp.float32)
        * score_scale
    )
    keys_back = (
        jnp.einsum("hts,thd->shd", score_low, queries, preferred_element_type=jnp.float32)
        * score_scale
    )
    values_back = jnp.einsum(
        "hts,thd->shd", probs_back.astype(jnp.bfloat16), out_low, preferred_element_type=jnp.float32
    )
    keys_grad_own, values_grad_own = (
        lax.psum_scatter(keys_back, STATE, scatter_dimension=0, tiled=True),
        lax.psum_scatter(values_back, STATE, scatter_dimension=0, tiled=True),
    )
    query_grad = (
        rotate(query_back, -own_position).reshape(row_count, head_count * HDIM).astype(jnp.bfloat16)
    )
    key_grad = (
        rotate(keys_grad_own, -own_position)
        .reshape(row_count, head_count * HDIM)
        .astype(jnp.bfloat16)
    )
    value_grad = values_grad_own.reshape(row_count, head_count * HDIM).astype(jnp.bfloat16)
    grad_query_main = left_dot(normed, query_grad)
    grad_key_main = left_dot(normed, key_grad)
    grad_value_main = left_dot(normed, value_grad)
    grad_query_upper = left_dot(query_red, query_grad)
    grad_key_upper = left_dot(key_red, key_grad)
    grad_value_upper = left_dot(value_red, value_grad)
    query_middle = right_dot(query_grad, query_upper)
    key_middle = right_dot(key_grad, key_upper)
    value_middle = right_dot(value_grad, value_upper)
    normed_part = (
        right_dot(query_grad, query_main)
        + right_dot(key_grad, key_main)
        + right_dot(value_grad, value_main)
    )
    normed_sum, query_msum, key_msum, value_msum = lax.psum(
        (normed_part, query_middle, key_middle, value_middle), HEAD
    )
    query_low = query_msum.astype(jnp.bfloat16)
    key_low = key_msum.astype(jnp.bfloat16)
    value_low = value_msum.astype(jnp.bfloat16)
    normed_grad = (
        normed_sum
        + right_dot(query_low, query_down)
        + right_dot(key_low, key_down)
        + right_dot(value_low, value_down)
    )
    grad_query_down = left_dot(normed, query_low)
    grad_key_down = left_dot(normed, key_low)
    grad_value_down = left_dot(normed, value_low)
    unused_joined, joined_back = jax.vjp(rms_norm, joined, attn_gain_f)
    joined_grad, grad_attn_gain = joined_back(normed_grad)
    grad_hidden = (first_grad + joined_grad[:, :model_width]).astype(jnp.bfloat16)
    grad_embedding = joined_grad[:, model_width:].astype(jnp.bfloat16)
    scattered = (
        lax.psum_scatter(grad_attn_gain, ZED, scatter_dimension=0, tiled=True),
        lax.psum_scatter(grad_query_main, ZED, scatter_dimension=0, tiled=True),
        lax.psum_scatter(grad_key_main, ZED, scatter_dimension=0, tiled=True),
        lax.psum_scatter(grad_value_main, ZED, scatter_dimension=0, tiled=True),
        lax.psum_scatter(grad_query_down, ZED, scatter_dimension=0, tiled=True),
        lax.psum_scatter(grad_key_down, ZED, scatter_dimension=0, tiled=True),
        lax.psum_scatter(grad_value_down, ZED, scatter_dimension=0, tiled=True),
        lax.psum_scatter(grad_query_upper, ZED, scatter_dimension=0, tiled=True),
        lax.psum_scatter(grad_key_upper, ZED, scatter_dimension=0, tiled=True),
        lax.psum_scatter(grad_value_upper, ZED, scatter_dimension=0, tiled=True),
        lax.psum_scatter(grad_attn_proj, ZED, scatter_dimension=1, tiled=True),
        lax.psum_scatter(grad_mlp_gain, ZED, scatter_dimension=0, tiled=True),
        lax.psum_scatter(grad_mlp_main, ZED, scatter_dimension=0, tiled=True),
        lax.psum_scatter(grad_mlp_down, ZED, scatter_dimension=0, tiled=True),
        lax.psum_scatter(grad_mlp_upper, ZED, scatter_dimension=0, tiled=True),
        lax.psum_scatter(grad_mlp_proj, ZED, scatter_dimension=1, tiled=True),
        lax.psum_scatter(grad_mixer_gain, ZED, scatter_dimension=0, tiled=True),
        lax.psum_scatter(grad_inner_main, ZED, scatter_dimension=0, tiled=True),
        lax.psum_scatter(grad_gate_main, ZED, scatter_dimension=0, tiled=True),
        lax.psum_scatter(grad_step_main, ZED, scatter_dimension=0, tiled=True),
        lax.psum_scatter(grad_output_main, ZED, scatter_dimension=1, tiled=True),
    )
    first_head = (head_index == 0).astype(jnp.float32)
    square_sum = jnp.zeros((), jnp.float32)
    for index in [1, 2, 3, 7, 8, 9, 10, 12, 14, 15]:
        square_sum = square_sum + jnp.sum(scattered[index] * scattered[index])
    for index in [4, 5, 6, 13]:
        square_sum = square_sum + first_head * jnp.sum(scattered[index] * scattered[index])
    head_params = jnp.stack([grad_shift, grad_rate, grad_skip], 0)
    totals = lax.psum(
        (
            square_sum,
            place_slice(grad_gated_gain, head_index, head_parts, 0),
            place_slice(grad_taps_x, head_index, head_parts, 1),
            place_slice(head_params, head_index, head_parts, 1),
            place_slice(grad_input_half, state_index, state_parts, 1),
            place_slice(grad_read_half, state_index, state_parts, 1),
            place_slice(grad_taps_b, state_index, state_parts, 1),
            place_slice(grad_taps_c, state_index, state_parts, 1),
        ),
        EVERY,
    )
    (
        square_total,
        gated_full,
        taps_full,
        heads_full,
        input_full,
        read_full,
        taps_input_full,
        taps_read_full,
    ) = totals
    head_width = gain_gated.shape[0]
    tap_width = taps_inner.shape[1]
    param_width = step_bias.shape[0]
    heads_own = take_slice(heads_full, head_index, param_width, 1)
    return (
        layer_out,
        grad_hidden,
        grad_embedding,
        scattered[0],
        scattered[1],
        scattered[2],
        scattered[3],
        scattered[4],
        scattered[5],
        scattered[6],
        scattered[7],
        scattered[8],
        scattered[9],
        scattered[10],
        scattered[11],
        scattered[12],
        scattered[13],
        scattered[14],
        scattered[15],
        scattered[16],
        scattered[17],
        scattered[18],
        scattered[19],
        input_full,
        read_full,
        take_slice(taps_full, head_index, tap_width, 1),
        taps_input_full,
        taps_read_full,
        heads_own[0],
        heads_own[1],
        heads_own[2],
        take_slice(gated_full, head_index, head_width, 0),
        scattered[20],
        jnp.sqrt(square_total),
    )


low = jnp.bfloat16
full = jnp.float32


def head_masks():
    count = lax.axis_size(HEAD)
    masks = [1 << bit for bit in range(count.bit_length() - 1)]
    return masks[:1] + masks[1:], masks[:1] + masks[1:][::-1]


def head_swap(value, mask):
    count = lax.axis_size(HEAD)
    return lax.ppermute(value, HEAD, [(i, i ^ mask) for i in range(count)])


def state_swap(value):
    return lax.ppermute(value, STATE, [(0, 1), (1, 0)])


def dp_swap(value):
    return lax.ppermute(value, DP, [(0, 1), (1, 0)])


def state_forward(value):
    return lax.ppermute(value, STATE, [(0, 1)])


def state_backward(value):
    return lax.ppermute(value, STATE, [(1, 0)])


def bit_of(mask):
    return (lax.axis_index(HEAD) // mask) % 2


def chunk_of(masks):
    chunk = 0
    for mask in masks:
        chunk = chunk * 2 + bit_of(mask)
    return chunk


def sum_rows(value, masks, axis):
    for mask in masks:
        bit = bit_of(mask)
        half = value.shape[axis] // 2
        away = lax.dynamic_slice_in_dim(value, (1 - bit) * half, half, axis).astype(low)
        kept = lax.dynamic_slice_in_dim(value, bit * half, half, axis)
        value = kept.astype(full) + head_swap(away, mask).astype(full)
    return value


def gather_rows(value, masks, axis):
    for mask in masks[::-1]:
        bit = bit_of(mask)
        got = head_swap(value, mask)
        value = jnp.concatenate(
            [jnp.where(bit == 1, got, value), jnp.where(bit == 1, value, got)], axis
        )
    return value


def sum_row16(value, masks):
    state = lax.axis_index(STATE)
    value = sum_rows(value, masks, 1)
    away = lax.dynamic_index_in_dim(value, 1 - state, 0, False).astype(low)
    kept = lax.dynamic_index_in_dim(value, state, 0, False)
    return kept + state_swap(away).astype(full)


def gather_row16(value, masks):
    state = lax.axis_index(STATE)
    got = state_swap(value)
    both = jnp.stack([jnp.where(state == 0, value, got), jnp.where(state == 0, got, value)], 0)
    return gather_rows(both, masks, 1)


def pick_state(pair, index):
    return jnp.where(index == 0, pair[0], pair[1])


def weight_pieces(shard, axis):
    state = lax.axis_index(STATE)
    dp = lax.axis_index(DP)
    half = shard.shape[axis] // 2
    mine = lax.dynamic_slice_in_dim(shard, state * half, half, axis)
    got = state_swap(lax.dynamic_slice_in_dim(shard, (1 - state) * half, half, axis))
    far_mine = dp_swap(mine)
    far_got = dp_swap(got)
    near = [jnp.where(state == 0, mine, got), jnp.where(state == 0, got, mine)]
    far = [jnp.where(state == 0, far_mine, far_got), jnp.where(state == 0, far_got, far_mine)]
    lower = [jnp.where(dp == 0, a, b) for a, b in zip(near, far)]
    upper = [jnp.where(dp == 0, b, a) for a, b in zip(near, far)]
    return jnp.concatenate(lower + upper, 1 - axis)


def grad_pieces(grad, axis):
    state = lax.axis_index(STATE)
    dp = lax.axis_index(DP)
    half = grad.shape[1 - axis] // 2
    away = lax.dynamic_slice_in_dim(grad, (1 - dp) * half, half, 1 - axis).astype(low)
    kept = lax.dynamic_slice_in_dim(grad, dp * half, half, 1 - axis)
    total = kept + dp_swap(away).astype(full)
    quarter = half // 2
    away = lax.dynamic_slice_in_dim(total, (1 - state) * quarter, quarter, 1 - axis).astype(low)
    kept = lax.dynamic_slice_in_dim(total, state * quarter, quarter, 1 - axis)
    got = state_swap(away).astype(full)
    return jnp.concatenate(
        [jnp.where(state == 0, kept, got), jnp.where(state == 0, got, kept)], axis
    )


def norm_scale(values):
    return lax.rsqrt(jnp.mean(values * values, -1, keepdims=True) + epsilon)


def norm_back(values, gain, grad):
    scale = norm_scale(values)
    scaled = grad * gain
    inner = jnp.mean(scaled * values, -1, keepdims=True)
    return (
        scale * scaled - values * (scale * scale * scale * inner),
        jnp.sum(grad * values * scale, 0),
    )


def conv_edge(values, edge, taps, segment, edge_segment):
    reach = taps.shape[0] - 1
    rows = values.shape[0]
    joined = jnp.concatenate([edge, values], 0)
    segs = jnp.concatenate([edge_segment, segment], 0)
    total = taps[0][None, :] * values
    for offset in range(1, taps.shape[0]):
        lower = reach - offset
        same = (segs[lower : lower + rows] == segment).astype(values.dtype)[:, None]
        total = total + taps[offset][None, :] * joined[lower : lower + rows] * same
    return total


def vmem_limit(mebibytes):
    return pltpu.CompilerParams(vmem_limit_bytes=mebibytes * 1024 * 1024)


def dot_nt(left, right):
    return lax.dot_general(left, right, (((1,), (1,)), ((), ())), preferred_element_type=full)


def dot_tn(left, right):
    return lax.dot_general(left, right, (((0,), (0,)), ((), ())), preferred_element_type=full)


def dot_nn(left, right):
    return lax.dot_general(left, right, (((1,), (0,)), ((), ())), preferred_element_type=full)


def dot_exact(left, right):
    return jnp.dot(left, right, preferred_element_type=full, precision=highest)


ROWS_Q = 256
ROWS_K = 512


def attend_kernel(low_ref, q_ref, k_ref, v_ref, seg_col, seg_row, out_ref, lse_ref):
    index = pl.program_id(1)
    scale = q_ref.shape[1] ** (-0.5)
    query = q_ref[...]
    own = seg_col[...]
    place = index * ROWS_Q + lax.broadcasted_iota(jnp.int32, (ROWS_Q, ROWS_K), 0)

    def step(block, carry):
        top, total, acc = carry
        span = pl.ds(pl.multiple_of(block * ROWS_K, ROWS_K), ROWS_K)
        scores = dot_nt(query, k_ref[span, :]) * scale
        other = block * ROWS_K + lax.broadcasted_iota(jnp.int32, (ROWS_Q, ROWS_K), 1)
        scores = jnp.where((own == seg_row[:, span]) & (other <= place), scores, -1e30)
        higher = jnp.maximum(top, jnp.max(scores, -1, keepdims=True))
        weights = jnp.exp(scores - higher)
        fade = jnp.exp(top - higher)
        total = total * fade + jnp.sum(weights, -1, keepdims=True)
        acc = acc * fade + dot_nn(weights.astype(low), v_ref[span, :])
        return higher, total, acc

    start = (
        jnp.full((ROWS_Q, 1), -1e30, full),
        jnp.zeros((ROWS_Q, 1), full),
        jnp.zeros((ROWS_Q, v_ref.shape[1]), full),
    )
    stop = (index * ROWS_Q + ROWS_Q + ROWS_K - 1) // ROWS_K
    top, total, acc = lax.fori_loop(low_ref[index], stop, step, start)
    out_ref[...] = (acc / total).astype(low)
    lse = jnp.broadcast_to(top + jnp.log(total), (ROWS_Q, 128))
    lse_ref[...] = lse.T[0:1, :][None]


def half_block(index, blocks):
    per_state = blocks // 2
    per_half = per_state // 2
    inside = index % per_state
    return inside // per_half * per_state + index // per_state * per_half + inside % per_half


def attend(queries, keys, values, segment, lows):
    length, columns = queries.shape
    heads = columns // HDIM
    blocks = length // ROWS_Q
    whole = pl.BlockSpec((length, HDIM), lambda h, i, *_: (0, h))
    block = pl.BlockSpec((ROWS_Q, HDIM), lambda h, i, *_: (i, h))
    placed = pl.BlockSpec((ROWS_Q, HDIM), lambda h, i, *_: (half_block(i, blocks), h))
    return pl.pallas_call(
        attend_kernel,
        grid_spec=pltpu.PrefetchScalarGridSpec(
            num_scalar_prefetch=1,
            grid=(heads, length // ROWS_Q),
            in_specs=[
                block,
                whole,
                whole,
                pl.BlockSpec((ROWS_Q, 1), lambda h, i, *_: (i, 0)),
                pl.BlockSpec((1, length), lambda h, i, *_: (0, 0)),
            ],
            out_specs=[placed, pl.BlockSpec((1, 1, ROWS_Q), lambda h, i, *_: (h, 0, i))],
        ),
        out_shape=[
            jax.ShapeDtypeStruct((length, columns), low),
            jax.ShapeDtypeStruct((heads, 1, length), full),
        ],
        compiler_params=vmem_limit(40),
        cost_estimate=pl.CostEstimate(
            flops=22 * length * length * columns, bytes_accessed=8 * length * columns,
            transcendentals=0,
        ),
    )(lows, queries, keys, values, segment[:, None], segment[None, :])


def attend_back_kernel(
    low_ref, q_ref, k_ref, v_ref, do_ref, o_ref, lse_ref, seg_col, seg_row, dq_ref, dk_ref, dv_ref
):
    index = pl.program_id(1)
    scale = q_ref.shape[1] ** (-0.5)
    query = q_ref[...]
    grad = do_ref[...]
    own = seg_row[...]
    lse = lse_ref[0]
    ones = jnp.ones((8, HDIM), full)
    delta = lax.dot_general(
        ones,
        grad.astype(full) * o_ref[...].astype(full),
        (((1,), (1,)), ((), ())),
        precision=highest,
        preferred_element_type=full,
    )[0:1, :]
    place = index * ROWS_Q + lax.broadcasted_iota(jnp.int32, (ROWS_K, ROWS_Q), 1)

    @pl.when(index == 0)
    def clear():
        dk_ref[...] = jnp.zeros_like(dk_ref)
        dv_ref[...] = jnp.zeros_like(dv_ref)

    def step(block, total):
        span = pl.ds(pl.multiple_of(block * ROWS_K, ROWS_K), ROWS_K)
        key = k_ref[span, :]
        scores = dot_nt(key, query) * scale
        other = block * ROWS_K + lax.broadcasted_iota(jnp.int32, (ROWS_K, ROWS_Q), 0)
        counted = (seg_col[span, :] == own) & (other <= place)
        probs = jnp.exp(jnp.where(counted, scores - lse, -1e30))
        dv_ref[span, :] += dot_nn(probs.astype(low), grad)
        slope = probs * (dot_nt(v_ref[span, :], grad) - delta)
        slope = slope.astype(low)
        dk_ref[span, :] += dot_nn(slope, query) * scale
        return total + dot_tn(slope, key)

    stop = (index * ROWS_Q + ROWS_Q + ROWS_K - 1) // ROWS_K
    total = lax.fori_loop(low_ref[index], stop, step, jnp.zeros((ROWS_Q, HDIM), full))
    dq_ref[...] = total * scale


def attend_back(queries, keys, values, grads, outs, lse, segment, lows):
    length, columns = queries.shape
    heads = columns // HDIM
    blocks = length // ROWS_Q
    whole = pl.BlockSpec((length, HDIM), lambda h, i, *_: (0, h))
    block = pl.BlockSpec((ROWS_Q, HDIM), lambda h, i, *_: (i, h))
    placed = pl.BlockSpec((ROWS_Q, HDIM), lambda h, i, *_: (half_block(i, blocks), h))
    line = pl.BlockSpec((1, 1, ROWS_Q), lambda h, i, *_: (h, 0, i))
    shape = jax.ShapeDtypeStruct((length, columns), full)
    return pl.pallas_call(
        attend_back_kernel,
        grid_spec=pltpu.PrefetchScalarGridSpec(
            num_scalar_prefetch=1,
            grid=(heads, length // ROWS_Q),
            in_specs=[
                block,
                whole,
                whole,
                placed,
                placed,
                line,
                pl.BlockSpec((length, 1), lambda h, i, *_: (0, 0)),
                pl.BlockSpec((1, ROWS_Q), lambda h, i, *_: (0, i)),
            ],
            out_specs=[block, whole, whole],
        ),
        out_shape=[shape, shape, shape],
        compiler_params=vmem_limit(40),
        cost_estimate=pl.CostEstimate(
            flops=30 * length * length * columns, bytes_accessed=20 * length * columns,
            transcendentals=0,
        ),
    )(lows, queries, keys, values, grads, outs, lse, segment[:, None], segment[None, :])


def rope_kernel(state_ref, own_ref, other_ref, cos_ref, sin_ref, q_ref, k_ref, v_ref):
    per_state = pl.num_programs(0) // 2
    own = pl.program_id(0) // per_state == state_ref[0]
    columns = q_ref.shape[1]
    for index, out in enumerate((q_ref, k_ref, v_ref)):
        for start in range(0, columns, HDIM):
            lanes = slice(index * columns + start, index * columns + start + HDIM)
            value = jnp.where(own, own_ref[:, lanes], other_ref[:, lanes])
            if index < 2:
                value = value * cos_ref[...] + pltpu.roll(value, HDIM // 2, 1) * sin_ref[...]
            out[:, start : start + HDIM] = value.astype(low)


def rope(state, own, other, cosine, sine):
    length = cosine.shape[0]
    columns = own.shape[1] // 3
    per_state = length // ROWS_Q // 2
    part = pl.BlockSpec((ROWS_Q, own.shape[1]), lambda i, *_: (i % per_state, 0))
    angle = pl.BlockSpec((ROWS_Q, HDIM), lambda i, *_: (i, 0))
    out = pl.BlockSpec((ROWS_Q, columns), lambda i, *_: (i, 0))
    return pl.pallas_call(
        rope_kernel,
        grid_spec=pltpu.PrefetchScalarGridSpec(
            num_scalar_prefetch=1,
            grid=(length // ROWS_Q,),
            in_specs=[part, part, angle, angle],
            out_specs=[out] * 3,
        ),
        out_shape=[jax.ShapeDtypeStruct((length, columns), low)] * 3,
        compiler_params=vmem_limit(32),
        cost_estimate=pl.CostEstimate(
            flops=12 * length * columns, bytes_accessed=36 * length * columns, transcendentals=0
        ),
    )(state[None], own, other, cosine, sine)


def rope_back_kernel(q_ref, k_ref, v_ref, cos_ref, sin_ref, out_ref):
    columns = q_ref.shape[1]
    for index, part in enumerate((q_ref, k_ref, v_ref)):
        for start in range(0, columns, HDIM):
            value = part[:, start : start + HDIM]
            if index < 2:
                value = value * cos_ref[...] - pltpu.roll(value, HDIM // 2, 1) * sin_ref[...]
            lanes = slice(index * columns + start, index * columns + start + HDIM)
            out_ref[:, lanes] = value.astype(low)


def rope_back(query, key, value, cosine, sine):
    length, columns = query.shape
    blocks = length // ROWS_Q
    part = pl.BlockSpec((ROWS_Q, columns), lambda i: (i, 0))
    angle = pl.BlockSpec((ROWS_Q, HDIM), lambda i: (i, 0))
    return pl.pallas_call(
        rope_back_kernel,
        grid=(blocks,),
        in_specs=[part, part, part, angle, angle],
        out_specs=pl.BlockSpec((ROWS_Q, 3 * columns), lambda i: (half_block(i, blocks), 0)),
        out_shape=jax.ShapeDtypeStruct((length, 3 * columns), low),
        compiler_params=vmem_limit(32),
        cost_estimate=pl.CostEstimate(
            flops=12 * length * columns, bytes_accessed=24 * length * columns, transcendentals=0
        ),
    )(query, key, value, cosine, sine)


def hold_kernel(*refs):
    pass


def hold(value, *after, cost=0):
    anywhere = pl.BlockSpec(memory_space=pl.ANY)
    return pl.pallas_call(
        hold_kernel,
        in_specs=[anywhere] * (1 + len(after)),
        out_specs=anywhere,
        out_shape=jax.ShapeDtypeStruct(value.shape, value.dtype),
        input_output_aliases={0: 0},
        cost_estimate=pl.CostEstimate(
            flops=cost * 1_100_000_000, bytes_accessed=0, transcendentals=0
        ),
    )(value, *after)


def first_blocks(segment):
    length = segment.shape[0]
    heads = segment[::ROWS_Q]
    starts = jnp.sum((segment[None, :] < heads[:, None]).astype(jnp.int32), 1)
    return starts // ROWS_K


def pair_lanes(left, right):
    lane = lax.broadcasted_iota(jnp.int32, (1, 2 * MDIM), 1)
    return jnp.where(lane < MDIM, left, right)


def block_decay(dt_ref, dt_row_ref, rate_ref, rate_col_ref):
    rows = lax.broadcasted_iota(jnp.int32, (GROUP, GROUP), 0)
    cols = lax.broadcasted_iota(jnp.int32, (GROUP, GROUP), 1)
    cumul = dot_exact((cols <= rows).astype(full), dt_ref[...] * rate_ref[...])
    cumul_row = dot_exact(dt_row_ref[...] * rate_col_ref[...], (rows <= cols).astype(full))
    return cumul, cumul_row, rows, cols


def edge_flags(ends_ref, index, seg_col):
    before = ends_ref[index]
    last = ends_ref[index + 1]
    carried = (seg_col[...] == before).astype(full)
    reach = (seg_col[...] == last).astype(full)
    keep = (before == last).astype(full)
    return carried, reach, keep


def pair_columns(values, pair):
    return pair_lanes(values[:, 2 * pair : 2 * pair + 1], values[:, 2 * pair + 1 : 2 * pair + 2])


def step_state(state, pair, scaled, cumul, reach, keep, vec_low):
    column = pair_columns(cumul, pair)
    end = column[GROUP - 1 : GROUP, :]
    weight = jnp.exp(end - column) * reach
    return state * (jnp.exp(end) * keep) + dot_tn(vec_low, (scaled * weight).astype(low)), weight


def scan_end_kernel(
    ends_ref, x_ref, dt_ref, dt_row_ref, rate_ref, rate_col_ref, b_ref, seg_col, out_ref
):
    index = pl.program_id(0)
    cumul, unused_row, unused_a, unused_b = block_decay(dt_ref, dt_row_ref, rate_ref, rate_col_ref)
    unused_c, reach, keep = edge_flags(ends_ref, index, seg_col)
    vec_low = b_ref[...].astype(low)

    @pl.when(index == 0)
    def clear():
        out_ref[...] = jnp.zeros_like(out_ref)

    for pair in range(dt_ref.shape[1] // 2):
        lanes = slice(pair * 2 * MDIM, (pair + 1) * 2 * MDIM)
        scaled = x_ref[:, lanes] * pair_columns(dt_ref[...], pair)
        out_ref[:, lanes], unused_d = step_state(
            out_ref[:, lanes], pair, scaled, cumul, reach, keep, vec_low
        )


def scan_kernel(
    ends_ref,
    x_ref,
    dt_ref,
    dt_row_ref,
    rate_ref,
    rate_col_ref,
    b_ref,
    c_ref,
    seg_col,
    seg_row,
    first_ref,
    out_ref,
    states_ref,
    state,
):
    index = pl.program_id(0)
    cumul, cumul_row, rows, cols = block_decay(dt_ref, dt_row_ref, rate_ref, rate_col_ref)
    carried, reach, keep = edge_flags(ends_ref, index, seg_col)
    vec_low = b_ref[...].astype(low)
    read_low = c_ref[...].astype(low)
    allowed = (seg_col[...] == seg_row[...]) & (cols <= rows)
    inner = jnp.where(allowed, dot_nt(read_low, vec_low), 0.0)

    @pl.when(index == 0)
    def begin():
        state[...] = first_ref[...]

    states_ref[0] = state[...]
    for pair in range(dt_ref.shape[1] // 2):
        lanes = slice(pair * 2 * MDIM, (pair + 1) * 2 * MDIM)
        scaled = x_ref[:, lanes] * pair_columns(dt_ref[...], pair)
        scaled_low = scaled.astype(low)
        parts = []
        for head in (2 * pair, 2 * pair + 1):
            gaps = cumul[:, head : head + 1] - cumul_row[head : head + 1, :]
            mixed = inner * jnp.exp(jnp.minimum(gaps, 0.0))
            parts.append(dot_nn(mixed.astype(low), scaled_low))
        entry = jnp.exp(pair_columns(cumul, pair)) * carried
        held = state[:, lanes]
        out_ref[:, lanes] = pair_lanes(*parts) + dot_nn(read_low, held.astype(low)) * entry
        state[:, lanes], unused = step_state(
            held, pair, scaled, cumul, reach, keep, vec_low
        )


def scan_start_grad_kernel(
    ends_ref, dt_ref, dt_row_ref, rate_ref, rate_col_ref, c_ref, seg_col, dy_ref, out_ref
):
    index = pl.num_programs(0) - 1 - pl.program_id(0)
    cumul, unused_row, unused_a, unused_b = block_decay(dt_ref, dt_row_ref, rate_ref, rate_col_ref)
    carried, unused_c, keep = edge_flags(ends_ref, index, seg_col)
    read_low = c_ref[...].astype(low)

    @pl.when(pl.program_id(0) == 0)
    def clear():
        out_ref[...] = jnp.zeros_like(out_ref)

    for pair in range(dt_ref.shape[1] // 2):
        lanes = slice(pair * 2 * MDIM, (pair + 1) * 2 * MDIM)
        column = pair_columns(cumul, pair)
        retain = jnp.exp(column[GROUP - 1 : GROUP, :]) * keep
        entry = jnp.exp(column) * carried
        out_ref[:, lanes] = out_ref[:, lanes] * retain + dot_tn(
            read_low, (dy_ref[:, lanes] * entry).astype(low)
        )


def scan_back_kernel(
    ends_ref,
    x_ref,
    dt_ref,
    dt_row_ref,
    rate_ref,
    rate_col_ref,
    b_ref,
    c_ref,
    seg_col,
    seg_row,
    dy_ref,
    states_ref,
    last_ref,
    dx_ref,
    ddt_ref,
    dlog_ref,
    dlog_row_ref,
    db_ref,
    dc_ref,
    state_grad,
    inner_grad,
):
    index = pl.num_programs(0) - 1 - pl.program_id(0)
    heads = dt_ref.shape[1]
    cumul, cumul_row, rows, cols = block_decay(dt_ref, dt_row_ref, rate_ref, rate_col_ref)
    carried, reach, keep = edge_flags(ends_ref, index, seg_col)
    vec_low = b_ref[...].astype(low)
    read_low = c_ref[...].astype(low)
    allowed = (seg_col[...] == seg_row[...]) & (cols <= rows)
    inner = jnp.where(allowed, dot_nt(read_low, vec_low), 0.0)
    head_lane = lax.broadcasted_iota(jnp.int32, (GROUP, heads), 1)
    head_row = lax.broadcasted_iota(jnp.int32, (heads, GROUP), 0)
    last_row = lax.broadcasted_iota(jnp.int32, (GROUP, 1), 0) == GROUP - 1
    lane = lax.broadcasted_iota(jnp.int32, (1, 2 * MDIM), 1)

    @pl.when(pl.program_id(0) == 0)
    def begin():
        state_grad[...] = last_ref[...]

    inner_grad[...] = jnp.zeros_like(inner_grad)
    decay_grad = jnp.zeros((GROUP, heads), full)
    decay_row = jnp.zeros((heads, GROUP), full)
    step_grad = jnp.zeros((GROUP, heads), full)
    vec_grad = jnp.zeros(b_ref.shape, full)
    read_grad = jnp.zeros(c_ref.shape, full)
    for pair in range(heads // 2):
        lanes = slice(pair * 2 * MDIM, (pair + 1) * 2 * MDIM)
        values = x_ref[:, lanes]
        steps = pair_columns(dt_ref[...], pair)
        scaled = values * steps
        scaled_low = scaled.astype(low)
        grad = dy_ref[:, lanes]
        grad_low = grad.astype(low)
        held = states_ref[0, :, lanes]
        held_low = held.astype(low)
        later = state_grad[:, lanes]
        later_low = later.astype(low)
        column = pair_columns(cumul, pair)
        end = column[GROUP - 1 : GROUP, :]
        weight = jnp.exp(end - column) * reach
        retain = jnp.exp(end) * keep
        entry = jnp.exp(column) * carried
        parts = []
        for side in range(2):
            head = 2 * pair + side
            gaps = cumul[:, head : head + 1] - cumul_row[head : head + 1, :]
            fading = jnp.where(allowed, jnp.exp(jnp.minimum(gaps, 0.0)), 0.0)
            mixed = inner * fading
            own_lanes = (lane < MDIM) == (side == 0)
            outer = dot_nt(jnp.where(own_lanes, grad, 0.0).astype(low), scaled_low)
            inner_grad[...] += outer * fading
            slope = outer * mixed
            decay_grad = jnp.where(
                head_lane == head, decay_grad + jnp.sum(slope, 1, keepdims=True), decay_grad
            )
            decay_row = jnp.where(
                head_row == head, jnp.sum(slope, 0, keepdims=True), decay_row
            )
            parts.append(dot_tn(mixed.astype(low), grad_low))
        weighted = scaled * weight
        entered = grad * entry
        entered_low = entered.astype(low)
        from_later = dot_nn(vec_low, later_low)
        scaled_grad = pair_lanes(*parts) + weight * from_later
        dx_ref[:, lanes] = scaled_grad * steps
        read_grad += dot_nt(entered_low, held_low)
        vec_grad += dot_nt(weighted.astype(low), later_low)
        fresh = weighted * from_later
        flow = entered * dot_nn(read_low, held_low) - fresh
        finish = jnp.sum(fresh, 0, keepdims=True) + retain * jnp.sum(later * held, 0, keepdims=True)
        steps_part = scaled_grad * values
        for side in range(2):
            head = 2 * pair + side
            own_lanes = (lane < MDIM) == (side == 0)
            total = jnp.sum(jnp.where(own_lanes, flow, 0.0), 1, keepdims=True)
            ending = jnp.sum(jnp.where(own_lanes, finish, 0.0), 1, keepdims=True)
            total = total + jnp.where(last_row, ending, 0.0)
            decay_grad = jnp.where(head_lane == head, decay_grad + total, decay_grad)
            step_grad = jnp.where(
                head_lane == head,
                jnp.sum(jnp.where(own_lanes, steps_part, 0.0), 1, keepdims=True),
                step_grad,
            )
        state_grad[:, lanes] = later * retain + dot_tn(read_low, entered_low)
    inner_low = inner_grad[...].astype(low)
    ddt_ref[...] = step_grad
    dlog_ref[...] = dot_exact((cols >= rows).astype(full), decay_grad)
    dlog_row_ref[...] = dot_exact(decay_row, (rows >= cols).astype(full))
    dc_ref[...] = read_grad + dot_nn(inner_low, vec_low)
    db_ref[...] = vec_grad + dot_tn(inner_low, read_low)


def scan_specs(heads, channels, states, reverse, count):
    def at(i):
        return count - 1 - i if reverse else i

    tall = lambda columns: pl.BlockSpec((GROUP, columns), lambda i, *_: (at(i), 0))
    flat = lambda rows: pl.BlockSpec((rows, GROUP), lambda i, *_: (0, at(i)))
    same = lambda rows, columns: pl.BlockSpec((rows, columns), lambda i, *_: (0, 0))
    return tall, flat, same, pl.BlockSpec((1, states, channels), lambda i, *_: (at(i), 0, 0))


def scan_call(kernel, reverse, ends, inputs, kinds, outs, out_kinds, scratch, dims, flops):
    heads, channels, states, count = dims
    tall, flat, same, cube = scan_specs(heads, channels, states, reverse, count)

    def spec(kind, shape):
        if kind == 0:
            return tall(shape[1])
        if kind == 1:
            return flat(shape[0])
        return same(*shape) if kind == 2 else cube

    return pl.pallas_call(
        kernel,
        grid_spec=pltpu.PrefetchScalarGridSpec(
            num_scalar_prefetch=1,
            grid=(count,),
            in_specs=[spec(kind, value.shape) for kind, value in zip(kinds, inputs)],
            out_specs=[spec(kind, shape) for kind, shape in zip(out_kinds, outs)],
            scratch_shapes=scratch,
        ),
        out_shape=[jax.ShapeDtypeStruct(shape, full) for shape in outs],
        compiler_params=vmem_limit(40),
        cost_estimate=pl.CostEstimate(
            flops=flops, bytes_accessed=8 * count * GROUP * channels, transcendentals=0
        ),
    )(ends, *inputs)


class Scan:
    def __init__(self, x, dt, rate, b, c, segment, before):
        self.rows, self.heads = dt.shape
        self.channels, self.states = x.shape[1], b.shape[1]
        self.count = self.rows // GROUP
        self.dims = (self.heads, self.channels, self.states, self.count)
        self.ends = jnp.concatenate([before[None], segment[GROUP - 1 :: GROUP]])
        self.x, self.b, self.c = x, b, c
        self.decay = [dt, dt.T, rate[None, :], rate[:, None]]
        self.seg_col, self.seg_row = segment[:, None], segment[None, :]
        self.state_shape = (self.states, self.channels)

    def end(self):
        return scan_call(
            scan_end_kernel,
            False,
            self.ends,
            [self.x, *self.decay, self.b, self.seg_col],
            [0, 0, 1, 2, 2, 0, 0],
            [self.state_shape],
            [2],
            [],
            self.dims,
            160 * self.rows * self.channels * self.states,
        )[0]

    def forward(self, first):
        return scan_call(
            scan_kernel,
            False,
            self.ends,
            [self.x, *self.decay, self.b, self.c, self.seg_col, self.seg_row, first],
            [0, 0, 1, 2, 2, 0, 0, 0, 1, 2],
            [self.x.shape, (self.count,) + self.state_shape],
            [0, 3],
            [pltpu.VMEM(self.state_shape, full)],
            self.dims,
            56 * self.rows * self.channels * GROUP,
        )

    def start_grad(self, grad):
        return scan_call(
            scan_start_grad_kernel,
            True,
            self.ends,
            [*self.decay, self.c, self.seg_col, grad],
            [0, 1, 2, 2, 0, 0, 0],
            [self.state_shape],
            [2],
            [],
            self.dims,
            160 * self.rows * self.channels * self.states,
        )[0]

    def backward(self, grad, states, last):
        wide = (self.rows, self.heads)
        return scan_call(
            scan_back_kernel,
            True,
            self.ends,
            [
                self.x,
                *self.decay,
                self.b,
                self.c,
                self.seg_col,
                self.seg_row,
                grad,
                states,
                last,
            ],
            [0, 0, 1, 2, 2, 0, 0, 0, 1, 0, 3, 2],
            [self.x.shape, wide, wide, wide[::-1], self.b.shape, self.c.shape],
            [0, 0, 0, 1, 0, 0],
            [pltpu.VMEM(self.state_shape, full), pltpu.VMEM((GROUP, GROUP), full)],
            self.dims,
            144 * self.rows * self.channels * GROUP,
        )


def natural_quarters(relative):
    state = lax.axis_index(STATE)
    dp = lax.axis_index(DP)
    near = [jnp.where(state == 0, *relative[:2]), jnp.where(state == 0, *relative[1::-1])]
    far = [jnp.where(state == 0, *relative[2:]), jnp.where(state == 0, *relative[:1:-1])]
    return [jnp.where(dp == 0, a, b) for a, b in zip(near, far)] + [
        jnp.where(dp == 0, b, a) for a, b in zip(near, far)
    ]


def natural_heads(value):
    count = lax.axis_size(HEAD).bit_length() - 1
    cubes = value.reshape((2,) * count + value.shape[1:])
    turned = list(range(count - 1, -1, -1)) + list(range(count, cubes.ndim))
    return cubes.transpose(turned).reshape(value.shape)


def cut_rows(value, order, axis):
    bit = bit_of(order[0])
    half = value.shape[axis] // 2
    return (
        lax.dynamic_slice_in_dim(value, (1 - bit) * half, half, axis),
        lax.dynamic_slice_in_dim(value, bit * half, half, axis),
    )


def sum_products(pieces, product, order, axis):
    away = product(pieces[0]).astype(low)
    value = product(pieces[1]) + head_swap(away, order[0]).astype(full)
    return away, sum_rows(value, order[1:], axis)


def finish_state(total, swap=lambda value: value):
    state = lax.axis_index(STATE)
    away = swap(lax.dynamic_index_in_dim(total, 1 - state, 0, False).astype(low))
    kept = lax.dynamic_index_in_dim(total, state, 0, False)
    return kept + state_swap(away).astype(full)


def swap_quarters(value):
    quarter = value.shape[-1] // 4
    part = [value[..., i * quarter : (i + 1) * quarter] for i in range(4)]
    return jnp.concatenate([part[1], part[0], part[3], part[2]], -1)


def fast_device(
    hidden,
    embedding,
    cotangent,
    lengths,
    gain_attn,
    w_query,
    w_key,
    w_value,
    down_query,
    down_key,
    down_value,
    up_query,
    up_key,
    up_value,
    attn_output,
    gain_mlp,
    mlp_input,
    down_mlp,
    up_mlp,
    mlp_output,
    gain_mixer,
    proj_inner,
    proj_gate,
    proj_step,
    proj_input,
    proj_read,
    taps_inner,
    taps_input,
    taps_read,
    step_bias,
    log_rate,
    skip_gain,
    gain_gated,
    proj_output,
):
    rows = hidden.shape[0]
    length = cotangent.shape[0]
    width = hidden.shape[1]
    middle = rows // 2
    head_parts = lax.axis_size(HEAD)
    piece = middle // head_parts
    state = lax.axis_index(STATE)
    dp = lax.axis_index(DP)
    head = lax.axis_index(HEAD)
    place = dp * 2 + state
    own_start = state * rows
    orders = head_masks()
    offsets = [chunk_of(orders[0]) * piece, middle + chunk_of(orders[1]) * piece]

    heads_wide = w_query.shape[1]
    half_cols = heads_wide // 2

    def state_columns(values, index):
        return jnp.concatenate(
            [lax.dynamic_slice_in_dim(v, index * half_cols, half_cols, 1) for v in values], 1
        )

    rank = down_query.shape[1]
    part_a = down_query.shape[0] // head_parts
    part_m = down_mlp.shape[0] // head_parts
    split_a, split_m = gain_attn.shape[0], gain_mlp.shape[0]
    up_rows = up_query.shape[0]

    def small_pack(index):
        return jnp.concatenate(
            [
                jnp.concatenate([gain_attn, gain_mlp, gain_mixer]).reshape(-1, rank),
                lax.dynamic_slice_in_dim(down_query, head * part_a, part_a, 0),
                lax.dynamic_slice_in_dim(down_key, head * part_a, part_a, 0),
                lax.dynamic_slice_in_dim(down_value, head * part_a, part_a, 0),
                lax.dynamic_slice_in_dim(down_mlp, head * part_m, part_m, 0),
                up_mlp.reshape(-1, rank),
                proj_step.reshape(-1, rank),
                state_columns((up_query, up_key, up_value), index).reshape(-1, rank),
            ],
            0,
        )

    pack = jnp.stack([small_pack(state), state_swap(small_pack(1 - state))], 0)
    pack_far = dp_swap(pack)
    mine = hold(state_columns((w_query, w_key, w_value), state), pack_far)
    got = state_swap(hold(state_columns((w_query, w_key, w_value), 1 - state), pack))
    cutting = mine.shape[0] // 2
    far_mine = [dp_swap(mine[:cutting]), dp_swap(mine[cutting:])]
    far_got = [dp_swap(got[:cutting]), dp_swap(got[cutting:])]

    share = rows // head_parts
    sent = jnp.stack(
        [
            lax.dynamic_slice_in_dim(value, chunk_of(order) * share, share, 0)
            for value, order in zip((hidden, embedding), orders)
        ],
        0,
    )
    sent = state_swap(sent)

    pack = jnp.concatenate([pack, pack_far], 0)
    gain_rows = (split_a + 2 * split_m) // rank
    gains = pack[:, :gain_rows].reshape(4, -1).astype(full)
    attn_gain = gains[:, :split_a].reshape(-1)
    gains = natural_quarters([gains[index] for index in range(4)])
    mlp_gain = jnp.concatenate([value[split_a : split_a + split_m] for value in gains])
    mixer_gain = jnp.concatenate([value[split_a + split_m :] for value in gains])
    down_end = gain_rows + 3 * part_a + part_m
    step_width = proj_step.shape[1]
    step_start = down_end + up_mlp.size // rank
    step_end = step_start + proj_step.size // rank
    mlp_upper = jnp.concatenate(
        natural_quarters(
            [pack[index, down_end:step_start].reshape(up_mlp.shape) for index in range(4)]
        ),
        0,
    )
    step_main = jnp.concatenate(
        natural_quarters(
            [pack[index, step_start:step_end].reshape(proj_step.shape) for index in range(4)]
        ),
        0,
    )
    ups = natural_quarters(
        [pack[index, step_end:].reshape(up_rows, 3 * half_cols) for index in range(4)]
    )
    ups = jnp.concatenate(ups, 0)
    column = lax.broadcasted_iota(jnp.int32, (1, 3 * half_cols), 1) // half_cols
    up_wide = jnp.concatenate(
        [jnp.where(column == index, ups, jnp.zeros_like(ups)) for index in range(3)], 0
    )
    masks = orders[0][::-1]
    downs_all = natural_heads(gather_rows(pack[None, :, gain_rows:down_end], orders[0], 0))

    def down_of(lower, part):
        return downs_all[:, :, lower : lower + part].transpose(1, 0, 2, 3)

    down_wide = jnp.concatenate(
        [down_of(index * part_a, part_a).reshape(-1, rank) for index in range(3)], 1
    )
    down_m = down_of(3 * part_a, part_m)
    mlp_down = jnp.concatenate(natural_quarters([down_m[i] for i in range(4)]), 0)
    mlp_down = mlp_down.reshape(-1, rank)

    segment, position, valid = row_layout(lengths[0], length)
    own_segment = lax.dynamic_slice_in_dim(segment, own_start, rows)
    own_valid = lax.dynamic_slice_in_dim(valid, own_start, rows)[:, None]
    lows = first_blocks(segment)
    half = HDIM // 2
    angle = position[:, None] * 10000.0 ** (-jnp.arange(half, dtype=full) / half)[None, :]
    cosine = jnp.concatenate([jnp.cos(angle), jnp.cos(angle)], 1)
    sine = jnp.concatenate([-jnp.sin(angle), jnp.sin(angle)], 1)

    def cut(value):
        return [lax.dynamic_slice_in_dim(value, offset, piece, 0) for offset in offsets]

    valid_cut = cut(own_valid)

    quarter = gain_attn.shape[0]

    def quarters(first, second):
        parts = []
        for index in range(4):
            start = (state ^ (index % 2)) * quarter
            part = [lax.dynamic_slice_in_dim(v, start, quarter, 1) for v in (first, second)]
            parts.append(jnp.where(dp == index // 2, *part).astype(full))
        return parts

    def joint_scale(first, second):
        squares = [jnp.sum(jnp.square(v.astype(full)), 1, keepdims=True) for v in (first, second)]
        return lax.rsqrt((squares[0] + squares[1]) / (2 * width) + epsilon)

    def normed_rows(first, second):
        scale = joint_scale(first, second)
        parts = [
            (part * scale * attn_gain[index * quarter : (index + 1) * quarter]).astype(low)
            for index, part in enumerate(quarters(first, second))
        ]
        return jnp.concatenate(parts[:2], 1), jnp.concatenate(parts[2:], 1)

    near_own, far_own = normed_rows(hidden, embedding)
    joined_cut = [
        jnp.concatenate(quarters(a, b), 1) for a, b in zip(cut(hidden), cut(embedding))
    ]

    others = [gather_rows(sent[i], orders[i], 0) for i in range(2)]
    others[0] = hold(others[0], others[1], cosine, sine, down_wide)
    near_other, far_other = normed_rows(*others)
    main_near = jnp.concatenate([mine, got], 0)

    def project_near(near, far):
        reduced = (plain_dot(near, down_wide[:width]) + plain_dot(far, down_wide[width:])).astype(low)
        return plain_dot(near, main_near) + plain_dot(reduced, up_wide), reduced

    pre_own, red_own = project_near(near_own, far_own)
    pre_other, red_other = project_near(near_other, far_other)
    far_got[0] = hold(far_got[0], pre_own, pre_other)
    main_far = jnp.concatenate(far_mine + far_got, 0)
    pre_own = pre_own + plain_dot(far_own, main_far)
    pre_other = pre_other + plain_dot(far_other, main_far)
    queries, keys, values = rope(state, pre_own, pre_other, cosine, sine)

    attn_output = hold(attn_output, *far_mine)
    attn_mine = lax.dynamic_slice_in_dim(attn_output, state * half_cols, half_cols, 0)
    attn_got = state_swap(
        lax.dynamic_slice_in_dim(attn_output, (1 - state) * half_cols, half_cols, 0)
    )
    attn_pair = jnp.stack([attn_mine, attn_got], 0)
    attn_far = dp_swap(attn_pair)
    attn_proj = jnp.concatenate(
        natural_quarters([attn_pair[0], attn_pair[1], attn_far[0], attn_far[1]]), 1
    )
    mlp_cut = mlp_input.shape[1] // 2
    mlp_input = hold(mlp_input, far_got[0], far_got[1], *far_mine, attn_far)
    mlp_first = lax.all_gather(mlp_input[:, :mlp_cut], ZED, axis=0, tiled=True)
    mlp_second = lax.all_gather(mlp_input[:, mlp_cut:], ZED, axis=0, tiled=True)
    mlp_main = jnp.concatenate([mlp_first, mlp_second], 1)
    attended, lse = attend(queries, keys, values, segment, lows)

    attended = hold(attended, mlp_first)
    attended_halves = [attended[:rows], attended[rows:]]
    def branch_product(part):
        return plain_dot(part.reshape(-1, part.shape[2]), attn_proj).reshape(2, -1, width)

    branch_cut = []
    for part, order in zip(attended_halves, orders):
        pieces = cut_rows(part.reshape(2, middle, -1), order, 1)
        branch_cut.append(finish_state(sum_products(pieces, branch_product, order, 1)[1]))
    mlp_proj = lax.all_gather(mlp_output, ZED, axis=1, tiled=True)
    mixer_main = lax.all_gather(
        jnp.concatenate([proj_inner, proj_gate], 1), ZED, axis=0, tiled=True
    )
    output_main = lax.all_gather(proj_output, ZED, axis=1, tiled=True)
    first_cut = [
        value.astype(full) + good * branch
        for value, good, branch in zip(cut(hidden), valid_cut, branch_cut)
    ]
    mlp_normed = [
        gather_rows(rms_norm(value, mlp_gain).astype(low), order, 0)
        for value, order in zip(first_cut, orders)
    ]
    mlp_red = [plain_dot(value, mlp_down).astype(low) for value in mlp_normed]
    hidden_pre = [
        plain_dot(value, mlp_main) + plain_dot(red, mlp_upper)
        for value, red in zip(mlp_normed, mlp_red)
    ]
    activated = [jax.nn.gelu(value, approximate=False).astype(low) for value in hidden_pre]
    second_cut = [
        value
        + good
        * sum_products(
            cut_rows(part, order, 0), lambda rows: plain_dot(rows, mlp_proj), order, 0
        )[1]
        for value, good, part, order in zip(first_cut, valid_cut, activated, orders)
    ]
    mixer_normed = jnp.concatenate(
        [
            gather_rows(rms_norm(value, mixer_gain).astype(low), order, 0)
            for value, order in zip(second_cut, orders)
        ],
        0,
    )

    inner_width = proj_inner.shape[1]
    mixer_heads = step_width
    states = proj_input.shape[1]
    small_main = jnp.concatenate([step_main, proj_input, proj_read], 1)
    small_pre = plain_dot(mixer_normed, small_main)
    mixer_pre = plain_dot(mixer_normed, mixer_main)
    inner_pre, gate_pre = mixer_pre[:, :inner_width], mixer_pre[:, inner_width:]
    reach = taps_inner.shape[0] - 1
    edge = state_forward(
        jnp.concatenate([inner_pre[rows - reach :], small_pre[rows - reach :, mixer_heads:]], 1)
    )
    edge_start = jnp.maximum(own_start - reach, 0)
    edge_segment = jnp.where(state == 0, -1, lax.dynamic_slice_in_dim(segment, edge_start, reach))

    def conv_piece(inner_in, small_in, edge_in, taps_x, taps_b, taps_c, shift_in):
        input_in = small_in[:, mixer_heads : mixer_heads + states]
        read_in = small_in[:, mixer_heads + states :]
        edge_b = edge_in[:, inner_width : inner_width + states]
        edge_c = edge_in[:, inner_width + states :]
        return (
            jax.nn.silu(
                conv_edge(inner_in, edge_in[:, :inner_width], taps_x, own_segment, edge_segment)
            ),
            jax.nn.silu(conv_edge(input_in, edge_b, taps_b, own_segment, edge_segment)),
            jax.nn.silu(conv_edge(read_in, edge_c, taps_c, own_segment, edge_segment)),
            jax.nn.softplus(small_in[:, :mixer_heads] + shift_in[None, :]),
        )

    (inner_conv, input_conv, read_conv, steps), conv_back = jax.vjp(
        conv_piece,
        inner_pre,
        small_pre,
        edge,
        taps_inner.astype(full),
        taps_input.astype(full),
        taps_read.astype(full),
        step_bias.astype(full),
    )
    rate = -jnp.exp(log_rate.astype(full))
    scan = Scan(inner_conv, steps, rate, input_conv, read_conv, own_segment, edge_segment[-1])
    first_state = state_forward(scan.end())
    scanned, block_states = scan.forward(first_state)

    def by_head(value):
        return value.reshape(rows, mixer_heads, MDIM)

    skip_full = jnp.repeat(skip_gain.astype(full), MDIM)[None, :]
    combined = scanned + skip_full * inner_conv
    gate_act = jax.nn.silu(gate_pre)
    united = combined * gate_act
    gated_gain = gain_gated.astype(full)[None, :]
    cot_own = lax.dynamic_slice_in_dim(cotangent, own_start, rows, 0)
    mix_grad = cot_own * own_valid.astype(low)
    gated_grad = right_dot(mix_grad, output_main)
    pair = jnp.stack(
        [jnp.sum(united * united, 1), jnp.sum(united * gated_gain * gated_grad, 1)], 0
    )
    for mask in orders[0]:
        pair = pair + head_swap(pair, mask)
    channels = inner_width * head_parts
    row_scale = lax.rsqrt(pair[0] / channels + epsilon)[:, None]
    row_total = pair[1][:, None]
    gated = (united * row_scale * gated_gain).astype(low)
    united_grad = (
        row_scale * gated_gain * gated_grad
        - united * row_scale * row_scale * row_scale * row_total / channels
    )
    combined_grad = united_grad * gate_act
    last_state_grad = state_backward(scan.start_grad(combined_grad))

    sigmoid_gate = jax.nn.sigmoid(gate_pre)
    gate_grad = united_grad * combined * sigmoid_gate * (1.0 + gate_pre * (1.0 - sigmoid_gate))
    grad_gated_gain = jnp.sum(gated_grad * united * row_scale, 0)
    grad_skip = jnp.sum(by_head(combined_grad * inner_conv), (0, 2))
    scan_grad, step_grad, log_grad, log_rows, input_grad, read_grad = scan.backward(
        combined_grad, block_states, last_state_grad
    )
    log_grad = log_grad - log_rows.T
    grad_rate = jnp.sum(log_grad * steps, 0) * rate
    (
        inner_grad,
        small_grad,
        edge_grad,
        grad_taps_x,
        grad_taps_b,
        grad_taps_c,
        grad_shift,
    ) = conv_back(
        (
            scan_grad + skip_full * combined_grad,
            input_grad,
            read_grad,
            step_grad + log_grad * rate[None, :],
        )
    )
    edge_back = state_backward(edge_grad)
    inner_grad = inner_grad.at[rows - reach :].add(edge_back[:, :inner_width])
    small_grad = small_grad.at[rows - reach :, mixer_heads:].add(edge_back[:, inner_width:])
    out_cut = [
        (
            value
            + good
            * sum_products(
                cut_rows(gated[index * middle : (index + 1) * middle], order, 0),
                lambda rows: plain_dot(rows, output_main),
                order,
                0,
            )[1]
        ).astype(low)
        for index, (value, good, order) in enumerate(zip(second_cut, valid_cut, orders))
    ]
    inner_low = jnp.concatenate([inner_grad, gate_grad], 1).astype(low)
    inner_low = hold(inner_low, *out_cut)
    small_low = small_grad.astype(low)
    def mixer_product(rows):
        return right_dot(rows[0], mixer_main) + right_dot(rows[1], small_main)

    mixer_parts, mixer_sum = [], []
    for index, order in enumerate(orders):
        part = slice(index * middle, (index + 1) * middle)
        pieces = zip(cut_rows(inner_low[part], order, 0), cut_rows(small_low[part], order, 0))
        away, total = sum_products(list(pieces), mixer_product, order, 0)
        mixer_parts.append(away)
        mixer_sum.append(total)
    inner_later = hold(inner_low, *mixer_parts)
    small_later = hold(small_low, *mixer_parts)

    def scatter(value, axis):
        return lax.psum_scatter(value.astype(low), ZED, scatter_dimension=axis, tiled=True)

    sum_output = scatter(left_dot(gated, hold(mix_grad, *mixer_parts)), 1)
    sum_mixer = scatter(left_dot(mixer_normed, inner_later), 0)
    upstream_cut = [value.astype(full) for value in cut(cot_own)]
    mixer_backs = [
        norm_back(value, mixer_gain, grad) for value, grad in zip(second_cut, mixer_sum)
    ]
    second_grad = [up + back[0] for up, back in zip(upstream_cut, mixer_backs)]
    grad_mixer_gain = mixer_backs[0][1] + mixer_backs[1][1]
    mlp_grad = [
        gather_rows((good * grad).astype(low), order, 0)
        for good, grad, order in zip(valid_cut, second_grad, orders)
    ]

    def gelu_part(value):
        return jax.nn.gelu(value, approximate=False)

    hidden_grad = [
        jax.vjp(gelu_part, pre)[1](right_dot(grad, mlp_proj))[0].astype(low)
        for pre, grad in zip(hidden_pre, mlp_grad)
    ]
    mlp_wide = jnp.concatenate([mlp_main, mlp_upper], 0)
    mlp_parts, mlp_sums = [], []
    for grad, order in zip(hidden_grad, orders):
        away, total = sum_products(
            cut_rows(grad, order, 0), lambda rows: right_dot(rows, mlp_wide), order, 0
        )
        mlp_parts.append(away)
        mlp_sums.append(total)
    middle_low = [value[:, width:].astype(low) for value in mlp_sums]
    mlp_backs = [
        norm_back(value, mlp_gain, total[:, :width] + right_dot(mid, mlp_down))
        for value, total, mid in zip(first_cut, mlp_sums, middle_low)
    ]
    first_grad = [grad + back[0] for grad, back in zip(second_grad, mlp_backs)]
    first_grad[0] = hold(first_grad[0], sum_output)
    mlp_grad_own = hold(jnp.concatenate(mlp_grad, 0), *mlp_parts)
    sum_mlp_output = scatter(left_dot(jnp.concatenate(activated, 0), mlp_grad_own), 1)
    grad_mlp_gain = mlp_backs[0][1] + mlp_backs[1][1]
    branch_halves = [
        gather_row16((good * grad).astype(low), order).reshape(rows, width)
        for good, grad, order in zip(valid_cut, first_grad, orders)
    ]

    attended_grad = jnp.concatenate(
        [right_dot(value, attn_proj).astype(low) for value in branch_halves], 0
    )
    attended_grad = hold(attended_grad, sum_mixer)
    query_back, key_back, value_back = attend_back(
        queries, keys, values, attended_grad, attended, lse, segment, lows
    )
    out_got = state_swap(jnp.stack(out_cut, 0))
    pre_grad = hold(rope_back(query_back, key_back, value_back, cosine, sine), out_got)
    main_wide = jnp.concatenate([main_near, main_far, up_wide], 0)
    joint = 2 * width
    def normed_product(part):
        return right_dot(part.reshape(-1, part.shape[2]), main_wide).reshape(2, -1, main_wide.shape[0])

    normed_parts, normed_totals = [], []
    for part, order in zip((pre_grad[:rows], pre_grad[rows:]), orders):
        pieces = cut_rows(part.reshape(2, middle, -1), order, 1)
        away, total = sum_products(pieces, normed_product, order, 1)
        normed_parts.append(away)
        normed_totals.append(total)
    normed_totals[0] = hold(normed_totals[0], sum_mlp_output)
    def swap_joint(value):
        return jnp.concatenate([swap_quarters(value[:, :joint]), value[:, joint:]], 1)

    normed_sums = [finish_state(total, swap_joint) for total in normed_totals]
    normed_sums[0] = hold(normed_sums[0], normed_sums[1], cost=100)
    pre_grad = hold(pre_grad, *normed_parts)
    cubes = pre_grad.reshape(2, 2, middle, -1)
    grad_own, grad_other = (
        lax.dynamic_index_in_dim(cubes, index, 1, False).reshape(rows, -1)
        for index in (state, 1 - state)
    )
    wide_grad = left_dot(red_own, grad_own) + left_dot(red_other, grad_other)
    up_grad = jnp.concatenate(
        [
            wide_grad[index * rank : (index + 1) * rank, index * half_cols : (index + 1) * half_cols]
            for index in range(3)
        ],
        1,
    )

    def main_grad(own, other, lower, index):
        part = slice(lower * quarter, (lower + 1) * quarter)
        main = left_dot(own[:, part], grad_own) + left_dot(other[:, part], grad_other)
        ups = lax.dynamic_slice_in_dim(up_grad, (place ^ index) * up_rows, up_rows, 0)
        return jnp.concatenate([main, ups], 0).astype(low)

    def by_dp(near, far):
        both = jnp.concatenate([jnp.where(dp == 0, near, far), jnp.where(dp == 0, far, near)], 0)
        return lax.psum_scatter(both, DP, scatter_dimension=0, tiled=True)

    beside = by_dp(main_grad(near_own, near_other, 1, 1), main_grad(far_own, far_other, 1, 3))
    main_total = by_dp(
        hold(main_grad(near_own, near_other, 0, 0), *normed_sums),
        main_grad(far_own, far_other, 0, 2),
    )
    beside_got = state_swap(hold(beside, *normed_sums))

    def spread(own, got, index):
        part = slice(index * half_cols, (index + 1) * half_cols)
        own, got = own[:, part].astype(full), got[:, part].astype(full)
        return jnp.concatenate(
            [jnp.where(state == 0, own, got), jnp.where(state == 0, got, own)], 1
        )

    lows_cut = [value[:, joint:].astype(low) for value in normed_sums]
    def by_order(value):
        bits = value.reshape((2,) * (len(orders[0])) + (piece, value.shape[1]))
        count = len(orders[0])
        turned = [0] + list(range(count - 1, 0, -1)) + [count, count + 1]
        return bits.transpose(turned).reshape(value.shape)

    lows_own = gather_rows(jnp.stack(lows_cut, 0), orders[0], 1)
    lows_own = [lows_own[0], by_order(lows_own[1])]
    lows_own = jnp.concatenate(lows_own, 0)
    def placed(value, axis):
        shape = list(value.shape)
        shape[axis] *= head_parts
        return lax.dynamic_update_slice_in_dim(
            jnp.zeros(shape, full), value, head * value.shape[axis], axis
        )

    small_main_grad = hold(left_dot(mixer_normed, small_later), *normed_totals)
    normed_cut = [
        lax.dynamic_slice_in_dim(value, chunk_of(order) * piece, piece, 0)
        for value, order in zip(mlp_normed, orders)
    ]
    mlp_down_grad = left_dot(jnp.concatenate(normed_cut, 0), jnp.concatenate(middle_low, 0))
    pair_grad = jnp.concatenate([small_main_grad[:, mixer_heads:], mlp_down_grad], 1)
    wide = pair_grad.shape[1]
    heads_grad = placed(jnp.stack([grad_shift, grad_rate, grad_skip]), 1)
    flat_sums = [
        placed(small_main_grad[:, :mixer_heads].T, 0),
        placed(grad_taps_x, 1),
        placed(grad_gated_gain, 0),
        grad_mlp_gain,
        grad_mixer_gain,
        jnp.concatenate([grad_taps_b, grad_taps_c], 1),
        jnp.pad(heads_grad.reshape(-1), (0, -heads_grad.size % wide)),
    ]
    packed = jnp.concatenate([value.reshape(-1, wide) for value in flat_sums], 0)
    lines = pair_grad.shape[0] // 8
    packed = jnp.pad(packed, ((0, -packed.shape[0] % lines), (0, 0)))
    pair_grad = jnp.concatenate([pair_grad, packed], 0)
    pair_grad = sum_rows(pair_grad, masks, 0)
    joined_backs = [
        norm_back(value, attn_gain, total[:, :joint] + right_dot(mid, down_wide))
        for value, total, mid in zip(joined_cut, normed_sums, lows_cut)
    ]
    grad_attn_gain = joined_backs[0][1] + joined_backs[1][1]

    def natural_columns(value):
        return jnp.concatenate(
            [
                lax.dynamic_slice_in_dim(value, (place ^ index) * quarter, quarter, -1)
                for index in range(4)
            ],
            -1,
        )

    input_cut = []
    for grad, back, own, got in zip(first_grad, joined_backs, out_cut, out_got):
        joined_grad = natural_columns(back[0])
        input_cut.append(
            jnp.concatenate(
                [
                    (joined_grad[:, :width] + grad).astype(low),
                    joined_grad[:, width:].astype(low),
                    jnp.where(state == 0, own, got),
                    jnp.where(state == 0, got, own),
                ],
                1,
            )
        )
    input_cut[0] = hold(input_cut[0], input_cut[1], lows_own, pair_grad, cost=100)
    input_cut[1] = hold(input_cut[1], lows_own, pair_grad)
    quads = []
    input_halves = []
    core = bit_of(orders[0][0])
    for value, order in zip(input_cut, orders):
        value = gather_rows(value, order[1:], 0)
        value = hold(value, beside_got)
        got = head_swap(value, order[0])
        input_halves += [value, got]
        quads += [(value, got), (got, value)]

    def whole_rows(start):
        columns = slice(start, start + width)
        return [jnp.where(core == 0, a[:, columns], b[:, columns]) for a, b in quads]

    grad_hidden = jnp.concatenate(whole_rows(0), 0)
    grad_embedding = jnp.concatenate(whole_rows(width), 0)
    layer_out = jnp.concatenate(whole_rows(2 * width) + whole_rows(3 * width), 0)

    attn_grad = left_dot(attended_halves[0], branch_halves[0]) + left_dot(
        attended_halves[1], branch_halves[1]
    )
    out_attn = grad_pieces(hold(attn_grad.astype(low), *input_halves), 0)
    def settled(value):
        return hold(value, *input_halves).astype(full)

    mlp_normed_own = jnp.concatenate(mlp_normed, 0)
    hidden_grad_own = hold(jnp.concatenate(hidden_grad, 0), *normed_parts)
    out_output = settled(sum_output)
    out_mixer = settled(sum_mixer)
    out_mlp_output = settled(sum_mlp_output)
    out_mlp_input = settled(scatter(left_dot(mlp_normed_own, hidden_grad_own), 0))
    out_up_mlp = settled(scatter(left_dot(jnp.concatenate(mlp_red, 0), hidden_grad_own), 0))

    down_parts = [
        left_dot(
            lax.dynamic_slice_in_dim(value, index * quarter + head * part_a, part_a, 1), lows_own
        )
        for value in (near_own, far_own)
        for index in range(2)
    ]
    away = jnp.stack([down_parts[1], down_parts[3]], 0).astype(low)
    away = state_swap(hold(away, *input_halves)).astype(full)
    down_sum = down_parts[0] + away[0] + dp_swap((down_parts[2] + away[1]).astype(low))
    down_all = gather_rows(down_sum.astype(low)[None], masks, 0).reshape(quarter, 3 * rank)
    down_all = down_all.astype(full)
    out_downs = [down_all[:, index * rank : (index + 1) * rank] for index in range(3)]

    pair_grad = hold(pair_grad, *input_halves)
    pair_grad = pair_grad + state_swap(pair_grad)
    pair_grad = pair_grad + dp_swap(pair_grad)
    row = lax.broadcasted_iota(jnp.int32, (pair_grad.shape[0], 1), 0)
    in_main = head * pair_grad.shape[0] + row < width
    down_m_squares = jnp.sum(jnp.where(in_main, jnp.square(pair_grad[:, 2 * states :]), 0.0))
    pair_grad = gather_rows(pair_grad.astype(low), masks, 0).astype(full)
    vector_grad = pair_grad[:width, : 2 * states]
    out_down_mlp = lax.dynamic_slice(pair_grad, (place * split_m, 2 * states), (split_m, rank))
    packed = pair_grad[width:]
    pieces = []
    for value in flat_sums:
        count = value.size // wide
        pieces.append(packed[:count].reshape(value.shape))
        packed = packed[count:]
    step_total, taps_x_total, gated_total, mlp_total, mixer_total, taps_total, head_total = pieces
    head_total = head_total[: heads_grad.size].reshape(heads_grad.shape)

    main_total = hold(main_total, *input_halves)
    out_all = [spread(main_total, beside_got, index) for index in range(3)]
    out_main = [value[:quarter] for value in out_all]
    out_up = [value[quarter:] for value in out_all]
    square_sum = jnp.sum(jnp.square(down_sum)) + 0.25 * down_m_squares
    for value in out_main + out_up + [out_attn, out_mlp_input, out_up_mlp, out_mlp_output]:
        square_sum = square_sum + jnp.sum(value * value)
    last = natural_columns(grad_attn_gain)
    last = jnp.concatenate([last, jnp.broadcast_to(square_sum, (rank,))]).reshape(-1, rank)
    for mask in orders[0]:
        last = last + head_swap(last, mask)
    last = last + state_swap(last)
    last = (last + dp_swap(last)).reshape(-1)
    attn_total, square_total = last[:joint], last[joint]

    def of_head(value, size):
        return lax.dynamic_slice_in_dim(value, head * size, size, value.ndim - 1)

    def of_place(value, size):
        return lax.dynamic_slice_in_dim(value, place * size, size)

    head_total = of_head(head_total, mixer_heads)
    out_step = lax.dynamic_slice(
        step_total, (head * mixer_heads, place * split_m), (mixer_heads, split_m)
    ).T
    return (
        layer_out,
        grad_hidden,
        grad_embedding,
        of_place(attn_total, split_a),
        out_main[0],
        out_main[1],
        out_main[2],
        out_downs[0],
        out_downs[1],
        out_downs[2],
        out_up[0],
        out_up[1],
        out_up[2],
        out_attn,
        of_place(mlp_total, split_m),
        out_mlp_input,
        out_down_mlp,
        out_up_mlp,
        out_mlp_output,
        of_place(mixer_total, split_m),
        out_mixer[:, :inner_width],
        out_mixer[:, inner_width:],
        out_step,
        vector_grad[:, :states],
        vector_grad[:, states:],
        of_head(taps_x_total, inner_width),
        taps_total[:, :states],
        taps_total[:, states:],
        head_total[0],
        head_total[1],
        head_total[2],
        of_head(gated_total, inner_width),
        out_output,
        jnp.sqrt(square_total),
    )


def pick_device(mesh):
    heads = mesh.shape[HEAD]
    per_head = DIN // HDIM // heads
    halves = mesh.shape[DP] == 2 and mesh.shape[STATE] == 2
    return fast_device if halves and heads & (heads - 1) == 0 and per_head % 2 == 0 else general_device


def solution(mesh):
    in_specs = (
        P(ZED, None),
        P(ZED, None),
        P(DP, None),
        P(DP, None),
        P(ZED),
        P(ZED, HEAD),
        P(ZED, HEAD),
        P(ZED, HEAD),
        P(ZED, None),
        P(ZED, None),
        P(ZED, None),
        P(ZED, HEAD),
        P(ZED, HEAD),
        P(ZED, HEAD),
        P(HEAD, ZED),
        P(ZED),
        P(ZED, HEAD),
        P(ZED, None),
        P(ZED, HEAD),
        P(HEAD, ZED),
        P(ZED),
        P(ZED, HEAD),
        P(ZED, HEAD),
        P(ZED, HEAD),
        P(),
        P(),
        P(None, HEAD),
        P(),
        P(),
        P(HEAD),
        P(HEAD),
        P(HEAD),
        P(HEAD),
        P(HEAD, ZED),
    )
    out_specs = (
        P(DP, None),
        P(ZED, None),
        P(ZED, None),
        P(ZED),
        P(ZED, HEAD),
        P(ZED, HEAD),
        P(ZED, HEAD),
        P(ZED, None),
        P(ZED, None),
        P(ZED, None),
        P(ZED, HEAD),
        P(ZED, HEAD),
        P(ZED, HEAD),
        P(HEAD, ZED),
        P(ZED),
        P(ZED, HEAD),
        P(ZED, None),
        P(ZED, HEAD),
        P(HEAD, ZED),
        P(ZED),
        P(ZED, HEAD),
        P(ZED, HEAD),
        P(ZED, HEAD),
        P(),
        P(),
        P(None, HEAD),
        P(),
        P(),
        P(HEAD),
        P(HEAD),
        P(HEAD),
        P(HEAD),
        P(HEAD, ZED),
        P(),
    )
    return jax.shard_map(
        pick_device(mesh), mesh=mesh, in_specs=in_specs, out_specs=out_specs, check_vma=False
    )
```

```python
import jax
import jax.numpy as jnp
from jax import lax
from jax.experimental import pallas as pl
from jax.experimental.pallas import tpu as pltpu
from jax.sharding import PartitionSpec as P

HDIM = 128
MDIM = 64
DIN = 4096
GROUP = 256
DP, HEAD, STATE = "dp", "head", "state"
ZED = (DP, STATE)
EVERY = (DP, HEAD, STATE)


highest = lax.Precision.HIGHEST
epsilon = 1e-05


def plain_dot(left, right):
    return jnp.dot(left, right, preferred_element_type=jnp.float32)


def left_dot(left, right):
    return lax.dot_general(
        left, right, (((0,), (0,)), ((), ())), preferred_element_type=jnp.float32
    )


def right_dot(left, right):
    return lax.dot_general(
        left, right, (((1,), (1,)), ((), ())), preferred_element_type=jnp.float32
    )


def exact_left(left, right):
    return lax.dot_general(
        left.astype(jnp.float32), right, (((0,), (0,)), ((), ())), precision=highest
    )


def exact_right(left, right):
    return lax.dot_general(
        left, right.astype(jnp.float32), (((1,), (1,)), ((), ())), precision=highest
    )


def rms_norm(values, gain):
    return values * lax.rsqrt(jnp.mean(values * values, -1, keepdims=True) + epsilon) * gain


def row_layout(doc_lengths, length):
    ends = jnp.cumsum(doc_lengths)
    places = jnp.arange(length, dtype=jnp.int32)
    segment = jnp.sum((places[:, None] >= ends[None, :]).astype(jnp.int32), axis=1)
    starts = jnp.concatenate([ends - doc_lengths, ends[-1:]])
    choose = segment[:, None] == jnp.arange(starts.shape[0], dtype=jnp.int32)[None, :]
    first_place = jnp.sum(jnp.where(choose, starts[None, :], 0), axis=1)
    position = (places - first_place).astype(jnp.float32)
    valid = (segment < doc_lengths.shape[0]).astype(jnp.float32)
    return (segment, position, valid)


def rotate(values, position):
    half = values.shape[-1] // 2
    freqs = 10000.0 ** (-jnp.arange(half, dtype=jnp.float32) / half)
    angle = position[:, None] * freqs[None, :]
    cosine = jnp.cos(angle)[:, None, :]
    sine = jnp.sin(angle)[:, None, :]
    former = values[..., :half]
    latter = values[..., half:]
    return jnp.concatenate([former * cosine - latter * sine, former * sine + latter * cosine], -1)


def head_probs(query_in, key_in, allowed):
    scale = query_in.shape[-1] ** (-0.5)
    scores = (
        jnp.einsum("thd,shd->hts", query_in, key_in, preferred_element_type=jnp.float32) * scale
    )
    scores = jnp.where(allowed[None, :, :], scores, -1e30)
    shifted = scores - jnp.max(scores, -1, keepdims=True)
    weights = jnp.exp(shifted)
    return weights / jnp.sum(weights, -1, keepdims=True)


def conv_mask(values, taps, segment):
    total = taps[0][None, :] * values
    for offset in range(1, taps.shape[0]):
        moved = jnp.concatenate(
            [jnp.zeros((offset, values.shape[1]), values.dtype), values[:-offset]], 0
        )
        moved_seg = jnp.concatenate([jnp.full((offset,), -1, jnp.int32), segment[:-offset]], 0)
        same = (moved_seg == segment).astype(values.dtype)[:, None]
        total = total + taps[offset][None, :] * moved * same
    return total


def state_scan(inputs, step_sizes, decay, input_vecs, read_vecs, segment, block):
    length, heads, width = inputs.shape
    count = length // block
    states = input_vecs.shape[1]

    def one_block(carry, pieces):
        state, before = carry
        group_in, group_dt, group_b, group_c, group_seg = pieces
        logs = group_dt * decay[None, :]
        cumul = jnp.cumsum(logs, 0)
        places = jnp.arange(block, dtype=jnp.int32)
        allowed = (group_seg[:, None] == group_seg[None, :]) & (places[None, :] <= places[:, None])
        gaps = cumul[:, None, :] - cumul[None, :, :]
        fading = jnp.where(
            allowed[:, :, None], jnp.exp(jnp.where(allowed[:, :, None], gaps, 0.0)), 0.0
        )
        inner = jnp.dot(group_c, group_b.T, precision=highest)
        scaled = group_in * group_dt[:, :, None]
        local_out = jnp.einsum(
            "tsh,shp->thp", inner[:, :, None] * fading, scaled, precision=highest
        )
        carried = (group_seg == before).astype(inputs.dtype)
        entry = jnp.exp(cumul) * carried[:, None]
        from_state = (
            jnp.einsum("tn,hnp->thp", group_c, state, precision=highest) * entry[:, :, None]
        )
        last_seg = group_seg[-1]
        reach = (group_seg == last_seg).astype(inputs.dtype)
        to_end = jnp.exp(cumul[-1][None, :] - cumul) * reach[:, None]
        retain = jnp.exp(cumul[-1]) * (last_seg == before).astype(inputs.dtype)
        fresh = jnp.einsum("sn,sh,shp->hnp", group_b, to_end, scaled, precision=highest)
        state = state * retain[:, None, None] + fresh
        return ((state, last_seg), local_out + from_state)

    pieces = (
        inputs.reshape(count, block, heads, width),
        step_sizes.reshape(count, block, heads),
        input_vecs.reshape(count, block, states),
        read_vecs.reshape(count, block, states),
        segment.reshape(count, block),
    )
    start = (jnp.zeros((heads, states, width), inputs.dtype), jnp.array(-1, jnp.int32))
    unused, outputs = lax.scan(jax.checkpoint(one_block), start, pieces)
    return outputs.reshape(length, heads, width)


def mixer_core(
    inner_pre,
    input_pre,
    read_pre,
    step_pre,
    taps_x,
    taps_b,
    taps_c,
    shift_in,
    rate_in,
    segment,
    width,
    block,
):
    inner_conv = jax.nn.silu(conv_mask(inner_pre, taps_x, segment))
    input_conv = jax.nn.silu(conv_mask(input_pre, taps_b, segment))
    read_conv = jax.nn.silu(conv_mask(read_pre, taps_c, segment))
    step_sizes = jax.nn.softplus(step_pre + shift_in[None, :])
    heads = step_sizes.shape[1]
    length = inner_conv.shape[0]
    outputs = state_scan(
        inner_conv.reshape(length, heads, width),
        step_sizes,
        -jnp.exp(rate_in),
        input_conv,
        read_conv,
        segment,
        block,
    )
    return (outputs.reshape(length, heads * width), inner_conv)


def place_slice(piece, index, parts, axis):
    shape = list(piece.shape)
    shape[axis] = shape[axis] * parts
    holder = jnp.zeros(tuple(shape), jnp.float32)
    return lax.dynamic_update_slice_in_dim(holder, piece, index * piece.shape[axis], axis)


def take_slice(whole, index, width, axis):
    return lax.dynamic_slice_in_dim(whole, index * width, width, axis)


def general_device(
    hidden,
    embedding,
    cotangent,
    lengths,
    gain_attn,
    w_query,
    w_key,
    w_value,
    down_query,
    down_key,
    down_value,
    up_query,
    up_key,
    up_value,
    attn_output,
    gain_mlp,
    mlp_input,
    down_mlp,
    up_mlp,
    mlp_output,
    gain_mixer,
    proj_inner,
    proj_gate,
    proj_step,
    proj_input,
    proj_read,
    taps_inner,
    taps_input,
    taps_read,
    step_bias,
    log_rate,
    skip_gain,
    gain_gated,
    proj_output,
):
    row_count = hidden.shape[0]
    length = cotangent.shape[0]
    model_width = hidden.shape[1]
    head_parts = lax.axis_size(HEAD)
    state_parts = lax.axis_size(STATE)
    state_index = lax.axis_index(STATE)
    head_index = lax.axis_index(HEAD)
    own_start = state_index * row_count
    segment, position, valid = row_layout(lengths[0], length)
    own_segment = lax.dynamic_slice_in_dim(segment, own_start, row_count)
    own_position = lax.dynamic_slice_in_dim(position, own_start, row_count)
    own_valid = lax.dynamic_slice_in_dim(valid, own_start, row_count)[:, None]
    full_valid = valid[:, None]
    places = jnp.arange(length, dtype=jnp.int32)
    own_places = own_start + jnp.arange(row_count, dtype=jnp.int32)
    own_mask = ((places >= own_start) & (places < own_start + row_count)).astype(jnp.float32)[
        :, None
    ]
    allowed = (own_segment[:, None] == segment[None, :]) & (places[None, :] <= own_places[:, None])
    gathered = (
        lax.all_gather(gain_attn, ZED, axis=0, tiled=True),
        lax.all_gather(w_query, ZED, axis=0, tiled=True),
        lax.all_gather(w_key, ZED, axis=0, tiled=True),
        lax.all_gather(w_value, ZED, axis=0, tiled=True),
        lax.all_gather(down_query, ZED, axis=0, tiled=True),
        lax.all_gather(down_key, ZED, axis=0, tiled=True),
        lax.all_gather(down_value, ZED, axis=0, tiled=True),
        lax.all_gather(up_query, ZED, axis=0, tiled=True),
        lax.all_gather(up_key, ZED, axis=0, tiled=True),
        lax.all_gather(up_value, ZED, axis=0, tiled=True),
        lax.all_gather(attn_output, ZED, axis=1, tiled=True),
        lax.all_gather(gain_mlp, ZED, axis=0, tiled=True),
        lax.all_gather(mlp_input, ZED, axis=0, tiled=True),
        lax.all_gather(down_mlp, ZED, axis=0, tiled=True),
        lax.all_gather(up_mlp, ZED, axis=0, tiled=True),
        lax.all_gather(mlp_output, ZED, axis=1, tiled=True),
        lax.all_gather(gain_mixer, ZED, axis=0, tiled=True),
        lax.all_gather(proj_inner, ZED, axis=0, tiled=True),
        lax.all_gather(proj_gate, ZED, axis=0, tiled=True),
        lax.all_gather(proj_step, ZED, axis=0, tiled=True),
        lax.all_gather(proj_output, ZED, axis=1, tiled=True),
    )
    (
        attn_gain,
        query_main,
        key_main,
        value_main,
        query_down,
        key_down,
        value_down,
        query_upper,
        key_upper,
        value_upper,
        attn_proj,
        mlp_gain,
        mlp_main,
        mlp_down,
        mlp_upper,
        mlp_proj,
        mixer_gain,
        inner_main,
        gate_main,
        step_main,
        output_main,
    ) = gathered
    joined = jnp.concatenate([hidden, embedding], 1).astype(jnp.float32)
    attn_gain_f = attn_gain.astype(jnp.float32)
    normed = rms_norm(joined, attn_gain_f).astype(jnp.bfloat16)
    head_count = query_main.shape[1] // HDIM

    def project(main, down, upper):
        reduced = plain_dot(normed, down).astype(jnp.bfloat16)
        return (plain_dot(normed, main) + plain_dot(reduced, upper), reduced)

    query_pre, query_red = project(query_main, query_down, query_upper)
    key_pre, key_red = project(key_main, key_down, key_upper)
    value_pre, value_red = project(value_main, value_down, value_upper)
    queries = rotate(query_pre.reshape(row_count, head_count, HDIM), own_position).astype(
        jnp.bfloat16
    )
    keys_own = rotate(key_pre.reshape(row_count, head_count, HDIM), own_position).astype(
        jnp.bfloat16
    )
    values_own = value_pre.reshape(row_count, head_count, HDIM).astype(jnp.bfloat16)
    keys_all, values_all = (
        lax.all_gather(keys_own, STATE, axis=0, tiled=True),
        lax.all_gather(values_own, STATE, axis=0, tiled=True),
    )
    probs_full = head_probs(queries, keys_all, allowed)
    attended_f = jnp.einsum(
        "hts,shd->thd",
        probs_full.astype(jnp.bfloat16),
        values_all,
        preferred_element_type=jnp.float32,
    )
    attended = attended_f.reshape(row_count, head_count * HDIM).astype(jnp.bfloat16)
    branch = lax.psum(plain_dot(attended, attn_proj), HEAD)
    first = hidden.astype(jnp.float32) + own_valid * branch
    mlp_gain_f = mlp_gain.astype(jnp.float32)
    mlp_normed = rms_norm(first, mlp_gain_f).astype(jnp.bfloat16)
    mlp_red = plain_dot(mlp_normed, mlp_down).astype(jnp.bfloat16)
    hidden_pre = plain_dot(mlp_normed, mlp_main) + plain_dot(mlp_red, mlp_upper)
    activated = jax.nn.gelu(hidden_pre, approximate=False).astype(jnp.bfloat16)
    mlp_branch = lax.psum(plain_dot(activated, mlp_proj), HEAD)
    second = first + own_valid * mlp_branch
    second_all = lax.all_gather(second, STATE, axis=0, tiled=True)
    mixer_gain_f = mixer_gain.astype(jnp.float32)
    mixer_normed = rms_norm(second_all, mixer_gain_f).astype(jnp.bfloat16)
    states_own = proj_input.shape[1] // state_parts
    input_half = take_slice(proj_input, state_index, states_own, 1)
    read_half = take_slice(proj_read, state_index, states_own, 1)
    taps_input_half = take_slice(taps_input, state_index, states_own, 1).astype(jnp.float32)
    taps_read_half = take_slice(taps_read, state_index, states_own, 1).astype(jnp.float32)
    inner_pre = plain_dot(mixer_normed, inner_main)
    gate_pre = plain_dot(mixer_normed, gate_main)
    step_pre = plain_dot(mixer_normed, step_main)
    input_pre = plain_dot(mixer_normed, input_half)
    read_pre = plain_dot(mixer_normed, read_half)

    def mixer_piece(
        inner_in, input_in, read_in, step_in, taps_x, taps_b, taps_c, shift_in, rate_in
    ):
        return mixer_core(
            inner_in,
            input_in,
            read_in,
            step_in,
            taps_x,
            taps_b,
            taps_c,
            shift_in,
            rate_in,
            segment,
            MDIM,
            GROUP,
        )

    (scanned_part, inner_conv), mixer_back = jax.vjp(
        mixer_piece,
        inner_pre,
        input_pre,
        read_pre,
        step_pre,
        taps_inner.astype(jnp.float32),
        taps_input_half,
        taps_read_half,
        step_bias.astype(jnp.float32),
        log_rate.astype(jnp.float32),
    )
    scanned = lax.psum(scanned_part, STATE)
    skip_full = jnp.repeat(skip_gain.astype(jnp.float32), MDIM)[None, :]
    combined = scanned + skip_full * inner_conv
    gate_act = jax.nn.silu(gate_pre)
    united = combined * gate_act
    squares = lax.psum(jnp.sum(united * united, 1), HEAD)
    row_scale = lax.rsqrt(squares / DIN + epsilon)[:, None]
    gated_gain = gain_gated.astype(jnp.float32)[None, :]
    united_own = lax.dynamic_slice_in_dim(united, own_start, row_count, 0)
    scale_own = lax.dynamic_slice_in_dim(row_scale, own_start, row_count, 0)
    gated_own = (united_own * scale_own * gated_gain).astype(jnp.bfloat16)
    mixed_own = lax.psum(plain_dot(gated_own, output_main), HEAD)
    mixed = lax.all_gather(mixed_own, STATE, axis=0, tiled=True)
    layer_out = (second_all + full_valid * mixed).astype(jnp.bfloat16)
    upstream = cotangent.astype(jnp.float32)
    mix_grad = (full_valid * upstream).astype(jnp.bfloat16)
    mix_grad_own = lax.dynamic_slice_in_dim(mix_grad, own_start, row_count, 0)
    grad_output_main = left_dot(gated_own, mix_grad_own)
    gated_grad = right_dot(mix_grad, output_main)
    row_total = jnp.sum(mix_grad.astype(jnp.float32) * mixed, 1)[:, None] / row_scale
    grad_gated_gain = jnp.sum(gated_grad * united * row_scale * own_mask, 0)
    united_grad = (
        row_scale * gated_gain * gated_grad
        - united * row_scale * row_scale * row_scale * row_total / DIN
    )
    combined_grad = united_grad * gate_act
    sigmoid_gate = jax.nn.sigmoid(gate_pre)
    gate_grad = (
        united_grad * combined * sigmoid_gate * (1.0 + gate_pre * (1.0 - sigmoid_gate)) * own_mask
    )
    mixer_heads = step_pre.shape[1]
    grad_skip = jnp.sum(
        (combined_grad * inner_conv * own_mask).reshape(length, mixer_heads, MDIM), (0, 2)
    )
    conv_extra = skip_full * combined_grad * own_mask
    (
        inner_grad,
        input_grad,
        read_grad,
        step_grad,
        grad_taps_x,
        grad_taps_b,
        grad_taps_c,
        grad_shift,
        grad_rate,
    ) = mixer_back((combined_grad, conv_extra))
    mixer_part = (
        exact_right(inner_grad, inner_main)
        + exact_right(gate_grad, gate_main)
        + exact_right(step_grad, step_main)
        + exact_right(input_grad, input_half)
        + exact_right(read_grad, read_half)
    )
    grad_inner_main = exact_left(mixer_normed, inner_grad)
    grad_gate_main = exact_left(mixer_normed, gate_grad)
    grad_step_main = exact_left(mixer_normed, step_grad)
    grad_input_half = exact_left(mixer_normed, input_grad)
    grad_read_half = exact_left(mixer_normed, read_grad)
    mixer_rows_own = lax.psum_scatter(mixer_part, STATE, scatter_dimension=0, tiled=True)
    mixer_own = lax.psum(mixer_rows_own, HEAD)
    unused_norm, second_back = jax.vjp(rms_norm, second, mixer_gain_f)
    second_norm_grad, grad_mixer_gain = second_back(mixer_own)
    upstream_own = lax.dynamic_slice_in_dim(upstream, own_start, row_count, 0)
    second_grad = upstream_own + second_norm_grad
    mlp_grad = (own_valid * second_grad).astype(jnp.bfloat16)
    grad_mlp_proj = left_dot(activated, mlp_grad)
    activated_grad = right_dot(mlp_grad, mlp_proj)
    unused_gelu, gelu_back = jax.vjp(
        lambda preact: jax.nn.gelu(preact, approximate=False), hidden_pre
    )
    hidden_grad = gelu_back(activated_grad)[0].astype(jnp.bfloat16)
    grad_mlp_main = left_dot(mlp_normed, hidden_grad)
    grad_mlp_upper = left_dot(mlp_red, hidden_grad)
    mlp_middle = right_dot(hidden_grad, mlp_upper)
    mlp_part = right_dot(hidden_grad, mlp_main)
    mlp_sum, middle_sum = lax.psum((mlp_part, mlp_middle), HEAD)
    middle_low = middle_sum.astype(jnp.bfloat16)
    mlp_normed_grad = mlp_sum + right_dot(middle_low, mlp_down)
    grad_mlp_down = left_dot(mlp_normed, middle_low)
    unused_first, first_back = jax.vjp(rms_norm, first, mlp_gain_f)
    first_norm_grad, grad_mlp_gain = first_back(mlp_normed_grad)
    first_grad = second_grad + first_norm_grad
    branch_grad = (own_valid * first_grad).astype(jnp.bfloat16)
    grad_attn_proj = left_dot(attended, branch_grad)
    attended_grad = right_dot(branch_grad, attn_proj).reshape(row_count, head_count, HDIM)
    probs_back = head_probs(queries, keys_all, allowed)
    score_scale = HDIM ** (-0.5)
    out_low = attended_grad.astype(jnp.bfloat16)
    prob_grad = jnp.einsum("thd,shd->hts", out_low, values_all, preferred_element_type=jnp.float32)
    score_grad = probs_back * (prob_grad - jnp.sum(probs_back * prob_grad, -1, keepdims=True))
    score_low = score_grad.astype(jnp.bfloat16)
    query_back = (
        jnp.einsum("hts,shd->thd", score_low, keys_all, preferred_element_type=jnp.float32)
        * score_scale
    )
    keys_back = (
        jnp.einsum("hts,thd->shd", score_low, queries, preferred_element_type=jnp.float32)
        * score_scale
    )
    values_back = jnp.einsum(
        "hts,thd->shd", probs_back.astype(jnp.bfloat16), out_low, preferred_element_type=jnp.float32
    )
    keys_grad_own, values_grad_own = (
        lax.psum_scatter(keys_back, STATE, scatter_dimension=0, tiled=True),
        lax.psum_scatter(values_back, STATE, scatter_dimension=0, tiled=True),
    )
    query_grad = (
        rotate(query_back, -own_position).reshape(row_count, head_count * HDIM).astype(jnp.bfloat16)
    )
    key_grad = (
        rotate(keys_grad_own, -own_position)
        .reshape(row_count, head_count * HDIM)
        .astype(jnp.bfloat16)
    )
    value_grad = values_grad_own.reshape(row_count, head_count * HDIM).astype(jnp.bfloat16)
    grad_query_main = left_dot(normed, query_grad)
    grad_key_main = left_dot(normed, key_grad)
    grad_value_main = left_dot(normed, value_grad)
    grad_query_upper = left_dot(query_red, query_grad)
    grad_key_upper = left_dot(key_red, key_grad)
    grad_value_upper = left_dot(value_red, value_grad)
    query_middle = right_dot(query_grad, query_upper)
    key_middle = right_dot(key_grad, key_upper)
    value_middle = right_dot(value_grad, value_upper)
    normed_part = (
        right_dot(query_grad, query_main)
        + right_dot(key_grad, key_main)
        + right_dot(value_grad, value_main)
    )
    normed_sum, query_msum, key_msum, value_msum = lax.psum(
        (normed_part, query_middle, key_middle, value_middle), HEAD
    )
    query_low = query_msum.astype(jnp.bfloat16)
    key_low = key_msum.astype(jnp.bfloat16)
    value_low = value_msum.astype(jnp.bfloat16)
    normed_grad = (
        normed_sum
        + right_dot(query_low, query_down)
        + right_dot(key_low, key_down)
        + right_dot(value_low, value_down)
    )
    grad_query_down = left_dot(normed, query_low)
    grad_key_down = left_dot(normed, key_low)
    grad_value_down = left_dot(normed, value_low)
    unused_joined, joined_back = jax.vjp(rms_norm, joined, attn_gain_f)
    joined_grad, grad_attn_gain = joined_back(normed_grad)
    grad_hidden = (first_grad + joined_grad[:, :model_width]).astype(jnp.bfloat16)
    grad_embedding = joined_grad[:, model_width:].astype(jnp.bfloat16)
    scattered = (
        lax.psum_scatter(grad_attn_gain, ZED, scatter_dimension=0, tiled=True),
        lax.psum_scatter(grad_query_main, ZED, scatter_dimension=0, tiled=True),
        lax.psum_scatter(grad_key_main, ZED, scatter_dimension=0, tiled=True),
        lax.psum_scatter(grad_value_main, ZED, scatter_dimension=0, tiled=True),
        lax.psum_scatter(grad_query_down, ZED, scatter_dimension=0, tiled=True),
        lax.psum_scatter(grad_key_down, ZED, scatter_dimension=0, tiled=True),
        lax.psum_scatter(grad_value_down, ZED, scatter_dimension=0, tiled=True),
        lax.psum_scatter(grad_query_upper, ZED, scatter_dimension=0, tiled=True),
        lax.psum_scatter(grad_key_upper, ZED, scatter_dimension=0, tiled=True),
        lax.psum_scatter(grad_value_upper, ZED, scatter_dimension=0, tiled=True),
        lax.psum_scatter(grad_attn_proj, ZED, scatter_dimension=1, tiled=True),
        lax.psum_scatter(grad_mlp_gain, ZED, scatter_dimension=0, tiled=True),
        lax.psum_scatter(grad_mlp_main, ZED, scatter_dimension=0, tiled=True),
        lax.psum_scatter(grad_mlp_down, ZED, scatter_dimension=0, tiled=True),
        lax.psum_scatter(grad_mlp_upper, ZED, scatter_dimension=0, tiled=True),
        lax.psum_scatter(grad_mlp_proj, ZED, scatter_dimension=1, tiled=True),
        lax.psum_scatter(grad_mixer_gain, ZED, scatter_dimension=0, tiled=True),
        lax.psum_scatter(grad_inner_main, ZED, scatter_dimension=0, tiled=True),
        lax.psum_scatter(grad_gate_main, ZED, scatter_dimension=0, tiled=True),
        lax.psum_scatter(grad_step_main, ZED, scatter_dimension=0, tiled=True),
        lax.psum_scatter(grad_output_main, ZED, scatter_dimension=1, tiled=True),
    )
    first_head = (head_index == 0).astype(jnp.float32)
    square_sum = jnp.zeros((), jnp.float32)
    for index in [1, 2, 3, 7, 8, 9, 10, 12, 14, 15]:
        square_sum = square_sum + jnp.sum(scattered[index] * scattered[index])
    for index in [4, 5, 6, 13]:
        square_sum = square_sum + first_head * jnp.sum(scattered[index] * scattered[index])
    head_params = jnp.stack([grad_shift, grad_rate, grad_skip], 0)
    totals = lax.psum(
        (
            square_sum,
            place_slice(grad_gated_gain, head_index, head_parts, 0),
            place_slice(grad_taps_x, head_index, head_parts, 1),
            place_slice(head_params, head_index, head_parts, 1),
            place_slice(grad_input_half, state_index, state_parts, 1),
            place_slice(grad_read_half, state_index, state_parts, 1),
            place_slice(grad_taps_b, state_index, state_parts, 1),
            place_slice(grad_taps_c, state_index, state_parts, 1),
        ),
        EVERY,
    )
    (
        square_total,
        gated_full,
        taps_full,
        heads_full,
        input_full,
        read_full,
        taps_input_full,
        taps_read_full,
    ) = totals
    head_width = gain_gated.shape[0]
    tap_width = taps_inner.shape[1]
    param_width = step_bias.shape[0]
    heads_own = take_slice(heads_full, head_index, param_width, 1)
    return (
        layer_out,
        grad_hidden,
        grad_embedding,
        scattered[0],
        scattered[1],
        scattered[2],
        scattered[3],
        scattered[4],
        scattered[5],
        scattered[6],
        scattered[7],
        scattered[8],
        scattered[9],
        scattered[10],
        scattered[11],
        scattered[12],
        scattered[13],
        scattered[14],
        scattered[15],
        scattered[16],
        scattered[17],
        scattered[18],
        scattered[19],
        input_full,
        read_full,
        take_slice(taps_full, head_index, tap_width, 1),
        taps_input_full,
        taps_read_full,
        heads_own[0],
        heads_own[1],
        heads_own[2],
        take_slice(gated_full, head_index, head_width, 0),
        scattered[20],
        jnp.sqrt(square_total),
    )


low = jnp.bfloat16
full = jnp.float32


def head_masks():
    count = lax.axis_size(HEAD)
    masks = [1 << bit for bit in range(count.bit_length() - 1)]
    return masks[:1] + masks[1:], masks[:1] + masks[1:][::-1]


def head_swap(value, mask):
    count = lax.axis_size(HEAD)
    return lax.ppermute(value, HEAD, [(i, i ^ mask) for i in range(count)])


def state_swap(value):
    return lax.ppermute(value, STATE, [(0, 1), (1, 0)])


def dp_swap(value):
    return lax.ppermute(value, DP, [(0, 1), (1, 0)])


def state_forward(value):
    return lax.ppermute(value, STATE, [(0, 1)])


def state_backward(value):
    return lax.ppermute(value, STATE, [(1, 0)])


def bit_of(mask):
    return (lax.axis_index(HEAD) // mask) % 2


def chunk_of(masks):
    chunk = 0
    for mask in masks:
        chunk = chunk * 2 + bit_of(mask)
    return chunk


def sum_rows(value, masks, axis):
    for mask in masks:
        bit = bit_of(mask)
        half = value.shape[axis] // 2
        away = lax.dynamic_slice_in_dim(value, (1 - bit) * half, half, axis).astype(low)
        kept = lax.dynamic_slice_in_dim(value, bit * half, half, axis)
        value = kept.astype(full) + head_swap(away, mask).astype(full)
    return value


def gather_rows(value, masks, axis):
    for mask in masks[::-1]:
        bit = bit_of(mask)
        got = head_swap(value, mask)
        value = jnp.concatenate(
            [jnp.where(bit == 1, got, value), jnp.where(bit == 1, value, got)], axis
        )
    return value


def sum_row16(value, masks):
    state = lax.axis_index(STATE)
    value = sum_rows(value, masks, 1)
    away = lax.dynamic_index_in_dim(value, 1 - state, 0, False).astype(low)
    kept = lax.dynamic_index_in_dim(value, state, 0, False)
    return kept + state_swap(away).astype(full)


def gather_row16(value, masks):
    state = lax.axis_index(STATE)
    got = state_swap(value)
    both = jnp.stack([jnp.where(state == 0, value, got), jnp.where(state == 0, got, value)], 0)
    return gather_rows(both, masks, 1)


def pick_state(pair, index):
    return jnp.where(index == 0, pair[0], pair[1])


def weight_pieces(shard, axis):
    state = lax.axis_index(STATE)
    dp = lax.axis_index(DP)
    half = shard.shape[axis] // 2
    mine = lax.dynamic_slice_in_dim(shard, state * half, half, axis)
    got = state_swap(lax.dynamic_slice_in_dim(shard, (1 - state) * half, half, axis))
    far_mine = dp_swap(mine)
    far_got = dp_swap(got)
    near = [jnp.where(state == 0, mine, got), jnp.where(state == 0, got, mine)]
    far = [jnp.where(state == 0, far_mine, far_got), jnp.where(state == 0, far_got, far_mine)]
    lower = [jnp.where(dp == 0, a, b) for a, b in zip(near, far)]
    upper = [jnp.where(dp == 0, b, a) for a, b in zip(near, far)]
    return jnp.concatenate(lower + upper, 1 - axis)


def grad_pieces(grad, axis):
    state = lax.axis_index(STATE)
    dp = lax.axis_index(DP)
    half = grad.shape[1 - axis] // 2
    away = lax.dynamic_slice_in_dim(grad, (1 - dp) * half, half, 1 - axis).astype(low)
    kept = lax.dynamic_slice_in_dim(grad, dp * half, half, 1 - axis)
    total = kept + dp_swap(away).astype(full)
    quarter = half // 2
    away = lax.dynamic_slice_in_dim(total, (1 - state) * quarter, quarter, 1 - axis).astype(low)
    kept = lax.dynamic_slice_in_dim(total, state * quarter, quarter, 1 - axis)
    got = state_swap(away).astype(full)
    return jnp.concatenate(
        [jnp.where(state == 0, kept, got), jnp.where(state == 0, got, kept)], axis
    )


def norm_scale(values):
    return lax.rsqrt(jnp.mean(values * values, -1, keepdims=True) + epsilon)


def norm_back(values, gain, grad):
    scale = norm_scale(values)
    scaled = grad * gain
    inner = jnp.mean(scaled * values, -1, keepdims=True)
    return (
        scale * scaled - values * (scale * scale * scale * inner),
        jnp.sum(grad * values * scale, 0),
    )


def conv_edge(values, edge, taps, segment, edge_segment):
    reach = taps.shape[0] - 1
    rows = values.shape[0]
    joined = jnp.concatenate([edge, values], 0)
    segs = jnp.concatenate([edge_segment, segment], 0)
    total = taps[0][None, :] * values
    for offset in range(1, taps.shape[0]):
        lower = reach - offset
        same = (segs[lower : lower + rows] == segment).astype(values.dtype)[:, None]
        total = total + taps[offset][None, :] * joined[lower : lower + rows] * same
    return total


def vmem_limit(mebibytes):
    return pltpu.CompilerParams(vmem_limit_bytes=mebibytes * 1024 * 1024)


def dot_nt(left, right):
    return lax.dot_general(left, right, (((1,), (1,)), ((), ())), preferred_element_type=full)


def dot_tn(left, right):
    return lax.dot_general(left, right, (((0,), (0,)), ((), ())), preferred_element_type=full)


def dot_nn(left, right):
    return lax.dot_general(left, right, (((1,), (0,)), ((), ())), preferred_element_type=full)


def dot_exact(left, right):
    return jnp.dot(left, right, preferred_element_type=full, precision=highest)


ROWS_Q = 256
ROWS_K = 512


def attend_kernel(low_ref, q_ref, k_ref, v_ref, seg_col, seg_row, out_ref, lse_ref):
    index = pl.program_id(1)
    scale = q_ref.shape[1] ** (-0.5)
    query = q_ref[...]
    own = seg_col[...]
    place = index * ROWS_Q + lax.broadcasted_iota(jnp.int32, (ROWS_Q, ROWS_K), 0)

    def step(block, carry):
        top, total, acc = carry
        span = pl.ds(pl.multiple_of(block * ROWS_K, ROWS_K), ROWS_K)
        scores = dot_nt(query, k_ref[span, :]) * scale
        other = block * ROWS_K + lax.broadcasted_iota(jnp.int32, (ROWS_Q, ROWS_K), 1)
        scores = jnp.where((own == seg_row[:, span]) & (other <= place), scores, -1e30)
        higher = jnp.maximum(top, jnp.max(scores, -1, keepdims=True))
        weights = jnp.exp(scores - higher)
        fade = jnp.exp(top - higher)
        total = total * fade + jnp.sum(weights, -1, keepdims=True)
        acc = acc * fade + dot_nn(weights.astype(low), v_ref[span, :])
        return higher, total, acc

    start = (
        jnp.full((ROWS_Q, 1), -1e30, full),
        jnp.zeros((ROWS_Q, 1), full),
        jnp.zeros((ROWS_Q, v_ref.shape[1]), full),
    )
    stop = (index * ROWS_Q + ROWS_Q + ROWS_K - 1) // ROWS_K
    top, total, acc = lax.fori_loop(low_ref[index], stop, step, start)
    out_ref[...] = (acc / total).astype(low)
    lse = jnp.broadcast_to(top + jnp.log(total), (ROWS_Q, 128))
    lse_ref[...] = lse.T[0:1, :][None]


def half_block(index, blocks):
    per_state = blocks // 2
    per_half = per_state // 2
    inside = index % per_state
    return inside // per_half * per_state + index // per_state * per_half + inside % per_half


def attend(queries, keys, values, segment, lows):
    length, columns = queries.shape
    heads = columns // HDIM
    blocks = length // ROWS_Q
    whole = pl.BlockSpec((length, HDIM), lambda h, i, *_: (0, h))
    block = pl.BlockSpec((ROWS_Q, HDIM), lambda h, i, *_: (i, h))
    placed = pl.BlockSpec((ROWS_Q, HDIM), lambda h, i, *_: (half_block(i, blocks), h))
    return pl.pallas_call(
        attend_kernel,
        grid_spec=pltpu.PrefetchScalarGridSpec(
            num_scalar_prefetch=1,
            grid=(heads, length // ROWS_Q),
            in_specs=[
                block,
                whole,
                whole,
                pl.BlockSpec((ROWS_Q, 1), lambda h, i, *_: (i, 0)),
                pl.BlockSpec((1, length), lambda h, i, *_: (0, 0)),
            ],
            out_specs=[placed, pl.BlockSpec((1, 1, ROWS_Q), lambda h, i, *_: (h, 0, i))],
        ),
        out_shape=[
            jax.ShapeDtypeStruct((length, columns), low),
            jax.ShapeDtypeStruct((heads, 1, length), full),
        ],
        compiler_params=vmem_limit(40),
        cost_estimate=pl.CostEstimate(
            flops=22 * length * length * columns, bytes_accessed=8 * length * columns,
            transcendentals=0,
        ),
    )(lows, queries, keys, values, segment[:, None], segment[None, :])


def attend_back_kernel(
    low_ref, q_ref, k_ref, v_ref, do_ref, o_ref, lse_ref, seg_col, seg_row, dq_ref, dk_ref, dv_ref
):
    index = pl.program_id(1)
    scale = q_ref.shape[1] ** (-0.5)
    query = q_ref[...]
    grad = do_ref[...]
    own = seg_row[...]
    lse = lse_ref[0]
    ones = jnp.ones((8, HDIM), full)
    delta = lax.dot_general(
        ones,
        grad.astype(full) * o_ref[...].astype(full),
        (((1,), (1,)), ((), ())),
        precision=highest,
        preferred_element_type=full,
    )[0:1, :]
    place = index * ROWS_Q + lax.broadcasted_iota(jnp.int32, (ROWS_K, ROWS_Q), 1)

    @pl.when(index == 0)
    def clear():
        dk_ref[...] = jnp.zeros_like(dk_ref)
        dv_ref[...] = jnp.zeros_like(dv_ref)

    def step(block, total):
        span = pl.ds(pl.multiple_of(block * ROWS_K, ROWS_K), ROWS_K)
        key = k_ref[span, :]
        scores = dot_nt(key, query) * scale
        other = block * ROWS_K + lax.broadcasted_iota(jnp.int32, (ROWS_K, ROWS_Q), 0)
        counted = (seg_col[span, :] == own) & (other <= place)
        probs = jnp.exp(jnp.where(counted, scores - lse, -1e30))
        dv_ref[span, :] += dot_nn(probs.astype(low), grad)
        slope = probs * (dot_nt(v_ref[span, :], grad) - delta)
        slope = slope.astype(low)
        dk_ref[span, :] += dot_nn(slope, query) * scale
        return total + dot_tn(slope, key)

    stop = (index * ROWS_Q + ROWS_Q + ROWS_K - 1) // ROWS_K
    total = lax.fori_loop(low_ref[index], stop, step, jnp.zeros((ROWS_Q, HDIM), full))
    dq_ref[...] = total * scale


def attend_back(queries, keys, values, grads, outs, lse, segment, lows):
    length, columns = queries.shape
    heads = columns // HDIM
    blocks = length // ROWS_Q
    whole = pl.BlockSpec((length, HDIM), lambda h, i, *_: (0, h))
    block = pl.BlockSpec((ROWS_Q, HDIM), lambda h, i, *_: (i, h))
    placed = pl.BlockSpec((ROWS_Q, HDIM), lambda h, i, *_: (half_block(i, blocks), h))
    line = pl.BlockSpec((1, 1, ROWS_Q), lambda h, i, *_: (h, 0, i))
    shape = jax.ShapeDtypeStruct((length, columns), full)
    return pl.pallas_call(
        attend_back_kernel,
        grid_spec=pltpu.PrefetchScalarGridSpec(
            num_scalar_prefetch=1,
            grid=(heads, length // ROWS_Q),
            in_specs=[
                block,
                whole,
                whole,
                placed,
                placed,
                line,
                pl.BlockSpec((length, 1), lambda h, i, *_: (0, 0)),
                pl.BlockSpec((1, ROWS_Q), lambda h, i, *_: (0, i)),
            ],
            out_specs=[block, whole, whole],
        ),
        out_shape=[shape, shape, shape],
        compiler_params=vmem_limit(40),
        cost_estimate=pl.CostEstimate(
            flops=30 * length * length * columns, bytes_accessed=20 * length * columns,
            transcendentals=0,
        ),
    )(lows, queries, keys, values, grads, outs, lse, segment[:, None], segment[None, :])


def rope_kernel(state_ref, own_ref, other_ref, cos_ref, sin_ref, q_ref, k_ref, v_ref):
    per_state = pl.num_programs(0) // 2
    own = pl.program_id(0) // per_state == state_ref[0]
    columns = q_ref.shape[1]
    for index, out in enumerate((q_ref, k_ref, v_ref)):
        for start in range(0, columns, HDIM):
            lanes = slice(index * columns + start, index * columns + start + HDIM)
            value = jnp.where(own, own_ref[:, lanes], other_ref[:, lanes])
            if index < 2:
                value = value * cos_ref[...] + pltpu.roll(value, HDIM // 2, 1) * sin_ref[...]
            out[:, start : start + HDIM] = value.astype(low)


def rope(state, own, other, cosine, sine):
    length = cosine.shape[0]
    columns = own.shape[1] // 3
    per_state = length // ROWS_Q // 2
    part = pl.BlockSpec((ROWS_Q, own.shape[1]), lambda i, *_: (i % per_state, 0))
    angle = pl.BlockSpec((ROWS_Q, HDIM), lambda i, *_: (i, 0))
    out = pl.BlockSpec((ROWS_Q, columns), lambda i, *_: (i, 0))
    return pl.pallas_call(
        rope_kernel,
        grid_spec=pltpu.PrefetchScalarGridSpec(
            num_scalar_prefetch=1,
            grid=(length // ROWS_Q,),
            in_specs=[part, part, angle, angle],
            out_specs=[out] * 3,
        ),
        out_shape=[jax.ShapeDtypeStruct((length, columns), low)] * 3,
        compiler_params=vmem_limit(32),
        cost_estimate=pl.CostEstimate(
            flops=12 * length * columns, bytes_accessed=36 * length * columns, transcendentals=0
        ),
    )(state[None], own, other, cosine, sine)


def rope_back_kernel(q_ref, k_ref, v_ref, cos_ref, sin_ref, out_ref):
    columns = q_ref.shape[1]
    for index, part in enumerate((q_ref, k_ref, v_ref)):
        for start in range(0, columns, HDIM):
            value = part[:, start : start + HDIM]
            if index < 2:
                value = value * cos_ref[...] - pltpu.roll(value, HDIM // 2, 1) * sin_ref[...]
            lanes = slice(index * columns + start, index * columns + start + HDIM)
            out_ref[:, lanes] = value.astype(low)


def rope_back(query, key, value, cosine, sine):
    length, columns = query.shape
    blocks = length // ROWS_Q
    part = pl.BlockSpec((ROWS_Q, columns), lambda i: (i, 0))
    angle = pl.BlockSpec((ROWS_Q, HDIM), lambda i: (i, 0))
    return pl.pallas_call(
        rope_back_kernel,
        grid=(blocks,),
        in_specs=[part, part, part, angle, angle],
        out_specs=pl.BlockSpec((ROWS_Q, 3 * columns), lambda i: (half_block(i, blocks), 0)),
        out_shape=jax.ShapeDtypeStruct((length, 3 * columns), low),
        compiler_params=vmem_limit(32),
        cost_estimate=pl.CostEstimate(
            flops=12 * length * columns, bytes_accessed=24 * length * columns, transcendentals=0
        ),
    )(query, key, value, cosine, sine)


def hold_kernel(*refs):
    pass


def hold(value, *after, cost=0):
    anywhere = pl.BlockSpec(memory_space=pl.ANY)
    return pl.pallas_call(
        hold_kernel,
        in_specs=[anywhere] * (1 + len(after)),
        out_specs=anywhere,
        out_shape=jax.ShapeDtypeStruct(value.shape, value.dtype),
        input_output_aliases={0: 0},
        cost_estimate=pl.CostEstimate(
            flops=cost * 1_100_000_000, bytes_accessed=0, transcendentals=0
        ),
    )(value, *after)


def first_blocks(segment):
    length = segment.shape[0]
    heads = segment[::ROWS_Q]
    starts = jnp.sum((segment[None, :] < heads[:, None]).astype(jnp.int32), 1)
    return starts // ROWS_K


def pair_lanes(left, right):
    lane = lax.broadcasted_iota(jnp.int32, (1, 2 * MDIM), 1)
    return jnp.where(lane < MDIM, left, right)


def block_decay(dt_ref, dt_row_ref, rate_ref, rate_col_ref):
    rows = lax.broadcasted_iota(jnp.int32, (GROUP, GROUP), 0)
    cols = lax.broadcasted_iota(jnp.int32, (GROUP, GROUP), 1)
    cumul = dot_exact((cols <= rows).astype(full), dt_ref[...] * rate_ref[...])
    cumul_row = dot_exact(dt_row_ref[...] * rate_col_ref[...], (rows <= cols).astype(full))
    return cumul, cumul_row, rows, cols


def edge_flags(ends_ref, index, seg_col):
    before = ends_ref[index]
    last = ends_ref[index + 1]
    carried = (seg_col[...] == before).astype(full)
    reach = (seg_col[...] == last).astype(full)
    keep = (before == last).astype(full)
    return carried, reach, keep


def pair_columns(values, pair):
    return pair_lanes(values[:, 2 * pair : 2 * pair + 1], values[:, 2 * pair + 1 : 2 * pair + 2])


def step_state(state, pair, scaled, cumul, reach, keep, vec_low):
    column = pair_columns(cumul, pair)
    end = column[GROUP - 1 : GROUP, :]
    weight = jnp.exp(end - column) * reach
    return state * (jnp.exp(end) * keep) + dot_tn(vec_low, (scaled * weight).astype(low)), weight


def scan_end_kernel(
    ends_ref, x_ref, dt_ref, dt_row_ref, rate_ref, rate_col_ref, b_ref, seg_col, out_ref
):
    index = pl.program_id(0)
    cumul, unused_row, unused_a, unused_b = block_decay(dt_ref, dt_row_ref, rate_ref, rate_col_ref)
    unused_c, reach, keep = edge_flags(ends_ref, index, seg_col)
    vec_low = b_ref[...].astype(low)

    @pl.when(index == 0)
    def clear():
        out_ref[...] = jnp.zeros_like(out_ref)

    for pair in range(dt_ref.shape[1] // 2):
        lanes = slice(pair * 2 * MDIM, (pair + 1) * 2 * MDIM)
        scaled = x_ref[:, lanes] * pair_columns(dt_ref[...], pair)
        out_ref[:, lanes], unused_d = step_state(
            out_ref[:, lanes], pair, scaled, cumul, reach, keep, vec_low
        )


def scan_kernel(
    ends_ref,
    x_ref,
    dt_ref,
    dt_row_ref,
    rate_ref,
    rate_col_ref,
    b_ref,
    c_ref,
    seg_col,
    seg_row,
    first_ref,
    out_ref,
    states_ref,
    state,
):
    index = pl.program_id(0)
    cumul, cumul_row, rows, cols = block_decay(dt_ref, dt_row_ref, rate_ref, rate_col_ref)
    carried, reach, keep = edge_flags(ends_ref, index, seg_col)
    vec_low = b_ref[...].astype(low)
    read_low = c_ref[...].astype(low)
    allowed = (seg_col[...] == seg_row[...]) & (cols <= rows)
    inner = jnp.where(allowed, dot_nt(read_low, vec_low), 0.0)

    @pl.when(index == 0)
    def begin():
        state[...] = first_ref[...]

    states_ref[0] = state[...]
    for pair in range(dt_ref.shape[1] // 2):
        lanes = slice(pair * 2 * MDIM, (pair + 1) * 2 * MDIM)
        scaled = x_ref[:, lanes] * pair_columns(dt_ref[...], pair)
        scaled_low = scaled.astype(low)
        parts = []
        for head in (2 * pair, 2 * pair + 1):
            gaps = cumul[:, head : head + 1] - cumul_row[head : head + 1, :]
            mixed = inner * jnp.exp(jnp.minimum(gaps, 0.0))
            parts.append(dot_nn(mixed.astype(low), scaled_low))
        entry = jnp.exp(pair_columns(cumul, pair)) * carried
        held = state[:, lanes]
        out_ref[:, lanes] = pair_lanes(*parts) + dot_nn(read_low, held.astype(low)) * entry
        state[:, lanes], unused = step_state(
            held, pair, scaled, cumul, reach, keep, vec_low
        )


def scan_start_grad_kernel(
    ends_ref, dt_ref, dt_row_ref, rate_ref, rate_col_ref, c_ref, seg_col, dy_ref, out_ref
):
    index = pl.num_programs(0) - 1 - pl.program_id(0)
    cumul, unused_row, unused_a, unused_b = block_decay(dt_ref, dt_row_ref, rate_ref, rate_col_ref)
    carried, unused_c, keep = edge_flags(ends_ref, index, seg_col)
    read_low = c_ref[...].astype(low)

    @pl.when(pl.program_id(0) == 0)
    def clear():
        out_ref[...] = jnp.zeros_like(out_ref)

    for pair in range(dt_ref.shape[1] // 2):
        lanes = slice(pair * 2 * MDIM, (pair + 1) * 2 * MDIM)
        column = pair_columns(cumul, pair)
        retain = jnp.exp(column[GROUP - 1 : GROUP, :]) * keep
        entry = jnp.exp(column) * carried
        out_ref[:, lanes] = out_ref[:, lanes] * retain + dot_tn(
            read_low, (dy_ref[:, lanes] * entry).astype(low)
        )


def scan_back_kernel(
    ends_ref,
    x_ref,
    dt_ref,
    dt_row_ref,
    rate_ref,
    rate_col_ref,
    b_ref,
    c_ref,
    seg_col,
    seg_row,
    dy_ref,
    states_ref,
    last_ref,
    dx_ref,
    ddt_ref,
    dlog_ref,
    dlog_row_ref,
    db_ref,
    dc_ref,
    state_grad,
    inner_grad,
):
    index = pl.num_programs(0) - 1 - pl.program_id(0)
    heads = dt_ref.shape[1]
    cumul, cumul_row, rows, cols = block_decay(dt_ref, dt_row_ref, rate_ref, rate_col_ref)
    carried, reach, keep = edge_flags(ends_ref, index, seg_col)
    vec_low = b_ref[...].astype(low)
    read_low = c_ref[...].astype(low)
    allowed = (seg_col[...] == seg_row[...]) & (cols <= rows)
    inner = jnp.where(allowed, dot_nt(read_low, vec_low), 0.0)
    head_lane = lax.broadcasted_iota(jnp.int32, (GROUP, heads), 1)
    head_row = lax.broadcasted_iota(jnp.int32, (heads, GROUP), 0)
    last_row = lax.broadcasted_iota(jnp.int32, (GROUP, 1), 0) == GROUP - 1
    lane = lax.broadcasted_iota(jnp.int32, (1, 2 * MDIM), 1)

    @pl.when(pl.program_id(0) == 0)
    def begin():
        state_grad[...] = last_ref[...]

    inner_grad[...] = jnp.zeros_like(inner_grad)
    decay_grad = jnp.zeros((GROUP, heads), full)
    decay_row = jnp.zeros((heads, GROUP), full)
    step_grad = jnp.zeros((GROUP, heads), full)
    vec_grad = jnp.zeros(b_ref.shape, full)
    read_grad = jnp.zeros(c_ref.shape, full)
    for pair in range(heads // 2):
        lanes = slice(pair * 2 * MDIM, (pair + 1) * 2 * MDIM)
        values = x_ref[:, lanes]
        steps = pair_columns(dt_ref[...], pair)
        scaled = values * steps
        scaled_low = scaled.astype(low)
        grad = dy_ref[:, lanes]
        grad_low = grad.astype(low)
        held = states_ref[0, :, lanes]
        held_low = held.astype(low)
        later = state_grad[:, lanes]
        later_low = later.astype(low)
        column = pair_columns(cumul, pair)
        end = column[GROUP - 1 : GROUP, :]
        weight = jnp.exp(end - column) * reach
        retain = jnp.exp(end) * keep
        entry = jnp.exp(column) * carried
        parts = []
        for side in range(2):
            head = 2 * pair + side
            gaps = cumul[:, head : head + 1] - cumul_row[head : head + 1, :]
            fading = jnp.where(allowed, jnp.exp(jnp.minimum(gaps, 0.0)), 0.0)
            mixed = inner * fading
            own_lanes = (lane < MDIM) == (side == 0)
            outer = dot_nt(jnp.where(own_lanes, grad, 0.0).astype(low), scaled_low)
            inner_grad[...] += outer * fading
            slope = outer * mixed
            decay_grad = jnp.where(
                head_lane == head, decay_grad + jnp.sum(slope, 1, keepdims=True), decay_grad
            )
            decay_row = jnp.where(
                head_row == head, jnp.sum(slope, 0, keepdims=True), decay_row
            )
            parts.append(dot_tn(mixed.astype(low), grad_low))
        weighted = scaled * weight
        entered = grad * entry
        entered_low = entered.astype(low)
        from_later = dot_nn(vec_low, later_low)
        scaled_grad = pair_lanes(*parts) + weight * from_later
        dx_ref[:, lanes] = scaled_grad * steps
        read_grad += dot_nt(entered_low, held_low)
        vec_grad += dot_nt(weighted.astype(low), later_low)
        fresh = weighted * from_later
        flow = entered * dot_nn(read_low, held_low) - fresh
        finish = jnp.sum(fresh, 0, keepdims=True) + retain * jnp.sum(later * held, 0, keepdims=True)
        steps_part = scaled_grad * values
        for side in range(2):
            head = 2 * pair + side
            own_lanes = (lane < MDIM) == (side == 0)
            total = jnp.sum(jnp.where(own_lanes, flow, 0.0), 1, keepdims=True)
            ending = jnp.sum(jnp.where(own_lanes, finish, 0.0), 1, keepdims=True)
            total = total + jnp.where(last_row, ending, 0.0)
            decay_grad = jnp.where(head_lane == head, decay_grad + total, decay_grad)
            step_grad = jnp.where(
                head_lane == head,
                jnp.sum(jnp.where(own_lanes, steps_part, 0.0), 1, keepdims=True),
                step_grad,
            )
        state_grad[:, lanes] = later * retain + dot_tn(read_low, entered_low)
    inner_low = inner_grad[...].astype(low)
    ddt_ref[...] = step_grad
    dlog_ref[...] = dot_exact((cols >= rows).astype(full), decay_grad)
    dlog_row_ref[...] = dot_exact(decay_row, (rows >= cols).astype(full))
    dc_ref[...] = read_grad + dot_nn(inner_low, vec_low)
    db_ref[...] = vec_grad + dot_tn(inner_low, read_low)


def scan_specs(heads, channels, states, reverse, count):
    def at(i):
        return count - 1 - i if reverse else i

    tall = lambda columns: pl.BlockSpec((GROUP, columns), lambda i, *_: (at(i), 0))
    flat = lambda rows: pl.BlockSpec((rows, GROUP), lambda i, *_: (0, at(i)))
    same = lambda rows, columns: pl.BlockSpec((rows, columns), lambda i, *_: (0, 0))
    return tall, flat, same, pl.BlockSpec((1, states, channels), lambda i, *_: (at(i), 0, 0))


def scan_call(kernel, reverse, ends, inputs, kinds, outs, out_kinds, scratch, dims, flops):
    heads, channels, states, count = dims
    tall, flat, same, cube = scan_specs(heads, channels, states, reverse, count)

    def spec(kind, shape):
        if kind == 0:
            return tall(shape[1])
        if kind == 1:
            return flat(shape[0])
        return same(*shape) if kind == 2 else cube

    return pl.pallas_call(
        kernel,
        grid_spec=pltpu.PrefetchScalarGridSpec(
            num_scalar_prefetch=1,
            grid=(count,),
            in_specs=[spec(kind, value.shape) for kind, value in zip(kinds, inputs)],
            out_specs=[spec(kind, shape) for kind, shape in zip(out_kinds, outs)],
            scratch_shapes=scratch,
        ),
        out_shape=[jax.ShapeDtypeStruct(shape, full) for shape in outs],
        compiler_params=vmem_limit(40),
        cost_estimate=pl.CostEstimate(
            flops=flops, bytes_accessed=8 * count * GROUP * channels, transcendentals=0
        ),
    )(ends, *inputs)


class Scan:
    def __init__(self, x, dt, rate, b, c, segment, before):
        self.rows, self.heads = dt.shape
        self.channels, self.states = x.shape[1], b.shape[1]
        self.count = self.rows // GROUP
        self.dims = (self.heads, self.channels, self.states, self.count)
        self.ends = jnp.concatenate([before[None], segment[GROUP - 1 :: GROUP]])
        self.x, self.b, self.c = x, b, c
        self.decay = [dt, dt.T, rate[None, :], rate[:, None]]
        self.seg_col, self.seg_row = segment[:, None], segment[None, :]
        self.state_shape = (self.states, self.channels)

    def end(self):
        return scan_call(
            scan_end_kernel,
            False,
            self.ends,
            [self.x, *self.decay, self.b, self.seg_col],
            [0, 0, 1, 2, 2, 0, 0],
            [self.state_shape],
            [2],
            [],
            self.dims,
            160 * self.rows * self.channels * self.states,
        )[0]

    def forward(self, first):
        return scan_call(
            scan_kernel,
            False,
            self.ends,
            [self.x, *self.decay, self.b, self.c, self.seg_col, self.seg_row, first],
            [0, 0, 1, 2, 2, 0, 0, 0, 1, 2],
            [self.x.shape, (self.count,) + self.state_shape],
            [0, 3],
            [pltpu.VMEM(self.state_shape, full)],
            self.dims,
            56 * self.rows * self.channels * GROUP,
        )

    def start_grad(self, grad):
        return scan_call(
            scan_start_grad_kernel,
            True,
            self.ends,
            [*self.decay, self.c, self.seg_col, grad],
            [0, 1, 2, 2, 0, 0, 0],
            [self.state_shape],
            [2],
            [],
            self.dims,
            160 * self.rows * self.channels * self.states,
        )[0]

    def backward(self, grad, states, last):
        wide = (self.rows, self.heads)
        return scan_call(
            scan_back_kernel,
            True,
            self.ends,
            [
                self.x,
                *self.decay,
                self.b,
                self.c,
                self.seg_col,
                self.seg_row,
                grad,
                states,
                last,
            ],
            [0, 0, 1, 2, 2, 0, 0, 0, 1, 0, 3, 2],
            [self.x.shape, wide, wide, wide[::-1], self.b.shape, self.c.shape],
            [0, 0, 0, 1, 0, 0],
            [pltpu.VMEM(self.state_shape, full), pltpu.VMEM((GROUP, GROUP), full)],
            self.dims,
            144 * self.rows * self.channels * GROUP,
        )


def natural_quarters(relative):
    state = lax.axis_index(STATE)
    dp = lax.axis_index(DP)
    near = [jnp.where(state == 0, *relative[:2]), jnp.where(state == 0, *relative[1::-1])]
    far = [jnp.where(state == 0, *relative[2:]), jnp.where(state == 0, *relative[:1:-1])]
    return [jnp.where(dp == 0, a, b) for a, b in zip(near, far)] + [
        jnp.where(dp == 0, b, a) for a, b in zip(near, far)
    ]


def natural_heads(value):
    count = lax.axis_size(HEAD).bit_length() - 1
    cubes = value.reshape((2,) * count + value.shape[1:])
    turned = list(range(count - 1, -1, -1)) + list(range(count, cubes.ndim))
    return cubes.transpose(turned).reshape(value.shape)


def cut_rows(value, order, axis):
    bit = bit_of(order[0])
    half = value.shape[axis] // 2
    return (
        lax.dynamic_slice_in_dim(value, (1 - bit) * half, half, axis),
        lax.dynamic_slice_in_dim(value, bit * half, half, axis),
    )


def sum_products(pieces, product, order, axis):
    away = product(pieces[0]).astype(low)
    value = product(pieces[1]) + head_swap(away, order[0]).astype(full)
    return away, sum_rows(value, order[1:], axis)


def finish_state(total, swap=lambda value: value):
    state = lax.axis_index(STATE)
    away = swap(lax.dynamic_index_in_dim(total, 1 - state, 0, False).astype(low))
    kept = lax.dynamic_index_in_dim(total, state, 0, False)
    return kept + state_swap(away).astype(full)


def swap_quarters(value):
    quarter = value.shape[-1] // 4
    part = [value[..., i * quarter : (i + 1) * quarter] for i in range(4)]
    return jnp.concatenate([part[1], part[0], part[3], part[2]], -1)


def fast_device(
    hidden,
    embedding,
    cotangent,
    lengths,
    gain_attn,
    w_query,
    w_key,
    w_value,
    down_query,
    down_key,
    down_value,
    up_query,
    up_key,
    up_value,
    attn_output,
    gain_mlp,
    mlp_input,
    down_mlp,
    up_mlp,
    mlp_output,
    gain_mixer,
    proj_inner,
    proj_gate,
    proj_step,
    proj_input,
    proj_read,
    taps_inner,
    taps_input,
    taps_read,
    step_bias,
    log_rate,
    skip_gain,
    gain_gated,
    proj_output,
):
    rows = hidden.shape[0]
    length = cotangent.shape[0]
    width = hidden.shape[1]
    middle = rows // 2
    head_parts = lax.axis_size(HEAD)
    piece = middle // head_parts
    state = lax.axis_index(STATE)
    dp = lax.axis_index(DP)
    head = lax.axis_index(HEAD)
    place = dp * 2 + state
    own_start = state * rows
    orders = head_masks()
    offsets = [chunk_of(orders[0]) * piece, middle + chunk_of(orders[1]) * piece]

    heads_wide = w_query.shape[1]
    half_cols = heads_wide // 2

    def state_columns(values, index):
        return jnp.concatenate(
            [lax.dynamic_slice_in_dim(v, index * half_cols, half_cols, 1) for v in values], 1
        )

    rank = down_query.shape[1]
    part_a = down_query.shape[0] // head_parts
    part_m = down_mlp.shape[0] // head_parts
    split_a, split_m = gain_attn.shape[0], gain_mlp.shape[0]
    up_rows = up_query.shape[0]

    def small_pack(index):
        return jnp.concatenate(
            [
                jnp.concatenate([gain_attn, gain_mlp, gain_mixer]).reshape(-1, rank),
                lax.dynamic_slice_in_dim(down_query, head * part_a, part_a, 0),
                lax.dynamic_slice_in_dim(down_key, head * part_a, part_a, 0),
                lax.dynamic_slice_in_dim(down_value, head * part_a, part_a, 0),
                lax.dynamic_slice_in_dim(down_mlp, head * part_m, part_m, 0),
                up_mlp.reshape(-1, rank),
                proj_step.reshape(-1, rank),
                state_columns((up_query, up_key, up_value), index).reshape(-1, rank),
            ],
            0,
        )

    pack = jnp.stack([small_pack(state), state_swap(small_pack(1 - state))], 0)
    pack_far = dp_swap(pack)
    mine = hold(state_columns((w_query, w_key, w_value), state), pack_far)
    got = state_swap(hold(state_columns((w_query, w_key, w_value), 1 - state), pack))
    cutting = mine.shape[0] // 2
    far_mine = [dp_swap(mine[:cutting]), dp_swap(mine[cutting:])]
    far_got = [dp_swap(got[:cutting]), dp_swap(got[cutting:])]

    share = rows // head_parts
    sent = jnp.stack(
        [
            lax.dynamic_slice_in_dim(value, chunk_of(order) * share, share, 0)
            for value, order in zip((hidden, embedding), orders)
        ],
        0,
    )
    sent = state_swap(sent)

    pack = jnp.concatenate([pack, pack_far], 0)
    gain_rows = (split_a + 2 * split_m) // rank
    gains = pack[:, :gain_rows].reshape(4, -1).astype(full)
    attn_gain = gains[:, :split_a].reshape(-1)
    gains = natural_quarters([gains[index] for index in range(4)])
    mlp_gain = jnp.concatenate([value[split_a : split_a + split_m] for value in gains])
    mixer_gain = jnp.concatenate([value[split_a + split_m :] for value in gains])
    down_end = gain_rows + 3 * part_a + part_m
    step_width = proj_step.shape[1]
    step_start = down_end + up_mlp.size // rank
    step_end = step_start + proj_step.size // rank
    mlp_upper = jnp.concatenate(
        natural_quarters(
            [pack[index, down_end:step_start].reshape(up_mlp.shape) for index in range(4)]
        ),
        0,
    )
    step_main = jnp.concatenate(
        natural_quarters(
            [pack[index, step_start:step_end].reshape(proj_step.shape) for index in range(4)]
        ),
        0,
    )
    ups = natural_quarters(
        [pack[index, step_end:].reshape(up_rows, 3 * half_cols) for index in range(4)]
    )
    ups = jnp.concatenate(ups, 0)
    column = lax.broadcasted_iota(jnp.int32, (1, 3 * half_cols), 1) // half_cols
    up_wide = jnp.concatenate(
        [jnp.where(column == index, ups, jnp.zeros_like(ups)) for index in range(3)], 0
    )
    masks = orders[0][::-1]
    downs_all = natural_heads(gather_rows(pack[None, :, gain_rows:down_end], orders[0], 0))

    def down_of(lower, part):
        return downs_all[:, :, lower : lower + part].transpose(1, 0, 2, 3)

    down_wide = jnp.concatenate(
        [down_of(index * part_a, part_a).reshape(-1, rank) for index in range(3)], 1
    )
    down_m = down_of(3 * part_a, part_m)
    mlp_down = jnp.concatenate(natural_quarters([down_m[i] for i in range(4)]), 0)
    mlp_down = mlp_down.reshape(-1, rank)

    segment, position, valid = row_layout(lengths[0], length)
    own_segment = lax.dynamic_slice_in_dim(segment, own_start, rows)
    own_valid = lax.dynamic_slice_in_dim(valid, own_start, rows)[:, None]
    lows = first_blocks(segment)
    half = HDIM // 2
    angle = position[:, None] * 10000.0 ** (-jnp.arange(half, dtype=full) / half)[None, :]
    cosine = jnp.concatenate([jnp.cos(angle), jnp.cos(angle)], 1)
    sine = jnp.concatenate([-jnp.sin(angle), jnp.sin(angle)], 1)

    def cut(value):
        return [lax.dynamic_slice_in_dim(value, offset, piece, 0) for offset in offsets]

    valid_cut = cut(own_valid)

    quarter = gain_attn.shape[0]

    def quarters(first, second):
        parts = []
        for index in range(4):
            start = (state ^ (index % 2)) * quarter
            part = [lax.dynamic_slice_in_dim(v, start, quarter, 1) for v in (first, second)]
            parts.append(jnp.where(dp == index // 2, *part).astype(full))
        return parts

    def joint_scale(first, second):
        squares = [jnp.sum(jnp.square(v.astype(full)), 1, keepdims=True) for v in (first, second)]
        return lax.rsqrt((squares[0] + squares[1]) / (2 * width) + epsilon)

    def normed_rows(first, second):
        scale = joint_scale(first, second)
        parts = [
            (part * scale * attn_gain[index * quarter : (index + 1) * quarter]).astype(low)
            for index, part in enumerate(quarters(first, second))
        ]
        return jnp.concatenate(parts[:2], 1), jnp.concatenate(parts[2:], 1)

    near_own, far_own = normed_rows(hidden, embedding)
    joined_cut = [
        jnp.concatenate(quarters(a, b), 1) for a, b in zip(cut(hidden), cut(embedding))
    ]

    others = [gather_rows(sent[i], orders[i], 0) for i in range(2)]
    others[0] = hold(others[0], others[1], cosine, sine, down_wide)
    near_other, far_other = normed_rows(*others)
    main_near = jnp.concatenate([mine, got], 0)

    def project_near(near, far):
        reduced = (plain_dot(near, down_wide[:width]) + plain_dot(far, down_wide[width:])).astype(low)
        return plain_dot(near, main_near) + plain_dot(reduced, up_wide), reduced

    pre_own, red_own = project_near(near_own, far_own)
    pre_other, red_other = project_near(near_other, far_other)
    far_got[0] = hold(far_got[0], pre_own, pre_other)
    main_far = jnp.concatenate(far_mine + far_got, 0)
    pre_own = pre_own + plain_dot(far_own, main_far)
    pre_other = pre_other + plain_dot(far_other, main_far)
    queries, keys, values = rope(state, pre_own, pre_other, cosine, sine)

    attn_output = hold(attn_output, *far_mine)
    attn_mine = lax.dynamic_slice_in_dim(attn_output, state * half_cols, half_cols, 0)
    attn_got = state_swap(
        lax.dynamic_slice_in_dim(attn_output, (1 - state) * half_cols, half_cols, 0)
    )
    attn_pair = jnp.stack([attn_mine, attn_got], 0)
    attn_far = dp_swap(attn_pair)
    attn_proj = jnp.concatenate(
        natural_quarters([attn_pair[0], attn_pair[1], attn_far[0], attn_far[1]]), 1
    )
    mlp_cut = mlp_input.shape[1] // 2
    mlp_input = hold(mlp_input, far_got[0], far_got[1], *far_mine, attn_far)
    mlp_first = lax.all_gather(mlp_input[:, :mlp_cut], ZED, axis=0, tiled=True)
    mlp_second = lax.all_gather(mlp_input[:, mlp_cut:], ZED, axis=0, tiled=True)
    mlp_main = jnp.concatenate([mlp_first, mlp_second], 1)
    attended, lse = attend(queries, keys, values, segment, lows)

    attended = hold(attended, mlp_first)
    attended_halves = [attended[:rows], attended[rows:]]
    def branch_product(part):
        return plain_dot(part.reshape(-1, part.shape[2]), attn_proj).reshape(2, -1, width)

    branch_cut = []
    for part, order in zip(attended_halves, orders):
        pieces = cut_rows(part.reshape(2, middle, -1), order, 1)
        branch_cut.append(finish_state(sum_products(pieces, branch_product, order, 1)[1]))
    mlp_proj = lax.all_gather(mlp_output, ZED, axis=1, tiled=True)
    mixer_main = lax.all_gather(
        jnp.concatenate([proj_inner, proj_gate], 1), ZED, axis=0, tiled=True
    )
    output_main = lax.all_gather(proj_output, ZED, axis=1, tiled=True)
    first_cut = [
        value.astype(full) + good * branch
        for value, good, branch in zip(cut(hidden), valid_cut, branch_cut)
    ]
    mlp_normed = [
        gather_rows(rms_norm(value, mlp_gain).astype(low), order, 0)
        for value, order in zip(first_cut, orders)
    ]
    mlp_red = [plain_dot(value, mlp_down).astype(low) for value in mlp_normed]
    hidden_pre = [
        plain_dot(value, mlp_main) + plain_dot(red, mlp_upper)
        for value, red in zip(mlp_normed, mlp_red)
    ]
    activated = [jax.nn.gelu(value, approximate=False).astype(low) for value in hidden_pre]
    second_cut = [
        value
        + good
        * sum_products(
            cut_rows(part, order, 0), lambda rows: plain_dot(rows, mlp_proj), order, 0
        )[1]
        for value, good, part, order in zip(first_cut, valid_cut, activated, orders)
    ]
    mixer_normed = jnp.concatenate(
        [
            gather_rows(rms_norm(value, mixer_gain).astype(low), order, 0)
            for value, order in zip(second_cut, orders)
        ],
        0,
    )

    inner_width = proj_inner.shape[1]
    mixer_heads = step_width
    states = proj_input.shape[1]
    small_main = jnp.concatenate([step_main, proj_input, proj_read], 1)
    small_pre = plain_dot(mixer_normed, small_main)
    mixer_pre = plain_dot(mixer_normed, mixer_main)
    inner_pre, gate_pre = mixer_pre[:, :inner_width], mixer_pre[:, inner_width:]
    reach = taps_inner.shape[0] - 1
    edge = state_forward(
        jnp.concatenate([inner_pre[rows - reach :], small_pre[rows - reach :, mixer_heads:]], 1)
    )
    edge_start = jnp.maximum(own_start - reach, 0)
    edge_segment = jnp.where(state == 0, -1, lax.dynamic_slice_in_dim(segment, edge_start, reach))

    def conv_piece(inner_in, small_in, edge_in, taps_x, taps_b, taps_c, shift_in):
        input_in = small_in[:, mixer_heads : mixer_heads + states]
        read_in = small_in[:, mixer_heads + states :]
        edge_b = edge_in[:, inner_width : inner_width + states]
        edge_c = edge_in[:, inner_width + states :]
        return (
            jax.nn.silu(
                conv_edge(inner_in, edge_in[:, :inner_width], taps_x, own_segment, edge_segment)
            ),
            jax.nn.silu(conv_edge(input_in, edge_b, taps_b, own_segment, edge_segment)),
            jax.nn.silu(conv_edge(read_in, edge_c, taps_c, own_segment, edge_segment)),
            jax.nn.softplus(small_in[:, :mixer_heads] + shift_in[None, :]),
        )

    (inner_conv, input_conv, read_conv, steps), conv_back = jax.vjp(
        conv_piece,
        inner_pre,
        small_pre,
        edge,
        taps_inner.astype(full),
        taps_input.astype(full),
        taps_read.astype(full),
        step_bias.astype(full),
    )
    rate = -jnp.exp(log_rate.astype(full))
    scan = Scan(inner_conv, steps, rate, input_conv, read_conv, own_segment, edge_segment[-1])
    first_state = state_forward(scan.end())
    scanned, block_states = scan.forward(first_state)

    def by_head(value):
        return value.reshape(rows, mixer_heads, MDIM)

    skip_full = jnp.repeat(skip_gain.astype(full), MDIM)[None, :]
    combined = scanned + skip_full * inner_conv
    gate_act = jax.nn.silu(gate_pre)
    united = combined * gate_act
    gated_gain = gain_gated.astype(full)[None, :]
    cot_own = lax.dynamic_slice_in_dim(cotangent, own_start, rows, 0)
    mix_grad = cot_own * own_valid.astype(low)
    gated_grad = right_dot(mix_grad, output_main)
    pair = jnp.stack(
        [jnp.sum(united * united, 1), jnp.sum(united * gated_gain * gated_grad, 1)], 0
    )
    for mask in orders[0]:
        pair = pair + head_swap(pair, mask)
    channels = inner_width * head_parts
    row_scale = lax.rsqrt(pair[0] / channels + epsilon)[:, None]
    row_total = pair[1][:, None]
    gated = (united * row_scale * gated_gain).astype(low)
    united_grad = (
        row_scale * gated_gain * gated_grad
        - united * row_scale * row_scale * row_scale * row_total / channels
    )
    combined_grad = united_grad * gate_act
    last_state_grad = state_backward(scan.start_grad(combined_grad))

    sigmoid_gate = jax.nn.sigmoid(gate_pre)
    gate_grad = united_grad * combined * sigmoid_gate * (1.0 + gate_pre * (1.0 - sigmoid_gate))
    grad_gated_gain = jnp.sum(gated_grad * united * row_scale, 0)
    grad_skip = jnp.sum(by_head(combined_grad * inner_conv), (0, 2))
    scan_grad, step_grad, log_grad, log_rows, input_grad, read_grad = scan.backward(
        combined_grad, block_states, last_state_grad
    )
    log_grad = log_grad - log_rows.T
    grad_rate = jnp.sum(log_grad * steps, 0) * rate
    (
        inner_grad,
        small_grad,
        edge_grad,
        grad_taps_x,
        grad_taps_b,
        grad_taps_c,
        grad_shift,
    ) = conv_back(
        (
            scan_grad + skip_full * combined_grad,
            input_grad,
            read_grad,
            step_grad + log_grad * rate[None, :],
        )
    )
    edge_back = state_backward(edge_grad)
    inner_grad = inner_grad.at[rows - reach :].add(edge_back[:, :inner_width])
    small_grad = small_grad.at[rows - reach :, mixer_heads:].add(edge_back[:, inner_width:])
    out_cut = [
        (
            value
            + good
            * sum_products(
                cut_rows(gated[index * middle : (index + 1) * middle], order, 0),
                lambda rows: plain_dot(rows, output_main),
                order,
                0,
            )[1]
        ).astype(low)
        for index, (value, good, order) in enumerate(zip(second_cut, valid_cut, orders))
    ]
    inner_low = jnp.concatenate([inner_grad, gate_grad], 1).astype(low)
    inner_low = hold(inner_low, *out_cut)
    small_low = small_grad.astype(low)
    def mixer_product(rows):
        return right_dot(rows[0], mixer_main) + right_dot(rows[1], small_main)

    mixer_parts, mixer_sum = [], []
    for index, order in enumerate(orders):
        part = slice(index * middle, (index + 1) * middle)
        pieces = zip(cut_rows(inner_low[part], order, 0), cut_rows(small_low[part], order, 0))
        away, total = sum_products(list(pieces), mixer_product, order, 0)
        mixer_parts.append(away)
        mixer_sum.append(total)
    inner_later = hold(inner_low, *mixer_parts)
    small_later = hold(small_low, *mixer_parts)

    def scatter(value, axis):
        return lax.psum_scatter(value.astype(low), ZED, scatter_dimension=axis, tiled=True)

    sum_output = scatter(left_dot(gated, hold(mix_grad, *mixer_parts)), 1)
    sum_mixer = scatter(left_dot(mixer_normed, inner_later), 0)
    upstream_cut = [value.astype(full) for value in cut(cot_own)]
    mixer_backs = [
        norm_back(value, mixer_gain, grad) for value, grad in zip(second_cut, mixer_sum)
    ]
    second_grad = [up + back[0] for up, back in zip(upstream_cut, mixer_backs)]
    grad_mixer_gain = mixer_backs[0][1] + mixer_backs[1][1]
    mlp_grad = [
        gather_rows((good * grad).astype(low), order, 0)
        for good, grad, order in zip(valid_cut, second_grad, orders)
    ]

    def gelu_part(value):
        return jax.nn.gelu(value, approximate=False)

    hidden_grad = [
        jax.vjp(gelu_part, pre)[1](right_dot(grad, mlp_proj))[0].astype(low)
        for pre, grad in zip(hidden_pre, mlp_grad)
    ]
    mlp_wide = jnp.concatenate([mlp_main, mlp_upper], 0)
    mlp_parts, mlp_sums = [], []
    for grad, order in zip(hidden_grad, orders):
        away, total = sum_products(
            cut_rows(grad, order, 0), lambda rows: right_dot(rows, mlp_wide), order, 0
        )
        mlp_parts.append(away)
        mlp_sums.append(total)
    middle_low = [value[:, width:].astype(low) for value in mlp_sums]
    mlp_backs = [
        norm_back(value, mlp_gain, total[:, :width] + right_dot(mid, mlp_down))
        for value, total, mid in zip(first_cut, mlp_sums, middle_low)
    ]
    first_grad = [grad + back[0] for grad, back in zip(second_grad, mlp_backs)]
    first_grad[0] = hold(first_grad[0], sum_output)
    mlp_grad_own = hold(jnp.concatenate(mlp_grad, 0), *mlp_parts)
    sum_mlp_output = scatter(left_dot(jnp.concatenate(activated, 0), mlp_grad_own), 1)
    grad_mlp_gain = mlp_backs[0][1] + mlp_backs[1][1]
    branch_halves = [
        gather_row16((good * grad).astype(low), order).reshape(rows, width)
        for good, grad, order in zip(valid_cut, first_grad, orders)
    ]

    attended_grad = jnp.concatenate(
        [right_dot(value, attn_proj).astype(low) for value in branch_halves], 0
    )
    attended_grad = hold(attended_grad, sum_mixer)
    query_back, key_back, value_back = attend_back(
        queries, keys, values, attended_grad, attended, lse, segment, lows
    )
    out_got = state_swap(jnp.stack(out_cut, 0))
    pre_grad = hold(rope_back(query_back, key_back, value_back, cosine, sine), out_got)
    main_wide = jnp.concatenate([main_near, main_far, up_wide], 0)
    joint = 2 * width
    def normed_product(part):
        return right_dot(part.reshape(-1, part.shape[2]), main_wide).reshape(2, -1, main_wide.shape[0])

    normed_parts, normed_totals = [], []
    for part, order in zip((pre_grad[:rows], pre_grad[rows:]), orders):
        pieces = cut_rows(part.reshape(2, middle, -1), order, 1)
        away, total = sum_products(pieces, normed_product, order, 1)
        normed_parts.append(away)
        normed_totals.append(total)
    normed_totals[0] = hold(normed_totals[0], sum_mlp_output)
    def swap_joint(value):
        return jnp.concatenate([swap_quarters(value[:, :joint]), value[:, joint:]], 1)

    normed_sums = [finish_state(total, swap_joint) for total in normed_totals]
    normed_sums[0] = hold(normed_sums[0], normed_sums[1], cost=100)
    pre_grad = hold(pre_grad, *normed_parts)
    cubes = pre_grad.reshape(2, 2, middle, -1)
    grad_own, grad_other = (
        lax.dynamic_index_in_dim(cubes, index, 1, False).reshape(rows, -1)
        for index in (state, 1 - state)
    )
    wide_grad = left_dot(red_own, grad_own) + left_dot(red_other, grad_other)
    up_grad = jnp.concatenate(
        [
            wide_grad[index * rank : (index + 1) * rank, index * half_cols : (index + 1) * half_cols]
            for index in range(3)
        ],
        1,
    )

    def main_grad(own, other, lower, index):
        part = slice(lower * quarter, (lower + 1) * quarter)
        main = left_dot(own[:, part], grad_own) + left_dot(other[:, part], grad_other)
        ups = lax.dynamic_slice_in_dim(up_grad, (place ^ index) * up_rows, up_rows, 0)
        return jnp.concatenate([main, ups], 0).astype(low)

    def by_dp(near, far):
        both = jnp.concatenate([jnp.where(dp == 0, near, far), jnp.where(dp == 0, far, near)], 0)
        return lax.psum_scatter(both, DP, scatter_dimension=0, tiled=True)

    beside = by_dp(main_grad(near_own, near_other, 1, 1), main_grad(far_own, far_other, 1, 3))
    main_total = by_dp(
        hold(main_grad(near_own, near_other, 0, 0), *normed_sums),
        main_grad(far_own, far_other, 0, 2),
    )
    beside_got = state_swap(hold(beside, *normed_sums))

    def spread(own, got, index):
        part = slice(index * half_cols, (index + 1) * half_cols)
        own, got = own[:, part].astype(full), got[:, part].astype(full)
        return jnp.concatenate(
            [jnp.where(state == 0, own, got), jnp.where(state == 0, got, own)], 1
        )

    lows_cut = [value[:, joint:].astype(low) for value in normed_sums]
    def by_order(value):
        bits = value.reshape((2,) * (len(orders[0])) + (piece, value.shape[1]))
        count = len(orders[0])
        turned = [0] + list(range(count - 1, 0, -1)) + [count, count + 1]
        return bits.transpose(turned).reshape(value.shape)

    lows_own = gather_rows(jnp.stack(lows_cut, 0), orders[0], 1)
    lows_own = [lows_own[0], by_order(lows_own[1])]
    lows_own = jnp.concatenate(lows_own, 0)
    def placed(value, axis):
        shape = list(value.shape)
        shape[axis] *= head_parts
        return lax.dynamic_update_slice_in_dim(
            jnp.zeros(shape, full), value, head * value.shape[axis], axis
        )

    small_main_grad = hold(left_dot(mixer_normed, small_later), *normed_totals)
    normed_cut = [
        lax.dynamic_slice_in_dim(value, chunk_of(order) * piece, piece, 0)
        for value, order in zip(mlp_normed, orders)
    ]
    mlp_down_grad = left_dot(jnp.concatenate(normed_cut, 0), jnp.concatenate(middle_low, 0))
    pair_grad = jnp.concatenate([small_main_grad[:, mixer_heads:], mlp_down_grad], 1)
    wide = pair_grad.shape[1]
    heads_grad = placed(jnp.stack([grad_shift, grad_rate, grad_skip]), 1)
    flat_sums = [
        placed(small_main_grad[:, :mixer_heads].T, 0),
        placed(grad_taps_x, 1),
        placed(grad_gated_gain, 0),
        grad_mlp_gain,
        grad_mixer_gain,
        jnp.concatenate([grad_taps_b, grad_taps_c], 1),
        jnp.pad(heads_grad.reshape(-1), (0, -heads_grad.size % wide)),
    ]
    packed = jnp.concatenate([value.reshape(-1, wide) for value in flat_sums], 0)
    lines = pair_grad.shape[0] // 8
    packed = jnp.pad(packed, ((0, -packed.shape[0] % lines), (0, 0)))
    pair_grad = jnp.concatenate([pair_grad, packed], 0)
    pair_grad = sum_rows(pair_grad, orders[0], 0)
    joined_backs = [
        norm_back(value, attn_gain, total[:, :joint] + right_dot(mid, down_wide))
        for value, total, mid in zip(joined_cut, normed_sums, lows_cut)
    ]
    grad_attn_gain = joined_backs[0][1] + joined_backs[1][1]

    def natural_columns(value):
        return jnp.concatenate(
            [
                lax.dynamic_slice_in_dim(value, (place ^ index) * quarter, quarter, -1)
                for index in range(4)
            ],
            -1,
        )

    input_cut = []
    for grad, back, own, got in zip(first_grad, joined_backs, out_cut, out_got):
        joined_grad = natural_columns(back[0])
        input_cut.append(
            jnp.concatenate(
                [
                    (joined_grad[:, :width] + grad).astype(low),
                    joined_grad[:, width:].astype(low),
                    jnp.where(state == 0, own, got),
                    jnp.where(state == 0, got, own),
                ],
                1,
            )
        )
    input_cut[0] = hold(input_cut[0], input_cut[1], lows_own, pair_grad, cost=100)
    input_cut[1] = hold(input_cut[1], lows_own, pair_grad)
    quads = []
    input_halves = []
    core = bit_of(orders[0][0])
    for value, order in zip(input_cut, orders):
        value = gather_rows(value, order[1:], 0)
        value = hold(value, beside_got)
        got = head_swap(value, order[0])
        input_halves += [value, got]
        quads += [(value, got), (got, value)]

    attn_grad = left_dot(attended_halves[0], branch_halves[0]) + left_dot(
        attended_halves[1], branch_halves[1]
    )
    out_attn = grad_pieces(hold(attn_grad.astype(low), *input_halves), 0)
    def settled(value):
        return hold(value, *input_halves).astype(full)

    mlp_normed_own = jnp.concatenate(mlp_normed, 0)
    hidden_grad_own = hold(jnp.concatenate(hidden_grad, 0), *normed_parts)
    out_output = settled(sum_output)
    out_mixer = settled(sum_mixer)
    out_mlp_output = settled(sum_mlp_output)
    out_mlp_input = settled(scatter(left_dot(mlp_normed_own, hidden_grad_own), 0))
    out_up_mlp = settled(scatter(left_dot(jnp.concatenate(mlp_red, 0), hidden_grad_own), 0))

    down_parts = [
        left_dot(
            lax.dynamic_slice_in_dim(value, index * quarter + head * part_a, part_a, 1), lows_own
        )
        for value in (near_own, far_own)
        for index in range(2)
    ]
    away = jnp.stack([down_parts[1], down_parts[3]], 0).astype(low)
    away = state_swap(hold(away, *input_halves)).astype(full)
    down_sum = down_parts[0] + away[0] + dp_swap((down_parts[2] + away[1]).astype(low))
    down_all = natural_heads(gather_rows(down_sum.astype(low)[None], orders[0], 0))
    down_all = down_all.reshape(quarter, 3 * rank)
    down_all = down_all.astype(full)
    out_downs = [down_all[:, index * rank : (index + 1) * rank] for index in range(3)]

    pair_grad = hold(pair_grad, *input_halves)
    pair_grad = pair_grad + state_swap(pair_grad)
    pair_grad = pair_grad + dp_swap(pair_grad)
    quads = [(hold(a, down_sum, pair_grad), b) for a, b in (quads[0], quads[2])]
    quads = [pair for a, b in quads for pair in ((a, b), (b, a))]

    def whole_rows(start):
        columns = slice(start, start + width)
        return [jnp.where(core == 0, a[:, columns], b[:, columns]) for a, b in quads]

    grad_hidden = jnp.concatenate(whole_rows(0), 0)
    grad_embedding = jnp.concatenate(whole_rows(width), 0)
    layer_out = jnp.concatenate(whole_rows(2 * width) + whole_rows(3 * width), 0)

    row = lax.broadcasted_iota(jnp.int32, (pair_grad.shape[0], 1), 0)
    in_main = chunk_of(orders[0]) * pair_grad.shape[0] + row < width
    down_m_squares = jnp.sum(jnp.where(in_main, jnp.square(pair_grad[:, 2 * states :]), 0.0))
    pair_grad = gather_rows(pair_grad.astype(low), orders[0], 0).astype(full)
    vector_grad = pair_grad[:width, : 2 * states]
    out_down_mlp = lax.dynamic_slice(pair_grad, (place * split_m, 2 * states), (split_m, rank))
    packed = pair_grad[width:]
    pieces = []
    for value in flat_sums:
        count = value.size // wide
        pieces.append(packed[:count].reshape(value.shape))
        packed = packed[count:]
    step_total, taps_x_total, gated_total, mlp_total, mixer_total, taps_total, head_total = pieces
    head_total = head_total[: heads_grad.size].reshape(heads_grad.shape)

    main_total = hold(main_total, *input_halves)
    out_all = [spread(main_total, beside_got, index) for index in range(3)]
    out_main = [value[:quarter] for value in out_all]
    out_up = [value[quarter:] for value in out_all]
    square_sum = jnp.sum(jnp.square(down_sum)) + 0.25 * down_m_squares
    for value in out_main + out_up + [out_attn, out_mlp_input, out_up_mlp, out_mlp_output]:
        square_sum = square_sum + jnp.sum(value * value)
    last = natural_columns(grad_attn_gain)
    last = jnp.concatenate([last, jnp.broadcast_to(square_sum, (rank,))]).reshape(-1, rank)
    for mask in orders[0]:
        last = last + head_swap(last, mask)
    last = last + state_swap(last)
    last = (last + dp_swap(last)).reshape(-1)
    attn_total, square_total = last[:joint], last[joint]

    def of_head(value, size):
        return lax.dynamic_slice_in_dim(value, head * size, size, value.ndim - 1)

    def of_place(value, size):
        return lax.dynamic_slice_in_dim(value, place * size, size)

    head_total = of_head(head_total, mixer_heads)
    out_step = lax.dynamic_slice(
        step_total, (head * mixer_heads, place * split_m), (mixer_heads, split_m)
    ).T
    return (
        layer_out,
        grad_hidden,
        grad_embedding,
        of_place(attn_total, split_a),
        out_main[0],
        out_main[1],
        out_main[2],
        out_downs[0],
        out_downs[1],
        out_downs[2],
        out_up[0],
        out_up[1],
        out_up[2],
        out_attn,
        of_place(mlp_total, split_m),
        out_mlp_input,
        out_down_mlp,
        out_up_mlp,
        out_mlp_output,
        of_place(mixer_total, split_m),
        out_mixer[:, :inner_width],
        out_mixer[:, inner_width:],
        out_step,
        vector_grad[:, :states],
        vector_grad[:, states:],
        of_head(taps_x_total, inner_width),
        taps_total[:, :states],
        taps_total[:, states:],
        head_total[0],
        head_total[1],
        head_total[2],
        of_head(gated_total, inner_width),
        out_output,
        jnp.sqrt(square_total),
    )


def pick_device(mesh):
    heads = mesh.shape[HEAD]
    per_head = DIN // HDIM // heads
    halves = mesh.shape[DP] == 2 and mesh.shape[STATE] == 2
    return fast_device if halves and heads & (heads - 1) == 0 and per_head % 2 == 0 else general_device


def solution(mesh):
    in_specs = (
        P(ZED, None),
        P(ZED, None),
        P(DP, None),
        P(DP, None),
        P(ZED),
        P(ZED, HEAD),
        P(ZED, HEAD),
        P(ZED, HEAD),
        P(ZED, None),
        P(ZED, None),
        P(ZED, None),
        P(ZED, HEAD),
        P(ZED, HEAD),
        P(ZED, HEAD),
        P(HEAD, ZED),
        P(ZED),
        P(ZED, HEAD),
        P(ZED, None),
        P(ZED, HEAD),
        P(HEAD, ZED),
        P(ZED),
        P(ZED, HEAD),
        P(ZED, HEAD),
        P(ZED, HEAD),
        P(),
        P(),
        P(None, HEAD),
        P(),
        P(),
        P(HEAD),
        P(HEAD),
        P(HEAD),
        P(HEAD),
        P(HEAD, ZED),
    )
    out_specs = (
        P(DP, None),
        P(ZED, None),
        P(ZED, None),
        P(ZED),
        P(ZED, HEAD),
        P(ZED, HEAD),
        P(ZED, HEAD),
        P(ZED, None),
        P(ZED, None),
        P(ZED, None),
        P(ZED, HEAD),
        P(ZED, HEAD),
        P(ZED, HEAD),
        P(HEAD, ZED),
        P(ZED),
        P(ZED, HEAD),
        P(ZED, None),
        P(ZED, HEAD),
        P(HEAD, ZED),
        P(ZED),
        P(ZED, HEAD),
        P(ZED, HEAD),
        P(ZED, HEAD),
        P(),
        P(),
        P(None, HEAD),
        P(),
        P(),
        P(HEAD),
        P(HEAD),
        P(HEAD),
        P(HEAD),
        P(HEAD, ZED),
        P(),
    )
    return jax.shard_map(
        pick_device(mesh), mesh=mesh, in_specs=in_specs, out_specs=out_specs, check_vma=False
    )
```
